128 devices in a mesh: row: 8 (over y_lo, x), col: 16 (over y_hi, z, core).
Axes of the slice: x: 4, y: 4 (y_hi: 2, y_lo: 2; y = y_hi * 2 + y_lo), z: 4, core: 2. Of those that a mesh axis runs over, the one named last changes fastest.
Arguments:
- spectra: float32 [2, 4, 30, 16, 512], P(None, None, None, 'col', 'row'), may hold values from -500 to 500
- counts: int32 [16, 512], P('col', 'row'), may hold values from 1 to 30
Outputs:
- stacks: float32 [16, 512, 9, 2, 4, 512], P('col', 'row')
The draws below stay inside these ranges and needn't reach their ends.
All inputs are finite; a program needn't handle non-finite values.
Results may differ from the reference program's by a relative error of at most 0.004.
Values may be sent and summed in bfloat16 or wider, within the bound.
A program may use at most 64 MiB of HBM per device.

```python
import math
import jax
import jax.numpy as jnp
from jax import lax

F = 4
S = 30
NBLK = 16
BW = 512
HOPS = 9


def common_counts(key):
    return jax.random.randint(jax.random.fold_in(key, 101), (NBLK, BW), 1, S + 1, jnp.int32)


def draw_counts(key, part):
    valid_counts = common_counts(key)
    return valid_counts


def draw_spectra(key, part):
    valid_counts = common_counts(key)
    key = jax.random.fold_in(key, 11)
    key_base = jax.random.fold_in(key, 0)
    key_seg = jax.random.fold_in(key, 1)
    key_bin = jax.random.fold_in(key, 2)
    key_gap = jax.random.fold_in(key, 4)
    key_pick = jax.random.fold_in(key, 5)
    shape = (2, F, S, NBLK, BW)
    base = jax.random.truncated_normal(key_base, -4.0, 4.0, shape, jnp.float32)
    seg_scale = jnp.exp(jax.random.uniform(key_seg, (1, 1, S, NBLK, BW), jnp.float32, 0.0, math.log(10.0)))
    bin_scale = jnp.exp(jax.random.uniform(key_bin, (1, F, 1, NBLK, BW), jnp.float32, 0.0, math.log(10.0)))
    gap_length = jax.random.randint(key_gap, (NBLK, BW), 1, max(2, S // 6) + 1, jnp.int32)
    gapped = jax.random.randint(key_pick, (NBLK, BW), 0, 3, jnp.int32) == 0
    gap_start = jnp.maximum(1, valid_counts - gap_length)
    segment = jnp.arange(S, dtype=jnp.int32).reshape(S, 1, 1)
    zeroed = gapped[None] & (segment >= gap_start[None]) & (segment < valid_counts[None])
    keep = jnp.where(zeroed, 0.0, 1.0).astype(jnp.float32)[None, None]
    return (base * seg_scale * bin_scale * keep).astype(jnp.float32)


def setup_inputs(seed: int = 0) -> dict:
    seeds = jax.random.split(jax.random.key(seed), 3)
    return {
        "spectra": draw_spectra(jax.random.fold_in(seeds[2], 71), 0),
        "counts": draw_counts(jax.random.fold_in(seeds[2], 71), 0),
    }


def reference(spectra, counts):
    power_mean = lax.optimization_barrier(jnp.mean(spectra * spectra, axis=(0, 1, 2)))
    segment = jnp.arange(S, dtype=jnp.int32).reshape(1, 1, S, 1, 1)
    validity = (segment < counts[None, None, None]).astype(jnp.float32)
    whitened = (spectra * lax.rsqrt(power_mean + 1e-06) * validity).astype(jnp.bfloat16)
    widened = whitened.astype(jnp.float32)
    count_float = counts.astype(jnp.float32)

    def one_block(block_index):
        own_part = lax.dynamic_index_in_dim(widened, block_index, 3, keepdims=False)
        picked = (block_index + jnp.arange(HOPS, dtype=jnp.int32)) % NBLK
        partner = jnp.take(widened, picked, axis=3)
        highest = lax.Precision.HIGHEST
        real_part = jnp.einsum('fsw,fskv->wkfv', own_part[0], partner[0], precision=highest)
        real_part = real_part + jnp.einsum('fsw,fskv->wkfv', own_part[1], partner[1], precision=highest)
        imag_part = jnp.einsum('fsw,fskv->wkfv', own_part[1], partner[0], precision=highest)
        imag_part = imag_part - jnp.einsum('fsw,fskv->wkfv', own_part[0], partner[1], precision=highest)
        own_count = lax.dynamic_index_in_dim(count_float, block_index, 0, keepdims=False)
        partner_count = jnp.take(count_float, picked, axis=0)
        divisor = jnp.minimum(own_count[:, None, None], partner_count[None])
        stacked = jnp.stack([real_part, imag_part], axis=2)
        return stacked / divisor[:, :, None, None, :]
    return lax.map(one_block, jnp.arange(NBLK, dtype=jnp.int32))
```

```python
import functools

import jax
import jax.numpy as jnp
from jax import lax
from jax.experimental import pallas as pl
from jax.experimental.pallas import tpu as pltpu
from jax.sharding import PartitionSpec as P

MESH = pl.DeviceIdType.MESH
BINS = 4
SEGS = 30
USED = 2 * BINS * SEGS
COLS = 256
WIDTH = 64
HALF = 32
HOPS = 9
DMAS = 96


def gather_kernel(spec, cnt, g, lhs, rci, own, ssem, rsem, lsem):
    r, d = lax.axis_index("row"), lax.axis_index("col")
    x, ylo = r % 4, r // 4
    c, q = d % 2, d // 2
    z, yhi = q % 4, q // 4

    def dev(x_, ylo_, q_, c_):
        return (ylo_ * 4 + x_, q_ * 2 + c_)

    sibling = dev(x, ylo, q, 1 - c)
    other = 1 - ylo

    def at_y(rel):
        return other if rel else ylo

    plane = [(0, 1)] + [(j, rel) for j in range(1, 5) for rel in (0, 1)]

    barrier = pltpu.get_barrier_semaphore()
    sources = [dev(x, at_y(rel), (q + j) % 8, c) for j, rel in plane]
    sources += [dev((x + i) % 4, ylo, q, c) for i in (1, 2, 3)]
    sources += [dev(x, ylo, yhi * 4 + (z + e) % 4, c) for e in (1, 2, 3)]
    sources += [sibling]
    for source in sources:
        pl.semaphore_signal(barrier, inc=1, device_id=source, device_id_type=MESH)

    raw = spec[...]
    power = jnp.sum(raw * raw, axis=0, keepdims=True) / float(USED)
    row = lax.broadcasted_iota(jnp.int32, (USED, WIDTH), 0)
    group = jnp.zeros((USED, WIDTH), jnp.int32)
    for n in range(1, 2 * BINS):
        group = group + (row >= n * SEGS).astype(jnp.int32)
    valid = (row - SEGS * group < cnt[...]).astype(jnp.float32)
    white = raw * lax.rsqrt(power + 1e-6) * valid
    white = white.astype(jnp.bfloat16).astype(jnp.float32)
    count = cnt[...].astype(jnp.float32)
    pad = jnp.zeros((COLS - USED - 8, WIDTH), jnp.float32)
    first = lax.broadcasted_iota(jnp.int32, (8, WIDTH), 0) == 0
    tail = jnp.where(first, count, 0.0)
    straight = jnp.concatenate([white, tail, pad], axis=0).T
    own[...] = straight.astype(jnp.bfloat16)

    copies = []

    def remote(src, dst, device):
        n = len(copies)
        copy = pltpu.make_async_remote_copy(
            src_ref=src,
            dst_ref=dst,
            send_sem=ssem.at[n],
            recv_sem=rsem.at[n],
            device_id=device,
            device_id_type=MESH,
        )
        copies.append(copy)
        copy.start()
        return copy

    lo, hi = pl.ds(0, HALF), pl.ds(HALF, HALF)

    pl.semaphore_wait(barrier, len(sources))
    local = pltpu.make_async_copy(own, g.at[0, ylo, x], lsem)
    local.start()
    b1 = [
        remote(own.at[hi], g.at[0, ylo, x, hi], dev((x + i) % 4, ylo, q, c))
        for i in (1, 3, 2)
    ]
    a1 = {}
    for j, rel in plane:
        a1[j, rel] = remote(
            own.at[lo], g.at[2 * j, ylo, x, lo], dev(x, at_y(rel), (q - j) % 8, c)
        )

    swapped = jnp.concatenate(
        [white[USED // 2 :], -white[: USED // 2], jnp.zeros((COLS - USED, WIDTH), jnp.float32)],
        axis=0,
    ).T
    shape = (WIDTH, 8, COLS)
    sub = lax.broadcasted_iota(jnp.int32, (8, COLS), 0)
    lane = lax.broadcasted_iota(jnp.int32, (8, COLS), 1)
    low = (sub % BINS) * SEGS
    here = ((lane >= low) & (lane < low + SEGS)) | (
        (lane >= low + USED // 2) & (lane < low + USED // 2 + SEGS)
    )
    pick = jnp.where(
        (sub < BINS)[None],
        jnp.broadcast_to(straight[:, None, :], shape),
        jnp.broadcast_to(swapped[:, None, :], shape),
    )
    pick = jnp.where(here[None], pick, 0.0)
    lhs[0 : WIDTH * 8, :] = pick.reshape(WIDTH * 8, COLS).astype(jnp.bfloat16)
    sel = lax.broadcasted_iota(jnp.int32, (16, COLS), 1) == USED
    lhs[WIDTH * 8 :, :] = sel.astype(jnp.float32).astype(jnp.bfloat16)
    rci[...] = jnp.broadcast_to(1.0 / straight[:, USED : USED + 1], (WIDTH, 128))

    local.wait()

    for copy in b1:
        copy.wait_recv()
    b2 = [
        remote(
            g.at[0, ylo, :, hi],
            g.at[2 * j, ylo, :, hi],
            dev(x, at_y(rel), (q - j) % 8, c),
        )
        for j, rel in ((4, 1), (0, 1), (4, 0))
    ]

    right, left = dev((x + 1) % 4, ylo, q, c), dev((x + 3) % 4, ylo, q, c)
    a2 = {}
    for j in range(5):
        for rel in (0, 1):
            if (j, rel) in a1:
                a1[j, rel].wait_recv()
        piece = g.at[2 * j, :, x, lo]
        a2[j] = (remote(piece, piece, right), remote(piece, piece, left))

    for copy in b2:
        copy.wait_recv()
    b3 = []
    for e in (1, 3, 2):
        zt = (z + 4 - e) % 4
        slot = jnp.where(zt > z, 8, 0)
        b3.append(
            remote(g.at[slot, :, :, hi], g.at[2 * e, :, :, hi], dev(x, ylo, yhi * 4 + zt, c))
        )

    def share(src_j, index):
        src = g.at[(2 * src_j,) + index]
        dst = g.at[(2 * src_j - 1 + 2 * c,) + index]
        return remote(src, dst, sibling)

    end_j = 4 * (1 - c)
    shared = [share(end_j, (slice(None), slice(None), hi))]
    for j in (1, 2, 3):
        shared.append(share(j, (slice(None), x, lo)))
    shared.append(share(end_j, (slice(None), x, lo)))

    fwd = {}
    xl, xr, xo = (x + 3) % 4, (x + 1) % 4, (x + 2) % 4
    for j in (0, 1, 2, 3, 4):
        for copy in a2[j]:
            copy.wait_recv()
        from_left = g.at[2 * j, 0, xl, lo]
        from_right = g.at[2 * j, 1, xr, lo]
        fwd[j] = (remote(from_left, from_left, right), remote(from_right, from_right, left))
        if 1 <= j <= 3:
            shared.append(share(j, (slice(None), xl, lo)))
            shared.append(share(j, (slice(None), xr, lo)))
    shared.append(share(end_j, (slice(None), xl, lo)))
    shared.append(share(end_j, (slice(None), xr, lo)))

    for copy, e in zip(b3, (1, 3, 2)):
        copy.wait_recv()
        shared.append(share(e, (slice(None), slice(None), hi)))
    for j in (0, 1, 2, 3, 4):
        for copy in fwd[j]:
            copy.wait_recv()
        if 1 <= j <= 3:
            shared.append(share(j, (slice(None), xo, lo)))
    shared.append(share(end_j, (slice(None), xo, lo)))

    for copy in shared:
        copy.wait_recv()
    for copy in copies:
        copy.wait_send()


def stack_kernel(g, lhs, rci, out):
    result = lax.dot_general(
        lhs[...], g[0], (((1,), (1,)), ((), ())), preferred_element_type=jnp.float32
    )
    rows = WIDTH * 8
    recip = 1.0 / result[rows : rows + 1, :]
    mine = jnp.broadcast_to(rci[:, 0:1], (WIDTH, 512))
    scale = jnp.maximum(mine, jnp.broadcast_to(recip, (WIDTH, 512)))
    value = result[:rows].reshape(WIDTH, 8, 512) * scale[:, None, :]
    out[:, 0, 0] = value[:, 0:BINS]
    out[:, 0, 1] = value[:, BINS:]


def per_device(spectra, counts):
    spec = spectra.reshape(USED, WIDTH)
    vmem = pl.BlockSpec(memory_space=pltpu.VMEM)
    g, lhs, rci = pl.pallas_call(
        gather_kernel,
        name="whiten_gather",
        out_shape=(
            jax.ShapeDtypeStruct((HOPS, 2, 4, WIDTH, COLS), jnp.bfloat16),
            jax.ShapeDtypeStruct((WIDTH * 8 + 16, COLS), jnp.bfloat16),
            jax.ShapeDtypeStruct((WIDTH, 128), jnp.float32),
        ),
        in_specs=[vmem, vmem],
        out_specs=(pl.BlockSpec(memory_space=pl.ANY), vmem, vmem),
        scratch_shapes=[
            pltpu.VMEM((WIDTH, COLS), jnp.bfloat16),
            pltpu.SemaphoreType.DMA((DMAS,)),
            pltpu.SemaphoreType.DMA((DMAS,)),
            pltpu.SemaphoreType.DMA,
        ],
        compiler_params=pltpu.CompilerParams(
            collective_id=0, has_side_effects=True, vmem_limit_bytes=8 * 2**20
        ),
    )(spec, counts)
    g = g.reshape(HOPS, 512, COLS)
    out = pl.pallas_call(
        stack_kernel,
        name="stack",
        grid=(HOPS,),
        out_shape=jax.ShapeDtypeStruct((WIDTH, HOPS, 2, BINS, 512), jnp.float32),
        in_specs=[
            pl.BlockSpec((1, 512, COLS), lambda k: (k, 0, 0)),
            pl.BlockSpec((WIDTH * 8 + 16, COLS), lambda k: (0, 0)),
            pl.BlockSpec((WIDTH, 128), lambda k: (0, 0)),
        ],
        out_specs=pl.BlockSpec((WIDTH, 1, 2, BINS, 512), lambda k: (0, k, 0, 0, 0)),
        compiler_params=pltpu.CompilerParams(vmem_limit_bytes=16 * 2**20),
        cost_estimate=pl.CostEstimate(
            flops=2 * 528 * COLS * 512 * HOPS,
            bytes_accessed=HOPS * 512 * (COLS * 2 + WIDTH * 8 * 4),
            transcendentals=0,
        ),
    )(g, lhs, rci)
    return out[None]


def solution(mesh):
    return jax.shard_map(
        per_device,
        mesh=mesh,
        in_specs=(P(None, None, None, "col", "row"), P("col", "row")),
        out_specs=P("col", "row", None, None, None, None),
        check_vma=False,
    )
```

```python
import functools

import jax
import jax.numpy as jnp
from jax import lax
from jax.experimental import pallas as pl
from jax.experimental.pallas import tpu as pltpu
from jax.sharding import PartitionSpec as P

MESH = pl.DeviceIdType.MESH
BINS = 4
SEGS = 30
USED = 2 * BINS * SEGS
COLS = 256
WIDTH = 64
HALF = 32
HOPS = 9
SEL = 16
DMAS = 96


def gather_kernel(spec_in, cnt_in, g, lhs, rci, spec, cnt, own, ssem, rsem, lsem):
    fetch = (
        pltpu.make_async_copy(spec_in, spec, lsem.at[1]),
        pltpu.make_async_copy(cnt_in, cnt, lsem.at[2]),
    )
    for copy in fetch:
        copy.start()
    r, d = lax.axis_index("row"), lax.axis_index("col")
    x, ylo = r % 4, r // 4
    c, q = d % 2, d // 2
    z, yhi = q % 4, q // 4

    def dev(x_, ylo_, q_, c_):
        return (ylo_ * 4 + x_, q_ * 2 + c_)

    sibling = dev(x, ylo, q, 1 - c)
    other = 1 - ylo

    def at_y(rel):
        return other if rel else ylo

    plane = [(0, 1)] + [(j, rel) for j in range(1, 5) for rel in (0, 1)]

    barrier = pltpu.get_barrier_semaphore()
    sources = [dev(x, at_y(rel), (q + j) % 8, c) for j, rel in plane]
    sources += [dev((x + i) % 4, ylo, q, c) for i in (1, 2, 3)]
    sources += [dev(x, ylo, yhi * 4 + (z + e) % 4, c) for e in (1, 2, 3)]
    sources += [sibling]
    for source in sources:
        pl.semaphore_signal(barrier, inc=1, device_id=source, device_id_type=MESH)

    for copy in fetch:
        copy.wait()
    raw = spec[...]
    power = jnp.sum(raw * raw, axis=0, keepdims=True) / float(USED)
    row = lax.broadcasted_iota(jnp.int32, (USED, WIDTH), 0)
    group = jnp.zeros((USED, WIDTH), jnp.int32)
    for n in range(1, 2 * BINS):
        group = group + (row >= n * SEGS).astype(jnp.int32)
    valid = (row - SEGS * group < cnt[...]).astype(jnp.float32)
    white = raw * lax.rsqrt(power + 1e-6) * valid
    white = white.astype(jnp.bfloat16).astype(jnp.float32)
    count = cnt[...].astype(jnp.float32)
    pad = jnp.zeros((COLS - USED - 8, WIDTH), jnp.float32)
    first = lax.broadcasted_iota(jnp.int32, (8, WIDTH), 0) == 0
    tail = jnp.where(first, count, 0.0)
    straight = jnp.concatenate([white, tail, pad], axis=0).T
    own[...] = straight.astype(jnp.bfloat16)

    copies = []

    def remote(src, dst, device):
        n = len(copies)
        copy = pltpu.make_async_remote_copy(
            src_ref=src,
            dst_ref=dst,
            send_sem=ssem.at[n],
            recv_sem=rsem.at[n],
            device_id=device,
            device_id_type=MESH,
        )
        copies.append(copy)
        copy.start()
        return copy

    lo, hi = pl.ds(0, HALF), pl.ds(HALF, HALF)

    pl.semaphore_wait(barrier, len(sources))
    local = pltpu.make_async_copy(own, g.at[0, ylo, x], lsem.at[0])
    local.start()
    b1 = [
        remote(own.at[hi], g.at[0, ylo, x, hi], dev((x + i) % 4, ylo, q, c))
        for i in (1, 3, 2)
    ]
    a1 = {}
    for j, rel in plane:
        a1[j, rel] = remote(
            own.at[lo], g.at[2 * j, ylo, x, lo], dev(x, at_y(rel), (q - j) % 8, c)
        )

    swapped = jnp.concatenate(
        [white[USED // 2 :], -white[: USED // 2], jnp.zeros((COLS - USED, WIDTH), jnp.float32)],
        axis=0,
    ).T
    shape = (WIDTH, 8, COLS)
    sub = lax.broadcasted_iota(jnp.int32, (8, COLS), 0)
    lane = lax.broadcasted_iota(jnp.int32, (8, COLS), 1)
    low = (sub % BINS) * SEGS
    here = ((lane >= low) & (lane < low + SEGS)) | (
        (lane >= low + USED // 2) & (lane < low + USED // 2 + SEGS)
    )
    pick = jnp.where(
        (sub < BINS)[None],
        jnp.broadcast_to(straight[:, None, :], shape),
        jnp.broadcast_to(swapped[:, None, :], shape),
    )
    pick = jnp.where(here[None], pick, 0.0)
    sel = lax.broadcasted_iota(jnp.int32, (SEL, COLS), 1) == USED
    lhs[:SEL, :] = sel.astype(jnp.float32).astype(jnp.bfloat16)
    lhs[SEL:, :] = pick.reshape(WIDTH * 8, COLS).astype(jnp.bfloat16)
    mine = jnp.broadcast_to(1.0 / straight[:, USED : USED + 1], (WIDTH, 128))
    rci[...] = jnp.broadcast_to(mine[:, None, :], (WIDTH, 8, 128)).reshape(WIDTH * 8, 128)

    local.wait()

    for copy in b1:
        copy.wait_recv()
    b2 = [
        remote(
            g.at[0, ylo, :, hi],
            g.at[2 * j, ylo, :, hi],
            dev(x, at_y(rel), (q - j) % 8, c),
        )
        for j, rel in ((4, 1), (0, 1), (4, 0))
    ]

    right, left = dev((x + 1) % 4, ylo, q, c), dev((x + 3) % 4, ylo, q, c)
    a2 = {}
    for j in range(5):
        for rel in (0, 1):
            if (j, rel) in a1:
                a1[j, rel].wait_recv()
        piece = g.at[2 * j, :, x, lo]
        a2[j] = (remote(piece, piece, right), remote(piece, piece, left))

    for copy in b2:
        copy.wait_recv()
    b3 = []
    for e in (1, 3, 2):
        zt = (z + 4 - e) % 4
        slot = jnp.where(zt > z, 8, 0)
        b3.append(
            remote(g.at[slot, :, :, hi], g.at[2 * e, :, :, hi], dev(x, ylo, yhi * 4 + zt, c))
        )

    def share(src_j, index):
        src = g.at[(2 * src_j,) + index]
        dst = g.at[(2 * src_j - 1 + 2 * c,) + index]
        return remote(src, dst, sibling)

    end_j = 4 * (1 - c)
    shared = [share(end_j, (slice(None), slice(None), hi))]
    for j in (1, 2, 3):
        shared.append(share(j, (slice(None), x, lo)))
    shared.append(share(end_j, (slice(None), x, lo)))

    fwd = {}
    xl, xr, xo = (x + 3) % 4, (x + 1) % 4, (x + 2) % 4
    for j in (0, 1, 2, 3, 4):
        for copy in a2[j]:
            copy.wait_recv()
        from_left = g.at[2 * j, 0, xl, lo]
        from_right = g.at[2 * j, 1, xr, lo]
        fwd[j] = (remote(from_left, from_left, right), remote(from_right, from_right, left))
        if 1 <= j <= 3:
            shared.append(share(j, (slice(None), xl, lo)))
            shared.append(share(j, (slice(None), xr, lo)))
    shared.append(share(end_j, (slice(None), xl, lo)))
    shared.append(share(end_j, (slice(None), xr, lo)))

    for copy, e in zip(b3, (1, 3, 2)):
        copy.wait_recv()
        shared.append(share(e, (slice(None), slice(None), hi)))
    for j in (0, 1, 2, 3, 4):
        for copy in fwd[j]:
            copy.wait_recv()
        if 1 <= j <= 3:
            shared.append(share(j, (slice(None), xo, lo)))
    shared.append(share(end_j, (slice(None), xo, lo)))

    for copy in shared:
        copy.wait_recv()
    for copy in copies:
        copy.wait_send()


def stack_kernel(g, lhs, rci, out, stage, sems):
    mine = rci[...]

    def to_out(k):
        return pltpu.make_async_copy(stage.at[k], out.at[:, k], sems.at[k])

    @pl.loop(0, HOPS)
    def _(k):
        for n in (0, 1):
            result = lax.dot_general(
                lhs[...],
                g[k, n * 256 : (n + 1) * 256, :],
                (((1,), (1,)), ((), ())),
                preferred_element_type=jnp.float32,
            )
            recip = 1.0 / result[0:1]
            for t in (0, 1):
                lanes = slice(t * 128, (t + 1) * 128)
                scale = jnp.maximum(mine, recip[:, lanes])
                value = (result[SEL:, lanes] * scale).reshape(WIDTH, 8, 128)
                columns = slice(n * 256 + t * 128, n * 256 + (t + 1) * 128)
                stage[k, :, 0, :, columns] = value[:, :BINS]
                stage[k, :, 1, :, columns] = value[:, BINS:]
        to_out(k).start()

    @pl.loop(0, HOPS)
    def _(k):
        to_out(k).wait()


def per_device(spectra, counts):
    spec = spectra.reshape(USED, WIDTH)
    vmem = pl.BlockSpec(memory_space=pltpu.VMEM)
    hbm = pl.BlockSpec(memory_space=pltpu.HBM)
    g, lhs, rci = pl.pallas_call(
        gather_kernel,
        name="whiten_gather",
        out_shape=(
            jax.ShapeDtypeStruct((HOPS, 2, 4, WIDTH, COLS), jnp.bfloat16),
            jax.ShapeDtypeStruct((SEL + WIDTH * 8, COLS), jnp.bfloat16),
            jax.ShapeDtypeStruct((WIDTH * 8, 128), jnp.float32),
        ),
        in_specs=[hbm, hbm],
        out_specs=(vmem, vmem, vmem),
        scratch_shapes=[
            pltpu.VMEM((USED, WIDTH), jnp.float32),
            pltpu.VMEM((1, WIDTH), jnp.int32),
            pltpu.VMEM((WIDTH, COLS), jnp.bfloat16),
            pltpu.SemaphoreType.DMA((DMAS,)),
            pltpu.SemaphoreType.DMA((DMAS,)),
            pltpu.SemaphoreType.DMA((3,)),
        ],
        compiler_params=pltpu.CompilerParams(
            collective_id=0, has_side_effects=True, vmem_limit_bytes=16 * 2**20
        ),
    )(*(pltpu.with_memory_space_constraint(a, pltpu.HBM) for a in (spec, counts)))
    g = g.reshape(HOPS, 512, COLS)
    out = pl.pallas_call(
        stack_kernel,
        name="stack",
        out_shape=jax.ShapeDtypeStruct((WIDTH, HOPS, 2, BINS, 512), jnp.float32),
        in_specs=[vmem, vmem, vmem],
        out_specs=hbm,
        scratch_shapes=[
            pltpu.VMEM((HOPS, WIDTH, 2, BINS, 512), jnp.float32),
            pltpu.SemaphoreType.DMA((HOPS,)),
        ],
        compiler_params=pltpu.CompilerParams(vmem_limit_bytes=24 * 2**20),
        cost_estimate=pl.CostEstimate(
            flops=2 * (SEL + WIDTH * 8) * COLS * 512 * HOPS,
            bytes_accessed=HOPS * 512 * (COLS * 2 + WIDTH * 8 * 4),
            transcendentals=0,
        ),
    )(g, lhs, rci)
    return out[None]


def solution(mesh):
    return jax.shard_map(
        per_device,
        mesh=mesh,
        in_specs=(P(None, None, None, "col", "row"), P("col", "row")),
        out_specs=P("col", "row", None, None, None, None),
        check_vma=False,
    )
```

```python
import functools

import jax
import jax.numpy as jnp
from jax import lax
from jax.experimental import pallas as pl
from jax.experimental.pallas import tpu as pltpu
from jax.sharding import PartitionSpec as P

MESH = pl.DeviceIdType.MESH
BINS = 4
SEGS = 30
USED = 2 * BINS * SEGS
COLS = 256
WIDTH = 64
HALF = 32
HOPS = 9
SEL = 16
DMAS = 108
Z_TWO = 104


def gather_kernel(spec_in, cnt_in, g, lhs, rci, spec, cnt, own, ssem, rsem, lsem):
    fetch = (
        pltpu.make_async_copy(spec_in, spec, lsem.at[1]),
        pltpu.make_async_copy(cnt_in, cnt, lsem.at[2]),
    )
    for copy in fetch:
        copy.start()
    r, d = lax.axis_index("row"), lax.axis_index("col")
    x, ylo = r % 4, r // 4
    c, q = d % 2, d // 2
    z, yhi = q % 4, q // 4

    def dev(x_, ylo_, q_, c_):
        return (ylo_ * 4 + x_, q_ * 2 + c_)

    sibling = dev(x, ylo, q, 1 - c)
    across = 1 - ylo
    pair = dev(x, across, q, c)
    far = dev(x, across, (q + 4) % 8, c)
    at_x = [dev((x + i) % 4, ylo, q, c) for i in range(4)]
    right, left = at_x[1], at_x[3]
    below = dev(x, ylo, yhi * 4 + (z + 3) % 4, c)
    above = dev(x, ylo, yhi * 4 + (z + 1) % 4, c)

    barrier = pltpu.get_barrier_semaphore()
    sources = [at_x[1], at_x[2], at_x[3], pair, far, below, above, sibling]
    for source in sources:
        pl.semaphore_signal(barrier, inc=1, device_id=source, device_id_type=MESH)

    for copy in fetch:
        copy.wait()
    raw = spec[...]
    power = jnp.sum(raw * raw, axis=0, keepdims=True) / float(USED)
    row = lax.broadcasted_iota(jnp.int32, (USED, WIDTH), 0)
    group = jnp.zeros((USED, WIDTH), jnp.int32)
    for n in range(1, 2 * BINS):
        group = group + (row >= n * SEGS).astype(jnp.int32)
    valid = (row - SEGS * group < cnt[...]).astype(jnp.float32)
    white = raw * lax.rsqrt(power + 1e-6) * valid
    white = white.astype(jnp.bfloat16).astype(jnp.float32)
    count = cnt[...].astype(jnp.float32)
    pad = jnp.zeros((COLS - USED - 8, WIDTH), jnp.float32)
    first = lax.broadcasted_iota(jnp.int32, (8, WIDTH), 0) == 0
    tail = jnp.where(first, count, 0.0)
    straight = jnp.concatenate([white, tail, pad], axis=0).T
    own[...] = straight.astype(jnp.bfloat16)

    started = []

    def plan(src, dst, device):
        n = len(started)
        copy = pltpu.make_async_remote_copy(
            src_ref=src,
            dst_ref=dst,
            send_sem=ssem.at[n],
            recv_sem=rsem.at[n],
            device_id=device,
            device_id_type=MESH,
        )
        started.append((copy, None))
        return copy

    def remote(src, dst, device):
        copy = plan(src, dst, device)
        copy.start()
        return copy

    def start_if(cond, copy):
        pl.when(cond)(copy.start)

    def share(j, index):
        src = g.at[(2 * j,) + index]
        dst = g.at[(2 * j - 1 + 2 * c,) + index]
        return remote(src, dst, sibling)

    lo, hi = pl.ds(0, HALF), pl.ds(HALF, HALF)
    both = slice(None)
    xs = [(x + i) % 4 for i in range(4)]
    row_of = (ylo, across)
    end_j = 4 * (1 - c)
    down_own, up_own = z >= 1, z == 3
    taken = {1: jnp.where(down_own, 0, 8), 3: jnp.where(up_own, 0, 8)}
    own_block = {1: down_own, 3: up_own}
    z_to = {1: below, 3: above}

    def z_plan(e, rel, index):
        return plan(
            g.at[(taken[e], row_of[rel]) + index], g.at[(2 * e, row_of[rel]) + index], z_to[e]
        )

    z_lo = {(e, rel): z_plan(e, rel, (x, lo)) for e in (1, 3) for rel in (0, 1)}
    z_hi = {(e, rel): z_plan(e, rel, (both, hi)) for e in (1, 3) for rel in (0, 1)}

    def x_send(j, rel):
        piece = g.at[2 * j, row_of[rel], x, lo]
        return (remote(piece, piece, right), remote(piece, piece, left))

    def x_forward(j, rel):
        piece = g.at[2 * j, row_of[rel], xs[1 if rel else 3], lo]
        return remote(piece, piece, left if rel else right)

    pl.semaphore_wait(barrier, len(sources))
    x_own = {i: remote(own, g.at[0, ylo, x], at_x[i]) for i in (1, 3, 2)}
    y_pair = {0: remote(own, g.at[0, ylo, x], pair)}
    y_far = {0: remote(own, g.at[8, ylo, x], far)}
    local = pltpu.make_async_copy(own, g.at[0, ylo, x], lsem.at[0])
    local.start()

    swapped = jnp.concatenate(
        [white[USED // 2 :], -white[: USED // 2], jnp.zeros((COLS - USED, WIDTH), jnp.float32)],
        axis=0,
    ).T
    shape = (WIDTH, 8, COLS)
    sub = lax.broadcasted_iota(jnp.int32, (8, COLS), 0)
    lane = lax.broadcasted_iota(jnp.int32, (8, COLS), 1)
    low = (sub % BINS) * SEGS
    here = ((lane >= low) & (lane < low + SEGS)) | (
        (lane >= low + USED // 2) & (lane < low + USED // 2 + SEGS)
    )
    pick = jnp.where(
        (sub < BINS)[None],
        jnp.broadcast_to(straight[:, None, :], shape),
        jnp.broadcast_to(swapped[:, None, :], shape),
    )
    pick = jnp.where(here[None], pick, 0.0)
    sel = lax.broadcasted_iota(jnp.int32, (SEL, COLS), 1) == USED
    lhs[:SEL, :] = sel.astype(jnp.float32).astype(jnp.bfloat16)
    lhs[SEL:, :] = pick.reshape(WIDTH * 8, COLS).astype(jnp.bfloat16)
    mine = jnp.broadcast_to(1.0 / straight[:, USED : USED + 1], (WIDTH, 128))
    rci[...] = jnp.broadcast_to(mine[:, None, :], (WIDTH, 8, 128)).reshape(WIDTH * 8, 128)

    local.wait()
    for e in (1, 3):
        start_if(own_block[e], z_lo[e, 0])

    for i in (1, 3):
        x_own[4 - i].wait_recv()
        piece = (ylo, xs[i], hi)
        y_pair[i] = remote(g.at[(0,) + piece], g.at[(0,) + piece], pair)
        y_far[i] = remote(g.at[(0,) + piece], g.at[(8,) + piece], far)
    y_pair[0].wait_recv()
    y_far[0].wait_recv()
    piece = (across, x)
    y_two = {0: remote(g.at[(0,) + piece], g.at[(8,) + piece], far)}
    for e in (1, 3):
        z_lo[e, 1].start()
    x_sent = {(j, 1): x_send(j, 1) for j in (0, 4)}
    x_own[2].wait_recv()
    piece = (ylo, xs[2], hi)
    y_pair[2] = remote(g.at[(0,) + piece], g.at[(0,) + piece], pair)
    y_far[2] = remote(g.at[(0,) + piece], g.at[(8,) + piece], far)
    for e in (1, 3):
        start_if(own_block[e], z_hi[e, 0])

    for i in (1, 3, 2):
        y_pair[i].wait_recv()
        y_far[i].wait_recv()
        piece = (across, xs[i], hi)
        if i == 1:
            y_two[i] = remote(g.at[(0,) + piece], g.at[(8,) + piece], far)
        else:
            y_two[i] = remote(g.at[(8,) + piece], g.at[(8,) + piece], pair)
    for e in (1, 3):
        z_hi[e, 1].start()
    y_two[0].wait_recv()
    for e in (1, 3):
        start_if(jnp.logical_not(own_block[e]), z_lo[e, 0])
    x_sent[4, 0] = x_send(4, 0)
    for i in (1, 2, 3):
        y_two[i].wait_recv()
    for e in (1, 3):
        start_if(jnp.logical_not(own_block[e]), z_hi[e, 0])
    shared = [share(end_j, (both, x, lo)), share(end_j, (both, both, hi))]

    goes = {(1, 0): z >= 1, (1, 1): z == 1, (3, 1): z <= 2, (3, 0): z == 2}

    def z_forward(e, rel, index):
        src = g.at[(2 * e, row_of[rel]) + index]
        dst = g.at[(4, row_of[rel]) + index]
        copy = pltpu.make_async_remote_copy(
            src_ref=src,
            dst_ref=dst,
            send_sem=ssem.at[len(started)],
            recv_sem=rsem.at[Z_TWO + 2 * rel + (0 if index[0] is x else 1)],
            device_id=z_to[e],
            device_id_type=MESH,
        )
        started.append((copy, goes[e, rel]))
        start_if(goes[e, rel], copy)
        return copy

    z_two_lo, z_two_hi = {}, {}
    for e, rel in ((1, 0), (3, 1), (1, 1), (3, 0)):
        z_lo[e, rel].wait_recv()
        z_two_lo[rel] = z_forward(e, rel, (x, lo))
        x_sent[(e, rel)] = x_send(e, rel)
    x_gone = {}
    for j, rel in ((0, 1), (4, 1), (4, 0)):
        for copy in x_sent[j, rel]:
            copy.wait_recv()
        x_gone[j, rel] = x_forward(j, rel)
    for e, rel in ((1, 0), (3, 1), (1, 1), (3, 0)):
        z_hi[e, rel].wait_recv()
        z_two_hi[rel] = z_forward(e, rel, (both, hi))
        shared.append(share(e, (row_of[rel], both, hi)))
    for rel in (0, 1):
        z_two_lo[rel].wait_recv()
        x_sent[2, rel] = x_send(2, rel)
    for j in (1, 3):
        shared.append(share(j, (both, x, lo)))
        for rel in (0, 1):
            for copy in x_sent[j, rel]:
                copy.wait_recv()
            x_gone[j, rel] = x_forward(j, rel)
        for i in (1, 3):
            shared.append(share(j, (both, xs[i], lo)))
    for i in (1, 3):
        shared.append(share(end_j, (both, xs[i], lo)))
    shared.append(share(2, (both, x, lo)))
    for rel in (0, 1):
        for copy in x_sent[2, rel]:
            copy.wait_recv()
        x_gone[2, rel] = x_forward(2, rel)
    for i in (1, 3):
        shared.append(share(2, (both, xs[i], lo)))
    for rel in (0, 1):
        z_two_hi[rel].wait_recv()
        shared.append(share(2, (row_of[rel], both, hi)))
    for j, rel in ((0, 1), (4, 1), (4, 0)):
        x_gone[j, rel].wait_recv()
    shared.append(share(end_j, (both, xs[2], lo)))
    for j in (1, 3, 2):
        for rel in (0, 1):
            x_gone[j, rel].wait_recv()
        shared.append(share(j, (both, xs[2], lo)))

    for copy in shared:
        copy.wait_recv()
    for copy, cond in started:
        if cond is None:
            copy.wait_send()
        else:
            pl.when(cond)(copy.wait_send)


def stack_kernel(g, lhs, rci, out, stage, sems):
    mine = rci[...]

    def to_out(k):
        return pltpu.make_async_copy(stage.at[k], out.at[:, k], sems.at[k])

    @pl.loop(0, HOPS)
    def _(k):
        for n in (0, 1):
            result = lax.dot_general(
                lhs[...],
                g[k, n * 256 : (n + 1) * 256, :],
                (((1,), (1,)), ((), ())),
                preferred_element_type=jnp.float32,
            )
            recip = 1.0 / result[0:1]
            for t in (0, 1):
                lanes = slice(t * 128, (t + 1) * 128)
                scale = jnp.maximum(mine, recip[:, lanes])
                value = (result[SEL:, lanes] * scale).reshape(WIDTH, 8, 128)
                columns = slice(n * 256 + t * 128, n * 256 + (t + 1) * 128)
                stage[k, :, 0, :, columns] = value[:, :BINS]
                stage[k, :, 1, :, columns] = value[:, BINS:]
        to_out(k).start()

    @pl.loop(0, HOPS)
    def _(k):
        to_out(k).wait()


def per_device(spectra, counts):
    spec = spectra.reshape(USED, WIDTH)
    vmem = pl.BlockSpec(memory_space=pltpu.VMEM)
    hbm = pl.BlockSpec(memory_space=pltpu.HBM)
    g, lhs, rci = pl.pallas_call(
        gather_kernel,
        name="whiten_gather",
        out_shape=(
            jax.ShapeDtypeStruct((HOPS, 2, 4, WIDTH, COLS), jnp.bfloat16),
            jax.ShapeDtypeStruct((SEL + WIDTH * 8, COLS), jnp.bfloat16),
            jax.ShapeDtypeStruct((WIDTH * 8, 128), jnp.float32),
        ),
        in_specs=[hbm, hbm],
        out_specs=(vmem, vmem, vmem),
        scratch_shapes=[
            pltpu.VMEM((USED, WIDTH), jnp.float32),
            pltpu.VMEM((1, WIDTH), jnp.int32),
            pltpu.VMEM((WIDTH, COLS), jnp.bfloat16),
            pltpu.SemaphoreType.DMA((DMAS,)),
            pltpu.SemaphoreType.DMA((DMAS,)),
            pltpu.SemaphoreType.DMA((3,)),
        ],
        compiler_params=pltpu.CompilerParams(
            collective_id=0, has_side_effects=True, vmem_limit_bytes=16 * 2**20
        ),
    )(*(pltpu.with_memory_space_constraint(a, pltpu.HBM) for a in (spec, counts)))
    g = g.reshape(HOPS, 512, COLS)
    out = pl.pallas_call(
        stack_kernel,
        name="stack",
        out_shape=jax.ShapeDtypeStruct((WIDTH, HOPS, 2, BINS, 512), jnp.float32),
        in_specs=[vmem, vmem, vmem],
        out_specs=hbm,
        scratch_shapes=[
            pltpu.VMEM((HOPS, WIDTH, 2, BINS, 512), jnp.float32),
            pltpu.SemaphoreType.DMA((HOPS,)),
        ],
        compiler_params=pltpu.CompilerParams(vmem_limit_bytes=24 * 2**20),
        cost_estimate=pl.CostEstimate(
            flops=2 * (SEL + WIDTH * 8) * COLS * 512 * HOPS,
            bytes_accessed=HOPS * 512 * (COLS * 2 + WIDTH * 8 * 4),
            transcendentals=0,
        ),
    )(g, lhs, rci)
    return out[None]


def solution(mesh):
    return jax.shard_map(
        per_device,
        mesh=mesh,
        in_specs=(P(None, None, None, "col", "row"), P("col", "row")),
        out_specs=P("col", "row", None, None, None, None),
        check_vma=False,
    )
```

```python
import functools

import jax
import jax.numpy as jnp
from jax import lax
from jax.experimental import pallas as pl
from jax.experimental.pallas import tpu as pltpu
from jax.sharding import PartitionSpec as P

MESH = pl.DeviceIdType.MESH
BINS = 4
SEGS = 30
USED = 2 * BINS * SEGS
COLS = 256
WIDTH = 64
HALF = 32
HOPS = 9
SEL = 16


def gather_kernel(spec_in, cnt_in, g, lhs, rci, spec, cnt, own, ssem, rsem, lsem):
    fetch = (
        pltpu.make_async_copy(spec_in, spec, lsem.at[1]),
        pltpu.make_async_copy(cnt_in, cnt, lsem.at[2]),
    )
    for copy in fetch:
        copy.start()
    r, d = lax.axis_index("row"), lax.axis_index("col")
    x, ylo = r % 4, r // 4
    c, q = d % 2, d // 2
    z, yhi = q % 4, q // 4

    def dev(x_, ylo_, q_, c_):
        return (ylo_ * 4 + x_, q_ * 2 + c_)

    sibling = dev(x, ylo, q, 1 - c)
    other = 1 - ylo

    def at_y(rel):
        return other if rel else ylo

    plane = [(0, 1)] + [(j, rel) for j in range(1, 5) for rel in (0, 1)]

    barrier = pltpu.get_barrier_semaphore()
    sources = [dev(x, at_y(rel), (q + j) % 8, c) for j, rel in plane]
    sources += [dev((x + i) % 4, ylo, q, c) for i in (1, 2, 3)]
    sources += [dev(x, ylo, yhi * 4 + (z + e) % 4, c) for e in (1, 2, 3)]
    sources += [sibling]
    for source in sources:
        pl.semaphore_signal(barrier, inc=1, device_id=source, device_id_type=MESH)

    for copy in fetch:
        copy.wait()
    raw = spec[...]
    power = jnp.sum(raw * raw, axis=0, keepdims=True) / float(USED)
    row = lax.broadcasted_iota(jnp.int32, (USED, WIDTH), 0)
    group = jnp.zeros((USED, WIDTH), jnp.int32)
    for n in range(1, 2 * BINS):
        group = group + (row >= n * SEGS).astype(jnp.int32)
    valid = (row - SEGS * group < cnt[...]).astype(jnp.float32)
    white = raw * lax.rsqrt(power + 1e-6) * valid
    white = white.astype(jnp.bfloat16).astype(jnp.float32)
    count = cnt[...].astype(jnp.float32)
    pad = jnp.zeros((COLS - USED - 8, WIDTH), jnp.float32)
    first = lax.broadcasted_iota(jnp.int32, (8, WIDTH), 0) == 0
    tail = jnp.where(first, count, 0.0)
    straight = jnp.concatenate([white, tail, pad], axis=0).T
    own[...] = straight.astype(jnp.bfloat16)

    def remote(src, dst, device, send, recv):
        copy = pltpu.make_async_remote_copy(
            src_ref=src,
            dst_ref=dst,
            send_sem=ssem.at[send],
            recv_sem=rsem.at[recv],
            device_id=device,
            device_id_type=MESH,
        )
        copy.start()
        return copy

    def settle(region, sem):
        pltpu.make_async_copy(region, region, sem).wait()

    lo, hi = pl.ds(0, HALF), pl.ds(HALF, HALF)
    own_blocks = pl.ds(0, 5)

    pl.semaphore_wait(barrier, len(sources))
    for i in (1, 3, 2):
        remote(own.at[hi], g.at[0, ylo, x, hi], dev((x + i) % 4, ylo, q, c), 0, 0)
    for j, rel in plane:
        remote(own.at[lo], g.at[j, ylo, x, lo], dev(x, at_y(rel), (q - j) % 8, c), 1, 1)
    local = pltpu.make_async_copy(own, g.at[0, ylo, x], lsem.at[0])
    local.start()

    swapped = jnp.concatenate(
        [white[USED // 2 :], -white[: USED // 2], jnp.zeros((COLS - USED, WIDTH), jnp.float32)],
        axis=0,
    ).T
    shape = (WIDTH, 8, COLS)
    sub = lax.broadcasted_iota(jnp.int32, (8, COLS), 0)
    lane = lax.broadcasted_iota(jnp.int32, (8, COLS), 1)
    low = (sub % BINS) * SEGS
    here = ((lane >= low) & (lane < low + SEGS)) | (
        (lane >= low + USED // 2) & (lane < low + USED // 2 + SEGS)
    )
    pick = jnp.where(
        (sub < BINS)[None],
        jnp.broadcast_to(straight[:, None, :], shape),
        jnp.broadcast_to(swapped[:, None, :], shape),
    )
    pick = jnp.where(here[None], pick, 0.0)
    sel = lax.broadcasted_iota(jnp.int32, (SEL, COLS), 1) == USED
    lhs[:SEL, :] = sel.astype(jnp.float32).astype(jnp.bfloat16)
    lhs[SEL:, :] = pick.reshape(WIDTH * 8, COLS).astype(jnp.bfloat16)
    mine = jnp.broadcast_to(1.0 / straight[:, USED : USED + 1], (WIDTH, 128))
    rci[...] = jnp.broadcast_to(mine[:, None, :], (WIDTH, 8, 128)).reshape(WIDTH * 8, 128)

    local.wait()

    settle(g.at[pl.ds(0, 3), 0, 0, hi], rsem.at[0])
    row = g.at[0, ylo, :, hi]
    for j, rel in ((4, 1), (0, 1), (4, 0)):
        remote(row, g.at[j, ylo, :, hi], dev(x, at_y(rel), (q - j) % 8, c), 2, 2)

    right, left = dev((x + 1) % 4, ylo, q, c), dev((x + 3) % 4, ylo, q, c)
    settle(g.at[pl.ds(0, 9), 0, 0, lo], rsem.at[1])
    columns = [g.at[own_blocks, rel, x, lo] for rel in (0, 1)]
    to_right = [remote(columns[0], columns[0], right, 3, 3)]
    to_left = {1: remote(columns[1], columns[1], left, 3, 4)}
    to_right.append(remote(columns[1], columns[1], right, 3, 5))
    to_left[0] = remote(columns[0], columns[0], left, 3, 6)

    def share(src_index, dst_index, recv):
        remote(g.at[src_index], g.at[dst_index], sibling, 5, recv)

    def share_column(column):
        share((pl.ds(1 - c, 4), slice(None), column, lo), (pl.ds(5, 4), slice(None), column, lo), 12)

    def share_block(j):
        at = 4 + j + c
        share((j, slice(None), slice(None), hi), (at, slice(None), slice(None), hi), 12)

    settle(g.at[pl.ds(0, 3), 0, :, hi], rsem.at[2])
    along_z = {}
    for e in (1, 3, 2):
        zt = (z + 4 - e) % 4
        block = jnp.where(zt > z, 4, 0)
        along_z[e] = remote(
            g.at[block, :, :, hi], g.at[e, :, :, hi], dev(x, ylo, yhi * 4 + zt, c), 4, 6 + e
        )
    share_column(x)
    share_block(4 * (1 - c))

    xl, xr, xo = (x + 3) % 4, (x + 1) % 4, (x + 2) % 4
    to_right[0].wait_recv()
    piece = g.at[own_blocks, 0, xl, lo]
    on_right = remote(piece, piece, right, 3, 10)
    to_left[1].wait_recv()
    piece = g.at[own_blocks, 1, xr, lo]
    on_left = remote(piece, piece, left, 3, 11)
    to_right[1].wait_recv()
    share_column(xl)
    to_left[0].wait_recv()
    share_column(xr)
    for e in (1, 3):
        along_z[e].wait_recv()
        share_block(e)
    on_right.wait_recv()
    on_left.wait_recv()
    share_column(xo)
    along_z[2].wait_recv()
    share_block(2)

    settle(g.at[pl.ds(5, 4)], rsem.at[12])
    settle(g.at[pl.ds(0, 3), 0, 0, hi], ssem.at[0])
    settle(g.at[pl.ds(0, 9), 0, 0, lo], ssem.at[1])
    settle(g.at[pl.ds(0, 3), 0, :, hi], ssem.at[2])
    settle(g.at[pl.ds(0, 5), 0, pl.ds(0, 3)], ssem.at[3])
    settle(g.at[pl.ds(0, 3), :, :, hi], ssem.at[4])
    settle(g.at[pl.ds(5, 4)], ssem.at[5])


def stack_kernel(g, lhs, rci, out, stage, sems):
    mine = rci[...]

    def held(k):
        return jnp.where(k % 2 == 0, k // 2, 5 + k // 2)

    def to_out(k):
        return pltpu.make_async_copy(stage.at[k], out.at[:, k], sems.at[k])

    @pl.loop(0, HOPS)
    def _(k):
        for n in (0, 1):
            result = lax.dot_general(
                lhs[...],
                g[held(k), n * 256 : (n + 1) * 256, :],
                (((1,), (1,)), ((), ())),
                preferred_element_type=jnp.float32,
            )
            recip = 1.0 / result[0:1]
            for t in (0, 1):
                lanes = slice(t * 128, (t + 1) * 128)
                scale = jnp.maximum(mine, recip[:, lanes])
                value = (result[SEL:, lanes] * scale).reshape(WIDTH, 8, 128)
                columns = slice(n * 256 + t * 128, n * 256 + (t + 1) * 128)
                stage[k, :, 0, :, columns] = value[:, :BINS]
                stage[k, :, 1, :, columns] = value[:, BINS:]
        to_out(k).start()

    @pl.loop(0, HOPS)
    def _(k):
        to_out(k).wait()


def per_device(spectra, counts):
    spec = spectra.reshape(USED, WIDTH)
    vmem = pl.BlockSpec(memory_space=pltpu.VMEM)
    hbm = pl.BlockSpec(memory_space=pltpu.HBM)
    g, lhs, rci = pl.pallas_call(
        gather_kernel,
        name="whiten_gather",
        out_shape=(
            jax.ShapeDtypeStruct((HOPS, 2, 4, WIDTH, COLS), jnp.bfloat16),
            jax.ShapeDtypeStruct((SEL + WIDTH * 8, COLS), jnp.bfloat16),
            jax.ShapeDtypeStruct((WIDTH * 8, 128), jnp.float32),
        ),
        in_specs=[hbm, hbm],
        out_specs=(vmem, vmem, vmem),
        scratch_shapes=[
            pltpu.VMEM((USED, WIDTH), jnp.float32),
            pltpu.VMEM((1, WIDTH), jnp.int32),
            pltpu.VMEM((WIDTH, COLS), jnp.bfloat16),
            pltpu.SemaphoreType.DMA((6,)),
            pltpu.SemaphoreType.DMA((13,)),
            pltpu.SemaphoreType.DMA((3,)),
        ],
        compiler_params=pltpu.CompilerParams(
            collective_id=0, has_side_effects=True, vmem_limit_bytes=16 * 2**20
        ),
    )(*(pltpu.with_memory_space_constraint(a, pltpu.HBM) for a in (spec, counts)))
    g = g.reshape(HOPS, 512, COLS)
    out = pl.pallas_call(
        stack_kernel,
        name="stack",
        out_shape=jax.ShapeDtypeStruct((WIDTH, HOPS, 2, BINS, 512), jnp.float32),
        in_specs=[vmem, vmem, vmem],
        out_specs=hbm,
        scratch_shapes=[
            pltpu.VMEM((HOPS, WIDTH, 2, BINS, 512), jnp.float32),
            pltpu.SemaphoreType.DMA((HOPS,)),
        ],
        compiler_params=pltpu.CompilerParams(vmem_limit_bytes=24 * 2**20),
        cost_estimate=pl.CostEstimate(
            flops=2 * (SEL + WIDTH * 8) * COLS * 512 * HOPS,
            bytes_accessed=HOPS * 512 * (COLS * 2 + WIDTH * 8 * 4),
            transcendentals=0,
        ),
    )(g, lhs, rci)
    return out[None]


def solution(mesh):
    return jax.shard_map(
        per_device,
        mesh=mesh,
        in_specs=(P(None, None, None, "col", "row"), P("col", "row")),
        out_specs=P("col", "row", None, None, None, None),
        check_vma=False,
    )
```

```python
import functools

import jax
import jax.numpy as jnp
from jax import lax
from jax.experimental import pallas as pl
from jax.experimental.pallas import tpu as pltpu
from jax.sharding import PartitionSpec as P

MESH = pl.DeviceIdType.MESH
BINS = 4
SEGS = 30
USED = 2 * BINS * SEGS
COLS = 256
WIDTH = 64
SHARED = 12
HOPS = 9
SEL = 16


def gather_kernel(spec_in, cnt_in, g, lhs, rci, spec, cnt, own, ssem, rsem, lsem):
    fetch = (
        pltpu.make_async_copy(spec_in, spec, lsem.at[1]),
        pltpu.make_async_copy(cnt_in, cnt, lsem.at[2]),
    )
    for copy in fetch:
        copy.start()
    r, d = lax.axis_index("row"), lax.axis_index("col")
    x, ylo = r % 4, r // 4
    c, q = d % 2, d // 2
    z, yhi = q % 4, q // 4

    def dev(x_, ylo_, q_, c_):
        return (ylo_ * 4 + x_, q_ * 2 + c_)

    sibling = dev(x, ylo, q, 1 - c)
    across = 1 - ylo

    at_x = [dev((x + i) % 4, ylo, q, c) for i in range(4)]
    right, left = at_x[1], at_x[3]
    pair = dev(x, across, q, c)
    far = dev(x, across, (q + 4) % 8, c)
    below = dev(x, ylo, yhi * 4 + (z + 3) % 4, c)
    above = dev(x, ylo, yhi * 4 + (z + 1) % 4, c)
    row_of = (ylo, across)
    plane = [(j, rel) for rel in (1, 0) for j in (0, 4, 1, 3, 2) if (j, rel) != (0, 0)]

    def plane_at(j, rel):
        return dev(x, row_of[rel], (q + j) % 8, c)

    barrier = pltpu.get_barrier_semaphore()
    sources = (
        [plane_at(j, rel) for j, rel in plane] + [right, left, sibling],
        at_x[1:] + [pair, far, below, above, sibling],
    )

    def announce(core):
        for source in sources[core]:
            pl.semaphore_signal(barrier, inc=1, device_id=source, device_id_type=MESH)

    for core in (0, 1):
        pl.when(c == core)(functools.partial(announce, core))

    for copy in fetch:
        copy.wait()
    raw = spec[...]
    power = jnp.sum(raw * raw, axis=0, keepdims=True) / float(USED)
    row = lax.broadcasted_iota(jnp.int32, (USED, WIDTH), 0)
    group = jnp.zeros((USED, WIDTH), jnp.int32)
    for n in range(1, 2 * BINS):
        group = group + (row >= n * SEGS).astype(jnp.int32)
    valid = (row - SEGS * group < cnt[...]).astype(jnp.float32)
    white = raw * lax.rsqrt(power + 1e-6) * valid
    white = white.astype(jnp.bfloat16).astype(jnp.float32)
    count = cnt[...].astype(jnp.float32)
    pad = jnp.zeros((COLS - USED - 8, WIDTH), jnp.float32)
    first = lax.broadcasted_iota(jnp.int32, (8, WIDTH), 0) == 0
    tail = jnp.where(first, count, 0.0)
    straight = jnp.concatenate([white, tail, pad], axis=0).T
    own[...] = straight.astype(jnp.bfloat16)

    def remote(src, dst, device, send, recv):
        copy = pltpu.make_async_remote_copy(
            src_ref=src,
            dst_ref=dst,
            send_sem=ssem.at[send],
            recv_sem=rsem.at[recv],
            device_id=device,
            device_id_type=MESH,
        )
        copy.start()
        return copy

    def settle(region, sem):
        pltpu.make_async_copy(region, region, sem).wait()

    @pl.when(c == 0)
    def _():
        pl.semaphore_wait(barrier, len(sources[0]))
        for j, rel in plane:
            remote(own, g.at[j, ylo, x], plane_at(-j, rel), 0, rel)

    @pl.when(c == 1)
    def _():
        pl.semaphore_wait(barrier, len(sources[1]))
        for i in (1, 3, 2):
            remote(own, g.at[0, ylo, x], at_x[i], 0, 0)

    local = pltpu.make_async_copy(own, g.at[0, ylo, x], lsem.at[0])
    local.start()

    swapped = jnp.concatenate(
        [white[USED // 2 :], -white[: USED // 2], jnp.zeros((COLS - USED, WIDTH), jnp.float32)],
        axis=0,
    ).T
    shape = (WIDTH, 8, COLS)
    sub = lax.broadcasted_iota(jnp.int32, (8, COLS), 0)
    lane = lax.broadcasted_iota(jnp.int32, (8, COLS), 1)
    low = (sub % BINS) * SEGS
    here = ((lane >= low) & (lane < low + SEGS)) | (
        (lane >= low + USED // 2) & (lane < low + USED // 2 + SEGS)
    )
    pick = jnp.where(
        (sub < BINS)[None],
        jnp.broadcast_to(straight[:, None, :], shape),
        jnp.broadcast_to(swapped[:, None, :], shape),
    )
    pick = jnp.where(here[None], pick, 0.0)
    sel = lax.broadcasted_iota(jnp.int32, (SEL, COLS), 1) == USED
    lhs[:SEL, :] = sel.astype(jnp.float32).astype(jnp.bfloat16)
    lhs[SEL:, :] = pick.reshape(WIDTH * 8, COLS).astype(jnp.bfloat16)
    mine = jnp.broadcast_to(1.0 / straight[:, USED : USED + 1], (WIDTH, 128))
    rci[...] = jnp.broadcast_to(mine[:, None, :], (WIDTH, 8, 128)).reshape(WIDTH * 8, 128)

    local.wait()

    def to_sibling(src, dst):
        remote(src, dst, sibling, 1, SHARED)

    @pl.when(c == 0)
    def _():
        blocks = pl.ds(0, 5)

        def column(rel, at):
            return g.at[blocks, row_of[rel], at]

        def send(rel, at, device, recv):
            return remote(column(rel, at), column(rel, at), device, 2 + rel, recv)

        def share(at):
            to_sibling(g.at[pl.ds(1, 4), :, at], g.at[pl.ds(5, 4), :, at])

        xl, xr, xo = (x + 3) % 4, (x + 1) % 4, (x + 2) % 4
        settle(g.at[pl.ds(0, 5), 0, 0], rsem.at[1])
        left_1 = send(1, x, left, 2)
        settle(g.at[pl.ds(0, 4), 0, 0], rsem.at[0])
        right_0 = send(0, x, right, 3)
        left_0 = send(0, x, left, 4)
        right_1 = send(1, x, right, 5)
        share(x)
        left_1.wait_recv()
        on_left = send(1, xr, left, 6)
        right_0.wait_recv()
        on_right = send(0, xl, right, 7)
        left_0.wait_recv()
        share(xr)
        right_1.wait_recv()
        share(xl)
        on_left.wait_recv()
        on_right.wait_recv()
        share(xo)

        settle(g.at[pl.ds(0, 9), 0, 0], ssem.at[0])
        settle(g.at[pl.ds(0, 5), 0, pl.ds(0, 3)], ssem.at[2])
        settle(g.at[pl.ds(0, 5), 1, pl.ds(0, 3)], ssem.at[3])

    @pl.when(c == 1)
    def _():
        own_block = {1: z >= 1, 3: z == 3}
        taken = {e: jnp.where(own_block[e], 0, 4) for e in (1, 3)}
        z_to = {1: below, 3: above}
        first = pl.ds(0, 2)
        second = pl.ds(2, 2)

        def plan(src, dst, device, send, recv):
            return pltpu.make_async_remote_copy(
                src_ref=src,
                dst_ref=dst,
                send_sem=ssem.at[send],
                recv_sem=rsem.at[recv],
                device_id=device,
                device_id_type=MESH,
            )

        z_one = {
            (e, rel): plan(
                g.at[taken[e], row_of[rel]], g.at[e, row_of[rel]], z_to[e], 4, 1 + e + rel
            )
            for e in (1, 3)
            for rel in (0, 1)
        }
        settle(g.at[pl.ds(0, 3), 0, 0], rsem.at[0])
        row = g.at[0, ylo]
        from_pair = remote(row, row, pair, 2, 6)
        from_far = remote(row, g.at[4, ylo], far, 2, 7)
        for e in (1, 3):
            pl.when(own_block[e])(z_one[e, 0].start)

        from_pair.wait_recv()
        two_a = remote(g.at[0, across, first], g.at[4, across, first], far, 3, 8)
        from_far.wait_recv()
        two_b = remote(g.at[4, across, second], g.at[4, across, second], pair, 3, 9)
        for e in (1, 3):
            z_one[e, 1].start()
        to_sibling(g.at[0], g.at[5])
        two_a.wait_recv()
        two_b.wait_recv()
        for e in (1, 3):
            pl.when(jnp.logical_not(own_block[e]))(z_one[e, 0].start)

        goes = {(1, 0): z >= 1, (3, 1): z <= 2, (1, 1): z == 1, (3, 0): z == 2}
        z_two = {}
        for n, (e, rel) in enumerate(goes):
            z_one[e, rel].wait_recv()
            z_two[e, rel] = plan(
                g.at[e, row_of[rel]], g.at[2, row_of[rel]], z_to[e], 5 + n, 10 + rel
            )
            pl.when(goes[e, rel])(z_two[e, rel].start)
        to_sibling(g.at[pl.ds(1, 1)], g.at[pl.ds(6, 1)])
        to_sibling(g.at[pl.ds(3, 1)], g.at[pl.ds(8, 1)])
        for rel in (0, 1):
            z_two[1, rel].wait_recv()
            to_sibling(g.at[2, row_of[rel]], g.at[7, row_of[rel]])

        settle(g.at[pl.ds(0, 3), 0, 0], ssem.at[0])
        settle(g.at[pl.ds(0, 2), 0], ssem.at[2])
        settle(g.at[0, 0], ssem.at[3])
        settle(g.at[pl.ds(0, 4), 0], ssem.at[4])
        for key in goes:
            pl.when(goes[key])(z_two[key].wait_send)

    settle(g.at[pl.ds(5, 4)], rsem.at[SHARED])
    settle(g.at[pl.ds(5, 4)], ssem.at[1])


def stack_kernel(g, lhs, rci, out, stage, sems):
    mine = rci[...]

    def held(k):
        return jnp.where(k % 2 == 0, k // 2, 5 + k // 2)

    def to_out(k):
        return pltpu.make_async_copy(stage.at[k], out.at[:, k], sems.at[k])

    @pl.loop(0, HOPS)
    def _(k):
        for n in (0, 1):
            result = lax.dot_general(
                lhs[...],
                g[held(k), n * 256 : (n + 1) * 256, :],
                (((1,), (1,)), ((), ())),
                preferred_element_type=jnp.float32,
            )
            recip = 1.0 / result[0:1]
            for t in (0, 1):
                lanes = slice(t * 128, (t + 1) * 128)
                scale = jnp.maximum(mine, recip[:, lanes])
                value = (result[SEL:, lanes] * scale).reshape(WIDTH, 8, 128)
                columns = slice(n * 256 + t * 128, n * 256 + (t + 1) * 128)
                stage[k, :, 0, :, columns] = value[:, :BINS]
                stage[k, :, 1, :, columns] = value[:, BINS:]
        to_out(k).start()

    @pl.loop(0, HOPS)
    def _(k):
        to_out(k).wait()


def per_device(spectra, counts):
    spec = spectra.reshape(USED, WIDTH)
    vmem = pl.BlockSpec(memory_space=pltpu.VMEM)
    hbm = pl.BlockSpec(memory_space=pltpu.HBM)
    g, lhs, rci = pl.pallas_call(
        gather_kernel,
        name="whiten_gather",
        out_shape=(
            jax.ShapeDtypeStruct((HOPS, 2, 4, WIDTH, COLS), jnp.bfloat16),
            jax.ShapeDtypeStruct((SEL + WIDTH * 8, COLS), jnp.bfloat16),
            jax.ShapeDtypeStruct((WIDTH * 8, 128), jnp.float32),
        ),
        in_specs=[hbm, hbm],
        out_specs=(vmem, vmem, vmem),
        scratch_shapes=[
            pltpu.VMEM((USED, WIDTH), jnp.float32),
            pltpu.VMEM((1, WIDTH), jnp.int32),
            pltpu.VMEM((WIDTH, COLS), jnp.bfloat16),
            pltpu.SemaphoreType.DMA((9,)),
            pltpu.SemaphoreType.DMA((SHARED + 1,)),
            pltpu.SemaphoreType.DMA((3,)),
        ],
        compiler_params=pltpu.CompilerParams(
            collective_id=0, has_side_effects=True, vmem_limit_bytes=16 * 2**20
        ),
    )(*(pltpu.with_memory_space_constraint(a, pltpu.HBM) for a in (spec, counts)))
    g = g.reshape(HOPS, 512, COLS)
    out = pl.pallas_call(
        stack_kernel,
        name="stack",
        out_shape=jax.ShapeDtypeStruct((WIDTH, HOPS, 2, BINS, 512), jnp.float32),
        in_specs=[vmem, vmem, vmem],
        out_specs=hbm,
        scratch_shapes=[
            pltpu.VMEM((HOPS, WIDTH, 2, BINS, 512), jnp.float32),
            pltpu.SemaphoreType.DMA((HOPS,)),
        ],
        compiler_params=pltpu.CompilerParams(vmem_limit_bytes=24 * 2**20),
        cost_estimate=pl.CostEstimate(
            flops=2 * (SEL + WIDTH * 8) * COLS * 512 * HOPS,
            bytes_accessed=HOPS * 512 * (COLS * 2 + WIDTH * 8 * 4),
            transcendentals=0,
        ),
    )(g, lhs, rci)
    return out[None]


def solution(mesh):
    return jax.shard_map(
        per_device,
        mesh=mesh,
        in_specs=(P(None, None, None, "col", "row"), P("col", "row")),
        out_specs=P("col", "row", None, None, None, None),
        check_vma=False,
    )
```

```python
import functools

import jax
import jax.numpy as jnp
from jax import lax
from jax.experimental import pallas as pl
from jax.experimental.pallas import tpu as pltpu
from jax.sharding import PartitionSpec as P

MESH = pl.DeviceIdType.MESH
BINS = 4
SEGS = 30
USED = 2 * BINS * SEGS
COLS = 256
WIDTH = 64
HALF = 32
SHARED = 18
HOPS = 9
SEL = 16


def gather_kernel(spec_in, cnt_in, g, lhs, rci, spec, cnt, own, ssem, rsem, lsem):
    fetch = (
        pltpu.make_async_copy(spec_in, spec, lsem.at[1]),
        pltpu.make_async_copy(cnt_in, cnt, lsem.at[2]),
    )
    for copy in fetch:
        copy.start()
    r, d = lax.axis_index("row"), lax.axis_index("col")
    x, ylo = r % 4, r // 4
    c, q = d % 2, d // 2
    z, yhi = q % 4, q // 4

    def dev(x_, ylo_, q_, c_):
        return (ylo_ * 4 + x_, q_ * 2 + c_)

    sibling = dev(x, ylo, q, 1 - c)
    across = 1 - ylo

    at_x = [dev((x + i) % 4, ylo, q, c) for i in range(4)]
    right, left = at_x[1], at_x[3]
    pair = dev(x, across, q, c)
    far = dev(x, across, (q + 4) % 8, c)
    below = dev(x, ylo, yhi * 4 + (z + 3) % 4, c)
    above = dev(x, ylo, yhi * 4 + (z + 1) % 4, c)
    row_of = (ylo, across)
    plane = [(j, rel) for rel in (1, 0) for j in (0, 4, 1, 3, 2) if (j, rel) != (0, 0)]

    def plane_at(j, rel):
        return dev(x, row_of[rel], (q + j) % 8, c)

    barrier = pltpu.get_barrier_semaphore()
    sources = [plane_at(j, rel) for j, rel in plane] + at_x[1:] + [below, above, sibling]
    for source in sources:
        pl.semaphore_signal(barrier, inc=1, device_id=source, device_id_type=MESH)

    for copy in fetch:
        copy.wait()
    raw = spec[...]
    power = jnp.sum(raw * raw, axis=0, keepdims=True) / float(USED)
    row = lax.broadcasted_iota(jnp.int32, (USED, WIDTH), 0)
    group = jnp.zeros((USED, WIDTH), jnp.int32)
    for n in range(1, 2 * BINS):
        group = group + (row >= n * SEGS).astype(jnp.int32)
    valid = (row - SEGS * group < cnt[...]).astype(jnp.float32)
    white = raw * lax.rsqrt(power + 1e-6) * valid
    white = white.astype(jnp.bfloat16).astype(jnp.float32)
    count = cnt[...].astype(jnp.float32)
    pad = jnp.zeros((COLS - USED - 8, WIDTH), jnp.float32)
    first = lax.broadcasted_iota(jnp.int32, (8, WIDTH), 0) == 0
    tail = jnp.where(first, count, 0.0)
    straight = jnp.concatenate([white, tail, pad], axis=0).T
    own[...] = straight.astype(jnp.bfloat16)

    def plan(src, dst, device, send, recv):
        return pltpu.make_async_remote_copy(
            src_ref=src,
            dst_ref=dst,
            send_sem=ssem.at[send],
            recv_sem=rsem.at[recv],
            device_id=device,
            device_id_type=MESH,
        )

    def remote(src, dst, device, send, recv):
        copy = plan(src, dst, device, send, recv)
        copy.start()
        return copy

    def settle(region, sem):
        pltpu.make_async_copy(region, region, sem).wait()

    lo, hi = pl.ds(0, HALF), pl.ds(HALF, HALF)
    every = slice(None)
    pl.semaphore_wait(barrier, len(sources))
    for i in (1, 3, 2):
        remote(own.at[hi], g.at[0, ylo, x, hi], at_x[i], 0, 0)
    for j, rel in plane:
        remote(own.at[lo], g.at[j, ylo, x, lo], plane_at(-j, rel), 1, 1)
    local = pltpu.make_async_copy(own, g.at[0, ylo, x], lsem.at[0])
    local.start()

    swapped = jnp.concatenate(
        [white[USED // 2 :], -white[: USED // 2], jnp.zeros((COLS - USED, WIDTH), jnp.float32)],
        axis=0,
    ).T
    shape = (WIDTH, 8, COLS)
    sub = lax.broadcasted_iota(jnp.int32, (8, COLS), 0)
    lane = lax.broadcasted_iota(jnp.int32, (8, COLS), 1)
    low = (sub % BINS) * SEGS
    here = ((lane >= low) & (lane < low + SEGS)) | (
        (lane >= low + USED // 2) & (lane < low + USED // 2 + SEGS)
    )
    pick = jnp.where(
        (sub < BINS)[None],
        jnp.broadcast_to(straight[:, None, :], shape),
        jnp.broadcast_to(swapped[:, None, :], shape),
    )
    pick = jnp.where(here[None], pick, 0.0)
    sel = lax.broadcasted_iota(jnp.int32, (SEL, COLS), 1) == USED
    lhs[:SEL, :] = sel.astype(jnp.float32).astype(jnp.bfloat16)
    lhs[SEL:, :] = pick.reshape(WIDTH * 8, COLS).astype(jnp.bfloat16)
    mine = jnp.broadcast_to(1.0 / straight[:, USED : USED + 1], (WIDTH, 128))
    rci[...] = jnp.broadcast_to(mine[:, None, :], (WIDTH, 8, 128)).reshape(WIDTH * 8, 128)

    local.wait()

    def to_sibling(src_index, dst_index):
        remote(g.at[src_index], g.at[dst_index], sibling, 2, SHARED)

    def share_column(at):
        index = (every, at, lo)
        to_sibling((pl.ds(1 - c, 4),) + index, (pl.ds(5, 4),) + index)

    def share_rows(j, rows):
        to_sibling((j, rows, every, hi), (4 + j + c, rows, every, hi))

    own_block = {1: z >= 1, 3: z == 3}
    taken = {e: jnp.where(own_block[e], 0, 4) for e in (1, 3)}
    z_to = {1: below, 3: above}
    z_one = {
        (e, rel): plan(
            g.at[taken[e], row_of[rel], :, hi], g.at[e, row_of[rel], :, hi], z_to[e], 3, 1 + e + rel
        )
        for e in (1, 3)
        for rel in (0, 1)
    }

    settle(g.at[pl.ds(0, 3), 0, 0, hi], rsem.at[0])
    row = g.at[0, ylo, :, hi]
    from_pair = remote(row, row, pair, 4, 6)
    from_far = remote(row, g.at[4, ylo, :, hi], far, 4, 7)
    for e in (1, 3):
        pl.when(own_block[e])(z_one[e, 0].start)

    def column(rel, at):
        return g.at[pl.ds(0, 5), row_of[rel], at, lo]

    def along_x(rel, at, device, recv):
        return remote(column(rel, at), column(rel, at), device, 5, recv)

    xl, xr, xo = (x + 3) % 4, (x + 1) % 4, (x + 2) % 4
    settle(g.at[pl.ds(0, 9), 0, 0, lo], rsem.at[1])
    right_0 = along_x(0, x, right, 12)
    left_1 = along_x(1, x, left, 13)
    right_1 = along_x(1, x, right, 14)
    left_0 = along_x(0, x, left, 15)

    first, second = pl.ds(0, 2), pl.ds(2, 2)
    from_pair.wait_recv()
    two_a = remote(g.at[0, across, first, hi], g.at[4, across, first, hi], far, 6, 8)
    from_far.wait_recv()
    two_b = remote(g.at[4, across, second, hi], g.at[4, across, second, hi], pair, 6, 9)
    for e in (1, 3):
        z_one[e, 1].start()
    two_a.wait_recv()
    two_b.wait_recv()
    for e in (1, 3):
        pl.when(jnp.logical_not(own_block[e]))(z_one[e, 0].start)

    right_0.wait_recv()
    on_right = along_x(0, xl, right, 16)
    left_1.wait_recv()
    on_left = along_x(1, xr, left, 17)

    goes = {(1, 0): z >= 1, (3, 1): z <= 2, (1, 1): z == 1, (3, 0): z == 2}
    z_two = {}
    for n, (e, rel) in enumerate(goes):
        z_one[e, rel].wait_recv()
        z_two[e, rel] = plan(
            g.at[e, row_of[rel], :, hi], g.at[2, row_of[rel], :, hi], z_to[e], 7 + n, 10 + rel
        )
        pl.when(goes[e, rel])(z_two[e, rel].start)
        if n == 0:
            share_column(x)
            share_rows(4 * (1 - c), every)
    share_rows(1, every)
    share_rows(3, every)
    right_1.wait_recv()
    share_column(xl)
    left_0.wait_recv()
    share_column(xr)
    on_right.wait_recv()
    on_left.wait_recv()
    share_column(xo)
    for rel in (0, 1):
        z_two[1, rel].wait_recv()
        share_rows(2, row_of[rel])

    settle(g.at[pl.ds(5, 4)], rsem.at[SHARED])
    settle(g.at[pl.ds(0, 3), 0, 0, hi], ssem.at[0])
    settle(g.at[pl.ds(0, 9), 0, 0, lo], ssem.at[1])
    settle(g.at[pl.ds(5, 4)], ssem.at[2])
    settle(g.at[pl.ds(0, 4), 0, :, hi], ssem.at[3])
    settle(g.at[pl.ds(0, 2), 0, :, hi], ssem.at[4])
    settle(g.at[pl.ds(0, 5), 0, pl.ds(0, 3)], ssem.at[5])
    settle(g.at[0, 0, :, hi], ssem.at[6])
    for key in goes:
        pl.when(goes[key])(z_two[key].wait_send)


def stack_kernel(g, lhs, rci, out, stage, sems):
    mine = rci[...]

    def held(k):
        return jnp.where(k % 2 == 0, k // 2, 5 + k // 2)

    def to_out(k):
        return pltpu.make_async_copy(stage.at[k], out.at[:, k], sems.at[k])

    @pl.loop(0, HOPS)
    def _(k):
        for n in (0, 1):
            result = lax.dot_general(
                lhs[...],
                g[held(k), n * 256 : (n + 1) * 256, :],
                (((1,), (1,)), ((), ())),
                preferred_element_type=jnp.float32,
            )
            recip = 1.0 / result[0:1]
            for t in (0, 1):
                lanes = slice(t * 128, (t + 1) * 128)
                scale = jnp.maximum(mine, recip[:, lanes])
                value = (result[SEL:, lanes] * scale).reshape(WIDTH, 8, 128)
                columns = slice(n * 256 + t * 128, n * 256 + (t + 1) * 128)
                stage[k, :, 0, :, columns] = value[:, :BINS]
                stage[k, :, 1, :, columns] = value[:, BINS:]
        to_out(k).start()

    @pl.loop(0, HOPS)
    def _(k):
        to_out(k).wait()


def per_device(spectra, counts):
    spec = spectra.reshape(USED, WIDTH)
    vmem = pl.BlockSpec(memory_space=pltpu.VMEM)
    hbm = pl.BlockSpec(memory_space=pltpu.HBM)
    g, lhs, rci = pl.pallas_call(
        gather_kernel,
        name="whiten_gather",
        out_shape=(
            jax.ShapeDtypeStruct((HOPS, 2, 4, WIDTH, COLS), jnp.bfloat16),
            jax.ShapeDtypeStruct((SEL + WIDTH * 8, COLS), jnp.bfloat16),
            jax.ShapeDtypeStruct((WIDTH * 8, 128), jnp.float32),
        ),
        in_specs=[hbm, hbm],
        out_specs=(vmem, vmem, vmem),
        scratch_shapes=[
            pltpu.VMEM((USED, WIDTH), jnp.float32),
            pltpu.VMEM((1, WIDTH), jnp.int32),
            pltpu.VMEM((WIDTH, COLS), jnp.bfloat16),
            pltpu.SemaphoreType.DMA((11,)),
            pltpu.SemaphoreType.DMA((SHARED + 1,)),
            pltpu.SemaphoreType.DMA((3,)),
        ],
        compiler_params=pltpu.CompilerParams(
            collective_id=0, has_side_effects=True, vmem_limit_bytes=16 * 2**20
        ),
    )(*(pltpu.with_memory_space_constraint(a, pltpu.HBM) for a in (spec, counts)))
    g = g.reshape(HOPS, 512, COLS)
    out = pl.pallas_call(
        stack_kernel,
        name="stack",
        out_shape=jax.ShapeDtypeStruct((WIDTH, HOPS, 2, BINS, 512), jnp.float32),
        in_specs=[vmem, vmem, vmem],
        out_specs=hbm,
        scratch_shapes=[
            pltpu.VMEM((HOPS, WIDTH, 2, BINS, 512), jnp.float32),
            pltpu.SemaphoreType.DMA((HOPS,)),
        ],
        compiler_params=pltpu.CompilerParams(vmem_limit_bytes=24 * 2**20),
        cost_estimate=pl.CostEstimate(
            flops=2 * (SEL + WIDTH * 8) * COLS * 512 * HOPS,
            bytes_accessed=HOPS * 512 * (COLS * 2 + WIDTH * 8 * 4),
            transcendentals=0,
        ),
    )(g, lhs, rci)
    return out[None]


def solution(mesh):
    return jax.shard_map(
        per_device,
        mesh=mesh,
        in_specs=(P(None, None, None, "col", "row"), P("col", "row")),
        out_specs=P("col", "row", None, None, None, None),
        check_vma=False,
    )
```

```python
import functools

import jax
import jax.numpy as jnp
from jax import lax
from jax.experimental import pallas as pl
from jax.experimental.pallas import tpu as pltpu
from jax.sharding import PartitionSpec as P

MESH = pl.DeviceIdType.MESH
BINS = 4
SEGS = 30
USED = 2 * BINS * SEGS
COLS = 256
WIDTH = 64
HALF = 32
ROWS = 9
SHARED = 14
HOPS = 9
SEL = 16


def gather_kernel(spec_in, cnt_in, g, lhs, rci, spec, cnt, own, ssem, rsem, lsem):
    fetch = (
        pltpu.make_async_copy(spec_in, spec, lsem.at[1]),
        pltpu.make_async_copy(cnt_in, cnt, lsem.at[2]),
    )
    for copy in fetch:
        copy.start()
    r, d = lax.axis_index("row"), lax.axis_index("col")
    x, ylo = r % 4, r // 4
    c, q = d % 2, d // 2
    z, yhi = q % 4, q // 4

    def dev(x_, ylo_, q_, c_):
        return (ylo_ * 4 + x_, q_ * 2 + c_)

    sibling = dev(x, ylo, q, 1 - c)
    across = 1 - ylo

    at_x = [dev((x + i) % 4, ylo, q, c) for i in range(4)]
    right, left = at_x[1], at_x[3]
    pair = dev(x, across, q, c)
    far = dev(x, across, (q + 4) % 8, c)
    row_of = (ylo, across)
    plane = [(j, rel) for rel in (1, 0) for j in (0, 4, 1, 3, 2) if (j, rel) != (0, 0)]

    def plane_at(j, rel):
        return dev(x, row_of[rel], (q + j) % 8, c)

    barrier = pltpu.get_barrier_semaphore()
    sources = [plane_at(j, rel) for j, rel in plane] + at_x[1:] + [sibling]
    for source in sources:
        pl.semaphore_signal(barrier, inc=1, device_id=source, device_id_type=MESH)

    for copy in fetch:
        copy.wait()
    raw = spec[...]
    power = jnp.sum(raw * raw, axis=0, keepdims=True) / float(USED)
    row = lax.broadcasted_iota(jnp.int32, (USED, WIDTH), 0)
    group = jnp.zeros((USED, WIDTH), jnp.int32)
    for n in range(1, 2 * BINS):
        group = group + (row >= n * SEGS).astype(jnp.int32)
    valid = (row - SEGS * group < cnt[...]).astype(jnp.float32)
    white = raw * lax.rsqrt(power + 1e-6) * valid
    white = white.astype(jnp.bfloat16).astype(jnp.float32)
    count = cnt[...].astype(jnp.float32)
    pad = jnp.zeros((COLS - USED - 8, WIDTH), jnp.float32)
    first = lax.broadcasted_iota(jnp.int32, (8, WIDTH), 0) == 0
    tail = jnp.where(first, count, 0.0)
    straight = jnp.concatenate([white, tail, pad], axis=0).T
    own[...] = straight.astype(jnp.bfloat16)

    def plan(src, dst, device, send, recv):
        return pltpu.make_async_remote_copy(
            src_ref=src,
            dst_ref=dst,
            send_sem=ssem.at[send],
            recv_sem=rsem.at[recv],
            device_id=device,
            device_id_type=MESH,
        )

    def remote(src, dst, device, send, recv):
        copy = plan(src, dst, device, send, recv)
        copy.start()
        return copy

    def settle(region, sem):
        pltpu.make_async_copy(region, region, sem).wait()

    lo, hi = pl.ds(0, HALF), pl.ds(HALF, HALF)
    every = slice(None)
    pl.semaphore_wait(barrier, len(sources))
    for i in (1, 3, 2):
        remote(own, g.at[0, ylo, x], at_x[i], 0, 0)
    for j, rel in plane:
        remote(own.at[lo], g.at[j, ylo, x, lo], plane_at(-j, rel), 1, 1 + rel)
    local = pltpu.make_async_copy(own, g.at[0, ylo, x], lsem.at[0])
    local.start()

    swapped = jnp.concatenate(
        [white[USED // 2 :], -white[: USED // 2], jnp.zeros((COLS - USED, WIDTH), jnp.float32)],
        axis=0,
    ).T
    shape = (WIDTH, 8, COLS)
    sub = lax.broadcasted_iota(jnp.int32, (8, COLS), 0)
    lane = lax.broadcasted_iota(jnp.int32, (8, COLS), 1)
    low = (sub % BINS) * SEGS
    here = ((lane >= low) & (lane < low + SEGS)) | (
        (lane >= low + USED // 2) & (lane < low + USED // 2 + SEGS)
    )
    pick = jnp.where(
        (sub < BINS)[None],
        jnp.broadcast_to(straight[:, None, :], shape),
        jnp.broadcast_to(swapped[:, None, :], shape),
    )
    pick = jnp.where(here[None], pick, 0.0)
    sel = lax.broadcasted_iota(jnp.int32, (SEL, COLS), 1) == USED
    lhs[:SEL, :] = sel.astype(jnp.float32).astype(jnp.bfloat16)
    lhs[SEL:, :] = pick.reshape(WIDTH * 8, COLS).astype(jnp.bfloat16)
    mine = jnp.broadcast_to(1.0 / straight[:, USED : USED + 1], (WIDTH, 128))
    rci[...] = jnp.broadcast_to(mine[:, None, :], (WIDTH, 8, 128)).reshape(WIDTH * 8, 128)

    local.wait()

    def to_sibling(src_index, dst_index):
        remote(g.at[src_index], g.at[dst_index], sibling, 2, SHARED)

    def share_column(at):
        index = (every, at, lo)
        to_sibling((pl.ds(1 - c, 4),) + index, (pl.ds(5, 4),) + index)

    def share_rows(j, rows):
        to_sibling((j, rows, every, hi), (4 + j + c, rows, every, hi))

    settle(g.at[pl.ds(0, 3), 0, 0], rsem.at[0])
    for j, rel in plane:
        remote(g.at[0, ylo, :, hi], g.at[j, ylo, :, hi], plane_at(-j, rel), 3, ROWS + j)

    def along_x(rel, at, device, recv):
        blocks = pl.ds(0, 5) if rel else pl.ds(1, 4)
        column = g.at[blocks, row_of[rel], at, lo]
        return remote(column, column, device, 4 + rel, recv)

    xl, xr, xo = (x + 3) % 4, (x + 1) % 4, (x + 2) % 4
    settle(g.at[pl.ds(0, 5), 0, 0, lo], rsem.at[2])
    left_1 = along_x(1, x, left, 3)
    settle(g.at[pl.ds(0, 4), 0, 0, lo], rsem.at[1])
    right_0 = along_x(0, x, right, 4)
    right_1 = along_x(1, x, right, 5)
    left_0 = along_x(0, x, left, 6)
    share_column(x)

    left_1.wait_recv()
    on_left = along_x(1, xr, left, 7)
    right_0.wait_recv()
    on_right = along_x(0, xl, right, 8)

    settle(g.at[0, 0, :, hi], rsem.at[ROWS])
    settle(g.at[4, :, :, hi], rsem.at[ROWS + 4])
    share_rows(4 * (1 - c), every)
    for j in (1, 3):
        settle(g.at[j, :, :, hi], rsem.at[ROWS + j])
        share_rows(j, every)
    right_1.wait_recv()
    share_column(xl)
    left_0.wait_recv()
    share_column(xr)
    settle(g.at[2, :, :, hi], rsem.at[ROWS + 2])
    share_rows(2, every)
    on_right.wait_recv()
    on_left.wait_recv()
    share_column(xo)

    settle(g.at[pl.ds(5, 4)], rsem.at[SHARED])
    settle(g.at[pl.ds(0, 3), 0, 0], ssem.at[0])
    settle(g.at[pl.ds(0, 9), 0, 0, lo], ssem.at[1])
    settle(g.at[pl.ds(5, 4)], ssem.at[2])
    settle(g.at[pl.ds(0, 9), 0, :, hi], ssem.at[3])
    settle(g.at[pl.ds(0, 4), 0, pl.ds(0, 3), lo], ssem.at[4])
    settle(g.at[pl.ds(0, 5), 0, pl.ds(0, 3), lo], ssem.at[5])


def stack_kernel(g, lhs, rci, out, stage, sems):
    mine = rci[...]

    def held(k):
        return jnp.where(k % 2 == 0, k // 2, 5 + k // 2)

    def to_out(k):
        return pltpu.make_async_copy(stage.at[k], out.at[:, k], sems.at[k])

    @pl.loop(0, HOPS)
    def _(k):
        for n in (0, 1):
            result = lax.dot_general(
                lhs[...],
                g[held(k), n * 256 : (n + 1) * 256, :],
                (((1,), (1,)), ((), ())),
                preferred_element_type=jnp.float32,
            )
            recip = 1.0 / result[0:1]
            for t in (0, 1):
                lanes = slice(t * 128, (t + 1) * 128)
                scale = jnp.maximum(mine, recip[:, lanes])
                value = (result[SEL:, lanes] * scale).reshape(WIDTH, 8, 128)
                columns = slice(n * 256 + t * 128, n * 256 + (t + 1) * 128)
                stage[k, :, 0, :, columns] = value[:, :BINS]
                stage[k, :, 1, :, columns] = value[:, BINS:]
        to_out(k).start()

    @pl.loop(0, HOPS)
    def _(k):
        to_out(k).wait()


def per_device(spectra, counts):
    spec = spectra.reshape(USED, WIDTH)
    vmem = pl.BlockSpec(memory_space=pltpu.VMEM)
    hbm = pl.BlockSpec(memory_space=pltpu.HBM)
    g, lhs, rci = pl.pallas_call(
        gather_kernel,
        name="whiten_gather",
        out_shape=(
            jax.ShapeDtypeStruct((HOPS, 2, 4, WIDTH, COLS), jnp.bfloat16),
            jax.ShapeDtypeStruct((SEL + WIDTH * 8, COLS), jnp.bfloat16),
            jax.ShapeDtypeStruct((WIDTH * 8, 128), jnp.float32),
        ),
        in_specs=[hbm, hbm],
        out_specs=(vmem, vmem, vmem),
        scratch_shapes=[
            pltpu.VMEM((USED, WIDTH), jnp.float32),
            pltpu.VMEM((1, WIDTH), jnp.int32),
            pltpu.VMEM((WIDTH, COLS), jnp.bfloat16),
            pltpu.SemaphoreType.DMA((6,)),
            pltpu.SemaphoreType.DMA((SHARED + 1,)),
            pltpu.SemaphoreType.DMA((3,)),
        ],
        compiler_params=pltpu.CompilerParams(
            collective_id=0, has_side_effects=True, vmem_limit_bytes=16 * 2**20
        ),
    )(*(pltpu.with_memory_space_constraint(a, pltpu.HBM) for a in (spec, counts)))
    g = g.reshape(HOPS, 512, COLS)
    out = pl.pallas_call(
        stack_kernel,
        name="stack",
        out_shape=jax.ShapeDtypeStruct((WIDTH, HOPS, 2, BINS, 512), jnp.float32),
        in_specs=[vmem, vmem, vmem],
        out_specs=hbm,
        scratch_shapes=[
            pltpu.VMEM((HOPS, WIDTH, 2, BINS, 512), jnp.float32),
            pltpu.SemaphoreType.DMA((HOPS,)),
        ],
        compiler_params=pltpu.CompilerParams(vmem_limit_bytes=24 * 2**20),
        cost_estimate=pl.CostEstimate(
            flops=2 * (SEL + WIDTH * 8) * COLS * 512 * HOPS,
            bytes_accessed=HOPS * 512 * (COLS * 2 + WIDTH * 8 * 4),
            transcendentals=0,
        ),
    )(g, lhs, rci)
    return out[None]


def solution(mesh):
    return jax.shard_map(
        per_device,
        mesh=mesh,
        in_specs=(P(None, None, None, "col", "row"), P("col", "row")),
        out_specs=P("col", "row", None, None, None, None),
        check_vma=False,
    )
```

```python
import functools

import jax
import jax.numpy as jnp
from jax import lax
from jax.experimental import pallas as pl
from jax.experimental.pallas import tpu as pltpu
from jax.sharding import PartitionSpec as P

MESH = pl.DeviceIdType.MESH
BINS = 4
SEGS = 30
USED = 2 * BINS * SEGS
COLS = 256
WIDTH = 64
HALF = 32
SHARED = 13
HOPS = 9
SEL = 16


def gather_kernel(spec_in, cnt_in, gl, gh, lhs, rci, spec, cnt, own, ssem, rsem, lsem):
    fetch = (
        pltpu.make_async_copy(spec_in, spec, lsem.at[1]),
        pltpu.make_async_copy(cnt_in, cnt, lsem.at[2]),
    )
    for copy in fetch:
        copy.start()
    r, d = lax.axis_index("row"), lax.axis_index("col")
    x, ylo = r % 4, r // 4
    c, q = d % 2, d // 2
    z, yhi = q % 4, q // 4

    def dev(x_, ylo_, q_, c_):
        return (ylo_ * 4 + x_, q_ * 2 + c_)

    sibling = dev(x, ylo, q, 1 - c)
    across = 1 - ylo

    at_x = [dev((x + i) % 4, ylo, q, c) for i in range(4)]
    row_of = (ylo, across)
    plane = [(j, rel) for rel in (1, 0) for j in (0, 4, 1, 3, 2) if (j, rel) != (0, 0)]

    def plane_at(j, rel):
        return dev(x, row_of[rel], (q + j) % 8, c)

    barrier = pltpu.get_barrier_semaphore()
    layer = [(i, j, rel) for j, rel in ((4, 0), (4, 1), (0, 1), (0, 0)) for i in (2, 1, 3, 0)][:-1]

    def layer_at(i, j, rel):
        return dev((x + i) % 4, row_of[rel], (q + j) % 8, c)

    def along_z(e):
        return dev(x, ylo, yhi * 4 + (z + e) % 4, c)

    sources = [plane_at(j, rel) for j, rel in plane] + [layer_at(*at) for at in layer]
    sources += [along_z(e) for e in (1, 2, 3)] + [sibling]
    for source in sources:
        pl.semaphore_signal(barrier, inc=1, device_id=source, device_id_type=MESH)

    for copy in fetch:
        copy.wait()
    raw = spec[...]
    power = jnp.sum(raw * raw, axis=0, keepdims=True) / float(USED)
    row = lax.broadcasted_iota(jnp.int32, (USED, WIDTH), 0)
    group = jnp.zeros((USED, WIDTH), jnp.int32)
    for n in range(1, 2 * BINS):
        group = group + (row >= n * SEGS).astype(jnp.int32)
    valid = (row - SEGS * group < cnt[...]).astype(jnp.float32)
    white = raw * lax.rsqrt(power + 1e-6) * valid
    white = white.astype(jnp.bfloat16).astype(jnp.float32)
    count = cnt[...].astype(jnp.float32)
    pad = jnp.zeros((COLS - USED - 8, WIDTH), jnp.float32)
    first = lax.broadcasted_iota(jnp.int32, (8, WIDTH), 0) == 0
    tail = jnp.where(first, count, 0.0)
    straight = jnp.concatenate([white, tail, pad], axis=0).T
    own[...] = straight.astype(jnp.bfloat16)

    def plan(src, dst, device, send, recv):
        return pltpu.make_async_remote_copy(
            src_ref=src,
            dst_ref=dst,
            send_sem=ssem.at[send],
            recv_sem=rsem.at[recv],
            device_id=device,
            device_id_type=MESH,
        )

    def remote(src, dst, device, send, recv):
        copy = plan(src, dst, device, send, recv)
        copy.start()
        return copy

    def settle(region, sem):
        pltpu.make_async_copy(region, region, sem).wait()

    every = slice(None)
    own_lo, own_hi = own.at[pl.ds(0, HALF)], own.at[pl.ds(HALF, HALF)]
    pl.semaphore_wait(barrier, len(sources))
    for n, (j, rel) in enumerate(plane):
        remote(own_lo, gl.at[j, ylo, x], plane_at(-j, rel), 0, rel)
        for i, k, side in layer[2 * n : 2 * n + 2]:
            remote(own_hi, gh.at[k, ylo, x], layer_at(i, k, side), 1, 2 + k // 4)
    local = [
        pltpu.make_async_copy(own_lo, gl.at[0, ylo, x], lsem.at[0]),
        pltpu.make_async_copy(own_hi, gh.at[0, ylo, x], lsem.at[3]),
    ]
    for copy in local:
        copy.start()

    swapped = jnp.concatenate(
        [white[USED // 2 :], -white[: USED // 2], jnp.zeros((COLS - USED, WIDTH), jnp.float32)],
        axis=0,
    ).T
    shape = (WIDTH, 8, COLS)
    sub = lax.broadcasted_iota(jnp.int32, (8, COLS), 0)
    lane = lax.broadcasted_iota(jnp.int32, (8, COLS), 1)
    low = (sub % BINS) * SEGS
    here = ((lane >= low) & (lane < low + SEGS)) | (
        (lane >= low + USED // 2) & (lane < low + USED // 2 + SEGS)
    )
    pick = jnp.where(
        (sub < BINS)[None],
        jnp.broadcast_to(straight[:, None, :], shape),
        jnp.broadcast_to(swapped[:, None, :], shape),
    )
    pick = jnp.where(here[None], pick, 0.0)
    sel = lax.broadcasted_iota(jnp.int32, (SEL, COLS), 1) == USED
    lhs[:SEL, :] = sel.astype(jnp.float32).astype(jnp.bfloat16)
    lhs[SEL:, :] = pick.reshape(WIDTH * 8, COLS).astype(jnp.bfloat16)
    mine = jnp.broadcast_to(1.0 / straight[:, USED : USED + 1], (WIDTH, 128))
    rci[...] = jnp.broadcast_to(mine[:, None, :], (WIDTH, 8, 128)).reshape(WIDTH * 8, 128)

    for copy in local:
        copy.wait()

    def share_column(at):
        to = gl.at[pl.ds(5, 4), :, at]
        remote(gl.at[pl.ds(1 - c, 4), :, at], to, sibling, 2, SHARED)

    def share_block(j):
        remote(gh.at[j], gh.at[4 + j + c], sibling, 3, SHARED + 1)

    def along_x(rel, at, step, recv):
        column = gl.at[pl.ds(0, 5), row_of[rel], at]
        return remote(column, column, at_x[step], 4 + rel, recv)

    xl, xr, xo = (x + 3) % 4, (x + 1) % 4, (x + 2) % 4
    settle(gl.at[pl.ds(0, 5), 0, 0], rsem.at[1])
    left_1 = along_x(1, x, 3, 4)
    settle(gl.at[pl.ds(0, 4), 0, 0], rsem.at[0])
    two_0 = along_x(0, x, 2, 5)
    right_0 = along_x(0, x, 1, 6)
    left_0 = along_x(0, x, 3, 7)
    right_1 = along_x(1, x, 1, 8)

    z_copies = []
    for e in (2, 3, 1):
        zt = (z + 4 - e) % 4
        up = zt > z
        copy = plan(gh.at[jnp.where(up, 4, 0)], gh.at[e], along_z(-e), 6, 9 + e)
        z_copies.append((up, copy))
    settle(gh.at[pl.ds(0, 7), 0, 0], rsem.at[2])
    for up, copy in z_copies:
        pl.when(jnp.logical_not(up))(copy.start)
    settle(gh.at[0], rsem.at[3])
    for up, copy in z_copies:
        pl.when(up)(copy.start)
    share_column(x)
    share_block(4 * (1 - c))

    left_1.wait_recv()
    on_left = along_x(1, xr, 3, 9)
    right_0.wait_recv()
    left_0.wait_recv()
    share_column(xr)
    right_1.wait_recv()
    share_column(xl)
    for e in (1, 3):
        settle(gh.at[e], rsem.at[9 + e])
        share_block(e)
    two_0.wait_recv()
    on_left.wait_recv()
    share_column(xo)
    settle(gh.at[2], rsem.at[11])
    share_block(2)

    settle(gl.at[pl.ds(5, 4)], rsem.at[SHARED])
    settle(gh.at[pl.ds(5, 4)], rsem.at[SHARED + 1])
    settle(gl.at[pl.ds(0, 9), 0, 0], ssem.at[0])
    settle(gh.at[pl.ds(0, 5), 0, pl.ds(0, 3)], ssem.at[1])
    settle(gl.at[pl.ds(5, 4)], ssem.at[2])
    settle(gh.at[pl.ds(5, 4)], ssem.at[3])
    settle(gl.at[pl.ds(0, 5), 0, pl.ds(0, 3)], ssem.at[4])
    settle(gl.at[pl.ds(0, 5), 0, pl.ds(0, 3)], ssem.at[5])
    settle(gh.at[pl.ds(0, 3)], ssem.at[6])


def stack_kernel(gl, gh, lhs, rci, out, stage, sems):
    mine = rci[...]

    def held(k):
        return jnp.where(k % 2 == 0, k // 2, 5 + k // 2)

    def to_out(k):
        return pltpu.make_async_copy(stage.at[k], out.at[:, k], sems.at[k])

    @pl.loop(0, HOPS)
    def _(k):
        for n in (0, 1):
            right = [half[held(k), n, at] for at in range(4) for half in (gl, gh)]
            result = lax.dot_general(
                lhs[...],
                jnp.concatenate(right, axis=0),
                (((1,), (1,)), ((), ())),
                preferred_element_type=jnp.float32,
            )
            recip = 1.0 / result[0:1]
            for t in (0, 1):
                lanes = slice(t * 128, (t + 1) * 128)
                scale = jnp.maximum(mine, recip[:, lanes])
                value = (result[SEL:, lanes] * scale).reshape(WIDTH, 8, 128)
                columns = slice(n * 256 + t * 128, n * 256 + (t + 1) * 128)
                stage[k, :, 0, :, columns] = value[:, :BINS]
                stage[k, :, 1, :, columns] = value[:, BINS:]
        to_out(k).start()

    @pl.loop(0, HOPS)
    def _(k):
        to_out(k).wait()


def per_device(spectra, counts):
    spec = spectra.reshape(USED, WIDTH)
    vmem = pl.BlockSpec(memory_space=pltpu.VMEM)
    hbm = pl.BlockSpec(memory_space=pltpu.HBM)
    gl, gh, lhs, rci = pl.pallas_call(
        gather_kernel,
        name="whiten_gather",
        out_shape=(
            jax.ShapeDtypeStruct((HOPS, 2, 4, HALF, COLS), jnp.bfloat16),
            jax.ShapeDtypeStruct((HOPS, 2, 4, HALF, COLS), jnp.bfloat16),
            jax.ShapeDtypeStruct((SEL + WIDTH * 8, COLS), jnp.bfloat16),
            jax.ShapeDtypeStruct((WIDTH * 8, 128), jnp.float32),
        ),
        in_specs=[hbm, hbm],
        out_specs=(vmem,) * 4,
        scratch_shapes=[
            pltpu.VMEM((USED, WIDTH), jnp.float32),
            pltpu.VMEM((1, WIDTH), jnp.int32),
            pltpu.VMEM((WIDTH, COLS), jnp.bfloat16),
            pltpu.SemaphoreType.DMA((7,)),
            pltpu.SemaphoreType.DMA((SHARED + 2,)),
            pltpu.SemaphoreType.DMA((4,)),
        ],
        compiler_params=pltpu.CompilerParams(
            collective_id=0, has_side_effects=True, vmem_limit_bytes=16 * 2**20
        ),
    )(*(pltpu.with_memory_space_constraint(a, pltpu.HBM) for a in (spec, counts)))
    out = pl.pallas_call(
        stack_kernel,
        name="stack",
        out_shape=jax.ShapeDtypeStruct((WIDTH, HOPS, 2, BINS, 512), jnp.float32),
        in_specs=[vmem] * 4,
        out_specs=hbm,
        scratch_shapes=[
            pltpu.VMEM((HOPS, WIDTH, 2, BINS, 512), jnp.float32),
            pltpu.SemaphoreType.DMA((HOPS,)),
        ],
        compiler_params=pltpu.CompilerParams(vmem_limit_bytes=24 * 2**20),
        cost_estimate=pl.CostEstimate(
            flops=2 * (SEL + WIDTH * 8) * COLS * 512 * HOPS,
            bytes_accessed=HOPS * 512 * (COLS * 2 + WIDTH * 8 * 4),
            transcendentals=0,
        ),
    )(gl, gh, lhs, rci)
    return out[None]


def solution(mesh):
    return jax.shard_map(
        per_device,
        mesh=mesh,
        in_specs=(P(None, None, None, "col", "row"), P("col", "row")),
        out_specs=P("col", "row", None, None, None, None),
        check_vma=False,
    )
```

```python
import functools

import jax
import jax.numpy as jnp
from jax import lax
from jax.experimental import pallas as pl
from jax.experimental.pallas import tpu as pltpu
from jax.sharding import PartitionSpec as P

MESH = pl.DeviceIdType.MESH
BINS = 4
SEGS = 30
USED = 2 * BINS * SEGS
COLS = 256
WIDTH = 64
HALF = 32
HOPS = 9
SEL = 16


def gather_kernel(spec_in, cnt_in, g, lhs, rci, spec, cnt, own, ssem, rsem, lsem):
    fetch = (
        pltpu.make_async_copy(spec_in, spec, lsem.at[1]),
        pltpu.make_async_copy(cnt_in, cnt, lsem.at[2]),
    )
    for copy in fetch:
        copy.start()
    r, d = lax.axis_index("row"), lax.axis_index("col")
    x, ylo = r % 4, r // 4
    c, q = d % 2, d // 2
    z, yhi = q % 4, q // 4

    def dev(x_, ylo_, q_, c_):
        return (ylo_ * 4 + x_, q_ * 2 + c_)

    sibling = dev(x, ylo, q, 1 - c)
    other = 1 - ylo

    def at_y(rel):
        return other if rel else ylo

    plane = [(0, 1)] + [(j, rel) for j in range(1, 5) for rel in (0, 1)]

    barrier = pltpu.get_barrier_semaphore()
    sources = [dev(x, at_y(rel), (q + j) % 8, c) for j, rel in plane]
    sources += [dev((x + i) % 4, ylo, q, c) for i in (1, 2, 3)]
    sources += [dev(x, ylo, yhi * 4 + (z + e) % 4, c) for e in (1, 2, 3)]
    sources += [sibling]
    for source in sources:
        pl.semaphore_signal(barrier, inc=1, device_id=source, device_id_type=MESH)

    for copy in fetch:
        copy.wait()
    raw = spec[...]
    power = jnp.sum(raw * raw, axis=0, keepdims=True) / float(USED)
    row = lax.broadcasted_iota(jnp.int32, (USED, WIDTH), 0)
    group = jnp.zeros((USED, WIDTH), jnp.int32)
    for n in range(1, 2 * BINS):
        group = group + (row >= n * SEGS).astype(jnp.int32)
    valid = (row - SEGS * group < cnt[...]).astype(jnp.float32)
    white = raw * lax.rsqrt(power + 1e-6) * valid
    white = white.astype(jnp.bfloat16).astype(jnp.float32)
    count = cnt[...].astype(jnp.float32)
    pad = jnp.zeros((COLS - USED - 8, WIDTH), jnp.float32)
    first = lax.broadcasted_iota(jnp.int32, (8, WIDTH), 0) == 0
    tail = jnp.where(first, count, 0.0)
    straight = jnp.concatenate([white, tail, pad], axis=0).T
    own[...] = straight.astype(jnp.bfloat16)

    def remote(src, dst, device, send, recv):
        copy = pltpu.make_async_remote_copy(
            src_ref=src,
            dst_ref=dst,
            send_sem=ssem.at[send],
            recv_sem=rsem.at[recv],
            device_id=device,
            device_id_type=MESH,
        )
        copy.start()
        return copy

    def settle(region, sem):
        pltpu.make_async_copy(region, region, sem).wait()

    lo, hi = pl.ds(0, HALF), pl.ds(HALF, HALF)
    own_blocks = pl.ds(0, 5)

    pl.semaphore_wait(barrier, len(sources))
    for i in (1, 3, 2):
        remote(own.at[hi], g.at[0, ylo, x, hi], dev((x + i) % 4, ylo, q, c), 0, 0)
    for j, rel in plane:
        remote(own.at[lo], g.at[j, ylo, x, lo], dev(x, at_y(rel), (q - j) % 8, c), 1, 1)
    local = pltpu.make_async_copy(own, g.at[0, ylo, x], lsem.at[0])
    local.start()

    local.wait()

    settle(g.at[pl.ds(0, 3), 0, 0, hi], rsem.at[0])
    row = g.at[0, ylo, :, hi]
    for j, rel in ((4, 1), (0, 1), (4, 0)):
        remote(row, g.at[j, ylo, :, hi], dev(x, at_y(rel), (q - j) % 8, c), 2, 2)

    right, left = dev((x + 1) % 4, ylo, q, c), dev((x + 3) % 4, ylo, q, c)
    settle(g.at[pl.ds(0, 9), 0, 0, lo], rsem.at[1])
    columns = [g.at[own_blocks, rel, x, lo] for rel in (0, 1)]
    to_right = [remote(columns[0], columns[0], right, 3, 3)]
    to_left = {1: remote(columns[1], columns[1], left, 3, 4)}
    to_right.append(remote(columns[1], columns[1], right, 3, 5))
    to_left[0] = remote(columns[0], columns[0], left, 3, 6)

    def share(src_index, dst_index, recv):
        remote(g.at[src_index], g.at[dst_index], sibling, 5, recv)

    def share_column(column):
        share((pl.ds(1 - c, 4), slice(None), column, lo), (pl.ds(5, 4), slice(None), column, lo), 12)

    def share_block(j):
        at = 4 + j + c
        share((j, slice(None), slice(None), hi), (at, slice(None), slice(None), hi), 12)

    settle(g.at[pl.ds(0, 3), 0, :, hi], rsem.at[2])
    along_z = {}
    for e in (1, 3, 2):
        zt = (z + 4 - e) % 4
        block = jnp.where(zt > z, 4, 0)
        along_z[e] = remote(
            g.at[block, :, :, hi], g.at[e, :, :, hi], dev(x, ylo, yhi * 4 + zt, c), 4, 6 + e
        )
    share_column(x)
    share_block(4 * (1 - c))

    xl, xr, xo = (x + 3) % 4, (x + 1) % 4, (x + 2) % 4
    to_right[0].wait_recv()
    piece = g.at[own_blocks, 0, xl, lo]
    on_right = remote(piece, piece, right, 3, 10)
    to_left[1].wait_recv()
    piece = g.at[own_blocks, 1, xr, lo]
    on_left = remote(piece, piece, left, 3, 11)
    to_right[1].wait_recv()
    share_column(xl)
    to_left[0].wait_recv()
    share_column(xr)
    swapped = jnp.concatenate(
        [white[USED // 2 :], -white[: USED // 2], jnp.zeros((COLS - USED, WIDTH), jnp.float32)],
        axis=0,
    ).T
    shape = (WIDTH, 8, COLS)
    sub = lax.broadcasted_iota(jnp.int32, (8, COLS), 0)
    lane = lax.broadcasted_iota(jnp.int32, (8, COLS), 1)
    low = (sub % BINS) * SEGS
    here = ((lane >= low) & (lane < low + SEGS)) | (
        (lane >= low + USED // 2) & (lane < low + USED // 2 + SEGS)
    )
    pick = jnp.where(
        (sub < BINS)[None],
        jnp.broadcast_to(straight[:, None, :], shape),
        jnp.broadcast_to(swapped[:, None, :], shape),
    )
    pick = jnp.where(here[None], pick, 0.0)
    sel = lax.broadcasted_iota(jnp.int32, (SEL, COLS), 1) == USED
    lhs[:SEL, :] = sel.astype(jnp.float32).astype(jnp.bfloat16)
    lhs[SEL:, :] = pick.reshape(WIDTH * 8, COLS).astype(jnp.bfloat16)
    mine = jnp.broadcast_to(1.0 / straight[:, USED : USED + 1], (WIDTH, 128))
    rci[...] = jnp.broadcast_to(mine[:, None, :], (WIDTH, 8, 128)).reshape(WIDTH * 8, 128)

    for e in (1, 3):
        along_z[e].wait_recv()
        share_block(e)
    on_right.wait_recv()
    on_left.wait_recv()
    share_column(xo)
    along_z[2].wait_recv()
    share_block(2)

    settle(g.at[pl.ds(5, 4)], rsem.at[12])
    settle(g.at[pl.ds(0, 3), 0, 0, hi], ssem.at[0])
    settle(g.at[pl.ds(0, 9), 0, 0, lo], ssem.at[1])
    settle(g.at[pl.ds(0, 3), 0, :, hi], ssem.at[2])
    settle(g.at[pl.ds(0, 5), 0, pl.ds(0, 3)], ssem.at[3])
    settle(g.at[pl.ds(0, 3), :, :, hi], ssem.at[4])
    settle(g.at[pl.ds(5, 4)], ssem.at[5])


def stack_kernel(g, lhs, rci, out, stage, sems):
    mine = rci[...]

    def held(k):
        return jnp.where(k % 2 == 0, k // 2, 5 + k // 2)

    def to_out(k):
        return pltpu.make_async_copy(stage.at[k], out.at[:, k], sems.at[k])

    @pl.loop(0, HOPS)
    def _(k):
        for n in (0, 1):
            result = lax.dot_general(
                lhs[...],
                g[held(k), n * 256 : (n + 1) * 256, :],
                (((1,), (1,)), ((), ())),
                preferred_element_type=jnp.float32,
            )
            recip = 1.0 / result[0:1]
            for t in (0, 1):
                lanes = slice(t * 128, (t + 1) * 128)
                scale = jnp.maximum(mine, recip[:, lanes])
                value = (result[SEL:, lanes] * scale).reshape(WIDTH, 8, 128)
                columns = slice(n * 256 + t * 128, n * 256 + (t + 1) * 128)
                stage[k, :, 0, :, columns] = value[:, :BINS]
                stage[k, :, 1, :, columns] = value[:, BINS:]
        to_out(k).start()

    @pl.loop(0, HOPS)
    def _(k):
        to_out(k).wait()


def per_device(spectra, counts):
    spec = spectra.reshape(USED, WIDTH)
    vmem = pl.BlockSpec(memory_space=pltpu.VMEM)
    hbm = pl.BlockSpec(memory_space=pltpu.HBM)
    g, lhs, rci = pl.pallas_call(
        gather_kernel,
        name="whiten_gather",
        out_shape=(
            jax.ShapeDtypeStruct((HOPS, 2, 4, WIDTH, COLS), jnp.bfloat16),
            jax.ShapeDtypeStruct((SEL + WIDTH * 8, COLS), jnp.bfloat16),
            jax.ShapeDtypeStruct((WIDTH * 8, 128), jnp.float32),
        ),
        in_specs=[hbm, hbm],
        out_specs=(vmem, vmem, vmem),
        scratch_shapes=[
            pltpu.VMEM((USED, WIDTH), jnp.float32),
            pltpu.VMEM((1, WIDTH), jnp.int32),
            pltpu.VMEM((WIDTH, COLS), jnp.bfloat16),
            pltpu.SemaphoreType.DMA((6,)),
            pltpu.SemaphoreType.DMA((13,)),
            pltpu.SemaphoreType.DMA((3,)),
        ],
        compiler_params=pltpu.CompilerParams(
            collective_id=0, has_side_effects=True, vmem_limit_bytes=16 * 2**20
        ),
    )(*(pltpu.with_memory_space_constraint(a, pltpu.HBM) for a in (spec, counts)))
    g = g.reshape(HOPS, 512, COLS)
    out = pl.pallas_call(
        stack_kernel,
        name="stack",
        out_shape=jax.ShapeDtypeStruct((WIDTH, HOPS, 2, BINS, 512), jnp.float32),
        in_specs=[vmem, vmem, vmem],
        out_specs=hbm,
        scratch_shapes=[
            pltpu.VMEM((HOPS, WIDTH, 2, BINS, 512), jnp.float32),
            pltpu.SemaphoreType.DMA((HOPS,)),
        ],
        compiler_params=pltpu.CompilerParams(vmem_limit_bytes=24 * 2**20),
        cost_estimate=pl.CostEstimate(
            flops=2 * (SEL + WIDTH * 8) * COLS * 512 * HOPS,
            bytes_accessed=HOPS * 512 * (COLS * 2 + WIDTH * 8 * 4),
            transcendentals=0,
        ),
    )(g, lhs, rci)
    return out[None]


def solution(mesh):
    return jax.shard_map(
        per_device,
        mesh=mesh,
        in_specs=(P(None, None, None, "col", "row"), P("col", "row")),
        out_specs=P("col", "row", None, None, None, None),
        check_vma=False,
    )
```

```python
import functools

import jax
import jax.numpy as jnp
from jax import lax
from jax.experimental import pallas as pl
from jax.experimental.pallas import tpu as pltpu
from jax.sharding import PartitionSpec as P

MESH = pl.DeviceIdType.MESH
BINS = 4
SEGS = 30
USED = 2 * BINS * SEGS
COLS = 256
WIDTH = 64
HALF = 32
HOPS = 9
SEL = 16


def gather_kernel(spec_in, cnt_in, g, lhs, rci, spec, cnt, own, ssem, rsem, lsem):
    fetch = (
        pltpu.make_async_copy(spec_in, spec, lsem.at[1]),
        pltpu.make_async_copy(cnt_in, cnt, lsem.at[2]),
    )
    for copy in fetch:
        copy.start()
    r, d = lax.axis_index("row"), lax.axis_index("col")
    x, ylo = r % 4, r // 4
    c, q = d % 2, d // 2
    z, yhi = q % 4, q // 4

    def dev(x_, ylo_, q_, c_):
        return (ylo_ * 4 + x_, q_ * 2 + c_)

    sibling = dev(x, ylo, q, 1 - c)
    other = 1 - ylo

    def at_y(rel):
        return other if rel else ylo

    plane = [(0, 1)] + [(j, rel) for j in range(1, 5) for rel in (0, 1)]

    barrier = pltpu.get_barrier_semaphore()
    sources = [dev(x, at_y(rel), (q + j) % 8, c) for j, rel in plane]
    sources += [dev((x + i) % 4, ylo, q, c) for i in (1, 2, 3)]
    sources += [dev(x, ylo, yhi * 4 + (z + e) % 4, c) for e in (1, 2, 3)]
    sources += [sibling]
    for source in sources:
        pl.semaphore_signal(barrier, inc=1, device_id=source, device_id_type=MESH)

    for copy in fetch:
        copy.wait()
    raw = spec[...]
    power = jnp.sum(raw * raw, axis=0, keepdims=True) / float(USED)
    row = lax.broadcasted_iota(jnp.int32, (USED, WIDTH), 0)
    group = jnp.zeros((USED, WIDTH), jnp.int32)
    for n in range(1, 2 * BINS):
        group = group + (row >= n * SEGS).astype(jnp.int32)
    valid = (row - SEGS * group < cnt[...]).astype(jnp.float32)
    white = raw * lax.rsqrt(power + 1e-6) * valid
    white = white.astype(jnp.bfloat16).astype(jnp.float32)
    count = cnt[...].astype(jnp.float32)
    pad = jnp.zeros((COLS - USED - 8, WIDTH), jnp.float32)
    first = lax.broadcasted_iota(jnp.int32, (8, WIDTH), 0) == 0
    tail = jnp.where(first, count, 0.0)
    straight = jnp.concatenate([white, tail, pad], axis=0).T
    own[...] = straight.astype(jnp.bfloat16)

    def remote(src, dst, device, send, recv):
        copy = pltpu.make_async_remote_copy(
            src_ref=src,
            dst_ref=dst,
            send_sem=ssem.at[send],
            recv_sem=rsem.at[recv],
            device_id=device,
            device_id_type=MESH,
        )
        copy.start()
        return copy

    def settle(region, sem):
        pltpu.make_async_copy(region, region, sem).wait()

    lo, hi = pl.ds(0, HALF), pl.ds(HALF, HALF)
    own_blocks = pl.ds(0, 5)

    pl.semaphore_wait(barrier, len(sources))
    for i in (1, 3, 2):
        remote(own.at[hi], g.at[0, ylo, x, hi], dev((x + i) % 4, ylo, q, c), 0, 0)
    for j, rel in plane:
        remote(own.at[lo], g.at[j, ylo, x, lo], dev(x, at_y(rel), (q - j) % 8, c), 1, 1)
    local = pltpu.make_async_copy(own, g.at[0, ylo, x], lsem.at[0])
    local.start()

    local.wait()

    settle(g.at[pl.ds(0, 3), 0, 0, hi], rsem.at[0])
    row = g.at[0, ylo, :, hi]
    for j, rel in ((4, 1), (0, 1), (4, 0)):
        remote(row, g.at[j, ylo, :, hi], dev(x, at_y(rel), (q - j) % 8, c), 2, 2)

    settle(g.at[pl.ds(0, 9), 0, 0, lo], rsem.at[1])
    column = g.at[own_blocks, :, x, lo]
    two, from_left, from_right = (
        remote(column, column, dev((x + i) % 4, ylo, q, c), 3, 3 + n)
        for n, i in enumerate((2, 1, 3))
    )

    def share(src_index, dst_index, recv):
        remote(g.at[src_index], g.at[dst_index], sibling, 5, recv)

    def share_column(column):
        share((pl.ds(1 - c, 4), slice(None), column, lo), (pl.ds(5, 4), slice(None), column, lo), 12)

    def share_block(j):
        at = 4 + j + c
        share((j, slice(None), slice(None), hi), (at, slice(None), slice(None), hi), 12)

    settle(g.at[pl.ds(0, 3), 0, :, hi], rsem.at[2])
    along_z = {}
    for e in (1, 3, 2):
        zt = (z + 4 - e) % 4
        block = jnp.where(zt > z, 4, 0)
        along_z[e] = remote(
            g.at[block, :, :, hi], g.at[e, :, :, hi], dev(x, ylo, yhi * 4 + zt, c), 4, 6 + e
        )
    share_column(x)
    share_block(4 * (1 - c))

    xl, xr, xo = (x + 3) % 4, (x + 1) % 4, (x + 2) % 4
    from_left.wait_recv()
    share_column(xl)
    from_right.wait_recv()
    share_column(xr)
    swapped = jnp.concatenate(
        [white[USED // 2 :], -white[: USED // 2], jnp.zeros((COLS - USED, WIDTH), jnp.float32)],
        axis=0,
    ).T
    shape = (WIDTH, 8, COLS)
    sub = lax.broadcasted_iota(jnp.int32, (8, COLS), 0)
    lane = lax.broadcasted_iota(jnp.int32, (8, COLS), 1)
    low = (sub % BINS) * SEGS
    here = ((lane >= low) & (lane < low + SEGS)) | (
        (lane >= low + USED // 2) & (lane < low + USED // 2 + SEGS)
    )
    pick = jnp.where(
        (sub < BINS)[None],
        jnp.broadcast_to(straight[:, None, :], shape),
        jnp.broadcast_to(swapped[:, None, :], shape),
    )
    pick = jnp.where(here[None], pick, 0.0)
    sel = lax.broadcasted_iota(jnp.int32, (SEL, COLS), 1) == USED
    lhs[:SEL, :] = sel.astype(jnp.float32).astype(jnp.bfloat16)
    lhs[SEL:, :] = pick.reshape(WIDTH * 8, COLS).astype(jnp.bfloat16)
    mine = jnp.broadcast_to(1.0 / straight[:, USED : USED + 1], (WIDTH, 128))
    rci[...] = jnp.broadcast_to(mine[:, None, :], (WIDTH, 8, 128)).reshape(WIDTH * 8, 128)

    for e in (1, 3):
        along_z[e].wait_recv()
        share_block(e)
    two.wait_recv()
    share_column(xo)
    along_z[2].wait_recv()
    share_block(2)

    settle(g.at[pl.ds(5, 4)], rsem.at[12])
    settle(g.at[pl.ds(0, 3), 0, 0, hi], ssem.at[0])
    settle(g.at[pl.ds(0, 9), 0, 0, lo], ssem.at[1])
    settle(g.at[pl.ds(0, 3), 0, :, hi], ssem.at[2])
    settle(g.at[pl.ds(0, 5), 0, pl.ds(0, 3)], ssem.at[3])
    settle(g.at[pl.ds(0, 3), :, :, hi], ssem.at[4])
    settle(g.at[pl.ds(5, 4)], ssem.at[5])


def stack_kernel(g, lhs, rci, out, stage, sems):
    mine = rci[...]

    def held(k):
        return jnp.where(k % 2 == 0, k // 2, 5 + k // 2)

    def to_out(k):
        return pltpu.make_async_copy(stage.at[k], out.at[:, k], sems.at[k])

    @pl.loop(0, HOPS)
    def _(k):
        for n in (0, 1):
            result = lax.dot_general(
                lhs[...],
                g[held(k), n * 256 : (n + 1) * 256, :],
                (((1,), (1,)), ((), ())),
                preferred_element_type=jnp.float32,
            )
            recip = 1.0 / result[0:1]
            for t in (0, 1):
                lanes = slice(t * 128, (t + 1) * 128)
                scale = jnp.maximum(mine, recip[:, lanes])
                value = (result[SEL:, lanes] * scale).reshape(WIDTH, 8, 128)
                columns = slice(n * 256 + t * 128, n * 256 + (t + 1) * 128)
                stage[k, :, 0, :, columns] = value[:, :BINS]
                stage[k, :, 1, :, columns] = value[:, BINS:]
        to_out(k).start()

    @pl.loop(0, HOPS)
    def _(k):
        to_out(k).wait()


def per_device(spectra, counts):
    spec = spectra.reshape(USED, WIDTH)
    vmem = pl.BlockSpec(memory_space=pltpu.VMEM)
    hbm = pl.BlockSpec(memory_space=pltpu.HBM)
    g, lhs, rci = pl.pallas_call(
        gather_kernel,
        name="whiten_gather",
        out_shape=(
            jax.ShapeDtypeStruct((HOPS, 2, 4, WIDTH, COLS), jnp.bfloat16),
            jax.ShapeDtypeStruct((SEL + WIDTH * 8, COLS), jnp.bfloat16),
            jax.ShapeDtypeStruct((WIDTH * 8, 128), jnp.float32),
        ),
        in_specs=[hbm, hbm],
        out_specs=(vmem, vmem, vmem),
        scratch_shapes=[
            pltpu.VMEM((USED, WIDTH), jnp.float32),
            pltpu.VMEM((1, WIDTH), jnp.int32),
            pltpu.VMEM((WIDTH, COLS), jnp.bfloat16),
            pltpu.SemaphoreType.DMA((6,)),
            pltpu.SemaphoreType.DMA((13,)),
            pltpu.SemaphoreType.DMA((3,)),
        ],
        compiler_params=pltpu.CompilerParams(
            collective_id=0, has_side_effects=True, vmem_limit_bytes=16 * 2**20
        ),
    )(*(pltpu.with_memory_space_constraint(a, pltpu.HBM) for a in (spec, counts)))
    g = g.reshape(HOPS, 512, COLS)
    out = pl.pallas_call(
        stack_kernel,
        name="stack",
        out_shape=jax.ShapeDtypeStruct((WIDTH, HOPS, 2, BINS, 512), jnp.float32),
        in_specs=[vmem, vmem, vmem],
        out_specs=hbm,
        scratch_shapes=[
            pltpu.VMEM((HOPS, WIDTH, 2, BINS, 512), jnp.float32),
            pltpu.SemaphoreType.DMA((HOPS,)),
        ],
        compiler_params=pltpu.CompilerParams(vmem_limit_bytes=24 * 2**20),
        cost_estimate=pl.CostEstimate(
            flops=2 * (SEL + WIDTH * 8) * COLS * 512 * HOPS,
            bytes_accessed=HOPS * 512 * (COLS * 2 + WIDTH * 8 * 4),
            transcendentals=0,
        ),
    )(g, lhs, rci)
    return out[None]


def solution(mesh):
    return jax.shard_map(
        per_device,
        mesh=mesh,
        in_specs=(P(None, None, None, "col", "row"), P("col", "row")),
        out_specs=P("col", "row", None, None, None, None),
        check_vma=False,
    )
```

```python
import functools

import jax
import jax.numpy as jnp
from jax import lax
from jax.experimental import pallas as pl
from jax.experimental.pallas import tpu as pltpu
from jax.sharding import PartitionSpec as P

MESH = pl.DeviceIdType.MESH
BINS = 4
SEGS = 30
USED = 2 * BINS * SEGS
COLS = 256
WIDTH = 64
HALF = 32
HOPS = 9
SEL = 16


def gather_kernel(spec_in, cnt_in, g, lhs, rci, spec, cnt, own, ssem, rsem, lsem):
    fetch = (
        pltpu.make_async_copy(spec_in, spec, lsem.at[1]),
        pltpu.make_async_copy(cnt_in, cnt, lsem.at[2]),
    )
    for copy in fetch:
        copy.start()
    r, d = lax.axis_index("row"), lax.axis_index("col")
    x, ylo = r % 4, r // 4
    c, q = d % 2, d // 2
    z, yhi = q % 4, q // 4

    def dev(x_, ylo_, q_, c_):
        return (ylo_ * 4 + x_, q_ * 2 + c_)

    sibling = dev(x, ylo, q, 1 - c)
    other = 1 - ylo

    def at_y(rel):
        return other if rel else ylo

    plane = [(0, 1)] + [(j, rel) for j in range(1, 5) for rel in (0, 1)]

    barrier = pltpu.get_barrier_semaphore()
    sources = [dev(x, at_y(rel), (q + j) % 8, c) for j, rel in plane]
    sources += [dev((x + i) % 4, ylo, q, c) for i in (1, 2, 3)]
    sources += [dev(x, ylo, yhi * 4 + (z + e) % 4, c) for e in (1, 2, 3)]
    sources += [sibling]
    for source in sources:
        pl.semaphore_signal(barrier, inc=1, device_id=source, device_id_type=MESH)

    for copy in fetch:
        copy.wait()
    raw = spec[...]
    power = jnp.sum(raw * raw, axis=0, keepdims=True) / float(USED)
    row = lax.broadcasted_iota(jnp.int32, (USED, WIDTH), 0)
    group = jnp.zeros((USED, WIDTH), jnp.int32)
    for n in range(1, 2 * BINS):
        group = group + (row >= n * SEGS).astype(jnp.int32)
    valid = (row - SEGS * group < cnt[...]).astype(jnp.float32)
    white = raw * lax.rsqrt(power + 1e-6) * valid
    white = white.astype(jnp.bfloat16).astype(jnp.float32)
    count = cnt[...].astype(jnp.float32)
    pad = jnp.zeros((COLS - USED - 8, WIDTH), jnp.float32)
    first = lax.broadcasted_iota(jnp.int32, (8, WIDTH), 0) == 0
    tail = jnp.where(first, count, 0.0)
    straight = jnp.concatenate([white, tail, pad], axis=0).T
    own[...] = straight.astype(jnp.bfloat16)

    def remote(src, dst, device, send, recv):
        copy = pltpu.make_async_remote_copy(
            src_ref=src,
            dst_ref=dst,
            send_sem=ssem.at[send],
            recv_sem=rsem.at[recv],
            device_id=device,
            device_id_type=MESH,
        )
        copy.start()
        return copy

    def settle(region, sem):
        pltpu.make_async_copy(region, region, sem).wait()

    lo, hi = pl.ds(0, HALF), pl.ds(HALF, HALF)
    own_blocks = pl.ds(0, 5)

    pl.semaphore_wait(barrier, len(sources))
    for i in (1, 3, 2):
        remote(own.at[hi], g.at[0, ylo, x, hi], dev((x + i) % 4, ylo, q, c), 0, 0)
    for j, rel in plane:
        remote(own.at[lo], g.at[j, ylo, x, lo], dev(x, at_y(rel), (q - j) % 8, c), 1, 1)
    local = pltpu.make_async_copy(own, g.at[0, ylo, x], lsem.at[0])
    local.start()

    local.wait()

    settle(g.at[pl.ds(0, 3), 0, 0, hi], rsem.at[0])
    row = g.at[0, ylo, :, hi]
    for j, rel in ((4, 1), (0, 1), (4, 0)):
        remote(row, g.at[j, ylo, :, hi], dev(x, at_y(rel), (q - j) % 8, c), 2, 2)

    right, left = dev((x + 1) % 4, ylo, q, c), dev((x + 3) % 4, ylo, q, c)
    settle(g.at[pl.ds(0, 9), 0, 0, lo], rsem.at[1])
    columns = [g.at[own_blocks, rel, x, lo] for rel in (0, 1)]
    to_right = [remote(columns[0], columns[0], right, 3, 3)]
    to_left = {1: remote(columns[1], columns[1], left, 3, 4)}
    to_right.append(remote(columns[1], columns[1], right, 3, 5))
    to_left[0] = remote(columns[0], columns[0], left, 3, 6)

    def share(src_index, dst_index, recv):
        remote(g.at[src_index], g.at[dst_index], sibling, 5, recv)

    def share_column(column):
        share((pl.ds(1 - c, 4), slice(None), column, lo), (pl.ds(5, 4), slice(None), column, lo), 12)

    def share_block(j):
        at = 4 + j + c
        share((j, slice(None), slice(None), hi), (at, slice(None), slice(None), hi), 12)

    settle(g.at[pl.ds(0, 3), 0, :, hi], rsem.at[2])
    along_z = {}
    for e in (1, 3, 2):
        zt = (z + 4 - e) % 4
        block = jnp.where(zt > z, 4, 0)
        along_z[e] = remote(
            g.at[block, :, :, hi], g.at[e, :, :, hi], dev(x, ylo, yhi * 4 + zt, c), 4, 6 + e
        )
    share_column(x)
    share_block(4 * (1 - c))

    xl, xr, xo = (x + 3) % 4, (x + 1) % 4, (x + 2) % 4
    to_right[0].wait_recv()
    piece = g.at[own_blocks, 0, xl, lo]
    on_right = remote(piece, piece, right, 3, 10)
    to_left[1].wait_recv()
    piece = g.at[own_blocks, 1, xr, lo]
    on_left = remote(piece, piece, left, 3, 11)
    to_right[1].wait_recv()
    share_column(xl)
    to_left[0].wait_recv()
    share_column(xr)
    swapped = jnp.concatenate(
        [white[USED // 2 :], -white[: USED // 2], jnp.zeros((COLS - USED, WIDTH), jnp.float32)],
        axis=0,
    ).T
    shape = (WIDTH, 8, COLS)
    sub = lax.broadcasted_iota(jnp.int32, (8, COLS), 0)
    lane = lax.broadcasted_iota(jnp.int32, (8, COLS), 1)
    low = (sub % BINS) * SEGS
    here = ((lane >= low) & (lane < low + SEGS)) | (
        (lane >= low + USED // 2) & (lane < low + USED // 2 + SEGS)
    )
    one = jnp.broadcast_to(straight[:, None, :], shape)
    two = jnp.broadcast_to(swapped[:, None, :], shape)
    sel = lax.broadcasted_iota(jnp.int32, (SEL, COLS), 1) == USED
    for odd in (0, 1):
        pick = jnp.where(((sub < BINS) == (odd == 0))[None], one, two)
        pick = jnp.where(here[None], pick, 0.0)
        lhs[odd, :SEL, :] = sel.astype(jnp.float32).astype(jnp.bfloat16)
        lhs[odd, SEL:, :] = pick.reshape(WIDTH * 8, COLS).astype(jnp.bfloat16)
    mine = jnp.broadcast_to(1.0 / straight[:, USED : USED + 1], (WIDTH, 128))
    rci[...] = jnp.broadcast_to(mine[:, None, :], (WIDTH, 8, 128)).reshape(WIDTH * 8, 128)

    for e in (1, 3):
        along_z[e].wait_recv()
        share_block(e)
    on_right.wait_recv()
    on_left.wait_recv()
    share_column(xo)
    along_z[2].wait_recv()
    share_block(2)

    settle(g.at[pl.ds(5, 4)], rsem.at[12])
    settle(g.at[pl.ds(0, 3), 0, 0, hi], ssem.at[0])
    settle(g.at[pl.ds(0, 9), 0, 0, lo], ssem.at[1])
    settle(g.at[pl.ds(0, 3), 0, :, hi], ssem.at[2])
    settle(g.at[pl.ds(0, 5), 0, pl.ds(0, 3)], ssem.at[3])
    settle(g.at[pl.ds(0, 3), :, :, hi], ssem.at[4])
    settle(g.at[pl.ds(5, 4)], ssem.at[5])


def stack_kernel(g, lhs, rci, out, stage, sems):
    mine = rci[...]

    def held(k):
        return jnp.where(k % 2 == 0, k // 2, 5 + k // 2)

    def to_out(k):
        return pltpu.make_async_copy(stage.at[k], out.at[:, k], sems.at[k])

    @pl.loop(0, HOPS)
    def _(k):
        def tiles(odd):
            first = 128 * odd
            right = [g[held(k), at : at + 128, :] for at in (first, first + 256)]
            result = lax.dot_general(
                lhs[odd],
                jnp.concatenate(right, axis=0),
                (((1,), (1,)), ((), ())),
                preferred_element_type=jnp.float32,
            )
            recip = 1.0 / result[0:1]
            halves = (slice(0, 128), slice(128, 256))
            return [
                (result[SEL:, lanes] * jnp.maximum(mine, recip[:, lanes])).reshape(WIDTH, 8, 128)
                for lanes in halves
            ]

        lower = lax.broadcasted_iota(jnp.int32, (WIDTH, 8, 128), 1) < BINS
        for n, (even, odd) in enumerate(zip(tiles(0), tiles(1))):
            rows = pl.ds(8 * n, 8)
            stage[k, :, 0, rows] = jnp.where(lower, even, odd)
            stage[k, :, 1, rows] = pltpu.roll(jnp.where(lower, odd, even), BINS, 1)
        to_out(k).start()

    @pl.loop(0, HOPS)
    def _(k):
        to_out(k).wait()


def per_device(spectra, counts):
    spec = spectra.reshape(USED, WIDTH)
    vmem = pl.BlockSpec(memory_space=pltpu.VMEM)
    hbm = pl.BlockSpec(memory_space=pltpu.HBM)
    g, lhs, rci = pl.pallas_call(
        gather_kernel,
        name="whiten_gather",
        out_shape=(
            jax.ShapeDtypeStruct((HOPS, 2, 4, WIDTH, COLS), jnp.bfloat16),
            jax.ShapeDtypeStruct((2, SEL + WIDTH * 8, COLS), jnp.bfloat16),
            jax.ShapeDtypeStruct((WIDTH * 8, 128), jnp.float32),
        ),
        in_specs=[hbm, hbm],
        out_specs=(vmem, vmem, vmem),
        scratch_shapes=[
            pltpu.VMEM((USED, WIDTH), jnp.float32),
            pltpu.VMEM((1, WIDTH), jnp.int32),
            pltpu.VMEM((WIDTH, COLS), jnp.bfloat16),
            pltpu.SemaphoreType.DMA((6,)),
            pltpu.SemaphoreType.DMA((13,)),
            pltpu.SemaphoreType.DMA((3,)),
        ],
        compiler_params=pltpu.CompilerParams(
            collective_id=0, has_side_effects=True, vmem_limit_bytes=16 * 2**20
        ),
    )(*(pltpu.with_memory_space_constraint(a, pltpu.HBM) for a in (spec, counts)))
    g = g.reshape(HOPS, 512, COLS)
    out = pl.pallas_call(
        stack_kernel,
        name="stack",
        out_shape=jax.ShapeDtypeStruct((WIDTH, HOPS, 2, 4 * BINS, 128), jnp.float32),
        in_specs=[vmem, vmem, vmem],
        out_specs=hbm,
        scratch_shapes=[
            pltpu.VMEM((HOPS, WIDTH, 2, 4 * BINS, 128), jnp.float32),
            pltpu.SemaphoreType.DMA((HOPS,)),
        ],
        compiler_params=pltpu.CompilerParams(vmem_limit_bytes=24 * 2**20),
        cost_estimate=pl.CostEstimate(
            flops=2 * (SEL + WIDTH * 8) * COLS * 512 * HOPS,
            bytes_accessed=HOPS * 512 * (COLS * 2 + WIDTH * 8 * 4),
            transcendentals=0,
        ),
    )(g, lhs, rci)
    out = out.reshape(WIDTH, HOPS, 2, 4, BINS, 128).swapaxes(3, 4)
    return out.reshape(1, WIDTH, HOPS, 2, BINS, 512)


def solution(mesh):
    return jax.shard_map(
        per_device,
        mesh=mesh,
        in_specs=(P(None, None, None, "col", "row"), P("col", "row")),
        out_specs=P("col", "row", None, None, None, None),
        check_vma=False,
    )
```

```python
import functools

import jax
import jax.numpy as jnp
from jax import lax
from jax.experimental import pallas as pl
from jax.experimental.pallas import tpu as pltpu
from jax.sharding import PartitionSpec as P

MESH = pl.DeviceIdType.MESH
BINS = 4
SEGS = 30
USED = 2 * BINS * SEGS
COLS = 256
WIDTH = 64
HALF = 32
HOPS = 9
SEL = 16


def gather_kernel(spec_in, cnt_in, g, lhs, rci, spec, cnt, own, ssem, rsem, lsem):
    fetch = (
        pltpu.make_async_copy(spec_in, spec, lsem.at[1]),
        pltpu.make_async_copy(cnt_in, cnt, lsem.at[2]),
    )
    for copy in fetch:
        copy.start()
    r, d = lax.axis_index("row"), lax.axis_index("col")
    x, ylo = r % 4, r // 4
    c, q = d % 2, d // 2
    z, yhi = q % 4, q // 4

    def dev(x_, ylo_, q_, c_):
        return (ylo_ * 4 + x_, q_ * 2 + c_)

    sibling = dev(x, ylo, q, 1 - c)
    other = 1 - ylo

    def at_y(rel):
        return other if rel else ylo

    plane = [(j, rel) for j in (2, 4, 1, 3, 0) for rel in (0, 1) if j or rel]

    barrier = pltpu.get_barrier_semaphore()
    sources = [dev(x, at_y(rel), (q + j) % 8, c) for j, rel in plane]
    sources += [dev((x + i) % 4, ylo, q, c) for i in (1, 2, 3)]
    sources += [dev(x, ylo, yhi * 4 + (z + e) % 4, c) for e in (1, 2, 3)]
    sources += [sibling]
    for source in sources:
        pl.semaphore_signal(barrier, inc=1, device_id=source, device_id_type=MESH)

    for copy in fetch:
        copy.wait()
    raw = spec[...]
    power = jnp.sum(raw * raw, axis=0, keepdims=True) / float(USED)
    row = lax.broadcasted_iota(jnp.int32, (USED, WIDTH), 0)
    group = jnp.zeros((USED, WIDTH), jnp.int32)
    for n in range(1, 2 * BINS):
        group = group + (row >= n * SEGS).astype(jnp.int32)
    valid = (row - SEGS * group < cnt[...]).astype(jnp.float32)
    white = raw * lax.rsqrt(power + 1e-6) * valid
    white = white.astype(jnp.bfloat16).astype(jnp.float32)
    count = cnt[...].astype(jnp.float32)
    pad = jnp.zeros((COLS - USED - 8, WIDTH), jnp.float32)
    first = lax.broadcasted_iota(jnp.int32, (8, WIDTH), 0) == 0
    tail = jnp.where(first, count, 0.0)
    straight = jnp.concatenate([white, tail, pad], axis=0).T
    own[...] = straight.astype(jnp.bfloat16)

    def remote(src, dst, device, send, recv):
        copy = pltpu.make_async_remote_copy(
            src_ref=src,
            dst_ref=dst,
            send_sem=ssem.at[send],
            recv_sem=rsem.at[recv],
            device_id=device,
            device_id_type=MESH,
        )
        copy.start()
        return copy

    def settle(region, sem):
        pltpu.make_async_copy(region, region, sem).wait()

    lo, hi = pl.ds(0, HALF), pl.ds(HALF, HALF)
    own_blocks = pl.ds(0, 5)

    pl.semaphore_wait(barrier, len(sources))
    for i in (2, 1, 3):
        remote(own.at[hi], g.at[0, ylo, x, hi], dev((x + i) % 4, ylo, q, c), 0, 0)
    for j, rel in plane:
        remote(own.at[lo], g.at[j, ylo, x, lo], dev(x, at_y(rel), (q - j) % 8, c), 1, 1)
    local = pltpu.make_async_copy(own, g.at[0, ylo, x], lsem.at[0])
    local.start()

    local.wait()

    settle(g.at[pl.ds(0, 3), 0, 0, hi], rsem.at[0])
    row = g.at[0, ylo, :, hi]
    for j, rel in ((4, 0), (4, 1), (0, 1)):
        remote(row, g.at[j, ylo, :, hi], dev(x, at_y(rel), (q - j) % 8, c), 2, 2)

    right, left = dev((x + 1) % 4, ylo, q, c), dev((x + 3) % 4, ylo, q, c)
    settle(g.at[pl.ds(0, 9), 0, 0, lo], rsem.at[1])
    columns = [g.at[own_blocks, rel, x, lo] for rel in (0, 1)]
    to_right = [remote(columns[0], columns[0], right, 3, 3)]
    to_left = {1: remote(columns[1], columns[1], left, 3, 4)}
    to_right.append(remote(columns[1], columns[1], right, 3, 5))
    to_left[0] = remote(columns[0], columns[0], left, 3, 6)

    def share(src_index, dst_index, recv):
        remote(g.at[src_index], g.at[dst_index], sibling, 5, recv)

    def share_column(column):
        share((pl.ds(1 - c, 4), slice(None), column, lo), (pl.ds(5, 4), slice(None), column, lo), 12)

    def share_block(j):
        at = 4 + j + c
        share((j, slice(None), slice(None), hi), (at, slice(None), slice(None), hi), 12)

    share_column(x)

    settle(g.at[pl.ds(0, 3), 0, :, hi], rsem.at[2])
    along_z = {}
    for e in (2, 1, 3):
        zt = (z + 4 - e) % 4
        block = jnp.where(zt > z, 4, 0)
        along_z[e] = remote(
            g.at[block, :, :, hi], g.at[e, :, :, hi], dev(x, ylo, yhi * 4 + zt, c), 4, 6 + e
        )
    share_block(4 * (1 - c))

    xl, xr, xo = (x + 3) % 4, (x + 1) % 4, (x + 2) % 4
    to_right[0].wait_recv()
    piece = g.at[own_blocks, 0, xl, lo]
    on_right = remote(piece, piece, right, 3, 10)
    to_left[1].wait_recv()
    piece = g.at[own_blocks, 1, xr, lo]
    on_left = remote(piece, piece, left, 3, 11)
    to_right[1].wait_recv()
    share_column(xl)
    to_left[0].wait_recv()
    share_column(xr)
    swapped = jnp.concatenate(
        [white[USED // 2 :], -white[: USED // 2], jnp.zeros((COLS - USED, WIDTH), jnp.float32)],
        axis=0,
    ).T
    shape = (WIDTH, 8, COLS)
    sub = lax.broadcasted_iota(jnp.int32, (8, COLS), 0)
    lane = lax.broadcasted_iota(jnp.int32, (8, COLS), 1)
    low = (sub % BINS) * SEGS
    here = ((lane >= low) & (lane < low + SEGS)) | (
        (lane >= low + USED // 2) & (lane < low + USED // 2 + SEGS)
    )
    one = jnp.broadcast_to(straight[:, None, :], shape)
    two = jnp.broadcast_to(swapped[:, None, :], shape)
    sel = lax.broadcasted_iota(jnp.int32, (SEL, COLS), 1) == USED
    for odd in (0, 1):
        pick = jnp.where(((sub < BINS) == (odd == 0))[None], one, two)
        pick = jnp.where(here[None], pick, 0.0)
        lhs[odd, :SEL, :] = sel.astype(jnp.float32).astype(jnp.bfloat16)
        lhs[odd, SEL:, :] = pick.reshape(WIDTH * 8, COLS).astype(jnp.bfloat16)
    mine = jnp.broadcast_to(1.0 / straight[:, USED : USED + 1], (WIDTH, 128))
    rci[...] = jnp.broadcast_to(mine[:, None, :], (WIDTH, 8, 128)).reshape(WIDTH * 8, 128)

    for e in (1, 3):
        along_z[e].wait_recv()
        share_block(e)
    on_right.wait_recv()
    on_left.wait_recv()
    share_column(xo)
    along_z[2].wait_recv()
    share_block(2)

    settle(g.at[pl.ds(5, 4)], rsem.at[12])
    settle(g.at[pl.ds(0, 3), 0, 0, hi], ssem.at[0])
    settle(g.at[pl.ds(0, 9), 0, 0, lo], ssem.at[1])
    settle(g.at[pl.ds(0, 3), 0, :, hi], ssem.at[2])
    settle(g.at[pl.ds(0, 5), 0, pl.ds(0, 3)], ssem.at[3])
    settle(g.at[pl.ds(0, 3), :, :, hi], ssem.at[4])
    settle(g.at[pl.ds(5, 4)], ssem.at[5])


def stack_kernel(g, lhs, rci, out, stage, sems):
    mine = rci[...]

    def held(k):
        return jnp.where(k % 2 == 0, k // 2, 5 + k // 2)

    def to_out(k, half):
        some = pl.ds(half * HALF, HALF)
        return pltpu.make_async_copy(stage.at[k, some], out.at[some, k], sems.at[half, k])

    @pl.loop(0, HOPS)
    def _(k):
        def tiles(odd):
            first = 128 * odd
            right = [g[held(k), at : at + 128, :] for at in (first, first + 256)]
            result = lax.dot_general(
                lhs[odd],
                jnp.concatenate(right, axis=0),
                (((1,), (1,)), ((), ())),
                preferred_element_type=jnp.float32,
            )
            recip = 1.0 / result[0:1]
            halves = (slice(0, 128), slice(128, 256))
            return [
                (result[SEL:, lanes] * jnp.maximum(mine, recip[:, lanes])).reshape(WIDTH, 8, 128)
                for lanes in halves
            ]

        lower = lax.broadcasted_iota(jnp.int32, (WIDTH, 8, 128), 1) < BINS
        for n, (even, odd) in enumerate(zip(tiles(0), tiles(1))):
            rows = pl.ds(8 * n, 8)
            stage[k, :, 0, rows] = jnp.where(lower, even, odd)
            stage[k, :, 1, rows] = pltpu.roll(jnp.where(lower, odd, even), BINS, 1)
        for half in (0, 1):
            to_out(k, half).start(priority=half)

    @pl.loop(0, HOPS)
    def _(k):
        for half in (0, 1):
            to_out(k, half).wait()


def per_device(spectra, counts):
    spec = spectra.reshape(USED, WIDTH)
    vmem = pl.BlockSpec(memory_space=pltpu.VMEM)
    hbm = pl.BlockSpec(memory_space=pltpu.HBM)
    g, lhs, rci = pl.pallas_call(
        gather_kernel,
        name="whiten_gather",
        out_shape=(
            jax.ShapeDtypeStruct((HOPS, 2, 4, WIDTH, COLS), jnp.bfloat16),
            jax.ShapeDtypeStruct((2, SEL + WIDTH * 8, COLS), jnp.bfloat16),
            jax.ShapeDtypeStruct((WIDTH * 8, 128), jnp.float32),
        ),
        in_specs=[hbm, hbm],
        out_specs=(vmem, vmem, vmem),
        scratch_shapes=[
            pltpu.VMEM((USED, WIDTH), jnp.float32),
            pltpu.VMEM((1, WIDTH), jnp.int32),
            pltpu.VMEM((WIDTH, COLS), jnp.bfloat16),
            pltpu.SemaphoreType.DMA((6,)),
            pltpu.SemaphoreType.DMA((13,)),
            pltpu.SemaphoreType.DMA((3,)),
        ],
        compiler_params=pltpu.CompilerParams(
            collective_id=0, has_side_effects=True, vmem_limit_bytes=16 * 2**20
        ),
    )(*(pltpu.with_memory_space_constraint(a, pltpu.HBM) for a in (spec, counts)))
    g = g.reshape(HOPS, 512, COLS)
    out = pl.pallas_call(
        stack_kernel,
        name="stack",
        out_shape=jax.ShapeDtypeStruct((WIDTH, HOPS, 2, 4 * BINS, 128), jnp.float32),
        in_specs=[vmem, vmem, vmem],
        out_specs=hbm,
        scratch_shapes=[
            pltpu.VMEM((HOPS, WIDTH, 2, 4 * BINS, 128), jnp.float32),
            pltpu.SemaphoreType.DMA((2, HOPS)),
        ],
        compiler_params=pltpu.CompilerParams(vmem_limit_bytes=24 * 2**20),
        cost_estimate=pl.CostEstimate(
            flops=2 * (SEL + WIDTH * 8) * COLS * 512 * HOPS,
            bytes_accessed=HOPS * 512 * (COLS * 2 + WIDTH * 8 * 4),
            transcendentals=0,
        ),
    )(g, lhs, rci)
    out = out.reshape(WIDTH, HOPS, 2, 4, BINS, 128).swapaxes(3, 4)
    return out.reshape(1, WIDTH, HOPS, 2, BINS, 512)


def solution(mesh):
    return jax.shard_map(
        per_device,
        mesh=mesh,
        in_specs=(P(None, None, None, "col", "row"), P("col", "row")),
        out_specs=P("col", "row", None, None, None, None),
        check_vma=False,
    )
```

```python
import functools

import jax
import jax.numpy as jnp
from jax import lax
from jax.experimental import pallas as pl
from jax.experimental.pallas import tpu as pltpu
from jax.sharding import PartitionSpec as P

MESH = pl.DeviceIdType.MESH
BINS = 4
SEGS = 30
USED = 2 * BINS * SEGS
COLS = 256
WIDTH = 64
HALF = 32
SHARED = 13
HOPS = 9
SEL = 16


def gather_kernel(spec_in, cnt_in, gl, gh, lhs, rci, spec, cnt, own, ssem, rsem, lsem):
    fetch = (
        pltpu.make_async_copy(spec_in, spec, lsem.at[1]),
        pltpu.make_async_copy(cnt_in, cnt, lsem.at[2]),
    )
    for copy in fetch:
        copy.start()
    r, d = lax.axis_index("row"), lax.axis_index("col")
    x, ylo = r % 4, r // 4
    c, q = d % 2, d // 2
    z, yhi = q % 4, q // 4

    def dev(x_, ylo_, q_, c_):
        return (ylo_ * 4 + x_, q_ * 2 + c_)

    sibling = dev(x, ylo, q, 1 - c)
    across = 1 - ylo

    at_x = [dev((x + i) % 4, ylo, q, c) for i in range(4)]
    row_of = (ylo, across)
    plane = [(j, rel) for j in (3, 2, 1, 4, 0) for rel in (0, 1) if j or rel]

    def plane_at(j, rel):
        return dev(x, row_of[rel], (q + j) % 8, c)

    barrier = pltpu.get_barrier_semaphore()
    layer = [(i, j, rel) for j, rel in ((4, 0), (4, 1), (0, 1), (0, 0)) for i in (2, 1, 3, 0)][:-1]

    def layer_at(i, j, rel):
        return dev((x + i) % 4, row_of[rel], (q + j) % 8, c)

    def along_z(e):
        return dev(x, ylo, yhi * 4 + (z + e) % 4, c)

    sources = [plane_at(j, rel) for j, rel in plane] + [layer_at(*at) for at in layer]
    sources += [along_z(e) for e in (1, 2, 3)] + [sibling]
    for source in sources:
        pl.semaphore_signal(barrier, inc=1, device_id=source, device_id_type=MESH)

    for copy in fetch:
        copy.wait()
    raw = spec[...]
    power = jnp.sum(raw * raw, axis=0, keepdims=True) / float(USED)
    row = lax.broadcasted_iota(jnp.int32, (USED, WIDTH), 0)
    group = jnp.zeros((USED, WIDTH), jnp.int32)
    for n in range(1, 2 * BINS):
        group = group + (row >= n * SEGS).astype(jnp.int32)
    valid = (row - SEGS * group < cnt[...]).astype(jnp.float32)
    white = raw * lax.rsqrt(power + 1e-6) * valid
    white = white.astype(jnp.bfloat16).astype(jnp.float32)
    count = cnt[...].astype(jnp.float32)
    pad = jnp.zeros((COLS - USED - 8, WIDTH), jnp.float32)
    first = lax.broadcasted_iota(jnp.int32, (8, WIDTH), 0) == 0
    tail = jnp.where(first, count, 0.0)
    straight = jnp.concatenate([white, tail, pad], axis=0).T
    own[...] = straight.astype(jnp.bfloat16)

    def plan(src, dst, device, send, recv):
        return pltpu.make_async_remote_copy(
            src_ref=src,
            dst_ref=dst,
            send_sem=ssem.at[send],
            recv_sem=rsem.at[recv],
            device_id=device,
            device_id_type=MESH,
        )

    def remote(src, dst, device, send, recv):
        copy = plan(src, dst, device, send, recv)
        copy.start()
        return copy

    def settle(region, sem):
        pltpu.make_async_copy(region, region, sem).wait()

    every = slice(None)
    own_lo, own_hi = own.at[pl.ds(0, HALF)], own.at[pl.ds(HALF, HALF)]
    pl.semaphore_wait(barrier, len(sources))
    def over_plane(ways):
        for j, rel in ways:
            remote(own_lo, gl.at[j, ylo, x], plane_at(-j, rel), 0, j // 3)

    over_plane(plane[:2])
    for i, k, side in layer:
        remote(own_hi, gh.at[k, ylo, x], layer_at(i, k, side), 1, 2 + k // 4)
    over_plane(plane[2:])
    local = [
        pltpu.make_async_copy(own_lo, gl.at[0, ylo, x], lsem.at[0]),
        pltpu.make_async_copy(own_hi, gh.at[0, ylo, x], lsem.at[3]),
    ]
    for copy in local:
        copy.start()

    for copy in local:
        copy.wait()

    def share_column(at):
        to = gl.at[pl.ds(5, 4), :, at]
        remote(gl.at[pl.ds(1 - c, 4), :, at], to, sibling, 2, SHARED)

    def share_block(j):
        remote(gh.at[j], gh.at[4 + j + c], sibling, 3, SHARED + 1)

    groups = (pl.ds(0, 3), pl.ds(3, 2))

    def along_x(n):
        column = gl.at[groups[n], :, x]
        return [remote(column, column, at_x[i], 4 + n, 3 + 3 * n + i) for i in (2, 1, 3)]

    settle(gl.at[pl.ds(0, 5), 0, 0], rsem.at[0])
    early = along_x(0)
    settle(gl.at[pl.ds(0, 4), 0, 0], rsem.at[1])
    late = along_x(1)
    share_column(x)

    z_copies = []
    for e in (3, 2, 1):
        zt = (z + 4 - e) % 4
        up = zt > z
        copy = plan(gh.at[jnp.where(up, 4, 0)], gh.at[e], along_z(-e), 6, 9 + e)
        z_copies.append((up, copy))
    settle(gh.at[pl.ds(0, 7), 0, 0], rsem.at[2])
    for up, copy in z_copies:
        pl.when(jnp.logical_not(up))(copy.start)
    settle(gh.at[0], rsem.at[3])
    for up, copy in z_copies:
        pl.when(up)(copy.start)
    share_block(4 * (1 - c))

    swapped = jnp.concatenate(
        [white[USED // 2 :], -white[: USED // 2], jnp.zeros((COLS - USED, WIDTH), jnp.float32)],
        axis=0,
    ).T
    shape = (WIDTH, 8, COLS)
    sub = lax.broadcasted_iota(jnp.int32, (8, COLS), 0)
    lane = lax.broadcasted_iota(jnp.int32, (8, COLS), 1)
    low = (sub % BINS) * SEGS
    here = ((lane >= low) & (lane < low + SEGS)) | (
        (lane >= low + USED // 2) & (lane < low + USED // 2 + SEGS)
    )
    pick = jnp.where(
        (sub < BINS)[None],
        jnp.broadcast_to(straight[:, None, :], shape),
        jnp.broadcast_to(swapped[:, None, :], shape),
    )
    pick = jnp.where(here[None], pick, 0.0)
    sel = lax.broadcasted_iota(jnp.int32, (SEL, COLS), 1) == USED
    lhs[:SEL, :] = sel.astype(jnp.float32).astype(jnp.bfloat16)
    lhs[SEL:, :] = pick.reshape(WIDTH * 8, COLS).astype(jnp.bfloat16)
    mine = jnp.broadcast_to(1.0 / straight[:, USED : USED + 1], (WIDTH, 128))
    rci[...] = jnp.broadcast_to(mine[:, None, :], (WIDTH, 8, 128)).reshape(WIDTH * 8, 128)

    for copy in early:
        copy.wait_recv()
    for copy, i in zip(late, (2, 1, 3)):
        copy.wait_recv()
        share_column((x + 4 - i) % 4)
    for e in (3, 1, 2):
        settle(gh.at[e], rsem.at[9 + e])
        share_block(e)

    settle(gl.at[pl.ds(5, 4)], rsem.at[SHARED])
    settle(gh.at[pl.ds(5, 4)], rsem.at[SHARED + 1])
    settle(gl.at[pl.ds(0, 9), 0, 0], ssem.at[0])
    settle(gh.at[pl.ds(0, 5), 0, pl.ds(0, 3)], ssem.at[1])
    settle(gl.at[pl.ds(5, 4)], ssem.at[2])
    settle(gh.at[pl.ds(5, 4)], ssem.at[3])
    settle(gl.at[pl.ds(0, 3), :, pl.ds(0, 3)], ssem.at[4])
    settle(gl.at[pl.ds(0, 2), :, pl.ds(0, 3)], ssem.at[5])
    settle(gh.at[pl.ds(0, 3)], ssem.at[6])


def stack_kernel(gl, gh, lhs, rci, out, stage, sems):
    mine = rci[...]

    def held(k):
        return jnp.where(k % 2 == 0, k // 2, 5 + k // 2)

    def to_out(k):
        return pltpu.make_async_copy(stage.at[k], out.at[:, k], sems.at[k])

    @pl.loop(0, HOPS)
    def _(k):
        for n in (0, 1):
            right = [half[held(k), n, at] for at in range(4) for half in (gl, gh)]
            result = lax.dot_general(
                lhs[...],
                jnp.concatenate(right, axis=0),
                (((1,), (1,)), ((), ())),
                preferred_element_type=jnp.float32,
            )
            recip = 1.0 / result[0:1]
            for t in (0, 1):
                lanes = slice(t * 128, (t + 1) * 128)
                scale = jnp.maximum(mine, recip[:, lanes])
                value = (result[SEL:, lanes] * scale).reshape(WIDTH, 8, 128)
                columns = slice(n * 256 + t * 128, n * 256 + (t + 1) * 128)
                stage[k, :, 0, :, columns] = value[:, :BINS]
                stage[k, :, 1, :, columns] = value[:, BINS:]
        to_out(k).start()

    @pl.loop(0, HOPS)
    def _(k):
        to_out(k).wait()


def per_device(spectra, counts):
    spec = spectra.reshape(USED, WIDTH)
    vmem = pl.BlockSpec(memory_space=pltpu.VMEM)
    hbm = pl.BlockSpec(memory_space=pltpu.HBM)
    gl, gh, lhs, rci = pl.pallas_call(
        gather_kernel,
        name="whiten_gather",
        out_shape=(
            jax.ShapeDtypeStruct((HOPS, 2, 4, HALF, COLS), jnp.bfloat16),
            jax.ShapeDtypeStruct((HOPS, 2, 4, HALF, COLS), jnp.bfloat16),
            jax.ShapeDtypeStruct((SEL + WIDTH * 8, COLS), jnp.bfloat16),
            jax.ShapeDtypeStruct((WIDTH * 8, 128), jnp.float32),
        ),
        in_specs=[hbm, hbm],
        out_specs=(vmem,) * 4,
        scratch_shapes=[
            pltpu.VMEM((USED, WIDTH), jnp.float32),
            pltpu.VMEM((1, WIDTH), jnp.int32),
            pltpu.VMEM((WIDTH, COLS), jnp.bfloat16),
            pltpu.SemaphoreType.DMA((7,)),
            pltpu.SemaphoreType.DMA((SHARED + 2,)),
            pltpu.SemaphoreType.DMA((4,)),
        ],
        compiler_params=pltpu.CompilerParams(
            collective_id=0, has_side_effects=True, vmem_limit_bytes=16 * 2**20
        ),
    )(*(pltpu.with_memory_space_constraint(a, pltpu.HBM) for a in (spec, counts)))
    out = pl.pallas_call(
        stack_kernel,
        name="stack",
        out_shape=jax.ShapeDtypeStruct((WIDTH, HOPS, 2, BINS, 512), jnp.float32),
        in_specs=[vmem] * 4,
        out_specs=hbm,
        scratch_shapes=[
            pltpu.VMEM((HOPS, WIDTH, 2, BINS, 512), jnp.float32),
            pltpu.SemaphoreType.DMA((HOPS,)),
        ],
        compiler_params=pltpu.CompilerParams(vmem_limit_bytes=24 * 2**20),
        cost_estimate=pl.CostEstimate(
            flops=2 * (SEL + WIDTH * 8) * COLS * 512 * HOPS,
            bytes_accessed=HOPS * 512 * (COLS * 2 + WIDTH * 8 * 4),
            transcendentals=0,
        ),
    )(gl, gh, lhs, rci)
    return out[None]


def solution(mesh):
    return jax.shard_map(
        per_device,
        mesh=mesh,
        in_specs=(P(None, None, None, "col", "row"), P("col", "row")),
        out_specs=P("col", "row", None, None, None, None),
        check_vma=False,
    )
```

```python
import functools

import jax
import jax.numpy as jnp
from jax import lax
from jax.experimental import pallas as pl
from jax.experimental.pallas import tpu as pltpu
from jax.sharding import PartitionSpec as P

MESH = pl.DeviceIdType.MESH
BINS = 4
SEGS = 30
USED = 2 * BINS * SEGS
COLS = 256
WIDTH = 64
SHARED = 8
HOPS = 9
SEL = 16


def gather_kernel(spec_in, cnt_in, g, lhs, rci, spec, cnt, own, ssem, rsem, lsem):
    fetch = (
        pltpu.make_async_copy(spec_in, spec, lsem.at[1]),
        pltpu.make_async_copy(cnt_in, cnt, lsem.at[2]),
    )
    for copy in fetch:
        copy.start()
    r, d = lax.axis_index("row"), lax.axis_index("col")
    x, ylo = r % 4, r // 4
    c, q = d % 2, d // 2
    z, yhi = q % 4, q // 4

    def dev(x_, ylo_, q_, c_):
        return (ylo_ * 4 + x_, q_ * 2 + c_)

    sibling = dev(x, ylo, q, 1 - c)
    across = 1 - ylo

    at_x = [dev((x + i) % 4, ylo, q, c) for i in range(4)]
    right, left = at_x[1], at_x[3]

    def along_z(e):
        return dev(x, ylo, yhi * 4 + (z + e) % 4, c)

    y_peers = ((4, 0), (4, 1), (0, 1))
    row_of = (ylo, across)
    plane = [(j, rel) for rel in (1, 0) for j in (2, 3, 1, 4, 0) if j or rel]

    def plane_at(j, rel):
        return dev(x, row_of[rel], (q + j) % 8, c)

    barrier = pltpu.get_barrier_semaphore()
    sources = (
        [plane_at(j, rel) for j, rel in plane] + [right, left, sibling],
        at_x[1:] + [plane_at(*at) for at in y_peers] + [along_z(e) for e in (1, 2, 3)] + [sibling],
    )

    def announce(core):
        for source in sources[core]:
            pl.semaphore_signal(barrier, inc=1, device_id=source, device_id_type=MESH)

    for core in (0, 1):
        pl.when(c == core)(functools.partial(announce, core))

    for copy in fetch:
        copy.wait()
    raw = spec[...]
    power = jnp.sum(raw * raw, axis=0, keepdims=True) / float(USED)
    row = lax.broadcasted_iota(jnp.int32, (USED, WIDTH), 0)
    group = jnp.zeros((USED, WIDTH), jnp.int32)
    for n in range(1, 2 * BINS):
        group = group + (row >= n * SEGS).astype(jnp.int32)
    valid = (row - SEGS * group < cnt[...]).astype(jnp.float32)
    white = raw * lax.rsqrt(power + 1e-6) * valid
    white = white.astype(jnp.bfloat16).astype(jnp.float32)
    count = cnt[...].astype(jnp.float32)
    pad = jnp.zeros((COLS - USED - 8, WIDTH), jnp.float32)
    first = lax.broadcasted_iota(jnp.int32, (8, WIDTH), 0) == 0
    tail = jnp.where(first, count, 0.0)
    straight = jnp.concatenate([white, tail, pad], axis=0).T
    own[...] = straight.astype(jnp.bfloat16)

    def remote(src, dst, device, send, recv):
        copy = pltpu.make_async_remote_copy(
            src_ref=src,
            dst_ref=dst,
            send_sem=ssem.at[send],
            recv_sem=rsem.at[recv],
            device_id=device,
            device_id_type=MESH,
        )
        copy.start()
        return copy

    def settle(region, sem):
        pltpu.make_async_copy(region, region, sem).wait()

    @pl.when(c == 0)
    def _():
        pl.semaphore_wait(barrier, len(sources[0]))
        for j, rel in plane:
            remote(own, g.at[j, ylo, x], plane_at(-j, rel), 0, rel)

    @pl.when(c == 1)
    def _():
        pl.semaphore_wait(barrier, len(sources[1]))
        for i in (2, 1, 3):
            remote(own, g.at[0, ylo, x], at_x[i], 0, 0)

    local = pltpu.make_async_copy(own, g.at[0, ylo, x], lsem.at[0])
    local.start()

    swapped = jnp.concatenate(
        [white[USED // 2 :], -white[: USED // 2], jnp.zeros((COLS - USED, WIDTH), jnp.float32)],
        axis=0,
    ).T
    shape = (WIDTH, 8, COLS)
    sub = lax.broadcasted_iota(jnp.int32, (8, COLS), 0)
    lane = lax.broadcasted_iota(jnp.int32, (8, COLS), 1)
    low = (sub % BINS) * SEGS
    here = ((lane >= low) & (lane < low + SEGS)) | (
        (lane >= low + USED // 2) & (lane < low + USED // 2 + SEGS)
    )
    pick = jnp.where(
        (sub < BINS)[None],
        jnp.broadcast_to(straight[:, None, :], shape),
        jnp.broadcast_to(swapped[:, None, :], shape),
    )
    pick = jnp.where(here[None], pick, 0.0)
    sel = lax.broadcasted_iota(jnp.int32, (SEL, COLS), 1) == USED
    lhs[:SEL, :] = sel.astype(jnp.float32).astype(jnp.bfloat16)
    lhs[SEL:, :] = pick.reshape(WIDTH * 8, COLS).astype(jnp.bfloat16)
    mine = jnp.broadcast_to(1.0 / straight[:, USED : USED + 1], (WIDTH, 128))
    rci[...] = jnp.broadcast_to(mine[:, None, :], (WIDTH, 8, 128)).reshape(WIDTH * 8, 128)

    local.wait()

    def to_sibling(src, dst):
        remote(src, dst, sibling, 1, SHARED)

    @pl.when(c == 0)
    def _():
        blocks = pl.ds(0, 5)

        def column(rel, at):
            return g.at[blocks, row_of[rel], at]

        def send(rel, at, device, recv):
            return remote(column(rel, at), column(rel, at), device, 2 + rel, recv)

        def share(at):
            to_sibling(g.at[pl.ds(1, 4), :, at], g.at[pl.ds(5, 4), :, at])

        xl, xr, xo = (x + 3) % 4, (x + 1) % 4, (x + 2) % 4
        settle(g.at[pl.ds(0, 5), 0, 0], rsem.at[1])
        left_1 = send(1, x, left, 2)
        settle(g.at[pl.ds(0, 4), 0, 0], rsem.at[0])
        right_0 = send(0, x, right, 3)
        left_0 = send(0, x, left, 4)
        right_1 = send(1, x, right, 5)
        share(x)
        left_1.wait_recv()
        on_left = send(1, xr, left, 6)
        right_0.wait_recv()
        on_right = send(0, xl, right, 7)
        left_0.wait_recv()
        share(xr)
        right_1.wait_recv()
        share(xl)
        on_left.wait_recv()
        on_right.wait_recv()
        share(xo)

        settle(g.at[pl.ds(0, 9), 0, 0], ssem.at[0])
        settle(g.at[pl.ds(0, 5), 0, pl.ds(0, 3)], ssem.at[2])
        settle(g.at[pl.ds(0, 5), 1, pl.ds(0, 3)], ssem.at[3])

    @pl.when(c == 1)
    def _():
        settle(g.at[pl.ds(0, 3), 0, 0], rsem.at[0])
        for j, rel in y_peers:
            remote(g.at[0, ylo], g.at[j, ylo], plane_at(j, rel), 2, 1)
        settle(g.at[pl.ds(0, 3), 0], rsem.at[1])
        copies = {}
        for e in (3, 2, 1):
            block = jnp.where((z + 4 - e) % 4 > z, 4, 0)
            copies[e] = remote(g.at[block], g.at[e], along_z(-e), 3, 1 + e)
        to_sibling(g.at[0], g.at[5])
        for e in (3, 1, 2):
            copies[e].wait_recv()
            to_sibling(g.at[e], g.at[5 + e])

        settle(g.at[pl.ds(0, 3), 0, 0], ssem.at[0])
        settle(g.at[pl.ds(0, 3), 0], ssem.at[2])
        settle(g.at[pl.ds(0, 3)], ssem.at[3])

    settle(g.at[pl.ds(5, 4)], rsem.at[SHARED])
    settle(g.at[pl.ds(5, 4)], ssem.at[1])


def stack_kernel(g, lhs, rci, out, stage, sems):
    mine = rci[...]

    def held(k):
        return jnp.where(k % 2 == 0, k // 2, 5 + k // 2)

    def to_out(k):
        return pltpu.make_async_copy(stage.at[k], out.at[:, k], sems.at[k])

    @pl.loop(0, HOPS)
    def _(k):
        for n in (0, 1):
            result = lax.dot_general(
                lhs[...],
                g[held(k), n * 256 : (n + 1) * 256, :],
                (((1,), (1,)), ((), ())),
                preferred_element_type=jnp.float32,
            )
            recip = 1.0 / result[0:1]
            for t in (0, 1):
                lanes = slice(t * 128, (t + 1) * 128)
                scale = jnp.maximum(mine, recip[:, lanes])
                value = (result[SEL:, lanes] * scale).reshape(WIDTH, 8, 128)
                columns = slice(n * 256 + t * 128, n * 256 + (t + 1) * 128)
                stage[k, :, 0, :, columns] = value[:, :BINS]
                stage[k, :, 1, :, columns] = value[:, BINS:]
        to_out(k).start()

    @pl.loop(0, HOPS)
    def _(k):
        to_out(k).wait()


def per_device(spectra, counts):
    spec = spectra.reshape(USED, WIDTH)
    vmem = pl.BlockSpec(memory_space=pltpu.VMEM)
    hbm = pl.BlockSpec(memory_space=pltpu.HBM)
    g, lhs, rci = pl.pallas_call(
        gather_kernel,
        name="whiten_gather",
        out_shape=(
            jax.ShapeDtypeStruct((HOPS, 2, 4, WIDTH, COLS), jnp.bfloat16),
            jax.ShapeDtypeStruct((SEL + WIDTH * 8, COLS), jnp.bfloat16),
            jax.ShapeDtypeStruct((WIDTH * 8, 128), jnp.float32),
        ),
        in_specs=[hbm, hbm],
        out_specs=(vmem, vmem, vmem),
        scratch_shapes=[
            pltpu.VMEM((USED, WIDTH), jnp.float32),
            pltpu.VMEM((1, WIDTH), jnp.int32),
            pltpu.VMEM((WIDTH, COLS), jnp.bfloat16),
            pltpu.SemaphoreType.DMA((4,)),
            pltpu.SemaphoreType.DMA((SHARED + 1,)),
            pltpu.SemaphoreType.DMA((3,)),
        ],
        compiler_params=pltpu.CompilerParams(
            collective_id=0, has_side_effects=True, vmem_limit_bytes=16 * 2**20
        ),
    )(*(pltpu.with_memory_space_constraint(a, pltpu.HBM) for a in (spec, counts)))
    g = g.reshape(HOPS, 512, COLS)
    out = pl.pallas_call(
        stack_kernel,
        name="stack",
        out_shape=jax.ShapeDtypeStruct((WIDTH, HOPS, 2, BINS, 512), jnp.float32),
        in_specs=[vmem, vmem, vmem],
        out_specs=hbm,
        scratch_shapes=[
            pltpu.VMEM((HOPS, WIDTH, 2, BINS, 512), jnp.float32),
            pltpu.SemaphoreType.DMA((HOPS,)),
        ],
        compiler_params=pltpu.CompilerParams(vmem_limit_bytes=24 * 2**20),
        cost_estimate=pl.CostEstimate(
            flops=2 * (SEL + WIDTH * 8) * COLS * 512 * HOPS,
            bytes_accessed=HOPS * 512 * (COLS * 2 + WIDTH * 8 * 4),
            transcendentals=0,
        ),
    )(g, lhs, rci)
    return out[None]


def solution(mesh):
    return jax.shard_map(
        per_device,
        mesh=mesh,
        in_specs=(P(None, None, None, "col", "row"), P("col", "row")),
        out_specs=P("col", "row", None, None, None, None),
        check_vma=False,
    )
```

```python
import functools

import jax
import jax.numpy as jnp
from jax import lax
from jax.experimental import pallas as pl
from jax.experimental.pallas import tpu as pltpu
from jax.sharding import PartitionSpec as P

MESH = pl.DeviceIdType.MESH
BINS = 4
SEGS = 30
USED = 2 * BINS * SEGS
COLS = 256
WIDTH = 64
HALF = 32
HOPS = 9
SEL = 16


def gather_kernel(spec_in, cnt_in, gl, gh, lhs, rci, spec, cnt, own, ssem, rsem, lsem):
    fetch = (
        pltpu.make_async_copy(spec_in, spec, lsem.at[1]),
        pltpu.make_async_copy(cnt_in, cnt, lsem.at[2]),
    )
    for copy in fetch:
        copy.start()
    r, d = lax.axis_index("row"), lax.axis_index("col")
    x, ylo = r % 4, r // 4
    c, q = d % 2, d // 2
    z, yhi = q % 4, q // 4

    def dev(x_, ylo_, q_, c_):
        return (ylo_ * 4 + x_, q_ * 2 + c_)

    sibling = dev(x, ylo, q, 1 - c)
    other = 1 - ylo

    def at_y(rel):
        return other if rel else ylo

    plane = [(j, rel) for j in (2, 4, 1, 3, 0) for rel in (0, 1) if j or rel]

    barrier = pltpu.get_barrier_semaphore()
    sources = [dev(x, at_y(rel), (q + j) % 8, c) for j, rel in plane]
    sources += [dev((x + i) % 4, ylo, q, c) for i in (1, 2, 3)]
    sources += [dev(x, ylo, yhi * 4 + (z + e) % 4, c) for e in (1, 2, 3)]
    sources += [sibling]
    for source in sources:
        pl.semaphore_signal(barrier, inc=1, device_id=source, device_id_type=MESH)

    for copy in fetch:
        copy.wait()
    raw = spec[...]
    power = jnp.sum(raw * raw, axis=0, keepdims=True) / float(USED)
    row = lax.broadcasted_iota(jnp.int32, (USED, WIDTH), 0)
    group = jnp.zeros((USED, WIDTH), jnp.int32)
    for n in range(1, 2 * BINS):
        group = group + (row >= n * SEGS).astype(jnp.int32)
    valid = (row - SEGS * group < cnt[...]).astype(jnp.float32)
    white = raw * lax.rsqrt(power + 1e-6) * valid
    white = white.astype(jnp.bfloat16).astype(jnp.float32)
    count = cnt[...].astype(jnp.float32)
    pad = jnp.zeros((COLS - USED - 8, WIDTH), jnp.float32)
    first = lax.broadcasted_iota(jnp.int32, (8, WIDTH), 0) == 0
    tail = jnp.where(first, count, 0.0)
    straight = jnp.concatenate([white, tail, pad], axis=0).T
    own[...] = straight.astype(jnp.bfloat16)

    def remote(src, dst, device, send, recv):
        copy = pltpu.make_async_remote_copy(
            src_ref=src,
            dst_ref=dst,
            send_sem=ssem.at[send],
            recv_sem=rsem.at[recv],
            device_id=device,
            device_id_type=MESH,
        )
        copy.start()
        return copy

    def settle(region, sem):
        pltpu.make_async_copy(region, region, sem).wait()

    own_blocks = pl.ds(0, 5)
    own_lo, own_hi = own.at[pl.ds(0, HALF)], own.at[pl.ds(HALF, HALF)]

    pl.semaphore_wait(barrier, len(sources))
    for i in (2, 1, 3):
        remote(own_hi, gh.at[0, ylo, x], dev((x + i) % 4, ylo, q, c), 0, 0)
    for j, rel in plane:
        remote(own_lo, gl.at[j, ylo, x], dev(x, at_y(rel), (q - j) % 8, c), 1, 1)
    local = [
        pltpu.make_async_copy(own_lo, gl.at[0, ylo, x], lsem.at[0]),
        pltpu.make_async_copy(own_hi, gh.at[0, ylo, x], lsem.at[3]),
    ]
    for copy in local:
        copy.start()
    for copy in local:
        copy.wait()

    settle(gh.at[0, 0, pl.ds(0, 3)], rsem.at[0])
    row = gh.at[0, ylo]
    for j, rel in ((4, 0), (4, 1), (0, 1)):
        remote(row, gh.at[j, ylo], dev(x, at_y(rel), (q - j) % 8, c), 2, 2)

    right, left = dev((x + 1) % 4, ylo, q, c), dev((x + 3) % 4, ylo, q, c)
    settle(gl.at[pl.ds(0, 9), 0, 0], rsem.at[1])
    columns = [gl.at[own_blocks, rel, x] for rel in (0, 1)]
    to_right = [remote(columns[0], columns[0], right, 3, 3)]
    to_left = {1: remote(columns[1], columns[1], left, 3, 4)}
    to_right.append(remote(columns[1], columns[1], right, 3, 5))
    to_left[0] = remote(columns[0], columns[0], left, 3, 6)

    def share_column(at):
        remote(gl.at[pl.ds(1 - c, 4), :, at], gl.at[pl.ds(5, 4), :, at], sibling, 5, 12)

    def share_block(j):
        remote(gh.at[j], gh.at[4 + j + c], sibling, 6, 13)

    share_column(x)

    settle(gh.at[pl.ds(0, 3), 0], rsem.at[2])
    along_z = {}
    for e in (2, 1, 3):
        zt = (z + 4 - e) % 4
        block = jnp.where(zt > z, 4, 0)
        along_z[e] = remote(
            gh.at[block], gh.at[e], dev(x, ylo, yhi * 4 + zt, c), 4, 6 + e
        )
    share_block(4 * (1 - c))

    xl, xr, xo = (x + 3) % 4, (x + 1) % 4, (x + 2) % 4
    to_right[0].wait_recv()
    piece = gl.at[own_blocks, 0, xl]
    on_right = remote(piece, piece, right, 3, 10)
    to_left[1].wait_recv()
    piece = gl.at[own_blocks, 1, xr]
    on_left = remote(piece, piece, left, 3, 11)
    to_right[1].wait_recv()
    share_column(xl)
    to_left[0].wait_recv()
    share_column(xr)
    swapped = jnp.concatenate(
        [white[USED // 2 :], -white[: USED // 2], jnp.zeros((COLS - USED, WIDTH), jnp.float32)],
        axis=0,
    ).T
    shape = (WIDTH, 8, COLS)
    sub = lax.broadcasted_iota(jnp.int32, (8, COLS), 0)
    lane = lax.broadcasted_iota(jnp.int32, (8, COLS), 1)
    low = (sub % BINS) * SEGS
    here = ((lane >= low) & (lane < low + SEGS)) | (
        (lane >= low + USED // 2) & (lane < low + USED // 2 + SEGS)
    )
    one = jnp.broadcast_to(straight[:, None, :], shape)
    two = jnp.broadcast_to(swapped[:, None, :], shape)
    sel = lax.broadcasted_iota(jnp.int32, (SEL, COLS), 1) == USED
    for odd in (0, 1):
        pick = jnp.where(((sub < BINS) == (odd == 0))[None], one, two)
        pick = jnp.where(here[None], pick, 0.0)
        lhs[odd, :SEL, :] = sel.astype(jnp.float32).astype(jnp.bfloat16)
        lhs[odd, SEL:, :] = pick.reshape(WIDTH * 8, COLS).astype(jnp.bfloat16)
    mine = jnp.broadcast_to(1.0 / straight[:, USED : USED + 1], (WIDTH, 128))
    rci[...] = jnp.broadcast_to(mine[:, None, :], (WIDTH, 8, 128)).reshape(WIDTH * 8, 128)

    for e in (1, 3):
        along_z[e].wait_recv()
        share_block(e)
    on_right.wait_recv()
    on_left.wait_recv()
    share_column(xo)
    along_z[2].wait_recv()
    share_block(2)

    settle(gl.at[pl.ds(5, 4)], rsem.at[12])
    settle(gh.at[pl.ds(5, 4)], rsem.at[13])
    settle(gh.at[0, 0, pl.ds(0, 3)], ssem.at[0])
    settle(gl.at[pl.ds(0, 9), 0, 0], ssem.at[1])
    settle(gh.at[pl.ds(0, 3), 0], ssem.at[2])
    settle(gl.at[pl.ds(0, 5), :, pl.ds(0, 3)], ssem.at[3])
    settle(gh.at[pl.ds(0, 3)], ssem.at[4])
    settle(gl.at[pl.ds(5, 4)], ssem.at[5])
    settle(gh.at[pl.ds(5, 4)], ssem.at[6])


def stack_kernel(gl, gh_in, lhs, rci, out, gh, stage, gsem, sems):
    mine = rci[...]

    def held(k):
        return jnp.where(k % 2 == 0, k // 2, 5 + k // 2)

    def fetch(k):
        return pltpu.make_async_copy(gh_in.at[held(k)], gh.at[held(k)], gsem.at[k])

    @pl.loop(0, HOPS)
    def _(k):
        fetch(k).start()

    def to_out(k):
        return pltpu.make_async_copy(stage.at[k], out.at[:, k], sems.at[k])

    @pl.loop(0, HOPS)
    def _(k):
        fetch(k).wait()

        def tiles(odd):
            right = [
                half[held(k), n, at] for n in (0, 1) for at in (2 * odd, 2 * odd + 1) for half in (gl, gh)
            ]
            result = lax.dot_general(
                lhs[odd],
                jnp.concatenate(right, axis=0),
                (((1,), (1,)), ((), ())),
                preferred_element_type=jnp.float32,
            )
            recip = 1.0 / result[0:1]
            halves = (slice(0, 128), slice(128, 256))
            return [
                (result[SEL:, lanes] * jnp.maximum(mine, recip[:, lanes])).reshape(WIDTH, 8, 128)
                for lanes in halves
            ]

        lower = lax.broadcasted_iota(jnp.int32, (WIDTH, 8, 128), 1) < BINS
        for n, (even, odd) in enumerate(zip(tiles(0), tiles(1))):
            rows = pl.ds(8 * n, 8)
            stage[k, :, 0, rows] = jnp.where(lower, even, odd)
            stage[k, :, 1, rows] = pltpu.roll(jnp.where(lower, odd, even), BINS, 1)
        to_out(k).start()

    @pl.loop(0, HOPS)
    def _(k):
        to_out(k).wait()


def per_device(spectra, counts):
    spec = spectra.reshape(USED, WIDTH)
    vmem = pl.BlockSpec(memory_space=pltpu.VMEM)
    hbm = pl.BlockSpec(memory_space=pltpu.HBM)
    gl, gh, lhs, rci = pl.pallas_call(
        gather_kernel,
        name="whiten_gather",
        out_shape=(
            jax.ShapeDtypeStruct((HOPS, 2, 4, HALF, COLS), jnp.bfloat16),
            pltpu.HBM((HOPS, 2, 4, HALF, COLS), jnp.bfloat16),
            jax.ShapeDtypeStruct((2, SEL + WIDTH * 8, COLS), jnp.bfloat16),
            jax.ShapeDtypeStruct((WIDTH * 8, 128), jnp.float32),
        ),
        in_specs=[hbm, hbm],
        out_specs=(vmem, hbm, vmem, vmem),
        scratch_shapes=[
            pltpu.VMEM((USED, WIDTH), jnp.float32),
            pltpu.VMEM((1, WIDTH), jnp.int32),
            pltpu.VMEM((WIDTH, COLS), jnp.bfloat16),
            pltpu.SemaphoreType.DMA((7,)),
            pltpu.SemaphoreType.DMA((14,)),
            pltpu.SemaphoreType.DMA((4,)),
        ],
        compiler_params=pltpu.CompilerParams(
            collective_id=0, has_side_effects=True, vmem_limit_bytes=16 * 2**20
        ),
    )(*(pltpu.with_memory_space_constraint(a, pltpu.HBM) for a in (spec, counts)))
    gh = pltpu.with_memory_space_constraint(gh, pltpu.HBM)
    out = pl.pallas_call(
        stack_kernel,
        name="stack",
        out_shape=jax.ShapeDtypeStruct((WIDTH, HOPS, 2, 4 * BINS, 128), jnp.float32),
        in_specs=[vmem, hbm, vmem, vmem],
        out_specs=hbm,
        scratch_shapes=[
            pltpu.VMEM((HOPS, 2, 4, HALF, COLS), jnp.bfloat16),
            pltpu.VMEM((HOPS, WIDTH, 2, 4 * BINS, 128), jnp.float32),
            pltpu.SemaphoreType.DMA((HOPS,)),
            pltpu.SemaphoreType.DMA((HOPS,)),
        ],
        compiler_params=pltpu.CompilerParams(vmem_limit_bytes=24 * 2**20),
        cost_estimate=pl.CostEstimate(
            flops=2 * (SEL + WIDTH * 8) * COLS * 512 * HOPS,
            bytes_accessed=HOPS * 512 * (COLS * 2 + WIDTH * 8 * 4),
            transcendentals=0,
        ),
    )(gl, gh, lhs, rci)
    out = out.reshape(WIDTH, HOPS, 2, 4, BINS, 128).swapaxes(3, 4)
    return out.reshape(1, WIDTH, HOPS, 2, BINS, 512)


def solution(mesh):
    return jax.shard_map(
        per_device,
        mesh=mesh,
        in_specs=(P(None, None, None, "col", "row"), P("col", "row")),
        out_specs=P("col", "row", None, None, None, None),
        check_vma=False,
    )
```

```python
import functools

import jax
import jax.numpy as jnp
from jax import lax
from jax.experimental import pallas as pl
from jax.experimental.pallas import tpu as pltpu
from jax.sharding import PartitionSpec as P

MESH = pl.DeviceIdType.MESH
BINS = 4
SEGS = 30
USED = 2 * BINS * SEGS
COLS = 256
WIDTH = 64
HALF = 32
SHARED = 14
HOPS = 9
SEL = 16


def gather_kernel(spec_in, cnt_in, gl, gh, lhs, rci, spec, cnt, own, ssem, rsem, lsem):
    fetch = (
        pltpu.make_async_copy(spec_in, spec, lsem.at[1]),
        pltpu.make_async_copy(cnt_in, cnt, lsem.at[2]),
    )
    for copy in fetch:
        copy.start()
    r, d = lax.axis_index("row"), lax.axis_index("col")
    x, ylo = r % 4, r // 4
    c, q = d % 2, d // 2
    z, yhi = q % 4, q // 4

    def dev(x_, ylo_, q_, c_):
        return (ylo_ * 4 + x_, q_ * 2 + c_)

    sibling = dev(x, ylo, q, 1 - c)
    across = 1 - ylo

    steps = (2, 1, 3)
    y_steps = ((1, 0), (1, 1), (0, 1))

    def along_x(i):
        return dev((x + i) % 4, ylo, q, c)

    def along_y(four_on, rel):
        return dev(x, across if rel else ylo, (q + 4 * four_on) % 8, c)

    def along_z(e):
        return dev(x, ylo, yhi * 4 + (z + e) % 4, c)

    barrier = pltpu.get_barrier_semaphore()
    sources = [along_x(i) for i in steps] + [along_y(*at) for at in y_steps]
    sources += [along_z(e) for e in steps] + [sibling]
    for source in sources:
        pl.semaphore_signal(barrier, inc=1, device_id=source, device_id_type=MESH)

    for copy in fetch:
        copy.wait()
    raw = spec[...]
    power = jnp.sum(raw * raw, axis=0, keepdims=True) / float(USED)
    row = lax.broadcasted_iota(jnp.int32, (USED, WIDTH), 0)
    group = jnp.zeros((USED, WIDTH), jnp.int32)
    for n in range(1, 2 * BINS):
        group = group + (row >= n * SEGS).astype(jnp.int32)
    valid = (row - SEGS * group < cnt[...]).astype(jnp.float32)
    white = raw * lax.rsqrt(power + 1e-6) * valid
    white = white.astype(jnp.bfloat16).astype(jnp.float32)
    count = cnt[...].astype(jnp.float32)
    pad = jnp.zeros((COLS - USED - 8, WIDTH), jnp.float32)
    first = lax.broadcasted_iota(jnp.int32, (8, WIDTH), 0) == 0
    tail = jnp.where(first, count, 0.0)
    straight = jnp.concatenate([white, tail, pad], axis=0).T
    own[...] = straight.astype(jnp.bfloat16)

    def plan(src, dst, device, send, recv):
        return pltpu.make_async_remote_copy(
            src_ref=src,
            dst_ref=dst,
            send_sem=ssem.at[send],
            recv_sem=rsem.at[recv],
            device_id=device,
            device_id_type=MESH,
        )

    def remote(src, dst, device, send, recv):
        copy = plan(src, dst, device, send, recv)
        copy.start()
        return copy

    def settle(region, sem):
        pltpu.make_async_copy(region, region, sem).wait()

    every = slice(None)
    own_lo, own_hi = own.at[pl.ds(0, HALF)], own.at[pl.ds(HALF, HALF)]
    pl.semaphore_wait(barrier, len(sources))
    for i in steps:
        remote(own_hi, gh.at[0, ylo, x], along_x(i), 0, 0)
    for four_on, rel in y_steps:
        remote(own_lo, gl.at[four_on, ylo, x], along_y(four_on, rel), 1, 1)
    local = [
        pltpu.make_async_copy(own_lo, gl.at[0, ylo, x], lsem.at[0]),
        pltpu.make_async_copy(own_hi, gh.at[0, ylo, x], lsem.at[3]),
    ]
    for copy in local:
        copy.start()

    for copy in local:
        copy.wait()

    def share(half, index, to, send):
        remote(half.at[index], half.at[to], sibling, send, SHARED + send)

    def share_end(half, send):
        share(half, 1 - c, 8 - 3 * c, send)

    def x_copies(blocks, send, recv):
        column = gl.at[blocks, :, x]
        return {i: remote(column, column, along_x(i), send, recv + i) for i in steps}

    taken = {e: jnp.where((z + 4 - e) % 4 > z, 1, 0) for e in (3, 2, 1)}

    settle(gh.at[0, 0, pl.ds(0, 3)], rsem.at[0])
    for four_on, rel in y_steps:
        remote(gh.at[0, ylo], gh.at[four_on, ylo], along_y(four_on, rel), 4, 2)
    settle(gl.at[0, 0, pl.ds(0, 3)], rsem.at[1])
    for e in taken:
        remote(gl.at[taken[e], :, x], gl.at[1 + e, :, x], along_z(-e), 5, 3)
    near = x_copies(pl.ds(0, 2), 6, 4)

    settle(gh.at[pl.ds(0, 3), 0], rsem.at[2])
    z_copies = {e: remote(gh.at[taken[e]], gh.at[1 + e], along_z(-e), 7, 12 + e) for e in taken}
    share_end(gh, 2)
    settle(gl.at[0, pl.ds(0, 2), pl.ds(0, 3)], rsem.at[3])
    rest = pl.ds(2, 3)
    beyond = x_copies(rest, 8, 8)
    for i in steps:
        near[i].wait_recv()
    share_end(gl, 3)

    swapped = jnp.concatenate(
        [white[USED // 2 :], -white[: USED // 2], jnp.zeros((COLS - USED, WIDTH), jnp.float32)],
        axis=0,
    ).T
    shape = (WIDTH, 8, COLS)
    sub = lax.broadcasted_iota(jnp.int32, (8, COLS), 0)
    lane = lax.broadcasted_iota(jnp.int32, (8, COLS), 1)
    low = (sub % BINS) * SEGS
    here = ((lane >= low) & (lane < low + SEGS)) | (
        (lane >= low + USED // 2) & (lane < low + USED // 2 + SEGS)
    )
    pick = jnp.where(
        (sub < BINS)[None],
        jnp.broadcast_to(straight[:, None, :], shape),
        jnp.broadcast_to(swapped[:, None, :], shape),
    )
    pick = jnp.where(here[None], pick, 0.0)
    sel = lax.broadcasted_iota(jnp.int32, (SEL, COLS), 1) == USED
    lhs[:SEL, :] = sel.astype(jnp.float32).astype(jnp.bfloat16)
    lhs[SEL:, :] = pick.reshape(WIDTH * 8, COLS).astype(jnp.bfloat16)
    mine = jnp.broadcast_to(1.0 / straight[:, USED : USED + 1], (WIDTH, 128))
    rci[...] = jnp.broadcast_to(mine[:, None, :], (WIDTH, 8, 128)).reshape(WIDTH * 8, 128)

    for e in taken:
        z_copies[e].wait_recv()
        share(gh, 1 + e, 4 + e + c, 2)
    for i in (0,) + steps:
        if i:
            beyond[i].wait_recv()
        at = (x + 4 - i) % 4
        share(gl, (rest, every, at), (pl.ds(5 + c, 3), every, at), 3)

    settle(gh.at[pl.ds(5, 4)], rsem.at[SHARED + 2])
    settle(gl.at[pl.ds(5, 4)], rsem.at[SHARED + 3])
    settle(gh.at[0, 0, pl.ds(0, 3)], ssem.at[0])
    settle(gl.at[0, 0, pl.ds(0, 3)], ssem.at[1])
    settle(gh.at[pl.ds(5, 4)], ssem.at[2])
    settle(gl.at[pl.ds(5, 4)], ssem.at[3])
    settle(gh.at[pl.ds(0, 3), 0], ssem.at[4])
    settle(gl.at[0, pl.ds(0, 2), pl.ds(0, 3)], ssem.at[5])
    settle(gl.at[pl.ds(0, 2), :, pl.ds(0, 3)], ssem.at[6])
    settle(gh.at[pl.ds(0, 3)], ssem.at[7])
    settle(gl.at[pl.ds(0, 3), :, pl.ds(0, 3)], ssem.at[8])


def stack_kernel(gl, gh, lhs, rci, out, stage, sems):
    mine = rci[...]

    def held(k):
        even = jnp.where(k == 0, 0, jnp.where(k == 8, 1, 1 + k // 2))
        return jnp.where(k % 2 == 0, even, 5 + k // 2)

    def to_out(k):
        return pltpu.make_async_copy(stage.at[k], out.at[:, k], sems.at[k])

    @pl.loop(0, HOPS)
    def _(k):
        for n in (0, 1):
            right = [half[held(k), n, at] for at in range(4) for half in (gl, gh)]
            result = lax.dot_general(
                lhs[...],
                jnp.concatenate(right, axis=0),
                (((1,), (1,)), ((), ())),
                preferred_element_type=jnp.float32,
            )
            recip = 1.0 / result[0:1]
            for t in (0, 1):
                lanes = slice(t * 128, (t + 1) * 128)
                scale = jnp.maximum(mine, recip[:, lanes])
                value = (result[SEL:, lanes] * scale).reshape(WIDTH, 8, 128)
                columns = slice(n * 256 + t * 128, n * 256 + (t + 1) * 128)
                stage[k, :, 0, :, columns] = value[:, :BINS]
                stage[k, :, 1, :, columns] = value[:, BINS:]
        to_out(k).start()

    @pl.loop(0, HOPS)
    def _(k):
        to_out(k).wait()


def per_device(spectra, counts):
    spec = spectra.reshape(USED, WIDTH)
    vmem = pl.BlockSpec(memory_space=pltpu.VMEM)
    hbm = pl.BlockSpec(memory_space=pltpu.HBM)
    gl, gh, lhs, rci = pl.pallas_call(
        gather_kernel,
        name="whiten_gather",
        out_shape=(
            jax.ShapeDtypeStruct((HOPS, 2, 4, HALF, COLS), jnp.bfloat16),
            jax.ShapeDtypeStruct((HOPS, 2, 4, HALF, COLS), jnp.bfloat16),
            jax.ShapeDtypeStruct((SEL + WIDTH * 8, COLS), jnp.bfloat16),
            jax.ShapeDtypeStruct((WIDTH * 8, 128), jnp.float32),
        ),
        in_specs=[hbm, hbm],
        out_specs=(vmem,) * 4,
        scratch_shapes=[
            pltpu.VMEM((USED, WIDTH), jnp.float32),
            pltpu.VMEM((1, WIDTH), jnp.int32),
            pltpu.VMEM((WIDTH, COLS), jnp.bfloat16),
            pltpu.SemaphoreType.DMA((9,)),
            pltpu.SemaphoreType.DMA((SHARED + 4,)),
            pltpu.SemaphoreType.DMA((4,)),
        ],
        compiler_params=pltpu.CompilerParams(
            collective_id=0, has_side_effects=True, vmem_limit_bytes=16 * 2**20
        ),
    )(*(pltpu.with_memory_space_constraint(a, pltpu.HBM) for a in (spec, counts)))
    out = pl.pallas_call(
        stack_kernel,
        name="stack",
        out_shape=jax.ShapeDtypeStruct((WIDTH, HOPS, 2, BINS, 512), jnp.float32),
        in_specs=[vmem] * 4,
        out_specs=hbm,
        scratch_shapes=[
            pltpu.VMEM((HOPS, WIDTH, 2, BINS, 512), jnp.float32),
            pltpu.SemaphoreType.DMA((HOPS,)),
        ],
        compiler_params=pltpu.CompilerParams(vmem_limit_bytes=24 * 2**20),
        cost_estimate=pl.CostEstimate(
            flops=2 * (SEL + WIDTH * 8) * COLS * 512 * HOPS,
            bytes_accessed=HOPS * 512 * (COLS * 2 + WIDTH * 8 * 4),
            transcendentals=0,
        ),
    )(gl, gh, lhs, rci)
    return out[None]


def solution(mesh):
    return jax.shard_map(
        per_device,
        mesh=mesh,
        in_specs=(P(None, None, None, "col", "row"), P("col", "row")),
        out_specs=P("col", "row", None, None, None, None),
        check_vma=False,
    )
```

```python
import functools

import jax
import jax.numpy as jnp
from jax import lax
from jax.experimental import pallas as pl
from jax.experimental.pallas import tpu as pltpu
from jax.sharding import PartitionSpec as P

MESH = pl.DeviceIdType.MESH
BINS = 4
SEGS = 30
USED = 2 * BINS * SEGS
COLS = 256
WIDTH = 64
HALF = 32
HOPS = 9
SEL = 16


def gather_kernel(spec_in, cnt_in, g, lhs, rci, spec, cnt, own, ssem, rsem, lsem):
    fetch = (
        pltpu.make_async_copy(spec_in, spec, lsem.at[1]),
        pltpu.make_async_copy(cnt_in, cnt, lsem.at[2]),
    )
    for copy in fetch:
        copy.start()
    r, d = lax.axis_index("row"), lax.axis_index("col")
    x, ylo = r % 4, r // 4
    c, q = d % 2, d // 2
    z, yhi = q % 4, q // 4

    def dev(x_, ylo_, q_, c_):
        return (ylo_ * 4 + x_, q_ * 2 + c_)

    sibling = dev(x, ylo, q, 1 - c)
    other = 1 - ylo

    def at_y(rel):
        return other if rel else ylo

    plane = [(j, rel) for j in (2, 4, 1, 3, 0) for rel in (0, 1) if j or rel]

    barrier = pltpu.get_barrier_semaphore()
    sources = [dev(x, at_y(rel), (q + j) % 8, c) for j, rel in plane]
    sources += [dev((x + i) % 4, ylo, q, c) for i in (1, 2, 3)]
    sources += [dev(x, ylo, yhi * 4 + (z + e) % 4, c) for e in (1, 2, 3)]
    sources += [sibling]
    for source in sources:
        pl.semaphore_signal(barrier, inc=1, device_id=source, device_id_type=MESH)

    for copy in fetch:
        copy.wait()
    raw = spec[...]
    power = jnp.sum(raw * raw, axis=0, keepdims=True) / float(USED)
    row = lax.broadcasted_iota(jnp.int32, (USED, WIDTH), 0)
    group = jnp.zeros((USED, WIDTH), jnp.int32)
    for n in range(1, 2 * BINS):
        group = group + (row >= n * SEGS).astype(jnp.int32)
    valid = (row - SEGS * group < cnt[...]).astype(jnp.float32)
    white = raw * lax.rsqrt(power + 1e-6) * valid
    white = white.astype(jnp.bfloat16).astype(jnp.float32)
    count = cnt[...].astype(jnp.float32)
    pad = jnp.zeros((COLS - USED - 8, WIDTH), jnp.float32)
    first = lax.broadcasted_iota(jnp.int32, (8, WIDTH), 0) == 0
    tail = jnp.where(first, count, 0.0)
    straight = jnp.concatenate([white, tail, pad], axis=0).T
    own[...] = straight.astype(jnp.bfloat16)

    def remote(src, dst, device, send, recv):
        copy = pltpu.make_async_remote_copy(
            src_ref=src,
            dst_ref=dst,
            send_sem=ssem.at[send],
            recv_sem=rsem.at[recv],
            device_id=device,
            device_id_type=MESH,
        )
        copy.start()
        return copy

    def settle(region, sem):
        pltpu.make_async_copy(region, region, sem).wait()

    lo, hi = pl.ds(0, HALF), pl.ds(HALF, HALF)
    own_blocks = pl.ds(0, 5)

    pl.semaphore_wait(barrier, len(sources))
    for i in (2, 1, 3):
        remote(own.at[hi], g.at[0, ylo, x, hi], dev((x + i) % 4, ylo, q, c), 0, 0)
    for j, rel in plane:
        remote(own.at[lo], g.at[j, ylo, x, lo], dev(x, at_y(rel), (q - j) % 8, c), 1, 1)
    local = pltpu.make_async_copy(own, g.at[0, ylo, x], lsem.at[0])
    local.start()

    local.wait()

    settle(g.at[pl.ds(0, 3), 0, 0, hi], rsem.at[0])
    row = g.at[0, ylo, :, hi]
    for j, rel in ((4, 0), (4, 1), (0, 1)):
        remote(row, g.at[j, ylo, :, hi], dev(x, at_y(rel), (q - j) % 8, c), 2, 2)

    right, left = dev((x + 1) % 4, ylo, q, c), dev((x + 3) % 4, ylo, q, c)
    settle(g.at[pl.ds(0, 9), 0, 0, lo], rsem.at[1])
    columns = [g.at[own_blocks, rel, x, lo] for rel in (0, 1)]
    to_right = [remote(columns[0], columns[0], right, 3, 3)]
    to_left = {1: remote(columns[1], columns[1], left, 3, 4)}
    to_right.append(remote(columns[1], columns[1], right, 3, 5))
    to_left[0] = remote(columns[0], columns[0], left, 3, 6)

    def share(src_index, dst_index, recv):
        remote(g.at[src_index], g.at[dst_index], sibling, 5, recv)

    def share_column(column):
        share((pl.ds(1 - c, 4), slice(None), column, lo), (pl.ds(5, 4), slice(None), column, lo), 12)

    def share_block(j):
        at = 4 + j + c
        share((j, slice(None), slice(None), hi), (at, slice(None), slice(None), hi), 12)

    share_column(x)

    settle(g.at[pl.ds(0, 3), 0, :, hi], rsem.at[2])
    along_z = {}
    for e in (2, 1, 3):
        zt = (z + 4 - e) % 4
        block = jnp.where(zt > z, 4, 0)
        along_z[e] = remote(
            g.at[block, :, :, hi], g.at[e, :, :, hi], dev(x, ylo, yhi * 4 + zt, c), 4, 6 + e
        )
    share_block(4 * (1 - c))

    xl, xr, xo = (x + 3) % 4, (x + 1) % 4, (x + 2) % 4
    to_right[0].wait_recv()
    piece = g.at[own_blocks, 0, xl, lo]
    on_right = remote(piece, piece, right, 3, 10)
    to_left[1].wait_recv()
    piece = g.at[own_blocks, 1, xr, lo]
    on_left = remote(piece, piece, left, 3, 11)
    to_right[1].wait_recv()
    share_column(xl)
    to_left[0].wait_recv()
    share_column(xr)
    swapped = jnp.concatenate(
        [white[USED // 2 :], -white[: USED // 2], jnp.zeros((COLS - USED, WIDTH), jnp.float32)],
        axis=0,
    ).T
    shape = (WIDTH, 8, COLS)
    sub = lax.broadcasted_iota(jnp.int32, (8, COLS), 0)
    lane = lax.broadcasted_iota(jnp.int32, (8, COLS), 1)
    low = (sub % BINS) * SEGS
    here = ((lane >= low) & (lane < low + SEGS)) | (
        (lane >= low + USED // 2) & (lane < low + USED // 2 + SEGS)
    )
    one = jnp.broadcast_to(straight[:, None, :], shape)
    two = jnp.broadcast_to(swapped[:, None, :], shape)
    sel = lax.broadcasted_iota(jnp.int32, (SEL, COLS), 1) == USED
    for odd in (0, 1):
        pick = jnp.where(((sub < BINS) == (odd == 0))[None], one, two)
        pick = jnp.where(here[None], pick, 0.0)
        lhs[odd, :SEL, :] = sel.astype(jnp.float32).astype(jnp.bfloat16)
        lhs[odd, SEL:, :] = pick.reshape(WIDTH * 8, COLS).astype(jnp.bfloat16)
    mine = jnp.broadcast_to(1.0 / straight[:, USED : USED + 1], (WIDTH, 128))
    rci[...] = jnp.broadcast_to(mine[:, None, :], (WIDTH, 8, 128)).reshape(WIDTH * 8, 128)

    for e in (1, 3):
        along_z[e].wait_recv()
        share_block(e)
    on_right.wait_recv()
    on_left.wait_recv()
    share_column(xo)
    along_z[2].wait_recv()
    share_block(2)

    settle(g.at[pl.ds(5, 4)], rsem.at[12])
    settle(g.at[pl.ds(0, 3), 0, 0, hi], ssem.at[0])
    settle(g.at[pl.ds(0, 9), 0, 0, lo], ssem.at[1])
    settle(g.at[pl.ds(0, 3), 0, :, hi], ssem.at[2])
    settle(g.at[pl.ds(0, 5), 0, pl.ds(0, 3)], ssem.at[3])
    settle(g.at[pl.ds(0, 3), :, :, hi], ssem.at[4])
    settle(g.at[pl.ds(5, 4)], ssem.at[5])


def stack_kernel(g, lhs, rci, out, stage, sems):
    mine = rci[...]

    def held(k):
        return jnp.where(k % 2 == 0, k // 2, 5 + k // 2)

    def to_out(k):
        return pltpu.make_async_copy(stage.at[k], out.at[:, k], sems.at[k])

    @pl.loop(0, HOPS, unroll=3)
    def _(k):
        def tiles(odd):
            first = 128 * odd
            right = [g[held(k), at : at + 128, :] for at in (first, first + 256)]
            result = lax.dot_general(
                lhs[odd],
                jnp.concatenate(right, axis=0),
                (((1,), (1,)), ((), ())),
                preferred_element_type=jnp.float32,
            )
            recip = 1.0 / result[0:1]
            halves = (slice(0, 128), slice(128, 256))
            return [
                (result[SEL:, lanes] * jnp.maximum(mine, recip[:, lanes])).reshape(WIDTH, 8, 128)
                for lanes in halves
            ]

        lower = lax.broadcasted_iota(jnp.int32, (WIDTH, 8, 128), 1) < BINS
        for n, (even, odd) in enumerate(zip(tiles(0), tiles(1))):
            rows = pl.ds(8 * n, 8)
            stage[k, :, 0, rows] = jnp.where(lower, even, odd)
            stage[k, :, 1, rows] = pltpu.roll(jnp.where(lower, odd, even), BINS, 1)
        to_out(k).start()

    @pl.loop(0, HOPS)
    def _(k):
        to_out(k).wait()


def per_device(spectra, counts):
    spec = spectra.reshape(USED, WIDTH)
    vmem = pl.BlockSpec(memory_space=pltpu.VMEM)
    hbm = pl.BlockSpec(memory_space=pltpu.HBM)
    g, lhs, rci = pl.pallas_call(
        gather_kernel,
        name="whiten_gather",
        out_shape=(
            jax.ShapeDtypeStruct((HOPS, 2, 4, WIDTH, COLS), jnp.bfloat16),
            jax.ShapeDtypeStruct((2, SEL + WIDTH * 8, COLS), jnp.bfloat16),
            jax.ShapeDtypeStruct((WIDTH * 8, 128), jnp.float32),
        ),
        in_specs=[hbm, hbm],
        out_specs=(vmem, vmem, vmem),
        scratch_shapes=[
            pltpu.VMEM((USED, WIDTH), jnp.float32),
            pltpu.VMEM((1, WIDTH), jnp.int32),
            pltpu.VMEM((WIDTH, COLS), jnp.bfloat16),
            pltpu.SemaphoreType.DMA((6,)),
            pltpu.SemaphoreType.DMA((13,)),
            pltpu.SemaphoreType.DMA((3,)),
        ],
        compiler_params=pltpu.CompilerParams(
            collective_id=0, has_side_effects=True, vmem_limit_bytes=16 * 2**20
        ),
    )(*(pltpu.with_memory_space_constraint(a, pltpu.HBM) for a in (spec, counts)))
    g = g.reshape(HOPS, 512, COLS)
    out = pl.pallas_call(
        stack_kernel,
        name="stack",
        out_shape=jax.ShapeDtypeStruct((WIDTH, HOPS, 2, 4 * BINS, 128), jnp.float32),
        in_specs=[vmem, vmem, vmem],
        out_specs=hbm,
        scratch_shapes=[
            pltpu.VMEM((HOPS, WIDTH, 2, 4 * BINS, 128), jnp.float32),
            pltpu.SemaphoreType.DMA((HOPS,)),
        ],
        compiler_params=pltpu.CompilerParams(vmem_limit_bytes=24 * 2**20),
        cost_estimate=pl.CostEstimate(
            flops=2 * (SEL + WIDTH * 8) * COLS * 512 * HOPS,
            bytes_accessed=HOPS * 512 * (COLS * 2 + WIDTH * 8 * 4),
            transcendentals=0,
        ),
    )(g, lhs, rci)
    out = out.reshape(WIDTH, HOPS, 2, 4, BINS, 128).swapaxes(3, 4)
    return out.reshape(1, WIDTH, HOPS, 2, BINS, 512)


def solution(mesh):
    return jax.shard_map(
        per_device,
        mesh=mesh,
        in_specs=(P(None, None, None, "col", "row"), P("col", "row")),
        out_specs=P("col", "row", None, None, None, None),
        check_vma=False,
    )
```

```python
import functools

import jax
import jax.numpy as jnp
from jax import lax
from jax.experimental import pallas as pl
from jax.experimental.pallas import tpu as pltpu
from jax.sharding import PartitionSpec as P

MESH = pl.DeviceIdType.MESH
BINS = 4
SEGS = 30
USED = 2 * BINS * SEGS
COLS = 256
WIDTH = 64
HALF = 32
SHARED = 14
HOPS = 9
SEL = 16


def gather_kernel(spec_in, cnt_in, gl, gh, lhs, rci, spec, cnt, own, ssem, rsem, lsem):
    fetch = (
        pltpu.make_async_copy(spec_in, spec, lsem.at[1]),
        pltpu.make_async_copy(cnt_in, cnt, lsem.at[2]),
    )
    for copy in fetch:
        copy.start()
    r, d = lax.axis_index("row"), lax.axis_index("col")
    x, ylo = r % 4, r // 4
    c, q = d % 2, d // 2
    z, yhi = q % 4, q // 4

    def dev(x_, ylo_, q_, c_):
        return (ylo_ * 4 + x_, q_ * 2 + c_)

    sibling = dev(x, ylo, q, 1 - c)
    across = 1 - ylo

    steps = (2, 1, 3)
    y_steps = ((0, 1), (1, 1), (1, 0))

    def along_x(i):
        return dev((x + i) % 4, ylo, q, c)

    def along_y(four_on, rel):
        return dev(x, across if rel else ylo, (q + 4 * four_on) % 8, c)

    def along_z(e):
        return dev(x, ylo, yhi * 4 + (z + e) % 4, c)

    barrier = pltpu.get_barrier_semaphore()
    sources = [along_x(i) for i in steps] + [along_y(*at) for at in y_steps]
    sources += [along_z(e) for e in steps] + [sibling]
    for source in sources:
        pl.semaphore_signal(barrier, inc=1, device_id=source, device_id_type=MESH)

    for copy in fetch:
        copy.wait()
    raw = spec[...]
    power = jnp.sum(raw * raw, axis=0, keepdims=True) / float(USED)
    row = lax.broadcasted_iota(jnp.int32, (USED, WIDTH), 0)
    group = jnp.zeros((USED, WIDTH), jnp.int32)
    for n in range(1, 2 * BINS):
        group = group + (row >= n * SEGS).astype(jnp.int32)
    valid = (row - SEGS * group < cnt[...]).astype(jnp.float32)
    white = raw * lax.rsqrt(power + 1e-6) * valid
    white = white.astype(jnp.bfloat16).astype(jnp.float32)
    count = cnt[...].astype(jnp.float32)
    pad = jnp.zeros((COLS - USED - 8, WIDTH), jnp.float32)
    first = lax.broadcasted_iota(jnp.int32, (8, WIDTH), 0) == 0
    tail = jnp.where(first, count, 0.0)
    straight = jnp.concatenate([white, tail, pad], axis=0).T
    own[...] = straight.astype(jnp.bfloat16)

    def plan(src, dst, device, send, recv):
        return pltpu.make_async_remote_copy(
            src_ref=src,
            dst_ref=dst,
            send_sem=ssem.at[send],
            recv_sem=rsem.at[recv],
            device_id=device,
            device_id_type=MESH,
        )

    def remote(src, dst, device, send, recv):
        copy = plan(src, dst, device, send, recv)
        copy.start()
        return copy

    def settle(region, sem):
        pltpu.make_async_copy(region, region, sem).wait()

    every = slice(None)
    own_lo, own_hi = own.at[pl.ds(0, HALF)], own.at[pl.ds(HALF, HALF)]
    pl.semaphore_wait(barrier, len(sources))
    for i in steps:
        remote(own_hi, gh.at[0, ylo, x], along_x(i), 0, 0)
    for four_on, rel in y_steps:
        remote(own_lo, gl.at[four_on, ylo, x], along_y(four_on, rel), 1, 1)
    local = [
        pltpu.make_async_copy(own_lo, gl.at[0, ylo, x], lsem.at[0]),
        pltpu.make_async_copy(own_hi, gh.at[0, ylo, x], lsem.at[3]),
    ]
    for copy in local:
        copy.start()

    for copy in local:
        copy.wait()

    def share(half, index, to, send):
        remote(half.at[index], half.at[to], sibling, send, SHARED + send)

    def share_end(half, send):
        share(half, 1 - c, 8 - 3 * c, send)

    def x_copies(blocks, send, recv):
        column = gl.at[blocks, :, x]
        return {i: remote(column, column, along_x(i), send, recv + i) for i in steps}

    taken = {e: jnp.where((z + 4 - e) % 4 > z, 1, 0) for e in (3, 2, 1)}

    settle(gh.at[0, 0, pl.ds(0, 3)], rsem.at[0])
    for four_on, rel in y_steps:
        remote(gh.at[0, ylo], gh.at[four_on, ylo], along_y(four_on, rel), 4, 2 + 10 * four_on)
    settle(gl.at[0, 0, pl.ds(0, 3)], rsem.at[1])
    for e in taken:
        remote(gl.at[taken[e], :, x], gl.at[1 + e, :, x], along_z(-e), 5, 3)
    z_copies = {
        e: plan(gh.at[taken[e]], gh.at[1 + e], along_z(-e), 7, 12 + e) for e in taken
    }

    settle(gh.at[0, 0], rsem.at[2])
    for e in taken:
        pl.when(taken[e] == 0)(z_copies[e].start)
    near = x_copies(pl.ds(0, 2), 6, 4)
    settle(gh.at[0], rsem.at[12])
    for e in taken:
        pl.when(taken[e] == 1)(z_copies[e].start)
    share_end(gh, 2)
    settle(gl.at[0, pl.ds(0, 2), pl.ds(0, 3)], rsem.at[3])
    rest = pl.ds(2, 3)
    beyond = x_copies(rest, 8, 8)
    for i in steps:
        near[i].wait_recv()
    share_end(gl, 3)

    swapped = jnp.concatenate(
        [white[USED // 2 :], -white[: USED // 2], jnp.zeros((COLS - USED, WIDTH), jnp.float32)],
        axis=0,
    ).T
    shape = (WIDTH, 8, COLS)
    sub = lax.broadcasted_iota(jnp.int32, (8, COLS), 0)
    lane = lax.broadcasted_iota(jnp.int32, (8, COLS), 1)
    low = (sub % BINS) * SEGS
    here = ((lane >= low) & (lane < low + SEGS)) | (
        (lane >= low + USED // 2) & (lane < low + USED // 2 + SEGS)
    )
    one = jnp.broadcast_to(straight[:, None, :], shape)
    two = jnp.broadcast_to(swapped[:, None, :], shape)
    sel = lax.broadcasted_iota(jnp.int32, (SEL, COLS), 1) == USED
    for odd in (0, 1):
        pick = jnp.where(((sub < BINS) == (odd == 0))[None], one, two)
        pick = jnp.where(here[None], pick, 0.0)
        lhs[odd, :SEL, :] = sel.astype(jnp.float32).astype(jnp.bfloat16)
        lhs[odd, SEL:, :] = pick.reshape(WIDTH * 8, COLS).astype(jnp.bfloat16)
    mine = jnp.broadcast_to(1.0 / straight[:, USED : USED + 1], (WIDTH, 128))
    rci[...] = jnp.broadcast_to(mine[:, None, :], (WIDTH, 8, 128)).reshape(WIDTH * 8, 128)

    for e in taken:
        z_copies[e].wait_recv()
        share(gh, 1 + e, 4 + e + c, 2)
    for i in (0,) + steps:
        if i:
            beyond[i].wait_recv()
        at = (x + 4 - i) % 4
        share(gl, (rest, every, at), (pl.ds(5 + c, 3), every, at), 3)

    settle(gh.at[pl.ds(5, 4)], rsem.at[SHARED + 2])
    settle(gl.at[pl.ds(5, 4)], rsem.at[SHARED + 3])
    settle(gh.at[0, 0, pl.ds(0, 3)], ssem.at[0])
    settle(gl.at[0, 0, pl.ds(0, 3)], ssem.at[1])
    settle(gh.at[pl.ds(5, 4)], ssem.at[2])
    settle(gl.at[pl.ds(5, 4)], ssem.at[3])
    settle(gh.at[pl.ds(0, 3), 0], ssem.at[4])
    settle(gl.at[0, pl.ds(0, 2), pl.ds(0, 3)], ssem.at[5])
    settle(gl.at[pl.ds(0, 2), :, pl.ds(0, 3)], ssem.at[6])
    settle(gh.at[pl.ds(0, 3)], ssem.at[7])
    settle(gl.at[pl.ds(0, 3), :, pl.ds(0, 3)], ssem.at[8])


def stack_kernel(gl, gh, lhs, rci, out, stage, sems):
    mine = rci[...]

    def held(k):
        even = jnp.where(k == 0, 0, jnp.where(k == 8, 1, 1 + k // 2))
        return jnp.where(k % 2 == 0, even, 5 + k // 2)

    def to_out(k):
        return pltpu.make_async_copy(stage.at[k], out.at[:, k], sems.at[k])

    @pl.loop(0, HOPS, unroll=3)
    def _(k):
        def tiles(odd):
            pieces = [(n, at) for n in (0, 1) for at in (2 * odd, 2 * odd + 1)]
            right = [half[(held(k),) + piece] for piece in pieces for half in (gl, gh)]
            result = lax.dot_general(
                lhs[odd],
                jnp.concatenate(right, axis=0),
                (((1,), (1,)), ((), ())),
                preferred_element_type=jnp.float32,
            )
            recip = 1.0 / result[0:1]
            halves = (slice(0, 128), slice(128, 256))
            return [
                (result[SEL:, lanes] * jnp.maximum(mine, recip[:, lanes])).reshape(WIDTH, 8, 128)
                for lanes in halves
            ]

        lower = lax.broadcasted_iota(jnp.int32, (WIDTH, 8, 128), 1) < BINS
        for n, (even, odd) in enumerate(zip(tiles(0), tiles(1))):
            rows = pl.ds(8 * n, 8)
            stage[k, :, 0, rows] = jnp.where(lower, even, odd)
            stage[k, :, 1, rows] = pltpu.roll(jnp.where(lower, odd, even), BINS, 1)
        to_out(k).start()

    @pl.loop(0, HOPS)
    def _(k):
        to_out(k).wait()


def per_device(spectra, counts):
    spec = spectra.reshape(USED, WIDTH)
    vmem = pl.BlockSpec(memory_space=pltpu.VMEM)
    hbm = pl.BlockSpec(memory_space=pltpu.HBM)
    gl, gh, lhs, rci = pl.pallas_call(
        gather_kernel,
        name="whiten_gather",
        out_shape=(
            jax.ShapeDtypeStruct((HOPS, 2, 4, HALF, COLS), jnp.bfloat16),
            jax.ShapeDtypeStruct((HOPS, 2, 4, HALF, COLS), jnp.bfloat16),
            jax.ShapeDtypeStruct((2, SEL + WIDTH * 8, COLS), jnp.bfloat16),
            jax.ShapeDtypeStruct((WIDTH * 8, 128), jnp.float32),
        ),
        in_specs=[hbm, hbm],
        out_specs=(vmem,) * 4,
        scratch_shapes=[
            pltpu.VMEM((USED, WIDTH), jnp.float32),
            pltpu.VMEM((1, WIDTH), jnp.int32),
            pltpu.VMEM((WIDTH, COLS), jnp.bfloat16),
            pltpu.SemaphoreType.DMA((9,)),
            pltpu.SemaphoreType.DMA((SHARED + 4,)),
            pltpu.SemaphoreType.DMA((4,)),
        ],
        compiler_params=pltpu.CompilerParams(
            collective_id=0, has_side_effects=True, vmem_limit_bytes=16 * 2**20
        ),
    )(*(pltpu.with_memory_space_constraint(a, pltpu.HBM) for a in (spec, counts)))
    out = pl.pallas_call(
        stack_kernel,
        name="stack",
        out_shape=jax.ShapeDtypeStruct((WIDTH, HOPS, 2, 4 * BINS, 128), jnp.float32),
        in_specs=[vmem] * 4,
        out_specs=hbm,
        scratch_shapes=[
            pltpu.VMEM((HOPS, WIDTH, 2, 4 * BINS, 128), jnp.float32),
            pltpu.SemaphoreType.DMA((HOPS,)),
        ],
        compiler_params=pltpu.CompilerParams(vmem_limit_bytes=24 * 2**20),
        cost_estimate=pl.CostEstimate(
            flops=2 * (SEL + WIDTH * 8) * COLS * 512 * HOPS,
            bytes_accessed=HOPS * 512 * (COLS * 2 + WIDTH * 8 * 4),
            transcendentals=0,
        ),
    )(gl, gh, lhs, rci)
    out = out.reshape(WIDTH, HOPS, 2, 4, BINS, 128).swapaxes(3, 4)
    return out.reshape(1, WIDTH, HOPS, 2, BINS, 512)


def solution(mesh):
    return jax.shard_map(
        per_device,
        mesh=mesh,
        in_specs=(P(None, None, None, "col", "row"), P("col", "row")),
        out_specs=P("col", "row", None, None, None, None),
        check_vma=False,
    )
```

```python
import functools

import jax
import jax.numpy as jnp
from jax import lax
from jax.experimental import pallas as pl
from jax.experimental.pallas import tpu as pltpu
from jax.sharding import PartitionSpec as P

MESH = pl.DeviceIdType.MESH
BINS = 4
SEGS = 30
USED = 2 * BINS * SEGS
COLS = 256
WIDTH = 64
HALF = 32
SHARED = 14
HOPS = 9
SEL = 16


def one_hop(gl, gh, held, lhs, rci, to):
    mine = rci[...]

    def tiles(odd):
        pieces = [(held, n, at) for n in (0, 1) for at in (2 * odd, 2 * odd + 1)]
        right = [half[piece] for piece in pieces for half in (gl, gh)]
        result = lax.dot_general(
            lhs[odd],
            jnp.concatenate(right, axis=0),
            (((1,), (1,)), ((), ())),
            preferred_element_type=jnp.float32,
        )
        recip = 1.0 / result[0:1]
        halves = (slice(0, 128), slice(128, 256))
        return [
            (result[SEL:, lanes] * jnp.maximum(mine, recip[:, lanes])).reshape(WIDTH, 8, 128)
            for lanes in halves
        ]

    lower = lax.broadcasted_iota(jnp.int32, (WIDTH, 8, 128), 1) < BINS
    for n, (even, odd) in enumerate(zip(tiles(0), tiles(1))):
        rows = pl.ds(8 * n, 8)
        to[:, 0, rows] = jnp.where(lower, even, odd)
        to[:, 1, rows] = pltpu.roll(jnp.where(lower, odd, even), BINS, 1)


def gather_kernel(spec_in, cnt_in, gl, gh, lhs, rci, ready, spec, cnt, own, ssem, rsem, lsem):
    fetch = (
        pltpu.make_async_copy(spec_in, spec, lsem.at[1]),
        pltpu.make_async_copy(cnt_in, cnt, lsem.at[2]),
    )
    for copy in fetch:
        copy.start()
    r, d = lax.axis_index("row"), lax.axis_index("col")
    x, ylo = r % 4, r // 4
    c, q = d % 2, d // 2
    z, yhi = q % 4, q // 4

    def dev(x_, ylo_, q_, c_):
        return (ylo_ * 4 + x_, q_ * 2 + c_)

    sibling = dev(x, ylo, q, 1 - c)
    across = 1 - ylo

    steps = (2, 1, 3)
    y_steps = ((0, 1), (1, 1), (1, 0))

    def along_x(i):
        return dev((x + i) % 4, ylo, q, c)

    def along_y(four_on, rel):
        return dev(x, across if rel else ylo, (q + 4 * four_on) % 8, c)

    def along_z(e):
        return dev(x, ylo, yhi * 4 + (z + e) % 4, c)

    barrier = pltpu.get_barrier_semaphore()
    sources = [along_x(i) for i in steps] + [along_y(*at) for at in y_steps]
    sources += [along_z(e) for e in steps] + [sibling]
    for source in sources:
        pl.semaphore_signal(barrier, inc=1, device_id=source, device_id_type=MESH)

    for copy in fetch:
        copy.wait()
    raw = spec[...]
    power = jnp.sum(raw * raw, axis=0, keepdims=True) / float(USED)
    row = lax.broadcasted_iota(jnp.int32, (USED, WIDTH), 0)
    group = jnp.zeros((USED, WIDTH), jnp.int32)
    for n in range(1, 2 * BINS):
        group = group + (row >= n * SEGS).astype(jnp.int32)
    valid = (row - SEGS * group < cnt[...]).astype(jnp.float32)
    white = raw * lax.rsqrt(power + 1e-6) * valid
    white = white.astype(jnp.bfloat16).astype(jnp.float32)
    count = cnt[...].astype(jnp.float32)
    pad = jnp.zeros((COLS - USED - 8, WIDTH), jnp.float32)
    first = lax.broadcasted_iota(jnp.int32, (8, WIDTH), 0) == 0
    tail = jnp.where(first, count, 0.0)
    straight = jnp.concatenate([white, tail, pad], axis=0).T
    own[...] = straight.astype(jnp.bfloat16)

    def plan(src, dst, device, send, recv):
        return pltpu.make_async_remote_copy(
            src_ref=src,
            dst_ref=dst,
            send_sem=ssem.at[send],
            recv_sem=rsem.at[recv],
            device_id=device,
            device_id_type=MESH,
        )

    def remote(src, dst, device, send, recv):
        copy = plan(src, dst, device, send, recv)
        copy.start()
        return copy

    def settle(region, sem):
        pltpu.make_async_copy(region, region, sem).wait()

    every = slice(None)
    own_lo, own_hi = own.at[pl.ds(0, HALF)], own.at[pl.ds(HALF, HALF)]
    pl.semaphore_wait(barrier, len(sources))
    for i in steps:
        remote(own_hi, gh.at[0, ylo, x], along_x(i), 0, 0)
    for four_on, rel in y_steps:
        remote(own_lo, gl.at[four_on, ylo, x], along_y(four_on, rel), 1, 1)
    local = [
        pltpu.make_async_copy(own_lo, gl.at[0, ylo, x], lsem.at[0]),
        pltpu.make_async_copy(own_hi, gh.at[0, ylo, x], lsem.at[3]),
    ]
    for copy in local:
        copy.start()

    swapped = jnp.concatenate(
        [white[USED // 2 :], -white[: USED // 2], jnp.zeros((COLS - USED, WIDTH), jnp.float32)],
        axis=0,
    ).T
    shape = (WIDTH, 8, COLS)
    sub = lax.broadcasted_iota(jnp.int32, (8, COLS), 0)
    lane = lax.broadcasted_iota(jnp.int32, (8, COLS), 1)
    low = (sub % BINS) * SEGS
    here = ((lane >= low) & (lane < low + SEGS)) | (
        (lane >= low + USED // 2) & (lane < low + USED // 2 + SEGS)
    )
    one = jnp.broadcast_to(straight[:, None, :], shape)
    two = jnp.broadcast_to(swapped[:, None, :], shape)
    sel = lax.broadcasted_iota(jnp.int32, (SEL, COLS), 1) == USED
    for odd in (0, 1):
        pick = jnp.where(((sub < BINS) == (odd == 0))[None], one, two)
        pick = jnp.where(here[None], pick, 0.0)
        lhs[odd, :SEL, :] = sel.astype(jnp.float32).astype(jnp.bfloat16)
        lhs[odd, SEL:, :] = pick.reshape(WIDTH * 8, COLS).astype(jnp.bfloat16)
    mine = jnp.broadcast_to(1.0 / straight[:, USED : USED + 1], (WIDTH, 128))
    rci[...] = jnp.broadcast_to(mine[:, None, :], (WIDTH, 8, 128)).reshape(WIDTH * 8, 128)

    for copy in local:
        copy.wait()

    def share(half, index, to, send):
        remote(half.at[index], half.at[to], sibling, send, SHARED + send)

    def share_end(half, send):
        share(half, 1 - c, 8 - 3 * c, send)

    def x_copies(blocks, send, recv):
        column = gl.at[blocks, :, x]
        return {i: remote(column, column, along_x(i), send, recv + i) for i in steps}

    taken = {e: jnp.where((z + 4 - e) % 4 > z, 1, 0) for e in (3, 2, 1)}

    settle(gh.at[0, 0, pl.ds(0, 3)], rsem.at[0])
    for four_on, rel in y_steps:
        remote(gh.at[0, ylo], gh.at[four_on, ylo], along_y(four_on, rel), 4, 2 + 10 * four_on)
    settle(gl.at[0, 0, pl.ds(0, 3)], rsem.at[1])
    for e in taken:
        remote(gl.at[taken[e], :, x], gl.at[1 + e, :, x], along_z(-e), 5, 3)
    z_copies = {
        e: plan(gh.at[taken[e]], gh.at[1 + e], along_z(-e), 7, 12 + e) for e in taken
    }

    settle(gh.at[0, 0], rsem.at[2])
    for e in taken:
        pl.when(taken[e] == 0)(z_copies[e].start)
    near = x_copies(pl.ds(0, 2), 6, 4)
    settle(gh.at[0], rsem.at[12])
    for e in taken:
        pl.when(taken[e] == 1)(z_copies[e].start)
    share_end(gh, 2)
    settle(gl.at[0, pl.ds(0, 2), pl.ds(0, 3)], rsem.at[3])
    rest = pl.ds(2, 3)
    beyond = x_copies(rest, 8, 8)
    for i in steps:
        near[i].wait_recv()
    share_end(gl, 3)

    for n in (0, 1):
        one_hop(gl, gh, n, lhs, rci, ready.at[n])

    for e in taken:
        z_copies[e].wait_recv()
        share(gh, 1 + e, 4 + e + c, 2)
    for i in (0,) + steps:
        if i:
            beyond[i].wait_recv()
        at = (x + 4 - i) % 4
        share(gl, (rest, every, at), (pl.ds(5 + c, 3), every, at), 3)

    settle(gh.at[pl.ds(5, 4)], rsem.at[SHARED + 2])
    settle(gl.at[pl.ds(5, 4)], rsem.at[SHARED + 3])
    settle(gh.at[0, 0, pl.ds(0, 3)], ssem.at[0])
    settle(gl.at[0, 0, pl.ds(0, 3)], ssem.at[1])
    settle(gh.at[pl.ds(5, 4)], ssem.at[2])
    settle(gl.at[pl.ds(5, 4)], ssem.at[3])
    settle(gh.at[pl.ds(0, 3), 0], ssem.at[4])
    settle(gl.at[0, pl.ds(0, 2), pl.ds(0, 3)], ssem.at[5])
    settle(gl.at[pl.ds(0, 2), :, pl.ds(0, 3)], ssem.at[6])
    settle(gh.at[pl.ds(0, 3)], ssem.at[7])
    settle(gl.at[pl.ds(0, 3), :, pl.ds(0, 3)], ssem.at[8])


def stack_kernel(gl, gh, lhs, rci, ready, out, stage, sems):
    def to_out(src, k):
        return pltpu.make_async_copy(src, out.at[:, k], sems.at[k])

    early = [to_out(ready.at[n], 8 * n) for n in (0, 1)]
    for copy in early:
        copy.start()

    @pl.loop(1, HOPS - 1, unroll=True)
    def _(k):
        one_hop(gl, gh, jnp.where(k % 2 == 0, 1 + k // 2, 5 + k // 2), lhs, rci, stage.at[k - 1])
        to_out(stage.at[k - 1], k).start()

    for copy in early:
        copy.wait()

    @pl.loop(1, HOPS - 1)
    def _(k):
        to_out(stage.at[k - 1], k).wait()


def per_device(spectra, counts):
    spec = spectra.reshape(USED, WIDTH)
    vmem = pl.BlockSpec(memory_space=pltpu.VMEM)
    hbm = pl.BlockSpec(memory_space=pltpu.HBM)
    gl, gh, lhs, rci, ready = pl.pallas_call(
        gather_kernel,
        name="whiten_gather",
        out_shape=(
            jax.ShapeDtypeStruct((HOPS, 2, 4, HALF, COLS), jnp.bfloat16),
            jax.ShapeDtypeStruct((HOPS, 2, 4, HALF, COLS), jnp.bfloat16),
            jax.ShapeDtypeStruct((2, SEL + WIDTH * 8, COLS), jnp.bfloat16),
            jax.ShapeDtypeStruct((WIDTH * 8, 128), jnp.float32),
            jax.ShapeDtypeStruct((2, WIDTH, 2, 4 * BINS, 128), jnp.float32),
        ),
        in_specs=[hbm, hbm],
        out_specs=(vmem,) * 5,
        scratch_shapes=[
            pltpu.VMEM((USED, WIDTH), jnp.float32),
            pltpu.VMEM((1, WIDTH), jnp.int32),
            pltpu.VMEM((WIDTH, COLS), jnp.bfloat16),
            pltpu.SemaphoreType.DMA((9,)),
            pltpu.SemaphoreType.DMA((SHARED + 4,)),
            pltpu.SemaphoreType.DMA((4,)),
        ],
        compiler_params=pltpu.CompilerParams(
            collective_id=0, has_side_effects=True, vmem_limit_bytes=16 * 2**20
        ),
    )(*(pltpu.with_memory_space_constraint(a, pltpu.HBM) for a in (spec, counts)))
    out = pl.pallas_call(
        stack_kernel,
        name="stack",
        out_shape=jax.ShapeDtypeStruct((WIDTH, HOPS, 2, 4 * BINS, 128), jnp.float32),
        in_specs=[vmem] * 5,
        out_specs=hbm,
        scratch_shapes=[
            pltpu.VMEM((HOPS - 2, WIDTH, 2, 4 * BINS, 128), jnp.float32),
            pltpu.SemaphoreType.DMA((HOPS,)),
        ],
        compiler_params=pltpu.CompilerParams(vmem_limit_bytes=24 * 2**20),
        cost_estimate=pl.CostEstimate(
            flops=2 * (SEL + WIDTH * 8) * COLS * 512 * HOPS,
            bytes_accessed=HOPS * 512 * (COLS * 2 + WIDTH * 8 * 4),
            transcendentals=0,
        ),
    )(gl, gh, lhs, rci, ready)
    out = out.reshape(WIDTH, HOPS, 2, 4, BINS, 128).swapaxes(3, 4)
    return out.reshape(1, WIDTH, HOPS, 2, BINS, 512)


def solution(mesh):
    return jax.shard_map(
        per_device,
        mesh=mesh,
        in_specs=(P(None, None, None, "col", "row"), P("col", "row")),
        out_specs=P("col", "row", None, None, None, None),
        check_vma=False,
    )
```

```python
import functools

import jax
import jax.numpy as jnp
from jax import lax
from jax.experimental import pallas as pl
from jax.experimental.pallas import tpu as pltpu
from jax.sharding import PartitionSpec as P

MESH = pl.DeviceIdType.MESH
BINS = 4
SEGS = 30
USED = 2 * BINS * SEGS
COLS = 256
WIDTH = 64
HALF = 32
SHARED = 14
HOPS = 9
SEL = 16


def one_hop(gl, gh, held, lhs, rci, to):
    mine = rci[...]

    def tiles(odd):
        pieces = [(held, n, at) for n in (0, 1) for at in (2 * odd, 2 * odd + 1)]
        right = [half[piece] for piece in pieces for half in (gl, gh)]
        result = lax.dot_general(
            lhs[odd],
            jnp.concatenate(right, axis=0),
            (((1,), (1,)), ((), ())),
            preferred_element_type=jnp.float32,
        )
        recip = 1.0 / result[0:1]
        halves = (slice(0, 128), slice(128, 256))
        return [
            (result[SEL:, lanes] * jnp.maximum(mine, recip[:, lanes])).reshape(WIDTH, 8, 128)
            for lanes in halves
        ]

    lower = lax.broadcasted_iota(jnp.int32, (WIDTH, 8, 128), 1) < BINS
    for n, (even, odd) in enumerate(zip(tiles(0), tiles(1))):
        rows = pl.ds(8 * n, 8)
        to[:, 0, rows] = jnp.where(lower, even, odd)
        to[:, 1, rows] = pltpu.roll(jnp.where(lower, odd, even), BINS, 1)


def gather_kernel(spec_in, cnt_in, gl, gh, lhs, rci, ready, spec, cnt, own, ssem, rsem, lsem):
    fetch = (
        pltpu.make_async_copy(spec_in, spec, lsem.at[1]),
        pltpu.make_async_copy(cnt_in, cnt, lsem.at[2]),
    )
    for copy in fetch:
        copy.start()
    r, d = lax.axis_index("row"), lax.axis_index("col")
    x, ylo = r % 4, r // 4
    c, q = d % 2, d // 2
    z, yhi = q % 4, q // 4

    def dev(x_, ylo_, q_, c_):
        return (ylo_ * 4 + x_, q_ * 2 + c_)

    sibling = dev(x, ylo, q, 1 - c)
    across = 1 - ylo

    steps = (2, 1, 3)
    y_steps = ((0, 1), (1, 1), (1, 0))

    def along_x(i):
        return dev((x + i) % 4, ylo, q, c)

    def along_y(four_on, rel):
        return dev(x, across if rel else ylo, (q + 4 * four_on) % 8, c)

    def along_z(e):
        return dev(x, ylo, yhi * 4 + (z + e) % 4, c)

    barrier = pltpu.get_barrier_semaphore()
    sources = [along_x(i) for i in steps] + [along_y(*at) for at in y_steps]
    sources += [along_z(e) for e in (2, 3)] + [sibling]

    def announce(source):
        pl.semaphore_signal(barrier, inc=1, device_id=source, device_id_type=MESH)

    for source in sources:
        announce(source)
    pl.when(z != 3)(lambda: announce(along_z(1)))
    relays = (z == 1) | (z == 2)

    for copy in fetch:
        copy.wait()
    raw = spec[...]
    power = jnp.sum(raw * raw, axis=0, keepdims=True) / float(USED)
    row = lax.broadcasted_iota(jnp.int32, (USED, WIDTH), 0)
    group = jnp.zeros((USED, WIDTH), jnp.int32)
    for n in range(1, 2 * BINS):
        group = group + (row >= n * SEGS).astype(jnp.int32)
    valid = (row - SEGS * group < cnt[...]).astype(jnp.float32)
    white = raw * lax.rsqrt(power + 1e-6) * valid
    white = white.astype(jnp.bfloat16).astype(jnp.float32)
    count = cnt[...].astype(jnp.float32)
    pad = jnp.zeros((COLS - USED - 8, WIDTH), jnp.float32)
    first = lax.broadcasted_iota(jnp.int32, (8, WIDTH), 0) == 0
    tail = jnp.where(first, count, 0.0)
    straight = jnp.concatenate([white, tail, pad], axis=0).T
    own[...] = straight.astype(jnp.bfloat16)

    def plan(src, dst, device, send, recv):
        return pltpu.make_async_remote_copy(
            src_ref=src,
            dst_ref=dst,
            send_sem=ssem.at[send],
            recv_sem=rsem.at[recv],
            device_id=device,
            device_id_type=MESH,
        )

    def remote(src, dst, device, send, recv):
        copy = plan(src, dst, device, send, recv)
        copy.start()
        return copy

    def settle(region, sem):
        pltpu.make_async_copy(region, region, sem).wait()

    every = slice(None)
    own_lo, own_hi = own.at[pl.ds(0, HALF)], own.at[pl.ds(HALF, HALF)]
    pl.semaphore_wait(barrier, jnp.where(z == 0, 9, 10))
    for i in steps:
        remote(own_hi, gh.at[0, ylo, x], along_x(i), 0, 0)
    for four_on, rel in y_steps:
        remote(own_lo, gl.at[four_on, ylo, x], along_y(four_on, rel), 1, 1)
    local = [
        pltpu.make_async_copy(own_lo, gl.at[0, ylo, x], lsem.at[0]),
        pltpu.make_async_copy(own_hi, gh.at[0, ylo, x], lsem.at[3]),
    ]
    for copy in local:
        copy.start()

    swapped = jnp.concatenate(
        [white[USED // 2 :], -white[: USED // 2], jnp.zeros((COLS - USED, WIDTH), jnp.float32)],
        axis=0,
    ).T
    shape = (WIDTH, 8, COLS)
    sub = lax.broadcasted_iota(jnp.int32, (8, COLS), 0)
    lane = lax.broadcasted_iota(jnp.int32, (8, COLS), 1)
    low = (sub % BINS) * SEGS
    here = ((lane >= low) & (lane < low + SEGS)) | (
        (lane >= low + USED // 2) & (lane < low + USED // 2 + SEGS)
    )
    one = jnp.broadcast_to(straight[:, None, :], shape)
    two = jnp.broadcast_to(swapped[:, None, :], shape)
    sel = lax.broadcasted_iota(jnp.int32, (SEL, COLS), 1) == USED
    for odd in (0, 1):
        pick = jnp.where(((sub < BINS) == (odd == 0))[None], one, two)
        pick = jnp.where(here[None], pick, 0.0)
        lhs[odd, :SEL, :] = sel.astype(jnp.float32).astype(jnp.bfloat16)
        lhs[odd, SEL:, :] = pick.reshape(WIDTH * 8, COLS).astype(jnp.bfloat16)
    mine = jnp.broadcast_to(1.0 / straight[:, USED : USED + 1], (WIDTH, 128))
    rci[...] = jnp.broadcast_to(mine[:, None, :], (WIDTH, 8, 128)).reshape(WIDTH * 8, 128)

    for copy in local:
        copy.wait()

    def share(half, index, to, send):
        remote(half.at[index], half.at[to], sibling, send, SHARED + send)

    def share_end(half, send):
        share(half, 1 - c, 8 - 3 * c, send)

    def x_copies(blocks, send, recv):
        column = gl.at[blocks, :, x]
        return {i: remote(column, column, along_x(i), send, recv + i) for i in steps}

    taken = {e: jnp.where((z + 4 - e) % 4 > z, 1, 0) for e in (3, 2, 1)}

    settle(gh.at[0, 0, pl.ds(0, 3)], rsem.at[0])
    for four_on, rel in y_steps:
        remote(gh.at[0, ylo], gh.at[four_on, ylo], along_y(four_on, rel), 4, 2 + 10 * four_on)
    settle(gl.at[0, 0, pl.ds(0, 3)], rsem.at[1])
    for e in (3, 2):
        remote(gl.at[taken[e], :, x], gl.at[1 + e, :, x], along_z(-e), 5, 3)

    @pl.when(z != 0)
    def _():
        remote(gl.at[0, :, x], gl.at[2, :, x], along_z(-1), 5, 3)

    z_copies = {
        e: plan(gh.at[taken[e]], gh.at[1 + e], along_z(-e), 7, 12 + e) for e in taken
    }

    settle(gh.at[0, 0], rsem.at[2])
    for e in taken:
        pl.when(taken[e] == 0)(z_copies[e].start)
    near = x_copies(pl.ds(0, 2), 6, 4)
    settle(gh.at[0], rsem.at[12])
    for e in (3, 2):
        pl.when(taken[e] == 1)(z_copies[e].start)
    share_end(gh, 2)
    settle(gl.at[0, pl.ds(0, 2), pl.ds(0, 3)], rsem.at[3])
    relayed, relayed_row = jnp.where(z == 1, 4, 3), jnp.where(z == 1, 1, 0)
    top = dev(x, ylo, yhi * 4 + 3, c)

    @pl.when(relays)
    def _():
        remote(gl.at[relayed, relayed_row, x], gl.at[2, relayed_row, x], top, 9, 3)

    rest = pl.ds(2, 3)
    beyond = x_copies(rest, 8, 8)
    for i in steps:
        near[i].wait_recv()
    share_end(gl, 3)

    for n in (0, 1):
        one_hop(gl, gh, n, lhs, rci, ready.at[n])

    relay = plan(gh.at[relayed, relayed_row], gh.at[2, relayed_row], top, 10, 13)
    for e in taken:
        z_copies[e].wait_recv()
        if e > 1:
            pl.when(z == 4 - e)(relay.start)
        share(gh, 1 + e, 4 + e + c, 2)
    for i in (0,) + steps:
        if i:
            beyond[i].wait_recv()
        at = (x + 4 - i) % 4
        share(gl, (rest, every, at), (pl.ds(5 + c, 3), every, at), 3)

    settle(gh.at[pl.ds(5, 4)], rsem.at[SHARED + 2])
    settle(gl.at[pl.ds(5, 4)], rsem.at[SHARED + 3])
    settle(gh.at[0, 0, pl.ds(0, 3)], ssem.at[0])
    settle(gl.at[0, 0, pl.ds(0, 3)], ssem.at[1])
    settle(gh.at[pl.ds(5, 4)], ssem.at[2])
    settle(gl.at[pl.ds(5, 4)], ssem.at[3])
    settle(gh.at[pl.ds(0, 3), 0], ssem.at[4])
    settle(gl.at[pl.ds(0, 2), :, pl.ds(0, 3)], ssem.at[6])

    @pl.when(z == 0)
    def _():
        settle(gl.at[0, pl.ds(0, 2), pl.ds(0, 2)], ssem.at[5])
        settle(gh.at[pl.ds(0, 2)], ssem.at[7])

    @pl.when(z != 0)
    def _():
        settle(gl.at[0, pl.ds(0, 2), pl.ds(0, 3)], ssem.at[5])
        settle(gh.at[pl.ds(0, 3)], ssem.at[7])

    @pl.when(relays)
    def _():
        settle(gl.at[0, 0, 0], ssem.at[9])
        relay.wait_send()

    settle(gl.at[pl.ds(0, 3), :, pl.ds(0, 3)], ssem.at[8])


def stack_kernel(gl, gh, lhs, rci, ready, out, stage, sems):
    def to_out(src, k):
        return pltpu.make_async_copy(src, out.at[:, k], sems.at[k])

    early = [to_out(ready.at[n], 8 * n) for n in (0, 1)]
    for copy in early:
        copy.start()

    @pl.loop(1, HOPS - 1, unroll=True)
    def _(k):
        one_hop(gl, gh, jnp.where(k % 2 == 0, 1 + k // 2, 5 + k // 2), lhs, rci, stage.at[k - 1])
        to_out(stage.at[k - 1], k).start()

    for copy in early:
        copy.wait()

    @pl.loop(1, HOPS - 1)
    def _(k):
        to_out(stage.at[k - 1], k).wait()


def per_device(spectra, counts):
    spec = spectra.reshape(USED, WIDTH)
    vmem = pl.BlockSpec(memory_space=pltpu.VMEM)
    hbm = pl.BlockSpec(memory_space=pltpu.HBM)
    gl, gh, lhs, rci, ready = pl.pallas_call(
        gather_kernel,
        name="whiten_gather",
        out_shape=(
            jax.ShapeDtypeStruct((HOPS, 2, 4, HALF, COLS), jnp.bfloat16),
            jax.ShapeDtypeStruct((HOPS, 2, 4, HALF, COLS), jnp.bfloat16),
            jax.ShapeDtypeStruct((2, SEL + WIDTH * 8, COLS), jnp.bfloat16),
            jax.ShapeDtypeStruct((WIDTH * 8, 128), jnp.float32),
            jax.ShapeDtypeStruct((2, WIDTH, 2, 4 * BINS, 128), jnp.float32),
        ),
        in_specs=[hbm, hbm],
        out_specs=(vmem,) * 5,
        scratch_shapes=[
            pltpu.VMEM((USED, WIDTH), jnp.float32),
            pltpu.VMEM((1, WIDTH), jnp.int32),
            pltpu.VMEM((WIDTH, COLS), jnp.bfloat16),
            pltpu.SemaphoreType.DMA((11,)),
            pltpu.SemaphoreType.DMA((SHARED + 4,)),
            pltpu.SemaphoreType.DMA((4,)),
        ],
        compiler_params=pltpu.CompilerParams(
            collective_id=0, has_side_effects=True, vmem_limit_bytes=16 * 2**20
        ),
    )(*(pltpu.with_memory_space_constraint(a, pltpu.HBM) for a in (spec, counts)))
    out = pl.pallas_call(
        stack_kernel,
        name="stack",
        out_shape=jax.ShapeDtypeStruct((WIDTH, HOPS, 2, 4 * BINS, 128), jnp.float32),
        in_specs=[vmem] * 5,
        out_specs=hbm,
        scratch_shapes=[
            pltpu.VMEM((HOPS - 2, WIDTH, 2, 4 * BINS, 128), jnp.float32),
            pltpu.SemaphoreType.DMA((HOPS,)),
        ],
        compiler_params=pltpu.CompilerParams(vmem_limit_bytes=24 * 2**20),
        cost_estimate=pl.CostEstimate(
            flops=2 * (SEL + WIDTH * 8) * COLS * 512 * HOPS,
            bytes_accessed=HOPS * 512 * (COLS * 2 + WIDTH * 8 * 4),
            transcendentals=0,
        ),
    )(gl, gh, lhs, rci, ready)
    out = out.reshape(WIDTH, HOPS, 2, 4, BINS, 128).swapaxes(3, 4)
    return out.reshape(1, WIDTH, HOPS, 2, BINS, 512)


def solution(mesh):
    return jax.shard_map(
        per_device,
        mesh=mesh,
        in_specs=(P(None, None, None, "col", "row"), P("col", "row")),
        out_specs=P("col", "row", None, None, None, None),
        check_vma=False,
    )
```

```python
import functools

import jax
import jax.numpy as jnp
from jax import lax
from jax.experimental import pallas as pl
from jax.experimental.pallas import tpu as pltpu
from jax.sharding import PartitionSpec as P

MESH = pl.DeviceIdType.MESH
BINS = 4
SEGS = 30
USED = 2 * BINS * SEGS
COLS = 256
WIDTH = 64
HALF = 32
SHARED = 14
HOPS = 9
SEL = 16


def one_hop(gl, gh, held, lhs, rci, to):
    mine = rci[...]

    def tiles(odd):
        pieces = [(held, n, at) for n in (0, 1) for at in (2 * odd, 2 * odd + 1)]
        right = [half[piece] for piece in pieces for half in (gl, gh)]
        result = lax.dot_general(
            lhs[odd],
            jnp.concatenate(right, axis=0),
            (((1,), (1,)), ((), ())),
            preferred_element_type=jnp.float32,
        )
        recip = 1.0 / result[0:1]
        halves = (slice(0, 128), slice(128, 256))
        return [
            (result[SEL:, lanes] * jnp.maximum(mine, recip[:, lanes])).reshape(WIDTH, 8, 128)
            for lanes in halves
        ]

    lower = lax.broadcasted_iota(jnp.int32, (WIDTH, 8, 128), 1) < BINS
    for n, (even, odd) in enumerate(zip(tiles(0), tiles(1))):
        rows = pl.ds(8 * n, 8)
        to[:, 0, rows] = jnp.where(lower, even, odd)
        to[:, 1, rows] = pltpu.roll(jnp.where(lower, odd, even), BINS, 1)


def gather_kernel(spec_in, cnt_in, gl, gh, lhs, rci, ready, spec, cnt, own, ssem, rsem, lsem):
    fetch = (
        pltpu.make_async_copy(spec_in, spec, lsem.at[1]),
        pltpu.make_async_copy(cnt_in, cnt, lsem.at[2]),
    )
    for copy in fetch:
        copy.start()
    r, d = lax.axis_index("row"), lax.axis_index("col")
    x, ylo = r % 4, r // 4
    c, q = d % 2, d // 2
    z, yhi = q % 4, q // 4

    def dev(x_, ylo_, q_, c_):
        return (ylo_ * 4 + x_, q_ * 2 + c_)

    sibling = dev(x, ylo, q, 1 - c)
    across = 1 - ylo

    steps = (2, 1, 3)
    y_steps = ((0, 1), (1, 1), (1, 0))

    def along_x(i):
        return dev((x + i) % 4, ylo, q, c)

    def along_y(four_on, rel):
        return dev(x, across if rel else ylo, (q + 4 * four_on) % 8, c)

    def along_z(e):
        return dev(x, ylo, yhi * 4 + (z + e) % 4, c)

    barrier = pltpu.get_barrier_semaphore()
    sources = [along_x(i) for i in steps] + [along_y(*at) for at in y_steps]
    sources += [along_z(e) for e in steps] + [sibling]
    for source in sources:
        pl.semaphore_signal(barrier, inc=1, device_id=source, device_id_type=MESH)

    for copy in fetch:
        copy.wait()
    raw = spec[...]
    power = jnp.sum(raw * raw, axis=0, keepdims=True) / float(USED)
    row = lax.broadcasted_iota(jnp.int32, (USED, WIDTH), 0)
    group = jnp.zeros((USED, WIDTH), jnp.int32)
    for n in range(1, 2 * BINS):
        group = group + (row >= n * SEGS).astype(jnp.int32)
    valid = (row - SEGS * group < cnt[...]).astype(jnp.float32)
    white = raw * lax.rsqrt(power + 1e-6) * valid
    white = white.astype(jnp.bfloat16).astype(jnp.float32)
    count = cnt[...].astype(jnp.float32)
    pad = jnp.zeros((COLS - USED - 8, WIDTH), jnp.float32)
    first = lax.broadcasted_iota(jnp.int32, (8, WIDTH), 0) == 0
    tail = jnp.where(first, count, 0.0)
    straight = jnp.concatenate([white, tail, pad], axis=0).T
    own[...] = straight.astype(jnp.bfloat16)

    def plan(src, dst, device, send, recv):
        return pltpu.make_async_remote_copy(
            src_ref=src,
            dst_ref=dst,
            send_sem=ssem.at[send],
            recv_sem=rsem.at[recv],
            device_id=device,
            device_id_type=MESH,
        )

    def remote(src, dst, device, send, recv):
        copy = plan(src, dst, device, send, recv)
        copy.start()
        return copy

    def settle(region, sem):
        pltpu.make_async_copy(region, region, sem).wait()

    every = slice(None)
    own_lo, own_hi = own.at[pl.ds(0, HALF)], own.at[pl.ds(HALF, HALF)]
    pl.semaphore_wait(barrier, len(sources))
    for i in steps:
        remote(own_hi, gh.at[0, ylo, x], along_x(i), 0, 0)
    for four_on, rel in y_steps:
        remote(own_lo, gl.at[four_on, ylo, x], along_y(four_on, rel), 1, 1)
    local = [
        pltpu.make_async_copy(own_lo, gl.at[0, ylo, x], lsem.at[0]),
        pltpu.make_async_copy(own_hi, gh.at[0, ylo, x], lsem.at[3]),
    ]
    for copy in local:
        copy.start()

    swapped = jnp.concatenate(
        [white[USED // 2 :], -white[: USED // 2], jnp.zeros((COLS - USED, WIDTH), jnp.float32)],
        axis=0,
    ).T
    shape = (WIDTH, 8, COLS)
    sub = lax.broadcasted_iota(jnp.int32, (8, COLS), 0)
    lane = lax.broadcasted_iota(jnp.int32, (8, COLS), 1)
    low = (sub % BINS) * SEGS
    here = ((lane >= low) & (lane < low + SEGS)) | (
        (lane >= low + USED // 2) & (lane < low + USED // 2 + SEGS)
    )
    one = jnp.broadcast_to(straight[:, None, :], shape)
    two = jnp.broadcast_to(swapped[:, None, :], shape)
    sel = lax.broadcasted_iota(jnp.int32, (SEL, COLS), 1) == USED
    for odd in (0, 1):
        pick = jnp.where(((sub < BINS) == (odd == 0))[None], one, two)
        pick = jnp.where(here[None], pick, 0.0)
        lhs[odd, :SEL, :] = sel.astype(jnp.float32).astype(jnp.bfloat16)
        lhs[odd, SEL:, :] = pick.reshape(WIDTH * 8, COLS).astype(jnp.bfloat16)
    mine = jnp.broadcast_to(1.0 / straight[:, USED : USED + 1], (WIDTH, 128))
    rci[...] = jnp.broadcast_to(mine[:, None, :], (WIDTH, 8, 128)).reshape(WIDTH * 8, 128)

    for copy in local:
        copy.wait()

    def share(half, index, to, send, recv=SHARED):
        remote(half.at[index], half.at[to], sibling, send, recv + send)

    def share_end(half, send):
        share(half, 1 - c, 8 - 3 * c, send, SHARED + 2)

    def x_copies(blocks, send, recv):
        column = gl.at[blocks, :, x]
        return {i: remote(column, column, along_x(i), send, recv + i) for i in steps}

    taken = {e: jnp.where((z + 4 - e) % 4 > z, 1, 0) for e in (3, 2, 1)}

    settle(gl.at[0, 0, pl.ds(0, 3)], rsem.at[1])
    for e in taken:
        remote(gl.at[taken[e], :, x], gl.at[1 + e, :, x], along_z(-e), 5, 3)
    settle(gh.at[0, 0, pl.ds(0, 3)], rsem.at[0])
    for four_on, rel in y_steps:
        remote(gh.at[0, ylo], gh.at[four_on, ylo], along_y(four_on, rel), 4, 2 + 10 * four_on)
    z_copies = {
        e: plan(gh.at[taken[e]], gh.at[1 + e], along_z(-e), 7, 12 + e) for e in taken
    }

    settle(gh.at[0, 0], rsem.at[2])
    for e in taken:
        pl.when(taken[e] == 0)(z_copies[e].start)
    near = x_copies(pl.ds(0, 2), 6, 4)
    settle(gl.at[0, pl.ds(0, 2), pl.ds(0, 3)], rsem.at[3])
    rest = pl.ds(2, 3)
    beyond = x_copies(rest, 8, 8)
    settle(gh.at[0], rsem.at[12])
    for e in taken:
        pl.when(taken[e] == 1)(z_copies[e].start)
    share_end(gh, 2)
    for i in steps:
        near[i].wait_recv()
    share_end(gl, 3)

    for n in (0, 1):
        one_hop(gl, gh, n, lhs, rci, ready.at[n])
    settle(gh.at[0], rsem.at[SHARED + 4])
    settle(gl.at[0], rsem.at[SHARED + 5])
    one_hop(gl, gh, 5 + 3 * c, lhs, rci, ready.at[2])

    for e in taken:
        z_copies[e].wait_recv()
        share(gh, 1 + e, 4 + e + c, 2)
    for i in (0,) + steps:
        if i:
            beyond[i].wait_recv()
        at = (x + 4 - i) % 4
        share(gl, (rest, every, at), (pl.ds(5 + c, 3), every, at), 3)

    settle(gh.at[pl.ds(5, 3)], rsem.at[SHARED + 2])
    settle(gl.at[pl.ds(5, 3)], rsem.at[SHARED + 3])
    settle(gh.at[0, 0, pl.ds(0, 3)], ssem.at[0])
    settle(gl.at[0, 0, pl.ds(0, 3)], ssem.at[1])
    settle(gh.at[pl.ds(5, 4)], ssem.at[2])
    settle(gl.at[pl.ds(5, 4)], ssem.at[3])
    settle(gh.at[pl.ds(0, 3), 0], ssem.at[4])
    settle(gl.at[0, pl.ds(0, 2), pl.ds(0, 3)], ssem.at[5])
    settle(gl.at[pl.ds(0, 2), :, pl.ds(0, 3)], ssem.at[6])
    settle(gh.at[pl.ds(0, 3)], ssem.at[7])
    settle(gl.at[pl.ds(0, 3), :, pl.ds(0, 3)], ssem.at[8])


def stack_kernel(gl, gh, lhs, rci, ready, out, stage, sems):
    def to_out(src, k):
        return pltpu.make_async_copy(src, out.at[:, k], sems.at[k])

    c = lax.axis_index("col") % 2
    early = [to_out(ready.at[n], k) for n, k in enumerate((0, HOPS - 1, 1 + 6 * c))]
    for copy in early:
        copy.start()
    later = [2 - c + n for n in range(HOPS - 3)]
    copies = [to_out(stage.at[n], k) for n, k in enumerate(later)]
    for n, k in enumerate(later):
        held = jnp.where(k % 2 == 0, 1 + k // 2, 5 + k // 2)
        one_hop(gl, gh, held, lhs, rci, stage.at[n])
        copies[n].start()
    for copy in early + copies:
        copy.wait()


def per_device(spectra, counts):
    spec = spectra.reshape(USED, WIDTH)
    vmem = pl.BlockSpec(memory_space=pltpu.VMEM)
    hbm = pl.BlockSpec(memory_space=pltpu.HBM)
    gl, gh, lhs, rci, ready = pl.pallas_call(
        gather_kernel,
        name="whiten_gather",
        out_shape=(
            jax.ShapeDtypeStruct((HOPS, 2, 4, HALF, COLS), jnp.bfloat16),
            jax.ShapeDtypeStruct((HOPS, 2, 4, HALF, COLS), jnp.bfloat16),
            jax.ShapeDtypeStruct((2, SEL + WIDTH * 8, COLS), jnp.bfloat16),
            jax.ShapeDtypeStruct((WIDTH * 8, 128), jnp.float32),
            jax.ShapeDtypeStruct((3, WIDTH, 2, 4 * BINS, 128), jnp.float32),
        ),
        in_specs=[hbm, hbm],
        out_specs=(vmem,) * 5,
        scratch_shapes=[
            pltpu.VMEM((USED, WIDTH), jnp.float32),
            pltpu.VMEM((1, WIDTH), jnp.int32),
            pltpu.VMEM((WIDTH, COLS), jnp.bfloat16),
            pltpu.SemaphoreType.DMA((9,)),
            pltpu.SemaphoreType.DMA((SHARED + 6,)),
            pltpu.SemaphoreType.DMA((4,)),
        ],
        compiler_params=pltpu.CompilerParams(
            collective_id=0, has_side_effects=True, vmem_limit_bytes=16 * 2**20
        ),
    )(*(pltpu.with_memory_space_constraint(a, pltpu.HBM) for a in (spec, counts)))
    out = pl.pallas_call(
        stack_kernel,
        name="stack",
        out_shape=jax.ShapeDtypeStruct((WIDTH, HOPS, 2, 4 * BINS, 128), jnp.float32),
        in_specs=[vmem] * 5,
        out_specs=hbm,
        scratch_shapes=[
            pltpu.VMEM((HOPS - 3, WIDTH, 2, 4 * BINS, 128), jnp.float32),
            pltpu.SemaphoreType.DMA((HOPS,)),
        ],
        compiler_params=pltpu.CompilerParams(vmem_limit_bytes=24 * 2**20),
        cost_estimate=pl.CostEstimate(
            flops=2 * (SEL + WIDTH * 8) * COLS * 512 * HOPS,
            bytes_accessed=HOPS * 512 * (COLS * 2 + WIDTH * 8 * 4),
            transcendentals=0,
        ),
    )(gl, gh, lhs, rci, ready)
    out = out.reshape(WIDTH, HOPS, 2, 4, BINS, 128).swapaxes(3, 4)
    return out.reshape(1, WIDTH, HOPS, 2, BINS, 512)


def solution(mesh):
    return jax.shard_map(
        per_device,
        mesh=mesh,
        in_specs=(P(None, None, None, "col", "row"), P("col", "row")),
        out_specs=P("col", "row", None, None, None, None),
        check_vma=False,
    )
```

```python
import functools

import jax
import jax.numpy as jnp
from jax import lax
from jax.experimental import pallas as pl
from jax.experimental.pallas import tpu as pltpu
from jax.sharding import PartitionSpec as P

MESH = pl.DeviceIdType.MESH
BINS = 4
SEGS = 30
USED = 2 * BINS * SEGS
COLS = 256
WIDTH = 64
HALF = 32
SHARED = 14
HOPS = 9
SEL = 16


def one_hop(gl, gh, held, lhs, rci, to):
    mine = rci[...]

    def tiles(odd):
        pieces = [(held, n, at) for n in (0, 1) for at in (2 * odd, 2 * odd + 1)]
        right = [half[piece] for piece in pieces for half in (gl, gh)]
        result = lax.dot_general(
            lhs[odd],
            jnp.concatenate(right, axis=0),
            (((1,), (1,)), ((), ())),
            preferred_element_type=jnp.float32,
        )
        recip = 1.0 / result[0:1]
        halves = (slice(0, 128), slice(128, 256))
        return [
            (result[SEL:, lanes] * jnp.maximum(mine, recip[:, lanes])).reshape(WIDTH, 8, 128)
            for lanes in halves
        ]

    lower = lax.broadcasted_iota(jnp.int32, (WIDTH, 8, 128), 1) < BINS
    for n, (even, odd) in enumerate(zip(tiles(0), tiles(1))):
        rows = pl.ds(8 * n, 8)
        to[:, 0, rows] = jnp.where(lower, even, odd)
        to[:, 1, rows] = pltpu.roll(jnp.where(lower, odd, even), BINS, 1)


def gather_kernel(spec_in, cnt_in, gl, gh, lhs, rci, ready, spec, cnt, own, ssem, rsem, lsem):
    fetch = (
        pltpu.make_async_copy(spec_in, spec, lsem.at[1]),
        pltpu.make_async_copy(cnt_in, cnt, lsem.at[2]),
    )
    for copy in fetch:
        copy.start()
    r, d = lax.axis_index("row"), lax.axis_index("col")
    x, ylo = r % 4, r // 4
    c, q = d % 2, d // 2
    z, yhi = q % 4, q // 4

    def dev(x_, ylo_, q_, c_):
        return (ylo_ * 4 + x_, q_ * 2 + c_)

    sibling = dev(x, ylo, q, 1 - c)
    across = 1 - ylo

    steps = (2, 1, 3)
    y_steps = ((0, 1), (1, 1), (1, 0))

    def along_x(i):
        return dev((x + i) % 4, ylo, q, c)

    def along_y(four_on, rel):
        return dev(x, across if rel else ylo, (q + 4 * four_on) % 8, c)

    def along_z(e):
        return dev(x, ylo, yhi * 4 + (z + e) % 4, c)

    barrier = pltpu.get_barrier_semaphore()
    sources = [along_x(i) for i in steps] + [along_y(*at) for at in y_steps]
    sources += [along_z(e) for e in steps] + [sibling]
    for source in sources:
        pl.semaphore_signal(barrier, inc=1, device_id=source, device_id_type=MESH)

    for copy in fetch:
        copy.wait()
    raw = spec[...]
    power = jnp.sum(raw * raw, axis=0, keepdims=True) / float(USED)
    row = lax.broadcasted_iota(jnp.int32, (USED, WIDTH), 0)
    group = jnp.zeros((USED, WIDTH), jnp.int32)
    for n in range(1, 2 * BINS):
        group = group + (row >= n * SEGS).astype(jnp.int32)
    valid = (row - SEGS * group < cnt[...]).astype(jnp.float32)
    white = raw * lax.rsqrt(power + 1e-6) * valid
    white = white.astype(jnp.bfloat16).astype(jnp.float32)
    count = cnt[...].astype(jnp.float32)
    pad = jnp.zeros((COLS - USED - 8, WIDTH), jnp.float32)
    first = lax.broadcasted_iota(jnp.int32, (8, WIDTH), 0) == 0
    tail = jnp.where(first, count, 0.0)
    straight = jnp.concatenate([white, tail, pad], axis=0).T
    own[...] = straight.astype(jnp.bfloat16)

    def plan(src, dst, device, send, recv):
        return pltpu.make_async_remote_copy(
            src_ref=src,
            dst_ref=dst,
            send_sem=ssem.at[send],
            recv_sem=rsem.at[recv],
            device_id=device,
            device_id_type=MESH,
        )

    def remote(src, dst, device, send, recv):
        copy = plan(src, dst, device, send, recv)
        copy.start()
        return copy

    def settle(region, sem):
        pltpu.make_async_copy(region, region, sem).wait()

    every = slice(None)
    own_lo, own_hi = own.at[pl.ds(0, HALF)], own.at[pl.ds(HALF, HALF)]
    pl.semaphore_wait(barrier, len(sources))
    for i in steps:
        remote(own_hi, gh.at[0, ylo, x], along_x(i), 0, 0)
    for four_on, rel in y_steps:
        remote(own_lo, gl.at[four_on, ylo, x], along_y(four_on, rel), 1, 1)
    local = [
        pltpu.make_async_copy(own_lo, gl.at[0, ylo, x], lsem.at[0]),
        pltpu.make_async_copy(own_hi, gh.at[0, ylo, x], lsem.at[3]),
    ]
    for copy in local:
        copy.start()

    swapped = jnp.concatenate(
        [white[USED // 2 :], -white[: USED // 2], jnp.zeros((COLS - USED, WIDTH), jnp.float32)],
        axis=0,
    ).T
    shape = (WIDTH, 8, COLS)
    sub = lax.broadcasted_iota(jnp.int32, (8, COLS), 0)
    lane = lax.broadcasted_iota(jnp.int32, (8, COLS), 1)
    low = (sub % BINS) * SEGS
    here = ((lane >= low) & (lane < low + SEGS)) | (
        (lane >= low + USED // 2) & (lane < low + USED // 2 + SEGS)
    )
    one = jnp.broadcast_to(straight[:, None, :], shape)
    two = jnp.broadcast_to(swapped[:, None, :], shape)
    sel = lax.broadcasted_iota(jnp.int32, (SEL, COLS), 1) == USED
    for odd in (0, 1):
        pick = jnp.where(((sub < BINS) == (odd == 0))[None], one, two)
        pick = jnp.where(here[None], pick, 0.0)
        lhs[odd, :SEL, :] = sel.astype(jnp.float32).astype(jnp.bfloat16)
        lhs[odd, SEL:, :] = pick.reshape(WIDTH * 8, COLS).astype(jnp.bfloat16)
    mine = jnp.broadcast_to(1.0 / straight[:, USED : USED + 1], (WIDTH, 128))
    rci[...] = jnp.broadcast_to(mine[:, None, :], (WIDTH, 8, 128)).reshape(WIDTH * 8, 128)

    for copy in local:
        copy.wait()

    def share(half, index, to, send):
        remote(half.at[index], half.at[to], sibling, send, SHARED + send)

    def share_column(i):
        at = (x + 4 - i) % 4
        share(gl, (rest, every, at), (pl.ds(5 + c, 3), every, at), 3)

    rest = pl.ds(2, 3)

    def x_copies(blocks, send, recv):
        column = gl.at[blocks, :, x]
        return {i: remote(column, column, along_x(i), send, recv + i) for i in steps}

    taken = {e: jnp.where((z + 4 - e) % 4 > z, 1, 0) for e in (3, 2, 1)}

    def share_row(rel):
        @pl.when(c == 1)
        def _():
            row = across if rel else ylo
            share(gh, (0, row), (5, row), 2)

    settle(gh.at[0, 0, pl.ds(0, 3)], rsem.at[0])
    for four_on, rel in y_steps:
        remote(gh.at[0, ylo], gh.at[four_on, ylo], along_y(four_on, rel), 4, 2 + 10 * four_on)
    share_row(0)
    settle(gl.at[0, 0, pl.ds(0, 3)], rsem.at[1])
    for e in taken:
        remote(gl.at[taken[e], :, x], gl.at[1 + e, :, x], along_z(-e), 5, 3)
    z_copies = {
        e: plan(gh.at[taken[e]], gh.at[1 + e], along_z(-e), 7, 12 + e) for e in taken
    }

    settle(gh.at[0, 0], rsem.at[2])
    for e in taken:
        pl.when(taken[e] == 0)(z_copies[e].start)
    share_row(1)
    near = x_copies(pl.ds(0, 2), 6, 4)
    settle(gh.at[0], rsem.at[12])
    for e in taken:
        pl.when(taken[e] == 1)(z_copies[e].start)
    pl.when(c == 0)(lambda: share(gh, 1, 8, 2))
    settle(gl.at[0, pl.ds(0, 2), pl.ds(0, 3)], rsem.at[3])
    share_column(0)
    beyond = x_copies(rest, 8, 8)
    for i in steps:
        near[i].wait_recv()
    share(gl, 1 - c, 8 - 3 * c, 3)

    for n in (0, 1):
        one_hop(gl, gh, n, lhs, rci, ready.at[n])

    for e in (1, 2, 3):
        z_copies[e].wait_recv()
        share(gh, 1 + e, 4 + e + c, 2)
    for i in steps:
        beyond[i].wait_recv()
        share_column(i)

    settle(gh.at[pl.ds(5, 4)], rsem.at[SHARED + 2])
    settle(gl.at[pl.ds(5, 4)], rsem.at[SHARED + 3])
    settle(gh.at[0, 0, pl.ds(0, 3)], ssem.at[0])
    settle(gl.at[0, 0, pl.ds(0, 3)], ssem.at[1])
    settle(gh.at[pl.ds(5, 4)], ssem.at[2])
    settle(gl.at[pl.ds(5, 4)], ssem.at[3])
    settle(gh.at[pl.ds(0, 3), 0], ssem.at[4])
    settle(gl.at[0, pl.ds(0, 2), pl.ds(0, 3)], ssem.at[5])
    settle(gl.at[pl.ds(0, 2), :, pl.ds(0, 3)], ssem.at[6])
    settle(gh.at[pl.ds(0, 3)], ssem.at[7])
    settle(gl.at[pl.ds(0, 3), :, pl.ds(0, 3)], ssem.at[8])


def stack_kernel(gl, gh, lhs, rci, ready, out, stage, sems):
    def to_out(src, k):
        return pltpu.make_async_copy(src, out.at[:, k], sems.at[k])

    early = [to_out(ready.at[n], 8 * n) for n in (0, 1)]
    for copy in early:
        copy.start()

    @pl.loop(1, HOPS - 1, unroll=True)
    def _(k):
        one_hop(gl, gh, jnp.where(k % 2 == 0, 1 + k // 2, 5 + k // 2), lhs, rci, stage.at[k - 1])
        to_out(stage.at[k - 1], k).start()

    for copy in early:
        copy.wait()

    @pl.loop(1, HOPS - 1)
    def _(k):
        to_out(stage.at[k - 1], k).wait()


def per_device(spectra, counts):
    spec = spectra.reshape(USED, WIDTH)
    vmem = pl.BlockSpec(memory_space=pltpu.VMEM)
    hbm = pl.BlockSpec(memory_space=pltpu.HBM)
    gl, gh, lhs, rci, ready = pl.pallas_call(
        gather_kernel,
        name="whiten_gather",
        out_shape=(
            jax.ShapeDtypeStruct((HOPS, 2, 4, HALF, COLS), jnp.bfloat16),
            jax.ShapeDtypeStruct((HOPS, 2, 4, HALF, COLS), jnp.bfloat16),
            jax.ShapeDtypeStruct((2, SEL + WIDTH * 8, COLS), jnp.bfloat16),
            jax.ShapeDtypeStruct((WIDTH * 8, 128), jnp.float32),
            jax.ShapeDtypeStruct((2, WIDTH, 2, 4 * BINS, 128), jnp.float32),
        ),
        in_specs=[hbm, hbm],
        out_specs=(vmem,) * 5,
        scratch_shapes=[
            pltpu.VMEM((USED, WIDTH), jnp.float32),
            pltpu.VMEM((1, WIDTH), jnp.int32),
            pltpu.VMEM((WIDTH, COLS), jnp.bfloat16),
            pltpu.SemaphoreType.DMA((9,)),
            pltpu.SemaphoreType.DMA((SHARED + 4,)),
            pltpu.SemaphoreType.DMA((4,)),
        ],
        compiler_params=pltpu.CompilerParams(
            collective_id=0, has_side_effects=True, vmem_limit_bytes=16 * 2**20
        ),
    )(*(pltpu.with_memory_space_constraint(a, pltpu.HBM) for a in (spec, counts)))
    out = pl.pallas_call(
        stack_kernel,
        name="stack",
        out_shape=jax.ShapeDtypeStruct((WIDTH, HOPS, 2, 4 * BINS, 128), jnp.float32),
        in_specs=[vmem] * 5,
        out_specs=hbm,
        scratch_shapes=[
            pltpu.VMEM((HOPS - 2, WIDTH, 2, 4 * BINS, 128), jnp.float32),
            pltpu.SemaphoreType.DMA((HOPS,)),
        ],
        compiler_params=pltpu.CompilerParams(vmem_limit_bytes=24 * 2**20),
        cost_estimate=pl.CostEstimate(
            flops=2 * (SEL + WIDTH * 8) * COLS * 512 * HOPS,
            bytes_accessed=HOPS * 512 * (COLS * 2 + WIDTH * 8 * 4),
            transcendentals=0,
        ),
    )(gl, gh, lhs, rci, ready)
    out = out.reshape(WIDTH, HOPS, 2, 4, BINS, 128).swapaxes(3, 4)
    return out.reshape(1, WIDTH, HOPS, 2, BINS, 512)


def solution(mesh):
    return jax.shard_map(
        per_device,
        mesh=mesh,
        in_specs=(P(None, None, None, "col", "row"), P("col", "row")),
        out_specs=P("col", "row", None, None, None, None),
        check_vma=False,
    )
```

```python
import functools

import jax
import jax.numpy as jnp
from jax import lax
from jax.experimental import pallas as pl
from jax.experimental.pallas import tpu as pltpu
from jax.sharding import PartitionSpec as P

MESH = pl.DeviceIdType.MESH
BINS = 4
SEGS = 30
USED = 2 * BINS * SEGS
COLS = 256
WIDTH = 64
HALF = 32
SHARED = 14
HOPS = 9
SEL = 16


def one_hop(gl, gh, held, lhs, rci, to):
    mine = rci[...]

    def tiles(odd):
        pieces = [(held, n, at) for n in (0, 1) for at in (2 * odd, 2 * odd + 1)]
        right = [half[piece] for piece in pieces for half in (gl, gh)]
        result = lax.dot_general(
            lhs[odd],
            jnp.concatenate(right, axis=0),
            (((1,), (1,)), ((), ())),
            preferred_element_type=jnp.float32,
        )
        recip = 1.0 / result[0:1]
        halves = (slice(0, 128), slice(128, 256))
        return [
            (result[SEL:, lanes] * jnp.maximum(mine, recip[:, lanes])).reshape(WIDTH, 8, 128)
            for lanes in halves
        ]

    lower = lax.broadcasted_iota(jnp.int32, (WIDTH, 8, 128), 1) < BINS
    for n, (even, odd) in enumerate(zip(tiles(0), tiles(1))):
        rows = pl.ds(8 * n, 8)
        to[:, 0, rows] = jnp.where(lower, even, odd)
        to[:, 1, rows] = pltpu.roll(jnp.where(lower, odd, even), BINS, 1)


def gather_kernel(spec_in, cnt_in, gl, gh, lhs, rci, ready, spec, cnt, own, ssem, rsem, lsem):
    fetch = (
        pltpu.make_async_copy(spec_in, spec, lsem.at[1]),
        pltpu.make_async_copy(cnt_in, cnt, lsem.at[2]),
    )
    for copy in fetch:
        copy.start()
    r, d = lax.axis_index("row"), lax.axis_index("col")
    x, ylo = r % 4, r // 4
    c, q = d % 2, d // 2
    z, yhi = q % 4, q // 4

    def dev(x_, ylo_, q_, c_):
        return (ylo_ * 4 + x_, q_ * 2 + c_)

    sibling = dev(x, ylo, q, 1 - c)
    across = 1 - ylo

    steps = (2, 1, 3)
    y_steps = ((0, 1), (1, 1), (1, 0))

    def along_x(i):
        return dev((x + i) % 4, ylo, q, c)

    def along_y(four_on, rel):
        return dev(x, across if rel else ylo, (q + 4 * four_on) % 8, c)

    def along_z(e):
        return dev(x, ylo, yhi * 4 + (z + e) % 4, c)

    barrier = pltpu.get_barrier_semaphore()
    sources = [along_x(i) for i in steps] + [along_y(*at) for at in y_steps]
    sources += [along_z(e) for e in steps] + [sibling]
    for source in sources:
        pl.semaphore_signal(barrier, inc=1, device_id=source, device_id_type=MESH)

    for copy in fetch:
        copy.wait()
    raw = spec[...]
    power = jnp.sum(raw * raw, axis=0, keepdims=True) / float(USED)
    row = lax.broadcasted_iota(jnp.int32, (USED, WIDTH), 0)
    group = jnp.zeros((USED, WIDTH), jnp.int32)
    for n in range(1, 2 * BINS):
        group = group + (row >= n * SEGS).astype(jnp.int32)
    valid = (row - SEGS * group < cnt[...]).astype(jnp.float32)
    white = raw * lax.rsqrt(power + 1e-6) * valid
    white = white.astype(jnp.bfloat16).astype(jnp.float32)
    count = cnt[...].astype(jnp.float32)
    pad = jnp.zeros((COLS - USED - 8, WIDTH), jnp.float32)
    first = lax.broadcasted_iota(jnp.int32, (8, WIDTH), 0) == 0
    tail = jnp.where(first, count, 0.0)
    straight = jnp.concatenate([white, tail, pad], axis=0).T
    own[...] = straight.astype(jnp.bfloat16)

    def plan(src, dst, device, send, recv):
        return pltpu.make_async_remote_copy(
            src_ref=src,
            dst_ref=dst,
            send_sem=ssem.at[send],
            recv_sem=rsem.at[recv],
            device_id=device,
            device_id_type=MESH,
        )

    def remote(src, dst, device, send, recv):
        copy = plan(src, dst, device, send, recv)
        copy.start()
        return copy

    def settle(region, sem):
        pltpu.make_async_copy(region, region, sem).wait()

    every = slice(None)
    own_lo, own_hi = own.at[pl.ds(0, HALF)], own.at[pl.ds(HALF, HALF)]
    pl.semaphore_wait(barrier, len(sources))
    for i in steps:
        remote(own_hi, gh.at[0, ylo, x], along_x(i), 0, 0)
    for four_on, rel in y_steps:
        remote(own_lo, gl.at[four_on, ylo, x], along_y(four_on, rel), 1, 1)
    local = [
        pltpu.make_async_copy(own_lo, gl.at[0, ylo, x], lsem.at[0]),
        pltpu.make_async_copy(own_hi, gh.at[0, ylo, x], lsem.at[3]),
    ]
    for copy in local:
        copy.start()

    swapped = jnp.concatenate(
        [white[USED // 2 :], -white[: USED // 2], jnp.zeros((COLS - USED, WIDTH), jnp.float32)],
        axis=0,
    ).T
    shape = (WIDTH, 8, COLS)
    sub = lax.broadcasted_iota(jnp.int32, (8, COLS), 0)
    lane = lax.broadcasted_iota(jnp.int32, (8, COLS), 1)
    low = (sub % BINS) * SEGS
    here = ((lane >= low) & (lane < low + SEGS)) | (
        (lane >= low + USED // 2) & (lane < low + USED // 2 + SEGS)
    )
    one = jnp.broadcast_to(straight[:, None, :], shape)
    two = jnp.broadcast_to(swapped[:, None, :], shape)
    sel = lax.broadcasted_iota(jnp.int32, (SEL, COLS), 1) == USED
    for odd in (0, 1):
        pick = jnp.where(((sub < BINS) == (odd == 0))[None], one, two)
        pick = jnp.where(here[None], pick, 0.0)
        lhs[odd, :SEL, :] = sel.astype(jnp.float32).astype(jnp.bfloat16)
        lhs[odd, SEL:, :] = pick.reshape(WIDTH * 8, COLS).astype(jnp.bfloat16)
    mine = jnp.broadcast_to(1.0 / straight[:, USED : USED + 1], (WIDTH, 128))
    rci[...] = jnp.broadcast_to(mine[:, None, :], (WIDTH, 8, 128)).reshape(WIDTH * 8, 128)

    for copy in local:
        copy.wait()

    def share(half, index, to, send):
        remote(half.at[index], half.at[to], sibling, send, SHARED + send)

    def share_column(i):
        at = (x + 4 - i) % 4
        share(gl, (rest, every, at), (pl.ds(5 + c, 3), every, at), 3)

    rest = pl.ds(2, 3)

    def x_copies(blocks, send, recv):
        column = gl.at[blocks, :, x]
        return {i: remote(column, column, along_x(i), send, recv + i) for i in (1, 3)}

    def x_forward(blocks, copies, send, recv):
        copies[1].wait_recv()
        piece = gl.at[blocks, 0, (x + 3) % 4]
        to_right = remote(piece, piece, along_x(1), send, recv)
        copies[3].wait_recv()
        piece = gl.at[blocks, 1, (x + 1) % 4]
        return to_right, remote(piece, piece, along_x(3), send, recv + 2)

    taken = {e: jnp.where((z + 4 - e) % 4 > z, 1, 0) for e in (3, 2, 1)}

    def share_row(rel):
        @pl.when(c == 1)
        def _():
            row = across if rel else ylo
            share(gh, (0, row), (5, row), 2)

    settle(gh.at[0, 0, pl.ds(0, 3)], rsem.at[0])
    for four_on, rel in y_steps:
        remote(gh.at[0, ylo], gh.at[four_on, ylo], along_y(four_on, rel), 4, 2 + 10 * four_on)
    share_row(0)
    settle(gl.at[0, 0, pl.ds(0, 3)], rsem.at[1])
    for e in taken:
        remote(gl.at[taken[e], :, x], gl.at[1 + e, :, x], along_z(-e), 5, 3)
    z_copies = {
        e: plan(gh.at[taken[e]], gh.at[1 + e], along_z(-e), 10 if e == 2 else 7, 12 + e)
        for e in taken
    }
    relay = plan(gh.at[2], gh.at[3], along_z(-1), 9, 14)

    settle(gh.at[0, 0], rsem.at[2])
    for e in (3, 1):
        pl.when(taken[e] == 0)(z_copies[e].start)
    share_row(1)
    ends = pl.ds(0, 2)
    near = x_copies(ends, 6, 4)
    settle(gh.at[0], rsem.at[12])
    for e in (1, 3):
        pl.when(taken[e] == 1)(z_copies[e].start)
    pl.when(z == 1)(z_copies[2].start)
    pl.when(c == 0)(lambda: share(gh, 1, 8, 2))
    settle(gl.at[0, pl.ds(0, 2), pl.ds(0, 3)], rsem.at[3])
    share_column(0)
    beyond = x_copies(rest, 8, 8)
    near_two = x_forward(ends, near, 6, 4)

    def one_down():
        z_copies[1].wait_recv()
        pl.when(z != 0)(relay.start)
        share(gh, 2, 5 + c, 2)

    pl.when(z != 3)(one_down)
    for copy in near_two:
        copy.wait_recv()
    share(gl, 1 - c, 8 - 3 * c, 3)
    beyond_two = x_forward(rest, beyond, 8, 8)
    for i in (1, 3):
        share_column(i)
    pl.when(z == 3)(one_down)

    for n in (0, 1):
        one_hop(gl, gh, n, lhs, rci, ready.at[n])

    for e in (3, 2):
        z_copies[e].wait_recv()
        share(gh, 1 + e, 4 + e + c, 2)
    for copy in beyond_two:
        copy.wait_recv()
    share_column(2)

    settle(gh.at[pl.ds(5, 4)], rsem.at[SHARED + 2])
    settle(gl.at[pl.ds(5, 4)], rsem.at[SHARED + 3])
    settle(gh.at[0, 0, pl.ds(0, 3)], ssem.at[0])
    settle(gl.at[0, 0, pl.ds(0, 3)], ssem.at[1])
    settle(gh.at[pl.ds(5, 4)], ssem.at[2])
    settle(gl.at[pl.ds(5, 4)], ssem.at[3])
    settle(gh.at[pl.ds(0, 3), 0], ssem.at[4])
    settle(gl.at[0, pl.ds(0, 2), pl.ds(0, 3)], ssem.at[5])
    settle(gl.at[pl.ds(0, 2), :, pl.ds(0, 3)], ssem.at[6])
    settle(gh.at[pl.ds(0, 2)], ssem.at[7])
    pl.when(z != 0)(relay.wait_send)
    pl.when(z == 1)(z_copies[2].wait_send)
    settle(gl.at[pl.ds(0, 3), :, pl.ds(0, 3)], ssem.at[8])


def stack_kernel(gl, gh, lhs, rci, ready, out, stage, sems):
    def to_out(src, k):
        return pltpu.make_async_copy(src, out.at[:, k], sems.at[k])

    early = [to_out(ready.at[n], 8 * n) for n in (0, 1)]
    for copy in early:
        copy.start()

    @pl.loop(1, HOPS - 1, unroll=True)
    def _(k):
        one_hop(gl, gh, jnp.where(k % 2 == 0, 1 + k // 2, 5 + k // 2), lhs, rci, stage.at[k - 1])
        to_out(stage.at[k - 1], k).start()

    for copy in early:
        copy.wait()

    @pl.loop(1, HOPS - 1)
    def _(k):
        to_out(stage.at[k - 1], k).wait()


def per_device(spectra, counts):
    spec = spectra.reshape(USED, WIDTH)
    vmem = pl.BlockSpec(memory_space=pltpu.VMEM)
    hbm = pl.BlockSpec(memory_space=pltpu.HBM)
    gl, gh, lhs, rci, ready = pl.pallas_call(
        gather_kernel,
        name="whiten_gather",
        out_shape=(
            jax.ShapeDtypeStruct((HOPS, 2, 4, HALF, COLS), jnp.bfloat16),
            jax.ShapeDtypeStruct((HOPS, 2, 4, HALF, COLS), jnp.bfloat16),
            jax.ShapeDtypeStruct((2, SEL + WIDTH * 8, COLS), jnp.bfloat16),
            jax.ShapeDtypeStruct((WIDTH * 8, 128), jnp.float32),
            jax.ShapeDtypeStruct((2, WIDTH, 2, 4 * BINS, 128), jnp.float32),
        ),
        in_specs=[hbm, hbm],
        out_specs=(vmem,) * 5,
        scratch_shapes=[
            pltpu.VMEM((USED, WIDTH), jnp.float32),
            pltpu.VMEM((1, WIDTH), jnp.int32),
            pltpu.VMEM((WIDTH, COLS), jnp.bfloat16),
            pltpu.SemaphoreType.DMA((11,)),
            pltpu.SemaphoreType.DMA((SHARED + 4,)),
            pltpu.SemaphoreType.DMA((4,)),
        ],
        compiler_params=pltpu.CompilerParams(
            collective_id=0, has_side_effects=True, vmem_limit_bytes=16 * 2**20
        ),
    )(*(pltpu.with_memory_space_constraint(a, pltpu.HBM) for a in (spec, counts)))
    out = pl.pallas_call(
        stack_kernel,
        name="stack",
        out_shape=jax.ShapeDtypeStruct((WIDTH, HOPS, 2, 4 * BINS, 128), jnp.float32),
        in_specs=[vmem] * 5,
        out_specs=hbm,
        scratch_shapes=[
            pltpu.VMEM((HOPS - 2, WIDTH, 2, 4 * BINS, 128), jnp.float32),
            pltpu.SemaphoreType.DMA((HOPS,)),
        ],
        compiler_params=pltpu.CompilerParams(vmem_limit_bytes=24 * 2**20),
        cost_estimate=pl.CostEstimate(
            flops=2 * (SEL + WIDTH * 8) * COLS * 512 * HOPS,
            bytes_accessed=HOPS * 512 * (COLS * 2 + WIDTH * 8 * 4),
            transcendentals=0,
        ),
    )(gl, gh, lhs, rci, ready)
    out = out.reshape(WIDTH, HOPS, 2, 4, BINS, 128).swapaxes(3, 4)
    return out.reshape(1, WIDTH, HOPS, 2, BINS, 512)


def solution(mesh):
    return jax.shard_map(
        per_device,
        mesh=mesh,
        in_specs=(P(None, None, None, "col", "row"), P("col", "row")),
        out_specs=P("col", "row", None, None, None, None),
        check_vma=False,
    )
```

```python
import functools

import jax
import jax.numpy as jnp
from jax import lax
from jax.experimental import pallas as pl
from jax.experimental.pallas import tpu as pltpu
from jax.sharding import PartitionSpec as P

MESH = pl.DeviceIdType.MESH
BINS = 4
SEGS = 30
USED = 2 * BINS * SEGS
COLS = 256
WIDTH = 64
HALF = 32
SHARED = 14
HOPS = 9
SEL = 16


def one_hop(gl, gh, held, lhs, rci, to):
    mine = rci[...]

    def tiles(odd):
        pieces = [(held, n, at) for n in (0, 1) for at in (2 * odd, 2 * odd + 1)]
        right = [half[piece] for piece in pieces for half in (gl, gh)]
        result = lax.dot_general(
            lhs[odd],
            jnp.concatenate(right, axis=0),
            (((1,), (1,)), ((), ())),
            preferred_element_type=jnp.float32,
        )
        recip = 1.0 / result[0:1]
        halves = (slice(0, 128), slice(128, 256))
        return [
            (result[SEL:, lanes] * jnp.maximum(mine, recip[:, lanes])).reshape(WIDTH, 8, 128)
            for lanes in halves
        ]

    lower = lax.broadcasted_iota(jnp.int32, (WIDTH, 8, 128), 1) < BINS
    for n, (even, odd) in enumerate(zip(tiles(0), tiles(1))):
        rows = pl.ds(8 * n, 8)
        to[:, 0, rows] = jnp.where(lower, even, odd)
        to[:, 1, rows] = pltpu.roll(jnp.where(lower, odd, even), BINS, 1)


def gather_kernel(spec_in, cnt_in, gl, gh, lhs, rci, ready, spec, cnt, own, ssem, rsem, lsem):
    fetch = (
        pltpu.make_async_copy(spec_in, spec, lsem.at[1]),
        pltpu.make_async_copy(cnt_in, cnt, lsem.at[2]),
    )
    for copy in fetch:
        copy.start()
    r, d = lax.axis_index("row"), lax.axis_index("col")
    x, ylo = r % 4, r // 4
    c, q = d % 2, d // 2
    z, yhi = q % 4, q // 4

    def dev(x_, ylo_, q_, c_):
        return (ylo_ * 4 + x_, q_ * 2 + c_)

    sibling = dev(x, ylo, q, 1 - c)
    across = 1 - ylo

    steps = (2, 1, 3)
    y_steps = ((0, 1), (1, 1), (1, 0))

    def along_x(i, core=c):
        return dev((x + i) % 4, ylo, q, core)

    def along_y(four_on, rel):
        return dev(x, across if rel else ylo, (q + 4 * four_on) % 8, c)

    def along_z(e, core=c):
        return dev(x, ylo, yhi * 4 + (z + e) % 4, core)

    barrier = pltpu.get_barrier_semaphore()
    sources = [along_x(i) for i in steps] + [along_y(*at) for at in y_steps]
    sources += [along_z(e) for e in steps] + [sibling]

    def announce(*to):
        for source in to:
            pl.semaphore_signal(barrier, inc=1, device_id=source, device_id_type=MESH)

    announce(*sources)
    both_cores = z == 0

    @pl.when(both_cores)
    def _():
        announce(*(along(n, 1 - c) for n in steps for along in (along_x, along_z)))


    for copy in fetch:
        copy.wait()
    raw = spec[...]
    power = jnp.sum(raw * raw, axis=0, keepdims=True) / float(USED)
    row = lax.broadcasted_iota(jnp.int32, (USED, WIDTH), 0)
    group = jnp.zeros((USED, WIDTH), jnp.int32)
    for n in range(1, 2 * BINS):
        group = group + (row >= n * SEGS).astype(jnp.int32)
    valid = (row - SEGS * group < cnt[...]).astype(jnp.float32)
    white = raw * lax.rsqrt(power + 1e-6) * valid
    white = white.astype(jnp.bfloat16).astype(jnp.float32)
    count = cnt[...].astype(jnp.float32)
    pad = jnp.zeros((COLS - USED - 8, WIDTH), jnp.float32)
    first = lax.broadcasted_iota(jnp.int32, (8, WIDTH), 0) == 0
    tail = jnp.where(first, count, 0.0)
    straight = jnp.concatenate([white, tail, pad], axis=0).T
    own[...] = straight.astype(jnp.bfloat16)

    def plan(src, dst, device, send, recv):
        return pltpu.make_async_remote_copy(
            src_ref=src,
            dst_ref=dst,
            send_sem=ssem.at[send],
            recv_sem=rsem.at[recv],
            device_id=device,
            device_id_type=MESH,
        )

    def remote(src, dst, device, send, recv):
        copy = plan(src, dst, device, send, recv)
        copy.start()
        return copy

    def settle(region, sem):
        pltpu.make_async_copy(region, region, sem).wait()

    every = slice(None)
    own_lo, own_hi = own.at[pl.ds(0, HALF)], own.at[pl.ds(HALF, HALF)]
    pl.semaphore_wait(barrier, len(sources) + jnp.where(both_cores, 3, 1))
    for i in steps:
        remote(own_hi, gh.at[0, ylo, x], along_x(i), 0, 0)
    for four_on, rel in y_steps:
        remote(own_lo, gl.at[four_on, ylo, x], along_y(four_on, rel), 1, 1)
    local = [
        pltpu.make_async_copy(own_lo, gl.at[0, ylo, x], lsem.at[0]),
        pltpu.make_async_copy(own_hi, gh.at[0, ylo, x], lsem.at[3]),
    ]
    for copy in local:
        copy.start()

    swapped = jnp.concatenate(
        [white[USED // 2 :], -white[: USED // 2], jnp.zeros((COLS - USED, WIDTH), jnp.float32)],
        axis=0,
    ).T
    shape = (WIDTH, 8, COLS)
    sub = lax.broadcasted_iota(jnp.int32, (8, COLS), 0)
    lane = lax.broadcasted_iota(jnp.int32, (8, COLS), 1)
    low = (sub % BINS) * SEGS
    here = ((lane >= low) & (lane < low + SEGS)) | (
        (lane >= low + USED // 2) & (lane < low + USED // 2 + SEGS)
    )
    one = jnp.broadcast_to(straight[:, None, :], shape)
    two = jnp.broadcast_to(swapped[:, None, :], shape)
    sel = lax.broadcasted_iota(jnp.int32, (SEL, COLS), 1) == USED
    for odd in (0, 1):
        pick = jnp.where(((sub < BINS) == (odd == 0))[None], one, two)
        pick = jnp.where(here[None], pick, 0.0)
        lhs[odd, :SEL, :] = sel.astype(jnp.float32).astype(jnp.bfloat16)
        lhs[odd, SEL:, :] = pick.reshape(WIDTH * 8, COLS).astype(jnp.bfloat16)
    mine = jnp.broadcast_to(1.0 / straight[:, USED : USED + 1], (WIDTH, 128))
    rci[...] = jnp.broadcast_to(mine[:, None, :], (WIDTH, 8, 128)).reshape(WIDTH * 8, 128)

    for copy in local:
        copy.wait()

    def share(half, index, to, send):
        remote(half.at[index], half.at[to], sibling, send, SHARED + send)

    def share_column(i):
        at = (x + 4 - i) % 4
        share(gl, (rest, every, at), (pl.ds(5 + c, 3), every, at), 3)

    rest = pl.ds(2, 3)

    def x_copies(blocks, send, recv):
        column = gl.at[blocks, :, x]
        return {i: remote(column, column, along_x(i), send, recv + i) for i in steps}

    taken = {e: jnp.where((z + 4 - e) % 4 > z, 1, 0) for e in (3, 2, 1)}

    def share_row(rel):
        @pl.when(c == 1)
        def _():
            row = across if rel else ylo
            share(gh, (0, row), (5, row), 2)

    settle(gh.at[0, 0, pl.ds(0, 3)], rsem.at[0])
    for four_on, rel in y_steps:
        remote(gh.at[0, ylo], gh.at[four_on, ylo], along_y(four_on, rel), 4, 2 + 10 * four_on)
    share_row(0)
    settle(gl.at[0, 0, pl.ds(0, 3)], rsem.at[1])
    for e in taken:
        remote(gl.at[taken[e], :, x], gl.at[1 + e, :, x], along_z(-e), 5, 3)
    z_copies = {
        e: plan(gh.at[taken[e]], gh.at[1 + e], along_z(-e), 7, 12 + e) for e in taken
    }

    settle(gh.at[0, 0], rsem.at[2])
    for e in taken:
        pl.when(taken[e] == 0)(z_copies[e].start)

    @pl.when(z != 0)
    def _():
        remote(gh.at[0], gh.at[4 + z + c], along_z(-z, 1 - c), 9, SHARED + 2)

    share_row(1)
    near = x_copies(pl.ds(0, 2), 6, 4)
    settle(gh.at[0], rsem.at[12])
    for e in taken:
        pl.when(taken[e] == 1)(z_copies[e].start)
    pl.when(c == 0)(lambda: share(gh, 1, 8, 2))
    settle(gl.at[0, pl.ds(0, 2), pl.ds(0, 3)], rsem.at[3])
    share_column(0)
    beyond = x_copies(rest, 8, 8)

    @pl.when(both_cores)
    def _():
        for i in steps:
            to = gl.at[pl.ds(5 + c, 3), :, x]
            remote(gl.at[rest, :, x], to, along_x(i, 1 - c), 10, SHARED + 3)

    for i in steps:
        near[i].wait_recv()
    share(gl, 1 - c, 8 - 3 * c, 3)

    for n in (0, 1):
        one_hop(gl, gh, n, lhs, rci, ready.at[n])

    for e in (1, 2, 3):
        z_copies[e].wait_recv()
        pl.when(z != 0)(functools.partial(share, gh, 1 + e, 4 + e + c, 2))
    for i in steps:
        beyond[i].wait_recv()
        pl.when(z != 0)(functools.partial(share_column, i))

    settle(gh.at[pl.ds(5, 4)], rsem.at[SHARED + 2])
    settle(gl.at[pl.ds(5, 4)], rsem.at[SHARED + 3])
    settle(gh.at[0, 0, pl.ds(0, 3)], ssem.at[0])
    settle(gl.at[0, 0, pl.ds(0, 3)], ssem.at[1])

    @pl.when(both_cores)
    def _():
        settle(gh.at[5], ssem.at[2])
        settle(gl.at[pl.ds(0, 7), :, 0], ssem.at[3])
        settle(gl.at[pl.ds(0, 3), :, pl.ds(0, 3)], ssem.at[10])

    @pl.when(z != 0)
    def _():
        settle(gh.at[pl.ds(5, 4)], ssem.at[2])
        settle(gl.at[pl.ds(5, 4)], ssem.at[3])
        settle(gh.at[0], ssem.at[9])

    settle(gh.at[pl.ds(0, 3), 0], ssem.at[4])
    settle(gl.at[0, pl.ds(0, 2), pl.ds(0, 3)], ssem.at[5])
    settle(gl.at[pl.ds(0, 2), :, pl.ds(0, 3)], ssem.at[6])
    settle(gh.at[pl.ds(0, 3)], ssem.at[7])
    settle(gl.at[pl.ds(0, 3), :, pl.ds(0, 3)], ssem.at[8])


def stack_kernel(gl, gh, lhs, rci, ready, out, stage, sems):
    def to_out(src, k):
        return pltpu.make_async_copy(src, out.at[:, k], sems.at[k])

    early = [to_out(ready.at[n], 8 * n) for n in (0, 1)]
    for copy in early:
        copy.start()

    @pl.loop(1, HOPS - 1, unroll=True)
    def _(k):
        one_hop(gl, gh, jnp.where(k % 2 == 0, 1 + k // 2, 5 + k // 2), lhs, rci, stage.at[k - 1])
        to_out(stage.at[k - 1], k).start()

    for copy in early:
        copy.wait()

    @pl.loop(1, HOPS - 1)
    def _(k):
        to_out(stage.at[k - 1], k).wait()


def per_device(spectra, counts):
    spec = spectra.reshape(USED, WIDTH)
    vmem = pl.BlockSpec(memory_space=pltpu.VMEM)
    hbm = pl.BlockSpec(memory_space=pltpu.HBM)
    gl, gh, lhs, rci, ready = pl.pallas_call(
        gather_kernel,
        name="whiten_gather",
        out_shape=(
            jax.ShapeDtypeStruct((HOPS, 2, 4, HALF, COLS), jnp.bfloat16),
            jax.ShapeDtypeStruct((HOPS, 2, 4, HALF, COLS), jnp.bfloat16),
            jax.ShapeDtypeStruct((2, SEL + WIDTH * 8, COLS), jnp.bfloat16),
            jax.ShapeDtypeStruct((WIDTH * 8, 128), jnp.float32),
            jax.ShapeDtypeStruct((2, WIDTH, 2, 4 * BINS, 128), jnp.float32),
        ),
        in_specs=[hbm, hbm],
        out_specs=(vmem,) * 5,
        scratch_shapes=[
            pltpu.VMEM((USED, WIDTH), jnp.float32),
            pltpu.VMEM((1, WIDTH), jnp.int32),
            pltpu.VMEM((WIDTH, COLS), jnp.bfloat16),
            pltpu.SemaphoreType.DMA((11,)),
            pltpu.SemaphoreType.DMA((SHARED + 4,)),
            pltpu.SemaphoreType.DMA((4,)),
        ],
        compiler_params=pltpu.CompilerParams(
            collective_id=0, has_side_effects=True, vmem_limit_bytes=16 * 2**20
        ),
    )(*(pltpu.with_memory_space_constraint(a, pltpu.HBM) for a in (spec, counts)))
    out = pl.pallas_call(
        stack_kernel,
        name="stack",
        out_shape=jax.ShapeDtypeStruct((WIDTH, HOPS, 2, 4 * BINS, 128), jnp.float32),
        in_specs=[vmem] * 5,
        out_specs=hbm,
        scratch_shapes=[
            pltpu.VMEM((HOPS - 2, WIDTH, 2, 4 * BINS, 128), jnp.float32),
            pltpu.SemaphoreType.DMA((HOPS,)),
        ],
        compiler_params=pltpu.CompilerParams(vmem_limit_bytes=24 * 2**20),
        cost_estimate=pl.CostEstimate(
            flops=2 * (SEL + WIDTH * 8) * COLS * 512 * HOPS,
            bytes_accessed=HOPS * 512 * (COLS * 2 + WIDTH * 8 * 4),
            transcendentals=0,
        ),
    )(gl, gh, lhs, rci, ready)
    out = out.reshape(WIDTH, HOPS, 2, 4, BINS, 128).swapaxes(3, 4)
    return out.reshape(1, WIDTH, HOPS, 2, BINS, 512)


def solution(mesh):
    return jax.shard_map(
        per_device,
        mesh=mesh,
        in_specs=(P(None, None, None, "col", "row"), P("col", "row")),
        out_specs=P("col", "row", None, None, None, None),
        check_vma=False,
    )
```

```python
import functools

import jax
import jax.numpy as jnp
from jax import lax
from jax.experimental import pallas as pl
from jax.experimental.pallas import tpu as pltpu
from jax.sharding import PartitionSpec as P

MESH = pl.DeviceIdType.MESH
BINS = 4
SEGS = 30
USED = 2 * BINS * SEGS
COLS = 256
WIDTH = 64
HALF = 32
SHARED = 14
HOPS = 9
SEL = 16


def one_hop(gl, gh, held, lhs, rci, to):
    mine = rci[...]

    def tiles(odd):
        pieces = [(held, n, at) for n in (0, 1) for at in (2 * odd, 2 * odd + 1)]
        right = [half[piece] for piece in pieces for half in (gl, gh)]
        result = lax.dot_general(
            lhs[odd],
            jnp.concatenate(right, axis=0),
            (((1,), (1,)), ((), ())),
            preferred_element_type=jnp.float32,
        )
        recip = 1.0 / result[0:1]
        halves = (slice(0, 128), slice(128, 256))
        return [
            (result[SEL:, lanes] * jnp.maximum(mine, recip[:, lanes])).reshape(WIDTH, 8, 128)
            for lanes in halves
        ]

    lower = lax.broadcasted_iota(jnp.int32, (WIDTH, 8, 128), 1) < BINS
    for n, (even, odd) in enumerate(zip(tiles(0), tiles(1))):
        rows = pl.ds(8 * n, 8)
        to[:, 0, rows] = jnp.where(lower, even, odd)
        to[:, 1, rows] = pltpu.roll(jnp.where(lower, odd, even), BINS, 1)


def gather_kernel(spec_in, cnt_in, gl, gh, lhs, rci, ready, spec, cnt, own, ssem, rsem, lsem):
    fetch = (
        pltpu.make_async_copy(spec_in, spec, lsem.at[1]),
        pltpu.make_async_copy(cnt_in, cnt, lsem.at[2]),
    )
    for copy in fetch:
        copy.start()
    r, d = lax.axis_index("row"), lax.axis_index("col")
    ylo = jnp.where(r >= 4, 1, 0)
    x = r - 4 * ylo
    yhi = jnp.where(d >= 8, 1, 0)
    rest_of_d = d - 8 * yhi
    z = sum(jnp.where(rest_of_d >= n, 1, 0) for n in (2, 4, 6))
    c = rest_of_d - 2 * z

    def wrap(n):
        return jnp.where(n >= 4, n - 4, n)

    def dev(x_, ylo_, yhi_, z_, c_):
        return (ylo_ * 4 + x_, yhi_ * 8 + z_ * 2 + c_)

    sibling = dev(x, ylo, yhi, z, 1 - c)
    across = 1 - ylo

    steps = (2, 1, 3)
    y_steps = ((0, 1), (1, 1), (1, 0))

    x_at = {i: wrap(x + i) for i in (1, 2, 3)}
    x_at[0] = x
    x_dev = {i: dev(x_at[i], ylo, yhi, z, c) for i in steps}
    z_dev = {e: dev(x, ylo, yhi, wrap(z + e), c) for e in steps}
    y_dev = {at: dev(x, across if at[1] else ylo, 1 - yhi if at[0] else yhi, z, c) for at in y_steps}

    def along_x(i):
        return x_dev[i]

    def along_y(*at):
        return y_dev[at]

    def along_z(e):
        return z_dev[e % 4]

    barrier = pltpu.get_barrier_semaphore()
    sources = [along_x(i) for i in steps] + [along_y(*at) for at in y_steps]
    sources += [along_z(e) for e in steps] + [sibling]
    for source in sources:
        pl.semaphore_signal(barrier, inc=1, device_id=source, device_id_type=MESH)

    for copy in fetch:
        copy.wait()
    raw = spec[...]
    power = jnp.sum(raw * raw, axis=0, keepdims=True) / float(USED)
    row = lax.broadcasted_iota(jnp.int32, (USED, WIDTH), 0)
    group = jnp.zeros((USED, WIDTH), jnp.int32)
    for n in range(1, 2 * BINS):
        group = group + (row >= n * SEGS).astype(jnp.int32)
    valid = (row - SEGS * group < cnt[...]).astype(jnp.float32)
    white = raw * lax.rsqrt(power + 1e-6) * valid
    white = white.astype(jnp.bfloat16).astype(jnp.float32)
    count = cnt[...].astype(jnp.float32)
    pad = jnp.zeros((COLS - USED - 8, WIDTH), jnp.float32)
    first = lax.broadcasted_iota(jnp.int32, (8, WIDTH), 0) == 0
    tail = jnp.where(first, count, 0.0)
    straight = jnp.concatenate([white, tail, pad], axis=0).T
    own[...] = straight.astype(jnp.bfloat16)

    def plan(src, dst, device, send, recv):
        return pltpu.make_async_remote_copy(
            src_ref=src,
            dst_ref=dst,
            send_sem=ssem.at[send],
            recv_sem=rsem.at[recv],
            device_id=device,
            device_id_type=MESH,
        )

    def remote(src, dst, device, send, recv):
        copy = plan(src, dst, device, send, recv)
        copy.start()
        return copy

    def settle(region, sem):
        pltpu.make_async_copy(region, region, sem).wait()

    every = slice(None)
    own_lo, own_hi = own.at[pl.ds(0, HALF)], own.at[pl.ds(HALF, HALF)]
    pl.semaphore_wait(barrier, len(sources))
    for i in steps:
        remote(own_hi, gh.at[0, ylo, x], along_x(i), 0, 0)
    for four_on, rel in y_steps:
        remote(own_lo, gl.at[four_on, ylo, x], along_y(four_on, rel), 1, 1)
    local = [
        pltpu.make_async_copy(own_lo, gl.at[0, ylo, x], lsem.at[0]),
        pltpu.make_async_copy(own_hi, gh.at[0, ylo, x], lsem.at[3]),
    ]
    for copy in local:
        copy.start()

    swapped = jnp.concatenate(
        [white[USED // 2 :], -white[: USED // 2], jnp.zeros((COLS - USED, WIDTH), jnp.float32)],
        axis=0,
    ).T
    shape = (WIDTH, 8, COLS)
    sub = lax.broadcasted_iota(jnp.int32, (8, COLS), 0)
    lane = lax.broadcasted_iota(jnp.int32, (8, COLS), 1)
    low = (sub % BINS) * SEGS
    here = ((lane >= low) & (lane < low + SEGS)) | (
        (lane >= low + USED // 2) & (lane < low + USED // 2 + SEGS)
    )
    one = jnp.broadcast_to(straight[:, None, :], shape)
    two = jnp.broadcast_to(swapped[:, None, :], shape)
    sel = lax.broadcasted_iota(jnp.int32, (SEL, COLS), 1) == USED
    for odd in (0, 1):
        pick = jnp.where(((sub < BINS) == (odd == 0))[None], one, two)
        pick = jnp.where(here[None], pick, 0.0)
        lhs[odd, :SEL, :] = sel.astype(jnp.float32).astype(jnp.bfloat16)
        lhs[odd, SEL:, :] = pick.reshape(WIDTH * 8, COLS).astype(jnp.bfloat16)
    mine = jnp.broadcast_to(1.0 / straight[:, USED : USED + 1], (WIDTH, 128))
    rci[...] = jnp.broadcast_to(mine[:, None, :], (WIDTH, 8, 128)).reshape(WIDTH * 8, 128)

    for copy in local:
        copy.wait()

    def share(half, index, to, send):
        remote(half.at[index], half.at[to], sibling, send, SHARED + send)

    def share_end(half, send):
        share(half, 1 - c, 8 - 3 * c, send)

    def x_copies(blocks, send, recv):
        column = gl.at[blocks, :, x]
        return {i: remote(column, column, along_x(i), send, recv + i) for i in steps}

    taken = {e: jnp.where(z < e, 1, 0) for e in (3, 2, 1)}

    settle(gh.at[0, 0, pl.ds(0, 3)], rsem.at[0])
    for four_on, rel in y_steps:
        remote(gh.at[0, ylo], gh.at[four_on, ylo], along_y(four_on, rel), 4, 2 + 10 * four_on)
    settle(gl.at[0, 0, pl.ds(0, 3)], rsem.at[1])
    for e in taken:
        remote(gl.at[taken[e], :, x], gl.at[1 + e, :, x], along_z(-e), 5, 3)
    z_copies = {
        e: plan(gh.at[taken[e]], gh.at[1 + e], along_z(-e), 7, 12 + e) for e in taken
    }

    settle(gh.at[0, 0], rsem.at[2])
    for e in taken:
        pl.when(taken[e] == 0)(z_copies[e].start)
    near = x_copies(pl.ds(0, 2), 6, 4)
    settle(gh.at[0], rsem.at[12])
    for e in taken:
        pl.when(taken[e] == 1)(z_copies[e].start)
    share_end(gh, 2)
    settle(gl.at[0, pl.ds(0, 2), pl.ds(0, 3)], rsem.at[3])
    rest = pl.ds(2, 3)
    beyond = x_copies(rest, 8, 8)
    for i in steps:
        near[i].wait_recv()
    share_end(gl, 3)

    for n in (0, 1):
        one_hop(gl, gh, n, lhs, rci, ready.at[n])

    for e in taken:
        z_copies[e].wait_recv()
        share(gh, 1 + e, 4 + e + c, 2)
    for i in (0,) + steps:
        if i:
            beyond[i].wait_recv()
        at = x_at[-i % 4]
        share(gl, (rest, every, at), (pl.ds(5 + c, 3), every, at), 3)

    settle(gh.at[pl.ds(5, 4)], rsem.at[SHARED + 2])
    settle(gl.at[pl.ds(5, 4)], rsem.at[SHARED + 3])
    settle(gh.at[0, 0, pl.ds(0, 3)], ssem.at[0])
    settle(gl.at[0, 0, pl.ds(0, 3)], ssem.at[1])
    settle(gh.at[pl.ds(5, 4)], ssem.at[2])
    settle(gl.at[pl.ds(5, 4)], ssem.at[3])
    settle(gh.at[pl.ds(0, 3), 0], ssem.at[4])
    settle(gl.at[0, pl.ds(0, 2), pl.ds(0, 3)], ssem.at[5])
    settle(gl.at[pl.ds(0, 2), :, pl.ds(0, 3)], ssem.at[6])
    settle(gh.at[pl.ds(0, 3)], ssem.at[7])
    settle(gl.at[pl.ds(0, 3), :, pl.ds(0, 3)], ssem.at[8])


def stack_kernel(gl, gh, lhs, rci, ready, out, stage, sems):
    def to_out(src, k):
        return pltpu.make_async_copy(src, out.at[:, k], sems.at[k])

    early = [to_out(ready.at[n], 8 * n) for n in (0, 1)]
    for copy in early:
        copy.start()

    @pl.loop(1, HOPS - 1, unroll=True)
    def _(k):
        one_hop(gl, gh, jnp.where(k % 2 == 0, 1 + k // 2, 5 + k // 2), lhs, rci, stage.at[k - 1])
        to_out(stage.at[k - 1], k).start()

    for copy in early:
        copy.wait()

    @pl.loop(1, HOPS - 1)
    def _(k):
        to_out(stage.at[k - 1], k).wait()


def per_device(spectra, counts):
    spec = spectra.reshape(USED, WIDTH)
    vmem = pl.BlockSpec(memory_space=pltpu.VMEM)
    hbm = pl.BlockSpec(memory_space=pltpu.HBM)
    gl, gh, lhs, rci, ready = pl.pallas_call(
        gather_kernel,
        name="whiten_gather",
        out_shape=(
            jax.ShapeDtypeStruct((HOPS, 2, 4, HALF, COLS), jnp.bfloat16),
            jax.ShapeDtypeStruct((HOPS, 2, 4, HALF, COLS), jnp.bfloat16),
            jax.ShapeDtypeStruct((2, SEL + WIDTH * 8, COLS), jnp.bfloat16),
            jax.ShapeDtypeStruct((WIDTH * 8, 128), jnp.float32),
            jax.ShapeDtypeStruct((2, WIDTH, 2, 4 * BINS, 128), jnp.float32),
        ),
        in_specs=[hbm, hbm],
        out_specs=(vmem,) * 5,
        scratch_shapes=[
            pltpu.VMEM((USED, WIDTH), jnp.float32),
            pltpu.VMEM((1, WIDTH), jnp.int32),
            pltpu.VMEM((WIDTH, COLS), jnp.bfloat16),
            pltpu.SemaphoreType.DMA((9,)),
            pltpu.SemaphoreType.DMA((SHARED + 4,)),
            pltpu.SemaphoreType.DMA((4,)),
        ],
        compiler_params=pltpu.CompilerParams(
            collective_id=0, has_side_effects=True, vmem_limit_bytes=16 * 2**20
        ),
    )(*(pltpu.with_memory_space_constraint(a, pltpu.HBM) for a in (spec, counts)))
    out = pl.pallas_call(
        stack_kernel,
        name="stack",
        out_shape=jax.ShapeDtypeStruct((WIDTH, HOPS, 2, 4 * BINS, 128), jnp.float32),
        in_specs=[vmem] * 5,
        out_specs=hbm,
        scratch_shapes=[
            pltpu.VMEM((HOPS - 2, WIDTH, 2, 4 * BINS, 128), jnp.float32),
            pltpu.SemaphoreType.DMA((HOPS,)),
        ],
        compiler_params=pltpu.CompilerParams(vmem_limit_bytes=24 * 2**20),
        cost_estimate=pl.CostEstimate(
            flops=2 * (SEL + WIDTH * 8) * COLS * 512 * HOPS,
            bytes_accessed=HOPS * 512 * (COLS * 2 + WIDTH * 8 * 4),
            transcendentals=0,
        ),
    )(gl, gh, lhs, rci, ready)
    out = out.reshape(WIDTH, HOPS, 2, 4, BINS, 128).swapaxes(3, 4)
    return out.reshape(1, WIDTH, HOPS, 2, BINS, 512)


def solution(mesh):
    return jax.shard_map(
        per_device,
        mesh=mesh,
        in_specs=(P(None, None, None, "col", "row"), P("col", "row")),
        out_specs=P("col", "row", None, None, None, None),
        check_vma=False,
    )
```

```python
import functools

import jax
import jax.numpy as jnp
from jax import lax
from jax.experimental import pallas as pl
from jax.experimental.pallas import tpu as pltpu
from jax.sharding import PartitionSpec as P

MESH = pl.DeviceIdType.MESH
BINS = 4
SEGS = 30
USED = 2 * BINS * SEGS
COLS = 256
WIDTH = 64
HALF = 32
SHARED = 14
HOPS = 9
SEL = 16


def one_hop(gl, gh, held, lhs, rci, to):
    mine = rci[...]

    def tiles(odd):
        pieces = [(held, n, at) for n in (0, 1) for at in (2 * odd, 2 * odd + 1)]
        right = [half[piece] for piece in pieces for half in (gl, gh)]
        result = lax.dot_general(
            lhs[odd],
            jnp.concatenate(right, axis=0),
            (((1,), (1,)), ((), ())),
            preferred_element_type=jnp.float32,
        )
        recip = 1.0 / result[0:1]
        halves = (slice(0, 128), slice(128, 256))
        return [
            (result[SEL:, lanes] * jnp.maximum(mine, recip[:, lanes])).reshape(WIDTH, 8, 128)
            for lanes in halves
        ]

    lower = lax.broadcasted_iota(jnp.int32, (WIDTH, 8, 128), 1) < BINS
    for n, (even, odd) in enumerate(zip(tiles(0), tiles(1))):
        rows = pl.ds(8 * n, 8)
        to[:, 0, rows] = jnp.where(lower, even, odd)
        to[:, 1, rows] = pltpu.roll(jnp.where(lower, odd, even), BINS, 1)


def gather_kernel(spec_in, cnt_in, gl, gh, lhs, rci, ready, spec, cnt, own, ssem, rsem, lsem):
    fetch = (
        pltpu.make_async_copy(spec_in, spec, lsem.at[1]),
        pltpu.make_async_copy(cnt_in, cnt, lsem.at[2]),
    )
    for copy in fetch:
        copy.start()
    r, d = lax.axis_index("row"), lax.axis_index("col")
    ylo = jnp.where(r >= 4, 1, 0)
    x = r - 4 * ylo
    yhi = jnp.where(d >= 8, 1, 0)
    rest_of_d = d - 8 * yhi
    z = sum(jnp.where(rest_of_d >= n, 1, 0) for n in (2, 4, 6))
    c = rest_of_d - 2 * z

    def wrap(n):
        return jnp.where(n >= 4, n - 4, n)

    def dev(x_, ylo_, yhi_, z_, c_):
        return (ylo_ * 4 + x_, yhi_ * 8 + z_ * 2 + c_)

    sibling = dev(x, ylo, yhi, z, 1 - c)
    across = 1 - ylo

    steps = (2, 1, 3)
    y_steps = ((0, 1), (1, 1), (1, 0))

    x_at = {i: wrap(x + i) for i in (1, 2, 3)}
    x_at[0] = x
    x_dev = {i: dev(x_at[i], ylo, yhi, z, c) for i in steps}
    z_dev = {e: dev(x, ylo, yhi, wrap(z + e), c) for e in steps}
    y_dev = {at: dev(x, across if at[1] else ylo, 1 - yhi if at[0] else yhi, z, c) for at in y_steps}

    def along_x(i):
        return x_dev[i]

    def along_y(*at):
        return y_dev[at]

    def along_z(e):
        return z_dev[e % 4]

    barrier = pltpu.get_barrier_semaphore()
    sources = [along_x(i) for i in steps] + [along_y(*at) for at in y_steps]
    sources += [along_z(e) for e in steps] + [sibling]
    for source in sources:
        pl.semaphore_signal(barrier, inc=1, device_id=source, device_id_type=MESH)

    for copy in fetch:
        copy.wait()
    raw = spec[...]
    power = jnp.sum(raw * raw, axis=0, keepdims=True) / float(USED)
    row = lax.broadcasted_iota(jnp.int32, (USED, WIDTH), 0)
    group = jnp.zeros((USED, WIDTH), jnp.int32)
    for n in range(1, 2 * BINS):
        group = group + (row >= n * SEGS).astype(jnp.int32)
    valid = (row - SEGS * group < cnt[...]).astype(jnp.float32)
    white = raw * lax.rsqrt(power + 1e-6) * valid
    white = white.astype(jnp.bfloat16).astype(jnp.float32)
    count = cnt[...].astype(jnp.float32)
    pad = jnp.zeros((COLS - USED - 8, WIDTH), jnp.float32)
    first = lax.broadcasted_iota(jnp.int32, (8, WIDTH), 0) == 0
    tail = jnp.where(first, count, 0.0)
    straight = jnp.concatenate([white, tail, pad], axis=0).T
    own[...] = straight.astype(jnp.bfloat16)

    def plan(src, dst, device, send, recv):
        return pltpu.make_async_remote_copy(
            src_ref=src,
            dst_ref=dst,
            send_sem=ssem.at[send],
            recv_sem=rsem.at[recv],
            device_id=device,
            device_id_type=MESH,
        )

    def remote(src, dst, device, send, recv):
        copy = plan(src, dst, device, send, recv)
        copy.start()
        return copy

    def settle(region, sem):
        pltpu.make_async_copy(region, region, sem).wait()

    every = slice(None)
    own_lo, own_hi = own.at[pl.ds(0, HALF)], own.at[pl.ds(HALF, HALF)]
    pl.semaphore_wait(barrier, len(sources))
    for i in steps:
        remote(own_hi, gh.at[0, ylo, x], along_x(i), 0, 0)
    for four_on, rel in y_steps:
        remote(own_lo, gl.at[four_on, ylo, x], along_y(four_on, rel), 1, 1)
    local = [
        pltpu.make_async_copy(own_lo, gl.at[0, ylo, x], lsem.at[0]),
        pltpu.make_async_copy(own_hi, gh.at[0, ylo, x], lsem.at[3]),
    ]
    for copy in local:
        copy.start()

    swapped = jnp.concatenate(
        [white[USED // 2 :], -white[: USED // 2], jnp.zeros((COLS - USED, WIDTH), jnp.float32)],
        axis=0,
    ).T
    shape = (WIDTH, 8, COLS)
    sub = lax.broadcasted_iota(jnp.int32, (8, COLS), 0)
    lane = lax.broadcasted_iota(jnp.int32, (8, COLS), 1)
    low = (sub % BINS) * SEGS
    here = ((lane >= low) & (lane < low + SEGS)) | (
        (lane >= low + USED // 2) & (lane < low + USED // 2 + SEGS)
    )
    one = jnp.broadcast_to(straight[:, None, :], shape)
    two = jnp.broadcast_to(swapped[:, None, :], shape)
    sel = lax.broadcasted_iota(jnp.int32, (SEL, COLS), 1) == USED
    for odd in (0, 1):
        pick = jnp.where(((sub < BINS) == (odd == 0))[None], one, two)
        pick = jnp.where(here[None], pick, 0.0)
        lhs[odd, :SEL, :] = sel.astype(jnp.float32).astype(jnp.bfloat16)
        lhs[odd, SEL:, :] = pick.reshape(WIDTH * 8, COLS).astype(jnp.bfloat16)
    mine = jnp.broadcast_to(1.0 / straight[:, USED : USED + 1], (WIDTH, 128))
    rci[...] = jnp.broadcast_to(mine[:, None, :], (WIDTH, 8, 128)).reshape(WIDTH * 8, 128)

    for copy in local:
        copy.wait()

    def share(half, index, to, send):
        remote(half.at[index], half.at[to], sibling, send, SHARED + send)

    def share_end(half, send):
        share(half, 1 - c, 8 - 3 * c, send)

    def x_copies(blocks, send, recv):
        column = gl.at[blocks, :, x]
        return {i: remote(column, column, along_x(i), send, recv + i) for i in (1, 3)}

    def x_forward(blocks, row, copy, i, send, recv):
        copy.wait_recv()
        piece = gl.at[blocks, row, x_at[-i % 4]]
        return remote(piece, piece, along_x(i), send, recv)

    taken = {e: jnp.where(z < e, 1, 0) for e in (3, 2, 1)}

    settle(gh.at[0, 0, pl.ds(0, 3)], rsem.at[0])
    for four_on, rel in y_steps:
        remote(gh.at[0, ylo], gh.at[four_on, ylo], along_y(four_on, rel), 4, 2 + 10 * four_on)
    settle(gl.at[0, 0, pl.ds(0, 3)], rsem.at[1])
    for e in taken:
        remote(gl.at[taken[e], :, x], gl.at[1 + e, :, x], along_z(-e), 5, 3)
    ends, rest = pl.ds(0, 2), pl.ds(2, 3)
    near = x_copies(ends, 6, 4)
    z_copies = {
        e: plan(gh.at[taken[e]], gh.at[1 + e], along_z(-e), 7, 12 + e) for e in taken
    }

    settle(gh.at[0, 0], rsem.at[2])
    for e in taken:
        pl.when(taken[e] == 0)(z_copies[e].start)
    near_two = [
        x_forward(ends, 0, near[1], 1, 6, 4),
        x_forward(ends, 1, near[3], 3, 6, 6),
    ]
    settle(gh.at[0], rsem.at[12])
    for e in taken:
        pl.when(taken[e] == 1)(z_copies[e].start)
    share_end(gh, 2)
    settle(gl.at[0, pl.ds(0, 2), pl.ds(0, 3)], rsem.at[3])
    piece = gl.at[rest, 0, x]
    beyond_two = [remote(piece, piece, along_x(2), 8, 8)]
    beyond = x_copies(rest, 8, 8)
    for copy in near_two:
        copy.wait_recv()
    share_end(gl, 3)

    for n in (0, 1):
        one_hop(gl, gh, n, lhs, rci, ready.at[n])

    beyond_two.append(x_forward(rest, 1, beyond[3], 3, 8, 10))

    def share_column(i):
        at = x_at[-i % 4]
        share(gl, (rest, every, at), (pl.ds(5 + c, 3), every, at), 3)

    share_column(0)
    for e in taken:
        z_copies[e].wait_recv()
        share(gh, 1 + e, 4 + e + c, 2)
    share_column(3)
    beyond[1].wait_recv()
    share_column(1)
    for copy in beyond_two:
        copy.wait_recv()
    share_column(2)

    settle(gh.at[pl.ds(5, 4)], rsem.at[SHARED + 2])
    settle(gl.at[pl.ds(5, 4)], rsem.at[SHARED + 3])
    settle(gh.at[0, 0, pl.ds(0, 3)], ssem.at[0])
    settle(gl.at[0, 0, pl.ds(0, 3)], ssem.at[1])
    settle(gh.at[pl.ds(5, 4)], ssem.at[2])
    settle(gl.at[pl.ds(5, 4)], ssem.at[3])
    settle(gh.at[pl.ds(0, 3), 0], ssem.at[4])
    settle(gl.at[0, pl.ds(0, 2), pl.ds(0, 3)], ssem.at[5])
    settle(gl.at[pl.ds(0, 2), :, pl.ds(0, 3)], ssem.at[6])
    settle(gh.at[pl.ds(0, 3)], ssem.at[7])
    settle(gl.at[pl.ds(0, 3), :, pl.ds(0, 3)], ssem.at[8])


def stack_kernel(gl, gh, lhs, rci, ready, out, stage, sems):
    def to_out(src, k):
        return pltpu.make_async_copy(src, out.at[:, k], sems.at[k])

    early = [to_out(ready.at[n], 8 * n) for n in (0, 1)]
    for copy in early:
        copy.start()

    @pl.loop(1, HOPS - 1, unroll=True)
    def _(k):
        one_hop(gl, gh, jnp.where(k % 2 == 0, 1 + k // 2, 5 + k // 2), lhs, rci, stage.at[k - 1])
        to_out(stage.at[k - 1], k).start()

    for copy in early:
        copy.wait()

    @pl.loop(1, HOPS - 1)
    def _(k):
        to_out(stage.at[k - 1], k).wait()


def per_device(spectra, counts):
    spec = spectra.reshape(USED, WIDTH)
    vmem = pl.BlockSpec(memory_space=pltpu.VMEM)
    hbm = pl.BlockSpec(memory_space=pltpu.HBM)
    gl, gh, lhs, rci, ready = pl.pallas_call(
        gather_kernel,
        name="whiten_gather",
        out_shape=(
            jax.ShapeDtypeStruct((HOPS, 2, 4, HALF, COLS), jnp.bfloat16),
            jax.ShapeDtypeStruct((HOPS, 2, 4, HALF, COLS), jnp.bfloat16),
            jax.ShapeDtypeStruct((2, SEL + WIDTH * 8, COLS), jnp.bfloat16),
            jax.ShapeDtypeStruct((WIDTH * 8, 128), jnp.float32),
            jax.ShapeDtypeStruct((2, WIDTH, 2, 4 * BINS, 128), jnp.float32),
        ),
        in_specs=[hbm, hbm],
        out_specs=(vmem,) * 5,
        scratch_shapes=[
            pltpu.VMEM((USED, WIDTH), jnp.float32),
            pltpu.VMEM((1, WIDTH), jnp.int32),
            pltpu.VMEM((WIDTH, COLS), jnp.bfloat16),
            pltpu.SemaphoreType.DMA((9,)),
            pltpu.SemaphoreType.DMA((SHARED + 4,)),
            pltpu.SemaphoreType.DMA((4,)),
        ],
        compiler_params=pltpu.CompilerParams(
            collective_id=0, has_side_effects=True, vmem_limit_bytes=16 * 2**20
        ),
    )(*(pltpu.with_memory_space_constraint(a, pltpu.HBM) for a in (spec, counts)))
    out = pl.pallas_call(
        stack_kernel,
        name="stack",
        out_shape=jax.ShapeDtypeStruct((WIDTH, HOPS, 2, 4 * BINS, 128), jnp.float32),
        in_specs=[vmem] * 5,
        out_specs=hbm,
        scratch_shapes=[
            pltpu.VMEM((HOPS - 2, WIDTH, 2, 4 * BINS, 128), jnp.float32),
            pltpu.SemaphoreType.DMA((HOPS,)),
        ],
        compiler_params=pltpu.CompilerParams(vmem_limit_bytes=24 * 2**20),
        cost_estimate=pl.CostEstimate(
            flops=2 * (SEL + WIDTH * 8) * COLS * 512 * HOPS,
            bytes_accessed=HOPS * 512 * (COLS * 2 + WIDTH * 8 * 4),
            transcendentals=0,
        ),
    )(gl, gh, lhs, rci, ready)
    out = out.reshape(WIDTH, HOPS, 2, 4, BINS, 128).swapaxes(3, 4)
    return out.reshape(1, WIDTH, HOPS, 2, BINS, 512)


def solution(mesh):
    return jax.shard_map(
        per_device,
        mesh=mesh,
        in_specs=(P(None, None, None, "col", "row"), P("col", "row")),
        out_specs=P("col", "row", None, None, None, None),
        check_vma=False,
    )
```

```python
import functools

import jax
import jax.numpy as jnp
from jax import lax
from jax.experimental import pallas as pl
from jax.experimental.pallas import tpu as pltpu
from jax.sharding import PartitionSpec as P

MESH = pl.DeviceIdType.MESH
BINS = 4
SEGS = 30
USED = 2 * BINS * SEGS
COLS = 256
WIDTH = 64
HALF = 32
SHARED = 14
HOPS = 9
SEL = 16


def one_hop(gl, gh, held, lhs, rci, to):
    mine = rci[...]

    def tiles(odd):
        pieces = [(held, n, at) for n in (0, 1) for at in (2 * odd, 2 * odd + 1)]
        right = [half[piece] for piece in pieces for half in (gl, gh)]
        result = lax.dot_general(
            lhs[odd],
            jnp.concatenate(right, axis=0),
            (((1,), (1,)), ((), ())),
            preferred_element_type=jnp.float32,
        )
        recip = 1.0 / result[0:1]
        halves = (slice(0, 128), slice(128, 256))
        return [
            (result[SEL:, lanes] * jnp.maximum(mine, recip[:, lanes])).reshape(WIDTH, 8, 128)
            for lanes in halves
        ]

    lower = lax.broadcasted_iota(jnp.int32, (WIDTH, 8, 128), 1) < BINS
    for n, (even, odd) in enumerate(zip(tiles(0), tiles(1))):
        rows = pl.ds(8 * n, 8)
        to[:, 0, rows] = jnp.where(lower, even, odd)
        to[:, 1, rows] = pltpu.roll(jnp.where(lower, odd, even), BINS, 1)


def gather_kernel(spec_in, cnt_in, gl, gh, lhs, rci, ready, spec, cnt, own, ssem, rsem, lsem):
    fetch = (
        pltpu.make_async_copy(spec_in, spec, lsem.at[1]),
        pltpu.make_async_copy(cnt_in, cnt, lsem.at[2]),
    )
    for copy in fetch:
        copy.start()
    r, d = lax.axis_index("row"), lax.axis_index("col")
    ylo = jnp.where(r >= 4, 1, 0)
    x = r - 4 * ylo
    yhi = jnp.where(d >= 8, 1, 0)
    rest_of_d = d - 8 * yhi
    z = sum(jnp.where(rest_of_d >= n, 1, 0) for n in (2, 4, 6))
    c = rest_of_d - 2 * z

    def wrap(n):
        return jnp.where(n >= 4, n - 4, n)

    def dev(x_, ylo_, yhi_, z_, c_):
        return (ylo_ * 4 + x_, yhi_ * 8 + z_ * 2 + c_)

    sibling = dev(x, ylo, yhi, z, 1 - c)
    across = 1 - ylo

    steps = (2, 1, 3)
    y_steps = ((0, 1), (1, 1), (1, 0))

    x_at = {i: wrap(x + i) for i in (1, 2, 3)}
    x_at[0] = x
    x_dev = {i: dev(x_at[i], ylo, yhi, z, c) for i in steps}
    z_dev = {e: dev(x, ylo, yhi, wrap(z + e), c) for e in steps}
    y_dev = {at: dev(x, across if at[1] else ylo, 1 - yhi if at[0] else yhi, z, c) for at in y_steps}

    def along_x(i):
        return x_dev[i]

    def along_y(*at):
        return y_dev[at]

    def along_z(e):
        return z_dev[e % 4]

    barrier = pltpu.get_barrier_semaphore()
    sources = [along_x(i) for i in steps] + [along_y(*at) for at in y_steps]
    sources += [along_z(e) for e in steps] + [sibling]
    for source in sources:
        pl.semaphore_signal(barrier, inc=1, device_id=source, device_id_type=MESH)

    for copy in fetch:
        copy.wait()
    raw = spec[...]
    power = jnp.sum(raw * raw, axis=0, keepdims=True) / float(USED)
    row = lax.broadcasted_iota(jnp.int32, (USED, WIDTH), 0)
    group = jnp.zeros((USED, WIDTH), jnp.int32)
    for n in range(1, 2 * BINS):
        group = group + (row >= n * SEGS).astype(jnp.int32)
    valid = (row - SEGS * group < cnt[...]).astype(jnp.float32)
    white = raw * lax.rsqrt(power + 1e-6) * valid
    white = white.astype(jnp.bfloat16).astype(jnp.float32)
    count = cnt[...].astype(jnp.float32)
    pad = jnp.zeros((COLS - USED - 8, WIDTH), jnp.float32)
    first = lax.broadcasted_iota(jnp.int32, (8, WIDTH), 0) == 0
    tail = jnp.where(first, count, 0.0)
    straight = jnp.concatenate([white, tail, pad], axis=0).T
    own[...] = straight.astype(jnp.bfloat16)

    def plan(src, dst, device, send, recv):
        return pltpu.make_async_remote_copy(
            src_ref=src,
            dst_ref=dst,
            send_sem=ssem.at[send],
            recv_sem=rsem.at[recv],
            device_id=device,
            device_id_type=MESH,
        )

    def remote(src, dst, device, send, recv):
        copy = plan(src, dst, device, send, recv)
        copy.start()
        return copy

    def settle(region, sem):
        pltpu.make_async_copy(region, region, sem).wait()

    every = slice(None)
    own_lo, own_hi = own.at[pl.ds(0, HALF)], own.at[pl.ds(HALF, HALF)]
    pl.semaphore_wait(barrier, len(sources))
    for i in steps:
        remote(own_hi, gh.at[0, ylo, x], along_x(i), 0, 0)
    for four_on, rel in y_steps:
        remote(own_lo, gl.at[four_on, ylo, x], along_y(four_on, rel), 1, 1)
    local = [
        pltpu.make_async_copy(own_lo, gl.at[0, ylo, x], lsem.at[0]),
        pltpu.make_async_copy(own_hi, gh.at[0, ylo, x], lsem.at[3]),
    ]
    for copy in local:
        copy.start()

    swapped = jnp.concatenate(
        [white[USED // 2 :], -white[: USED // 2], jnp.zeros((COLS - USED, WIDTH), jnp.float32)],
        axis=0,
    ).T
    shape = (WIDTH, 8, COLS)
    sub = lax.broadcasted_iota(jnp.int32, (8, COLS), 0)
    lane = lax.broadcasted_iota(jnp.int32, (8, COLS), 1)
    low = (sub % BINS) * SEGS
    here = ((lane >= low) & (lane < low + SEGS)) | (
        (lane >= low + USED // 2) & (lane < low + USED // 2 + SEGS)
    )
    one = jnp.broadcast_to(straight[:, None, :], shape)
    two = jnp.broadcast_to(swapped[:, None, :], shape)
    sel = lax.broadcasted_iota(jnp.int32, (SEL, COLS), 1) == USED
    for odd in (0, 1):
        pick = jnp.where(((sub < BINS) == (odd == 0))[None], one, two)
        pick = jnp.where(here[None], pick, 0.0)
        lhs[odd, :SEL, :] = sel.astype(jnp.float32).astype(jnp.bfloat16)
        lhs[odd, SEL:, :] = pick.reshape(WIDTH * 8, COLS).astype(jnp.bfloat16)
    mine = jnp.broadcast_to(1.0 / straight[:, USED : USED + 1], (WIDTH, 128))
    rci[...] = jnp.broadcast_to(mine[:, None, :], (WIDTH, 8, 128)).reshape(WIDTH * 8, 128)

    for copy in local:
        copy.wait()

    def share(half, index, to, send):
        remote(half.at[index], half.at[to], sibling, send, SHARED + send)

    def share_end(half, send):
        share(half, 1 - c, 8 - 3 * c, send)

    def x_copies(blocks, send, recv):
        column = gl.at[blocks, :, x]
        return {i: remote(column, column, along_x(i), send, recv + i) for i in steps}

    taken = {e: jnp.where(z < e, 1, 0) for e in (3, 2, 1)}

    settle(gl.at[0, 0, pl.ds(0, 3)], rsem.at[1])
    for e in taken:
        remote(gl.at[taken[e], :, x], gl.at[1 + e, :, x], along_z(-e), 5, 3)
    settle(gh.at[0, 0, pl.ds(0, 3)], rsem.at[0])
    for four_on, rel in y_steps:
        remote(gh.at[0, ylo], gh.at[four_on, ylo], along_y(four_on, rel), 4, 2 + 10 * four_on)
    z_copies = {
        e: plan(gh.at[taken[e]], gh.at[1 + e], along_z(-e), 7, 12 + e) for e in taken
    }

    settle(gh.at[0, 0], rsem.at[2])
    for e in taken:
        pl.when(taken[e] == 0)(z_copies[e].start)
    near = x_copies(pl.ds(0, 2), 6, 4)
    settle(gh.at[0], rsem.at[12])
    for e in taken:
        pl.when(taken[e] == 1)(z_copies[e].start)
    share_end(gh, 2)
    settle(gl.at[0, pl.ds(0, 2), pl.ds(0, 3)], rsem.at[3])
    rest = pl.ds(2, 3)
    beyond = x_copies(rest, 8, 8)

    def share_column(i):
        at = x_at[-i % 4]
        share(gl, (rest, every, at), (pl.ds(5 + c, 3), every, at), 3)

    share_column(0)
    for i in steps:
        near[i].wait_recv()
    share_end(gl, 3)

    for n in (0, 1):
        one_hop(gl, gh, n, lhs, rci, ready.at[n])

    for e in (1, 2, 3):
        z_copies[e].wait_recv()
        share(gh, 1 + e, 4 + e + c, 2)
    for i in steps:
        beyond[i].wait_recv()
        share_column(i)

    settle(gh.at[pl.ds(5, 4)], rsem.at[SHARED + 2])
    settle(gl.at[pl.ds(5, 4)], rsem.at[SHARED + 3])
    settle(gh.at[0, 0, pl.ds(0, 3)], ssem.at[0])
    settle(gl.at[0, 0, pl.ds(0, 3)], ssem.at[1])
    settle(gh.at[pl.ds(5, 4)], ssem.at[2])
    settle(gl.at[pl.ds(5, 4)], ssem.at[3])
    settle(gh.at[pl.ds(0, 3), 0], ssem.at[4])
    settle(gl.at[0, pl.ds(0, 2), pl.ds(0, 3)], ssem.at[5])
    settle(gl.at[pl.ds(0, 2), :, pl.ds(0, 3)], ssem.at[6])
    settle(gh.at[pl.ds(0, 3)], ssem.at[7])
    settle(gl.at[pl.ds(0, 3), :, pl.ds(0, 3)], ssem.at[8])


def stack_kernel(gl, gh, lhs, rci, ready, out, stage, sems):
    def to_out(src, k):
        return pltpu.make_async_copy(src, out.at[:, k], sems.at[k])

    early = [to_out(ready.at[n], 8 * n) for n in (0, 1)]
    for copy in early:
        copy.start()

    @pl.loop(1, HOPS - 1, unroll=True)
    def _(k):
        one_hop(gl, gh, jnp.where(k % 2 == 0, 1 + k // 2, 5 + k // 2), lhs, rci, stage.at[k - 1])
        to_out(stage.at[k - 1], k).start()

    for copy in early:
        copy.wait()

    @pl.loop(1, HOPS - 1)
    def _(k):
        to_out(stage.at[k - 1], k).wait()


def per_device(spectra, counts):
    spec = spectra.reshape(USED, WIDTH)
    vmem = pl.BlockSpec(memory_space=pltpu.VMEM)
    hbm = pl.BlockSpec(memory_space=pltpu.HBM)
    gl, gh, lhs, rci, ready = pl.pallas_call(
        gather_kernel,
        name="whiten_gather",
        out_shape=(
            jax.ShapeDtypeStruct((HOPS, 2, 4, HALF, COLS), jnp.bfloat16),
            jax.ShapeDtypeStruct((HOPS, 2, 4, HALF, COLS), jnp.bfloat16),
            jax.ShapeDtypeStruct((2, SEL + WIDTH * 8, COLS), jnp.bfloat16),
            jax.ShapeDtypeStruct((WIDTH * 8, 128), jnp.float32),
            jax.ShapeDtypeStruct((2, WIDTH, 2, 4 * BINS, 128), jnp.float32),
        ),
        in_specs=[hbm, hbm],
        out_specs=(vmem,) * 5,
        scratch_shapes=[
            pltpu.VMEM((USED, WIDTH), jnp.float32),
            pltpu.VMEM((1, WIDTH), jnp.int32),
            pltpu.VMEM((WIDTH, COLS), jnp.bfloat16),
            pltpu.SemaphoreType.DMA((9,)),
            pltpu.SemaphoreType.DMA((SHARED + 4,)),
            pltpu.SemaphoreType.DMA((4,)),
        ],
        compiler_params=pltpu.CompilerParams(
            collective_id=0, has_side_effects=True, vmem_limit_bytes=16 * 2**20
        ),
    )(*(pltpu.with_memory_space_constraint(a, pltpu.HBM) for a in (spec, counts)))
    out = pl.pallas_call(
        stack_kernel,
        name="stack",
        out_shape=jax.ShapeDtypeStruct((WIDTH, HOPS, 2, 4 * BINS, 128), jnp.float32),
        in_specs=[vmem] * 5,
        out_specs=hbm,
        scratch_shapes=[
            pltpu.VMEM((HOPS - 2, WIDTH, 2, 4 * BINS, 128), jnp.float32),
            pltpu.SemaphoreType.DMA((HOPS,)),
        ],
        compiler_params=pltpu.CompilerParams(vmem_limit_bytes=24 * 2**20),
        cost_estimate=pl.CostEstimate(
            flops=2 * (SEL + WIDTH * 8) * COLS * 512 * HOPS,
            bytes_accessed=HOPS * 512 * (COLS * 2 + WIDTH * 8 * 4),
            transcendentals=0,
        ),
    )(gl, gh, lhs, rci, ready)
    out = out.reshape(WIDTH, HOPS, 2, 4, BINS, 128).swapaxes(3, 4)
    return out.reshape(1, WIDTH, HOPS, 2, BINS, 512)


def solution(mesh):
    return jax.shard_map(
        per_device,
        mesh=mesh,
        in_specs=(P(None, None, None, "col", "row"), P("col", "row")),
        out_specs=P("col", "row", None, None, None, None),
        check_vma=False,
    )
```

```python
import functools

import jax
import jax.numpy as jnp
from jax import lax
from jax.experimental import pallas as pl
from jax.experimental.pallas import tpu as pltpu
from jax.sharding import PartitionSpec as P

MESH = pl.DeviceIdType.MESH
BINS = 4
SEGS = 30
USED = 2 * BINS * SEGS
COLS = 256
WIDTH = 64
HALF = 32
SHARED = 14
HOPS = 9
SEL = 16


def one_hop(gl, gh, held, lhs, rci, to):
    mine = rci[...]

    def tiles(odd):
        pieces = [(held, n, at) for n in (0, 1) for at in (2 * odd, 2 * odd + 1)]
        right = [half[piece] for piece in pieces for half in (gl, gh)]
        result = lax.dot_general(
            lhs[odd],
            jnp.concatenate(right, axis=0),
            (((1,), (1,)), ((), ())),
            preferred_element_type=jnp.float32,
        )
        recip = 1.0 / result[0:1]
        halves = (slice(0, 128), slice(128, 256))
        return [
            (result[SEL:, lanes] * jnp.maximum(mine, recip[:, lanes])).reshape(WIDTH, 8, 128)
            for lanes in halves
        ]

    lower = lax.broadcasted_iota(jnp.int32, (WIDTH, 8, 128), 1) < BINS
    for n, (even, odd) in enumerate(zip(tiles(0), tiles(1))):
        rows = pl.ds(8 * n, 8)
        to[:, 0, rows] = jnp.where(lower, even, odd)
        to[:, 1, rows] = pltpu.roll(jnp.where(lower, odd, even), BINS, 1)


def gather_kernel(spec_in, cnt_in, gl, gh, lhs, rci, ready, spec, cnt, own, ssem, rsem, lsem):
    fetch = (
        pltpu.make_async_copy(spec_in, spec, lsem.at[1]),
        pltpu.make_async_copy(cnt_in, cnt, lsem.at[2]),
    )
    for copy in fetch:
        copy.start()
    r, d = lax.axis_index("row"), lax.axis_index("col")
    ylo = jnp.where(r >= 4, 1, 0)
    x = r - 4 * ylo
    yhi = jnp.where(d >= 8, 1, 0)
    rest_of_d = d - 8 * yhi
    z = sum(jnp.where(rest_of_d >= n, 1, 0) for n in (2, 4, 6))
    c = rest_of_d - 2 * z

    def wrap(n):
        return jnp.where(n >= 4, n - 4, n)

    def dev(x_, ylo_, yhi_, z_, c_):
        return (ylo_ * 4 + x_, yhi_ * 8 + z_ * 2 + c_)

    sibling = dev(x, ylo, yhi, z, 1 - c)
    across = 1 - ylo

    steps = (2, 1, 3)
    y_steps = ((0, 1), (1, 1), (1, 0))

    x_at = {i: wrap(x + i) for i in (1, 2, 3)}
    x_at[0] = x
    x_dev = {i: dev(x_at[i], ylo, yhi, z, c) for i in steps}
    z_dev = {e: dev(x, ylo, yhi, wrap(z + e), c) for e in steps}
    y_dev = {at: dev(x, across if at[1] else ylo, 1 - yhi if at[0] else yhi, z, c) for at in y_steps}

    def along_x(i):
        return x_dev[i]

    def along_y(*at):
        return y_dev[at]

    def along_z(e):
        return z_dev[e % 4]

    barrier = pltpu.get_barrier_semaphore()
    sources = [along_x(i) for i in steps] + [along_y(*at) for at in y_steps]
    sources += [along_z(e) for e in steps] + [sibling]
    for source in sources:
        pl.semaphore_signal(barrier, inc=1, device_id=source, device_id_type=MESH)

    for copy in fetch:
        copy.wait()
    raw = spec[...]
    power = jnp.sum(raw * raw, axis=0, keepdims=True) / float(USED)
    row = lax.broadcasted_iota(jnp.int32, (USED, WIDTH), 0)
    group = jnp.zeros((USED, WIDTH), jnp.int32)
    for n in range(1, 2 * BINS):
        group = group + (row >= n * SEGS).astype(jnp.int32)
    valid = (row - SEGS * group < cnt[...]).astype(jnp.float32)
    white = raw * lax.rsqrt(power + 1e-6) * valid
    white = white.astype(jnp.bfloat16).astype(jnp.float32)
    count = cnt[...].astype(jnp.float32)
    pad = jnp.zeros((COLS - USED - 8, WIDTH), jnp.float32)
    first = lax.broadcasted_iota(jnp.int32, (8, WIDTH), 0) == 0
    tail = jnp.where(first, count, 0.0)
    straight = jnp.concatenate([white, tail, pad], axis=0).T
    own[...] = straight.astype(jnp.bfloat16)

    def plan(src, dst, device, send, recv):
        return pltpu.make_async_remote_copy(
            src_ref=src,
            dst_ref=dst,
            send_sem=ssem.at[send],
            recv_sem=rsem.at[recv],
            device_id=device,
            device_id_type=MESH,
        )

    def remote(src, dst, device, send, recv):
        copy = plan(src, dst, device, send, recv)
        copy.start()
        return copy

    def settle(region, sem):
        pltpu.make_async_copy(region, region, sem).wait()

    every = slice(None)
    own_lo, own_hi = own.at[pl.ds(0, HALF)], own.at[pl.ds(HALF, HALF)]
    pl.semaphore_wait(barrier, len(sources))
    for i in steps:
        remote(own_hi, gh.at[0, ylo, x], along_x(i), 0, 0)
    for four_on, rel in y_steps:
        remote(own_lo, gl.at[four_on, ylo, x], along_y(four_on, rel), 1, 1)
    local = [
        pltpu.make_async_copy(own_lo, gl.at[0, ylo, x], lsem.at[0]),
        pltpu.make_async_copy(own_hi, gh.at[0, ylo, x], lsem.at[3]),
    ]
    for copy in local:
        copy.start()

    swapped = jnp.concatenate(
        [white[USED // 2 :], -white[: USED // 2], jnp.zeros((COLS - USED, WIDTH), jnp.float32)],
        axis=0,
    ).T
    shape = (WIDTH, 8, COLS)
    sub = lax.broadcasted_iota(jnp.int32, (8, COLS), 0)
    lane = lax.broadcasted_iota(jnp.int32, (8, COLS), 1)
    low = (sub % BINS) * SEGS
    here = ((lane >= low) & (lane < low + SEGS)) | (
        (lane >= low + USED // 2) & (lane < low + USED // 2 + SEGS)
    )
    one = jnp.broadcast_to(straight[:, None, :], shape)
    two = jnp.broadcast_to(swapped[:, None, :], shape)
    sel = lax.broadcasted_iota(jnp.int32, (SEL, COLS), 1) == USED
    for odd in (0, 1):
        pick = jnp.where(((sub < BINS) == (odd == 0))[None], one, two)
        pick = jnp.where(here[None], pick, 0.0)
        lhs[odd, :SEL, :] = sel.astype(jnp.float32).astype(jnp.bfloat16)
        lhs[odd, SEL:, :] = pick.reshape(WIDTH * 8, COLS).astype(jnp.bfloat16)
    mine = jnp.broadcast_to(1.0 / straight[:, USED : USED + 1], (WIDTH, 128))
    rci[...] = jnp.broadcast_to(mine[:, None, :], (WIDTH, 8, 128)).reshape(WIDTH * 8, 128)

    for copy in local:
        copy.wait()

    def share(half, index, to, send):
        remote(half.at[index], half.at[to], sibling, send, SHARED + send)

    def share_end(half, send):
        share(half, 1 - c, 8 - 3 * c, send)

    def x_copies(blocks, send, recv):
        column = gl.at[blocks, :, x]
        return {i: remote(column, column, along_x(i), send, recv + i) for i in steps}

    taken = {e: jnp.where(z < e, 1, 0) for e in (3, 2, 1)}

    def y_send(at):
        four_on = at[0]
        remote(gh.at[0, ylo], gh.at[four_on, ylo], along_y(*at), 4, 2 + 10 * four_on)

    z_copies = {
        e: plan(gh.at[taken[e]], gh.at[1 + e], along_z(-e), 7, 12 + e) for e in taken
    }

    def send_down(row):
        for e in taken:
            copy = plan(gh.at[0, row], gh.at[1 + e, row], along_z(-e), 7, 12 + e)
            pl.when(taken[e] == 0)(copy.start)

    settle(gh.at[0, 0, pl.ds(0, 3)], rsem.at[0])
    y_send(y_steps[0])
    send_down(ylo)
    for at in y_steps[1:]:
        y_send(at)
    settle(gl.at[0, 0, pl.ds(0, 3)], rsem.at[1])
    for e in taken:
        remote(gl.at[taken[e], :, x], gl.at[1 + e, :, x], along_z(-e), 5, 3)

    settle(gh.at[0, 0], rsem.at[2])
    send_down(across)
    near = x_copies(pl.ds(0, 2), 6, 4)
    settle(gh.at[0], rsem.at[12])
    for e in taken:
        pl.when(taken[e] == 1)(z_copies[e].start)
    share_end(gh, 2)
    settle(gl.at[0, pl.ds(0, 2), pl.ds(0, 3)], rsem.at[3])
    rest = pl.ds(2, 3)
    beyond = x_copies(rest, 8, 8)
    for i in steps:
        near[i].wait_recv()
    share_end(gl, 3)

    for n in (0, 1):
        one_hop(gl, gh, n, lhs, rci, ready.at[n])

    for e in taken:
        z_copies[e].wait_recv()
        share(gh, 1 + e, 4 + e + c, 2)
    for i in (0,) + steps:
        if i:
            beyond[i].wait_recv()
        at = x_at[-i % 4]
        share(gl, (rest, every, at), (pl.ds(5 + c, 3), every, at), 3)

    settle(gh.at[pl.ds(5, 4)], rsem.at[SHARED + 2])
    settle(gl.at[pl.ds(5, 4)], rsem.at[SHARED + 3])
    settle(gh.at[0, 0, pl.ds(0, 3)], ssem.at[0])
    settle(gl.at[0, 0, pl.ds(0, 3)], ssem.at[1])
    settle(gh.at[pl.ds(5, 4)], ssem.at[2])
    settle(gl.at[pl.ds(5, 4)], ssem.at[3])
    settle(gh.at[pl.ds(0, 3), 0], ssem.at[4])
    settle(gl.at[0, pl.ds(0, 2), pl.ds(0, 3)], ssem.at[5])
    settle(gl.at[pl.ds(0, 2), :, pl.ds(0, 3)], ssem.at[6])
    settle(gh.at[pl.ds(0, 3)], ssem.at[7])
    settle(gl.at[pl.ds(0, 3), :, pl.ds(0, 3)], ssem.at[8])


def stack_kernel(gl, gh, lhs, rci, ready, out, stage, sems):
    def to_out(src, k):
        return pltpu.make_async_copy(src, out.at[:, k], sems.at[k])

    early = [to_out(ready.at[n], 8 * n) for n in (0, 1)]
    for copy in early:
        copy.start()

    @pl.loop(1, HOPS - 1, unroll=True)
    def _(k):
        one_hop(gl, gh, jnp.where(k % 2 == 0, 1 + k // 2, 5 + k // 2), lhs, rci, stage.at[k - 1])
        to_out(stage.at[k - 1], k).start()

    for copy in early:
        copy.wait()

    @pl.loop(1, HOPS - 1)
    def _(k):
        to_out(stage.at[k - 1], k).wait()


def per_device(spectra, counts):
    spec = spectra.reshape(USED, WIDTH)
    vmem = pl.BlockSpec(memory_space=pltpu.VMEM)
    hbm = pl.BlockSpec(memory_space=pltpu.HBM)
    gl, gh, lhs, rci, ready = pl.pallas_call(
        gather_kernel,
        name="whiten_gather",
        out_shape=(
            jax.ShapeDtypeStruct((HOPS, 2, 4, HALF, COLS), jnp.bfloat16),
            jax.ShapeDtypeStruct((HOPS, 2, 4, HALF, COLS), jnp.bfloat16),
            jax.ShapeDtypeStruct((2, SEL + WIDTH * 8, COLS), jnp.bfloat16),
            jax.ShapeDtypeStruct((WIDTH * 8, 128), jnp.float32),
            jax.ShapeDtypeStruct((2, WIDTH, 2, 4 * BINS, 128), jnp.float32),
        ),
        in_specs=[hbm, hbm],
        out_specs=(vmem,) * 5,
        scratch_shapes=[
            pltpu.VMEM((USED, WIDTH), jnp.float32),
            pltpu.VMEM((1, WIDTH), jnp.int32),
            pltpu.VMEM((WIDTH, COLS), jnp.bfloat16),
            pltpu.SemaphoreType.DMA((9,)),
            pltpu.SemaphoreType.DMA((SHARED + 4,)),
            pltpu.SemaphoreType.DMA((4,)),
        ],
        compiler_params=pltpu.CompilerParams(
            collective_id=0, has_side_effects=True, vmem_limit_bytes=16 * 2**20
        ),
    )(*(pltpu.with_memory_space_constraint(a, pltpu.HBM) for a in (spec, counts)))
    out = pl.pallas_call(
        stack_kernel,
        name="stack",
        out_shape=jax.ShapeDtypeStruct((WIDTH, HOPS, 2, 4 * BINS, 128), jnp.float32),
        in_specs=[vmem] * 5,
        out_specs=hbm,
        scratch_shapes=[
            pltpu.VMEM((HOPS - 2, WIDTH, 2, 4 * BINS, 128), jnp.float32),
            pltpu.SemaphoreType.DMA((HOPS,)),
        ],
        compiler_params=pltpu.CompilerParams(vmem_limit_bytes=24 * 2**20),
        cost_estimate=pl.CostEstimate(
            flops=2 * (SEL + WIDTH * 8) * COLS * 512 * HOPS,
            bytes_accessed=HOPS * 512 * (COLS * 2 + WIDTH * 8 * 4),
            transcendentals=0,
        ),
    )(gl, gh, lhs, rci, ready)
    out = out.reshape(WIDTH, HOPS, 2, 4, BINS, 128).swapaxes(3, 4)
    return out.reshape(1, WIDTH, HOPS, 2, BINS, 512)


def solution(mesh):
    return jax.shard_map(
        per_device,
        mesh=mesh,
        in_specs=(P(None, None, None, "col", "row"), P("col", "row")),
        out_specs=P("col", "row", None, None, None, None),
        check_vma=False,
    )
```

```python
import functools

import jax
import jax.numpy as jnp
from jax import lax
from jax.experimental import pallas as pl
from jax.experimental.pallas import tpu as pltpu
from jax.sharding import PartitionSpec as P

MESH = pl.DeviceIdType.MESH
BINS = 4
SEGS = 30
USED = 2 * BINS * SEGS
COLS = 256
WIDTH = 64
HALF = 32
SHARED = 14
HOPS = 9
SEL = 16


def one_hop(gl, gh, held, lhs, rci, to):
    mine = rci[...]

    def tiles(odd):
        pieces = [(held, n, at) for n in (0, 1) for at in (2 * odd, 2 * odd + 1)]
        right = [half[piece] for piece in pieces for half in (gl, gh)]
        result = lax.dot_general(
            lhs[odd],
            jnp.concatenate(right, axis=0),
            (((1,), (1,)), ((), ())),
            preferred_element_type=jnp.float32,
        )
        recip = 1.0 / result[0:1]
        halves = (slice(0, 128), slice(128, 256))
        return [
            (result[SEL:, lanes] * jnp.maximum(mine, recip[:, lanes])).reshape(WIDTH, 8, 128)
            for lanes in halves
        ]

    lower = lax.broadcasted_iota(jnp.int32, (WIDTH, 8, 128), 1) < BINS
    for n, (even, odd) in enumerate(zip(tiles(0), tiles(1))):
        rows = pl.ds(8 * n, 8)
        to[:, 0, rows] = jnp.where(lower, even, odd)
        to[:, 1, rows] = pltpu.roll(jnp.where(lower, odd, even), BINS, 1)


def gather_kernel(spec_in, cnt_in, gl, gh, lhs, rci, ready, spec, cnt, own, ssem, rsem, lsem):
    fetch = (
        pltpu.make_async_copy(spec_in, spec, lsem.at[1]),
        pltpu.make_async_copy(cnt_in, cnt, lsem.at[2]),
    )
    for copy in fetch:
        copy.start()
    r, d = lax.axis_index("row"), lax.axis_index("col")
    ylo = jnp.where(r >= 4, 1, 0)
    x = r - 4 * ylo
    yhi = jnp.where(d >= 8, 1, 0)
    rest_of_d = d - 8 * yhi
    z = sum(jnp.where(rest_of_d >= n, 1, 0) for n in (2, 4, 6))
    c = rest_of_d - 2 * z

    def wrap(n):
        return jnp.where(n >= 4, n - 4, n)

    def dev(x_, ylo_, yhi_, z_, c_):
        return (ylo_ * 4 + x_, yhi_ * 8 + z_ * 2 + c_)

    sibling = dev(x, ylo, yhi, z, 1 - c)
    across = 1 - ylo

    steps = (2, 1, 3)
    y_steps = ((0, 1), (1, 1), (1, 0))

    x_at = {i: wrap(x + i) for i in (1, 2, 3)}
    x_at[0] = x
    x_dev = {i: dev(x_at[i], ylo, yhi, z, c) for i in steps}
    z_dev = {e: dev(x, ylo, yhi, wrap(z + e), c) for e in steps}
    y_dev = {at: dev(x, across if at[1] else ylo, 1 - yhi if at[0] else yhi, z, c) for at in y_steps}

    def along_x(i):
        return x_dev[i]

    def along_y(*at):
        return y_dev[at]

    def along_z(e):
        return z_dev[e % 4]

    barrier = pltpu.get_barrier_semaphore()
    sources = [along_x(i) for i in steps] + [along_y(*at) for at in y_steps]
    sources += [along_z(e) for e in steps] + [sibling]
    for source in sources:
        pl.semaphore_signal(barrier, inc=1, device_id=source, device_id_type=MESH)

    for copy in fetch:
        copy.wait()
    raw = spec[...]
    power = jnp.sum(raw * raw, axis=0, keepdims=True) / float(USED)
    row = lax.broadcasted_iota(jnp.int32, (USED, WIDTH), 0)
    group = jnp.zeros((USED, WIDTH), jnp.int32)
    for n in range(1, 2 * BINS):
        group = group + (row >= n * SEGS).astype(jnp.int32)
    valid = (row - SEGS * group < cnt[...]).astype(jnp.float32)
    white = raw * lax.rsqrt(power + 1e-6) * valid
    white = white.astype(jnp.bfloat16).astype(jnp.float32)
    count = cnt[...].astype(jnp.float32)
    pad = jnp.zeros((COLS - USED - 8, WIDTH), jnp.float32)
    first = lax.broadcasted_iota(jnp.int32, (8, WIDTH), 0) == 0
    tail = jnp.where(first, count, 0.0)
    straight = jnp.concatenate([white, tail, pad], axis=0).T
    own[...] = straight.astype(jnp.bfloat16)

    def plan(src, dst, device, send, recv):
        return pltpu.make_async_remote_copy(
            src_ref=src,
            dst_ref=dst,
            send_sem=ssem.at[send],
            recv_sem=rsem.at[recv],
            device_id=device,
            device_id_type=MESH,
        )

    def remote(src, dst, device, send, recv):
        copy = plan(src, dst, device, send, recv)
        copy.start()
        return copy

    def settle(region, sem):
        pltpu.make_async_copy(region, region, sem).wait()

    every = slice(None)
    own_lo, own_hi = own.at[pl.ds(0, HALF)], own.at[pl.ds(HALF, HALF)]
    pl.semaphore_wait(barrier, len(sources))
    for i in steps:
        remote(own_hi, gh.at[0, ylo, x], along_x(i), 0, 0)
    for four_on, rel in y_steps:
        remote(own_lo, gl.at[four_on, ylo, x], along_y(four_on, rel), 1, 1)
    local = [
        pltpu.make_async_copy(own_lo, gl.at[0, ylo, x], lsem.at[0]),
        pltpu.make_async_copy(own_hi, gh.at[0, ylo, x], lsem.at[3]),
    ]
    for copy in local:
        copy.start()

    swapped = jnp.concatenate(
        [white[USED // 2 :], -white[: USED // 2], jnp.zeros((COLS - USED, WIDTH), jnp.float32)],
        axis=0,
    ).T
    shape = (WIDTH, 8, COLS)
    sub = lax.broadcasted_iota(jnp.int32, (8, COLS), 0)
    lane = lax.broadcasted_iota(jnp.int32, (8, COLS), 1)
    low = (sub % BINS) * SEGS
    here = ((lane >= low) & (lane < low + SEGS)) | (
        (lane >= low + USED // 2) & (lane < low + USED // 2 + SEGS)
    )
    one = jnp.broadcast_to(straight[:, None, :], shape)
    two = jnp.broadcast_to(swapped[:, None, :], shape)
    sel = lax.broadcasted_iota(jnp.int32, (SEL, COLS), 1) == USED
    for odd in (0, 1):
        pick = jnp.where(((sub < BINS) == (odd == 0))[None], one, two)
        pick = jnp.where(here[None], pick, 0.0)
        lhs[odd, :SEL, :] = sel.astype(jnp.float32).astype(jnp.bfloat16)
        lhs[odd, SEL:, :] = pick.reshape(WIDTH * 8, COLS).astype(jnp.bfloat16)
    mine = jnp.broadcast_to(1.0 / straight[:, USED : USED + 1], (WIDTH, 128))
    rci[...] = jnp.broadcast_to(mine[:, None, :], (WIDTH, 8, 128)).reshape(WIDTH * 8, 128)

    for copy in local:
        copy.wait()

    def share(half, index, to, send, recv=SHARED):
        remote(half.at[index], half.at[to], sibling, send, recv + send)

    def share_end(half, send):
        share(half, 1 - c, 8 - 3 * c, send, SHARED + 2)

    def x_copies(blocks, send, recv):
        column = gl.at[blocks, :, x]
        return {i: remote(column, column, along_x(i), send, recv + i) for i in steps}

    taken = {e: jnp.where(z < e, 1, 0) for e in (3, 2, 1)}

    settle(gh.at[0, 0, pl.ds(0, 3)], rsem.at[0])
    for four_on, rel in y_steps:
        remote(gh.at[0, ylo], gh.at[four_on, ylo], along_y(four_on, rel), 4, 2 + 10 * four_on)
    settle(gl.at[0, 0, pl.ds(0, 3)], rsem.at[1])
    for e in taken:
        remote(gl.at[taken[e], :, x], gl.at[1 + e, :, x], along_z(-e), 5, 3)
    z_copies = {
        e: plan(gh.at[taken[e]], gh.at[1 + e], along_z(-e), 7, 12 + e) for e in taken
    }

    settle(gh.at[0, 0], rsem.at[2])
    for e in taken:
        pl.when(taken[e] == 0)(z_copies[e].start)
    near = x_copies(pl.ds(0, 2), 6, 4)
    settle(gh.at[0], rsem.at[12])
    for e in taken:
        pl.when(taken[e] == 1)(z_copies[e].start)
    share_end(gh, 2)
    settle(gl.at[0, pl.ds(0, 2), pl.ds(0, 3)], rsem.at[3])
    rest = pl.ds(2, 3)
    beyond = x_copies(rest, 8, 8)
    for i in steps:
        near[i].wait_recv()
    share_end(gl, 3)

    for n in (0, 1):
        one_hop(gl, gh, n, lhs, rci, ready.at[n])

    for e in taken:
        z_copies[e].wait_recv()
        share(gh, 1 + e, 4 + e + c, 2)
    for i in (0,) + steps:
        if i:
            beyond[i].wait_recv()
        at = x_at[-i % 4]
        share(gl, (rest, every, at), (pl.ds(5 + c, 3), every, at), 3)

    settle(gh.at[0], rsem.at[SHARED + 4])
    settle(gl.at[0], rsem.at[SHARED + 5])
    one_hop(gl, gh, 5 + 3 * c, lhs, rci, ready.at[2])
    settle(gh.at[pl.ds(5, 3)], rsem.at[SHARED + 2])
    settle(gl.at[pl.ds(5, 3)], rsem.at[SHARED + 3])
    settle(gh.at[0, 0, pl.ds(0, 3)], ssem.at[0])
    settle(gl.at[0, 0, pl.ds(0, 3)], ssem.at[1])
    settle(gh.at[pl.ds(5, 4)], ssem.at[2])
    settle(gl.at[pl.ds(5, 4)], ssem.at[3])
    settle(gh.at[pl.ds(0, 3), 0], ssem.at[4])
    settle(gl.at[0, pl.ds(0, 2), pl.ds(0, 3)], ssem.at[5])
    settle(gl.at[pl.ds(0, 2), :, pl.ds(0, 3)], ssem.at[6])
    settle(gh.at[pl.ds(0, 3)], ssem.at[7])
    settle(gl.at[pl.ds(0, 3), :, pl.ds(0, 3)], ssem.at[8])


def stack_kernel(gl, gh, lhs, rci, ready, out, stage, sems):
    def to_out(src, k):
        return pltpu.make_async_copy(src, out.at[:, k], sems.at[k])

    c = lax.axis_index("col") % 2
    early = [to_out(ready.at[n], k) for n, k in enumerate((0, HOPS - 1, 1 + 6 * c))]
    for copy in early:
        copy.start()
    places = [(7 - 6 * c, 8 - 3 * c), (2, 2), (3, 6), (4, 3), (5, 7), (6, 4)]
    copies = [to_out(stage.at[n], k) for n, (k, held) in enumerate(places)]
    for n, (k, held) in enumerate(places):
        one_hop(gl, gh, held, lhs, rci, stage.at[n])
        copies[n].start()
    for copy in early + copies:
        copy.wait()


def per_device(spectra, counts):
    spec = spectra.reshape(USED, WIDTH)
    vmem = pl.BlockSpec(memory_space=pltpu.VMEM)
    hbm = pl.BlockSpec(memory_space=pltpu.HBM)
    gl, gh, lhs, rci, ready = pl.pallas_call(
        gather_kernel,
        name="whiten_gather",
        out_shape=(
            jax.ShapeDtypeStruct((HOPS, 2, 4, HALF, COLS), jnp.bfloat16),
            jax.ShapeDtypeStruct((HOPS, 2, 4, HALF, COLS), jnp.bfloat16),
            jax.ShapeDtypeStruct((2, SEL + WIDTH * 8, COLS), jnp.bfloat16),
            jax.ShapeDtypeStruct((WIDTH * 8, 128), jnp.float32),
            jax.ShapeDtypeStruct((3, WIDTH, 2, 4 * BINS, 128), jnp.float32),
        ),
        in_specs=[hbm, hbm],
        out_specs=(vmem,) * 5,
        scratch_shapes=[
            pltpu.VMEM((USED, WIDTH), jnp.float32),
            pltpu.VMEM((1, WIDTH), jnp.int32),
            pltpu.VMEM((WIDTH, COLS), jnp.bfloat16),
            pltpu.SemaphoreType.DMA((9,)),
            pltpu.SemaphoreType.DMA((SHARED + 6,)),
            pltpu.SemaphoreType.DMA((4,)),
        ],
        compiler_params=pltpu.CompilerParams(
            collective_id=0, has_side_effects=True, vmem_limit_bytes=16 * 2**20
        ),
    )(*(pltpu.with_memory_space_constraint(a, pltpu.HBM) for a in (spec, counts)))
    out = pl.pallas_call(
        stack_kernel,
        name="stack",
        out_shape=jax.ShapeDtypeStruct((WIDTH, HOPS, 2, 4 * BINS, 128), jnp.float32),
        in_specs=[vmem] * 5,
        out_specs=hbm,
        scratch_shapes=[
            pltpu.VMEM((HOPS - 3, WIDTH, 2, 4 * BINS, 128), jnp.float32),
            pltpu.SemaphoreType.DMA((HOPS,)),
        ],
        compiler_params=pltpu.CompilerParams(vmem_limit_bytes=24 * 2**20),
        cost_estimate=pl.CostEstimate(
            flops=2 * (SEL + WIDTH * 8) * COLS * 512 * HOPS,
            bytes_accessed=HOPS * 512 * (COLS * 2 + WIDTH * 8 * 4),
            transcendentals=0,
        ),
    )(gl, gh, lhs, rci, ready)
    out = out.reshape(WIDTH, HOPS, 2, 4, BINS, 128).swapaxes(3, 4)
    return out.reshape(1, WIDTH, HOPS, 2, BINS, 512)


def solution(mesh):
    return jax.shard_map(
        per_device,
        mesh=mesh,
        in_specs=(P(None, None, None, "col", "row"), P("col", "row")),
        out_specs=P("col", "row", None, None, None, None),
        check_vma=False,
    )
```

```python
import functools

import jax
import jax.numpy as jnp
from jax import lax
from jax.experimental import pallas as pl
from jax.experimental.pallas import tpu as pltpu
from jax.sharding import PartitionSpec as P

MESH = pl.DeviceIdType.MESH
BINS = 4
SEGS = 30
USED = 2 * BINS * SEGS
COLS = 256
WIDTH = 64
HALF = 32
HOPS = 9
SEL = 16


def one_hop(g, held, lhs, rci, to):
    mine = rci[...]

    def tiles(odd):
        pieces = [(held, n, at) for n in (0, 1) for at in (2 * odd, 2 * odd + 1)]
        right = [g[piece] for piece in pieces]
        result = lax.dot_general(
            lhs[odd],
            jnp.concatenate(right, axis=0),
            (((1,), (1,)), ((), ())),
            preferred_element_type=jnp.float32,
        )
        recip = 1.0 / result[0:1]
        halves = (slice(0, 128), slice(128, 256))
        return [
            (result[SEL:, lanes] * jnp.maximum(mine, recip[:, lanes])).reshape(WIDTH, 8, 128)
            for lanes in halves
        ]

    lower = lax.broadcasted_iota(jnp.int32, (WIDTH, 8, 128), 1) < BINS
    for n, (even, odd) in enumerate(zip(tiles(0), tiles(1))):
        rows = pl.ds(8 * n, 8)
        to[:, 0, rows] = jnp.where(lower, even, odd)
        to[:, 1, rows] = pltpu.roll(jnp.where(lower, odd, even), BINS, 1)


def gather_kernel(spec_in, cnt_in, g, lhs, rci, ready, spec, cnt, own, ssem, rsem, lsem):
    fetch = (
        pltpu.make_async_copy(spec_in, spec, lsem.at[1]),
        pltpu.make_async_copy(cnt_in, cnt, lsem.at[2]),
    )
    for copy in fetch:
        copy.start()
    r, d = lax.axis_index("row"), lax.axis_index("col")
    x, ylo = r % 4, r // 4
    c, q = d % 2, d // 2
    z, yhi = q % 4, q // 4

    def dev(x_, ylo_, q_, c_):
        return (ylo_ * 4 + x_, q_ * 2 + c_)

    sibling = dev(x, ylo, q, 1 - c)
    other = 1 - ylo

    def at_y(rel):
        return other if rel else ylo

    plane = [(j, rel) for j in (2, 4, 1, 3, 0) for rel in (0, 1) if j or rel]

    barrier = pltpu.get_barrier_semaphore()
    sources = [dev(x, at_y(rel), (q + j) % 8, c) for j, rel in plane]
    sources += [dev((x + i) % 4, ylo, q, c) for i in (1, 2, 3)]
    sources += [dev(x, ylo, yhi * 4 + (z + e) % 4, c) for e in (1, 2, 3)]
    sources += [sibling]
    for source in sources:
        pl.semaphore_signal(barrier, inc=1, device_id=source, device_id_type=MESH)

    for copy in fetch:
        copy.wait()
    raw = spec[...]
    power = jnp.sum(raw * raw, axis=0, keepdims=True) / float(USED)
    row = lax.broadcasted_iota(jnp.int32, (USED, WIDTH), 0)
    group = jnp.zeros((USED, WIDTH), jnp.int32)
    for n in range(1, 2 * BINS):
        group = group + (row >= n * SEGS).astype(jnp.int32)
    valid = (row - SEGS * group < cnt[...]).astype(jnp.float32)
    white = raw * lax.rsqrt(power + 1e-6) * valid
    white = white.astype(jnp.bfloat16).astype(jnp.float32)
    count = cnt[...].astype(jnp.float32)
    pad = jnp.zeros((COLS - USED - 8, WIDTH), jnp.float32)
    first = lax.broadcasted_iota(jnp.int32, (8, WIDTH), 0) == 0
    tail = jnp.where(first, count, 0.0)
    straight = jnp.concatenate([white, tail, pad], axis=0).T
    own[...] = straight.astype(jnp.bfloat16)

    def remote(src, dst, device, send, recv):
        copy = pltpu.make_async_remote_copy(
            src_ref=src,
            dst_ref=dst,
            send_sem=ssem.at[send],
            recv_sem=rsem.at[recv],
            device_id=device,
            device_id_type=MESH,
        )
        copy.start()
        return copy

    def settle(region, sem):
        pltpu.make_async_copy(region, region, sem).wait()

    lo, hi = pl.ds(0, HALF), pl.ds(HALF, HALF)
    own_blocks = pl.ds(0, 5)

    pl.semaphore_wait(barrier, len(sources))
    for i in (2, 1, 3):
        remote(own.at[hi], g.at[0, ylo, x, hi], dev((x + i) % 4, ylo, q, c), 0, 0)
    for j, rel in plane:
        remote(own.at[lo], g.at[j, ylo, x, lo], dev(x, at_y(rel), (q - j) % 8, c), 1, 1)
    local = pltpu.make_async_copy(own, g.at[0, ylo, x], lsem.at[0])
    local.start()

    local.wait()

    settle(g.at[pl.ds(0, 3), 0, 0, hi], rsem.at[0])
    row = g.at[0, ylo, :, hi]
    for j, rel in ((0, 1), (4, 1), (4, 0)):
        to = dev(x, at_y(rel), (q - j) % 8, c)
        remote(row, g.at[j, ylo, :, hi], to, 2, 13 if j else 2)

    along_z = {}
    for e in (3, 2, 1):
        along_z[e] = pltpu.make_async_remote_copy(
            src_ref=g.at[jnp.where(z < e, 4, 0), :, :, hi],
            dst_ref=g.at[e, :, :, hi],
            send_sem=ssem.at[4],
            recv_sem=rsem.at[6 + e],
            device_id=dev(x, ylo, yhi * 4 + (z + 4 - e) % 4, c),
            device_id_type=MESH,
        )
    settle(g.at[0, 0, :, hi], rsem.at[2])
    for e in (3, 2, 1):
        pl.when(z >= e)(along_z[e].start)

    right, left = dev((x + 1) % 4, ylo, q, c), dev((x + 3) % 4, ylo, q, c)
    settle(g.at[pl.ds(0, 9), 0, 0, lo], rsem.at[1])
    columns = [g.at[own_blocks, rel, x, lo] for rel in (0, 1)]
    to_right = [remote(columns[0], columns[0], right, 3, 3)]
    to_left = {1: remote(columns[1], columns[1], left, 3, 4)}
    to_right.append(remote(columns[1], columns[1], right, 3, 5))
    to_left[0] = remote(columns[0], columns[0], left, 3, 6)

    def share(src_index, dst_index, recv):
        remote(g.at[src_index], g.at[dst_index], sibling, 5, recv)

    def share_column(column):
        share((pl.ds(1 - c, 4), slice(None), column, lo), (pl.ds(5, 4), slice(None), column, lo), 12)

    def share_block(j):
        at = 4 + j + c
        share((j, slice(None), slice(None), hi), (at, slice(None), slice(None), hi), 12)

    share_column(x)

    settle(g.at[0, :, :, hi], rsem.at[13])
    for e in (3, 2, 1):
        pl.when(z < e)(along_z[e].start)
    share_block(4 * (1 - c))

    xl, xr, xo = (x + 3) % 4, (x + 1) % 4, (x + 2) % 4
    to_right[0].wait_recv()
    piece = g.at[own_blocks, 0, xl, lo]
    on_right = remote(piece, piece, right, 3, 10)
    to_left[1].wait_recv()
    piece = g.at[own_blocks, 1, xr, lo]
    on_left = remote(piece, piece, left, 3, 11)
    to_right[1].wait_recv()
    share_column(xl)
    to_left[0].wait_recv()
    share_column(xr)
    swapped = jnp.concatenate(
        [white[USED // 2 :], -white[: USED // 2], jnp.zeros((COLS - USED, WIDTH), jnp.float32)],
        axis=0,
    ).T
    shape = (WIDTH, 8, COLS)
    sub = lax.broadcasted_iota(jnp.int32, (8, COLS), 0)
    lane = lax.broadcasted_iota(jnp.int32, (8, COLS), 1)
    low = (sub % BINS) * SEGS
    here = ((lane >= low) & (lane < low + SEGS)) | (
        (lane >= low + USED // 2) & (lane < low + USED // 2 + SEGS)
    )
    one = jnp.broadcast_to(straight[:, None, :], shape)
    two = jnp.broadcast_to(swapped[:, None, :], shape)
    sel = lax.broadcasted_iota(jnp.int32, (SEL, COLS), 1) == USED
    for odd in (0, 1):
        pick = jnp.where(((sub < BINS) == (odd == 0))[None], one, two)
        pick = jnp.where(here[None], pick, 0.0)
        lhs[odd, :SEL, :] = sel.astype(jnp.float32).astype(jnp.bfloat16)
        lhs[odd, SEL:, :] = pick.reshape(WIDTH * 8, COLS).astype(jnp.bfloat16)
    mine = jnp.broadcast_to(1.0 / straight[:, USED : USED + 1], (WIDTH, 128))
    rci[...] = jnp.broadcast_to(mine[:, None, :], (WIDTH, 8, 128)).reshape(WIDTH * 8, 128)

    for e in (1, 3):
        along_z[e].wait_recv()
        share_block(e)
    on_right.wait_recv()
    on_left.wait_recv()
    share_column(xo)
    along_z[2].wait_recv()
    share_block(2)

    for n in (0, 1):
        one_hop(g, 4 * n, lhs, rci, ready.at[n])
    settle(g.at[pl.ds(5, 4)], rsem.at[12])
    settle(g.at[pl.ds(0, 3), 0, 0, hi], ssem.at[0])
    settle(g.at[pl.ds(0, 9), 0, 0, lo], ssem.at[1])
    settle(g.at[pl.ds(0, 3), 0, :, hi], ssem.at[2])
    settle(g.at[pl.ds(0, 5), 0, pl.ds(0, 3)], ssem.at[3])
    settle(g.at[pl.ds(0, 3), :, :, hi], ssem.at[4])
    settle(g.at[pl.ds(5, 4)], ssem.at[5])


def stack_kernel(g, lhs, rci, ready, out, stage, sems):
    def to_out(src, k):
        return pltpu.make_async_copy(src, out.at[:, k], sems.at[k])

    early = [to_out(ready.at[n], 8 * n) for n in (0, 1)]
    for copy in early:
        copy.start()

    @pl.loop(1, HOPS - 1, unroll=True)
    def _(k):
        one_hop(g, jnp.where(k % 2 == 0, k // 2, 5 + k // 2), lhs, rci, stage.at[k - 1])
        to_out(stage.at[k - 1], k).start()

    for copy in early:
        copy.wait()

    @pl.loop(1, HOPS - 1)
    def _(k):
        to_out(stage.at[k - 1], k).wait()


def per_device(spectra, counts):
    spec = spectra.reshape(USED, WIDTH)
    vmem = pl.BlockSpec(memory_space=pltpu.VMEM)
    hbm = pl.BlockSpec(memory_space=pltpu.HBM)
    g, lhs, rci, ready = pl.pallas_call(
        gather_kernel,
        name="whiten_gather",
        out_shape=(
            jax.ShapeDtypeStruct((HOPS, 2, 4, WIDTH, COLS), jnp.bfloat16),
            jax.ShapeDtypeStruct((2, SEL + WIDTH * 8, COLS), jnp.bfloat16),
            jax.ShapeDtypeStruct((WIDTH * 8, 128), jnp.float32),
            jax.ShapeDtypeStruct((2, WIDTH, 2, 4 * BINS, 128), jnp.float32),
        ),
        in_specs=[hbm, hbm],
        out_specs=(vmem,) * 4,
        scratch_shapes=[
            pltpu.VMEM((USED, WIDTH), jnp.float32),
            pltpu.VMEM((1, WIDTH), jnp.int32),
            pltpu.VMEM((WIDTH, COLS), jnp.bfloat16),
            pltpu.SemaphoreType.DMA((6,)),
            pltpu.SemaphoreType.DMA((14,)),
            pltpu.SemaphoreType.DMA((3,)),
        ],
        compiler_params=pltpu.CompilerParams(
            collective_id=0, has_side_effects=True, vmem_limit_bytes=16 * 2**20
        ),
    )(*(pltpu.with_memory_space_constraint(a, pltpu.HBM) for a in (spec, counts)))
    out = pl.pallas_call(
        stack_kernel,
        name="stack",
        out_shape=jax.ShapeDtypeStruct((WIDTH, HOPS, 2, 4 * BINS, 128), jnp.float32),
        in_specs=[vmem] * 4,
        out_specs=hbm,
        scratch_shapes=[
            pltpu.VMEM((HOPS - 2, WIDTH, 2, 4 * BINS, 128), jnp.float32),
            pltpu.SemaphoreType.DMA((HOPS,)),
        ],
        compiler_params=pltpu.CompilerParams(vmem_limit_bytes=24 * 2**20),
        cost_estimate=pl.CostEstimate(
            flops=2 * (SEL + WIDTH * 8) * COLS * 512 * HOPS,
            bytes_accessed=HOPS * 512 * (COLS * 2 + WIDTH * 8 * 4),
            transcendentals=0,
        ),
    )(g, lhs, rci, ready)
    out = out.reshape(WIDTH, HOPS, 2, 4, BINS, 128).swapaxes(3, 4)
    return out.reshape(1, WIDTH, HOPS, 2, BINS, 512)


def solution(mesh):
    return jax.shard_map(
        per_device,
        mesh=mesh,
        in_specs=(P(None, None, None, "col", "row"), P("col", "row")),
        out_specs=P("col", "row", None, None, None, None),
        check_vma=False,
    )
```

```python
import functools

import jax
import jax.numpy as jnp
from jax import lax
from jax.experimental import pallas as pl
from jax.experimental.pallas import tpu as pltpu
from jax.sharding import PartitionSpec as P

MESH = pl.DeviceIdType.MESH
BINS = 4
SEGS = 30
USED = 2 * BINS * SEGS
COLS = 256
WIDTH = 64
HALF = 32
SHARED = 14
HOPS = 9
SEL = 16


def one_hop(gl, gh, held, lhs, rci, to):
    mine = rci[...]

    def tiles(odd):
        pieces = [(held, n, at) for n in (0, 1) for at in (2 * odd, 2 * odd + 1)]
        right = [half[piece] for piece in pieces for half in (gl, gh)]
        result = lax.dot_general(
            lhs[odd],
            jnp.concatenate(right, axis=0),
            (((1,), (1,)), ((), ())),
            preferred_element_type=jnp.float32,
        )
        recip = 1.0 / result[0:1]
        halves = (slice(0, 128), slice(128, 256))
        return [
            (result[SEL:, lanes] * jnp.maximum(mine, recip[:, lanes])).reshape(WIDTH, 8, 128)
            for lanes in halves
        ]

    lower = lax.broadcasted_iota(jnp.int32, (WIDTH, 8, 128), 1) < BINS
    for n, (even, odd) in enumerate(zip(tiles(0), tiles(1))):
        rows = pl.ds(8 * n, 8)
        to[:, 0, rows] = jnp.where(lower, even, odd)
        to[:, 1, rows] = pltpu.roll(jnp.where(lower, odd, even), BINS, 1)


def gather_kernel(spec_in, cnt_in, gl, gh, lhs, rci, ready, spec, cnt, own, ssem, rsem, lsem):
    fetch = (
        pltpu.make_async_copy(spec_in, spec, lsem.at[1]),
        pltpu.make_async_copy(cnt_in, cnt, lsem.at[2]),
    )
    for copy in fetch:
        copy.start()
    r, d = lax.axis_index("row"), lax.axis_index("col")
    ylo = jnp.where(r >= 4, 1, 0)
    x = r - 4 * ylo
    yhi = jnp.where(d >= 8, 1, 0)
    rest_of_d = d - 8 * yhi
    z = sum(jnp.where(rest_of_d >= n, 1, 0) for n in (2, 4, 6))
    c = rest_of_d - 2 * z

    def wrap(n):
        return jnp.where(n >= 4, n - 4, n)

    def dev(x_, ylo_, yhi_, z_, c_):
        return (ylo_ * 4 + x_, yhi_ * 8 + z_ * 2 + c_)

    sibling = dev(x, ylo, yhi, z, 1 - c)
    across = 1 - ylo

    steps = (2, 1, 3)
    y_steps = ((0, 1), (1, 1), (1, 0))

    x_at = {i: wrap(x + i) for i in (1, 2, 3)}
    x_at[0] = x
    x_dev = {i: dev(x_at[i], ylo, yhi, z, c) for i in steps}
    z_dev = {e: dev(x, ylo, yhi, wrap(z + e), c) for e in steps}
    y_dev = {at: dev(x, across if at[1] else ylo, 1 - yhi if at[0] else yhi, z, c) for at in y_steps}

    def along_x(i):
        return x_dev[i]

    def along_y(*at):
        return y_dev[at]

    def along_z(e):
        return z_dev[e % 4]

    barrier = pltpu.get_barrier_semaphore()
    sources = [along_x(i) for i in steps] + [along_y(*at) for at in y_steps]
    sources += [along_z(e) for e in steps] + [sibling]
    for source in sources:
        pl.semaphore_signal(barrier, inc=1, device_id=source, device_id_type=MESH)

    for copy in fetch:
        copy.wait()
    raw = spec[...]
    power = jnp.sum(raw * raw, axis=0, keepdims=True) / float(USED)
    row = lax.broadcasted_iota(jnp.int32, (USED, WIDTH), 0)
    group = jnp.zeros((USED, WIDTH), jnp.int32)
    for n in range(1, 2 * BINS):
        group = group + (row >= n * SEGS).astype(jnp.int32)
    valid = (row - SEGS * group < cnt[...]).astype(jnp.float32)
    white = raw * lax.rsqrt(power + 1e-6) * valid
    white = white.astype(jnp.bfloat16).astype(jnp.float32)
    count = cnt[...].astype(jnp.float32)
    pad = jnp.zeros((COLS - USED - 8, WIDTH), jnp.float32)
    first = lax.broadcasted_iota(jnp.int32, (8, WIDTH), 0) == 0
    tail = jnp.where(first, count, 0.0)
    straight = jnp.concatenate([white, tail, pad], axis=0).T
    own[...] = straight.astype(jnp.bfloat16)

    def plan(src, dst, device, send, recv):
        return pltpu.make_async_remote_copy(
            src_ref=src,
            dst_ref=dst,
            send_sem=ssem.at[send],
            recv_sem=rsem.at[recv],
            device_id=device,
            device_id_type=MESH,
        )

    def remote(src, dst, device, send, recv):
        copy = plan(src, dst, device, send, recv)
        copy.start()
        return copy

    def settle(region, sem):
        pltpu.make_async_copy(region, region, sem).wait()

    every = slice(None)
    own_lo, own_hi = own.at[pl.ds(0, HALF)], own.at[pl.ds(HALF, HALF)]
    pl.semaphore_wait(barrier, len(sources))
    for i in steps:
        remote(own_hi, gh.at[0, ylo, x], along_x(i), 0, 0)
    for four_on, rel in y_steps:
        remote(own_lo, gl.at[four_on, ylo, x], along_y(four_on, rel), 1, 1)
    local = [
        pltpu.make_async_copy(own_lo, gl.at[0, ylo, x], lsem.at[0]),
        pltpu.make_async_copy(own_hi, gh.at[0, ylo, x], lsem.at[3]),
    ]
    for copy in local:
        copy.start()

    swapped = jnp.concatenate(
        [white[USED // 2 :], -white[: USED // 2], jnp.zeros((COLS - USED, WIDTH), jnp.float32)],
        axis=0,
    ).T
    shape = (WIDTH, 8, COLS)
    sub = lax.broadcasted_iota(jnp.int32, (8, COLS), 0)
    lane = lax.broadcasted_iota(jnp.int32, (8, COLS), 1)
    low = (sub % BINS) * SEGS
    here = ((lane >= low) & (lane < low + SEGS)) | (
        (lane >= low + USED // 2) & (lane < low + USED // 2 + SEGS)
    )
    one = jnp.broadcast_to(straight[:, None, :], shape)
    two = jnp.broadcast_to(swapped[:, None, :], shape)
    sel = lax.broadcasted_iota(jnp.int32, (SEL, COLS), 1) == USED
    for odd in (0, 1):
        pick = jnp.where(((sub < BINS) == (odd == 0))[None], one, two)
        pick = jnp.where(here[None], pick, 0.0)
        lhs[odd, :SEL, :] = sel.astype(jnp.float32).astype(jnp.bfloat16)
        lhs[odd, SEL:, :] = pick.reshape(WIDTH * 8, COLS).astype(jnp.bfloat16)
    mine = jnp.broadcast_to(1.0 / straight[:, USED : USED + 1], (WIDTH, 128))
    rci[...] = jnp.broadcast_to(mine[:, None, :], (WIDTH, 8, 128)).reshape(WIDTH * 8, 128)

    for copy in local:
        copy.wait()

    def share(half, index, to, send):
        remote(half.at[index], half.at[to], sibling, send, SHARED + send)

    def share_end(half, send):
        share(half, 1 - c, 8 - 3 * c, send)

    def x_copies(blocks, send, recv):
        column = gl.at[blocks, :, x]
        return {i: remote(column, column, along_x(i), send, recv + i) for i in steps}

    taken = {e: jnp.where(z < e, 1, 0) for e in (3, 2, 1)}

    settle(gh.at[0, 0, pl.ds(0, 3)], rsem.at[0])
    for four_on, rel in y_steps:
        remote(gh.at[0, ylo], gh.at[four_on, ylo], along_y(four_on, rel), 4, 2 + 10 * four_on)
    z_copies = {
        e: plan(gh.at[taken[e]], gh.at[1 + e], along_z(-e), 7, 12 + e) for e in taken
    }
    settle(gh.at[0, 0], rsem.at[2])
    for e in taken:
        pl.when(z == e)(z_copies[e].start)
    settle(gl.at[0, 0, pl.ds(0, 3)], rsem.at[1])
    for e in taken:
        remote(gl.at[taken[e], :, x], gl.at[1 + e, :, x], along_z(-e), 5, 3)
    for e in taken:
        pl.when(z > e)(z_copies[e].start)
    near = x_copies(pl.ds(0, 2), 6, 4)
    settle(gh.at[0], rsem.at[12])
    for e in taken:
        pl.when(taken[e] == 1)(z_copies[e].start)
    share_end(gh, 2)
    settle(gl.at[0, pl.ds(0, 2), pl.ds(0, 3)], rsem.at[3])
    rest = pl.ds(2, 3)
    beyond = x_copies(rest, 8, 8)
    for i in steps:
        near[i].wait_recv()
    share_end(gl, 3)

    for n in (0, 1):
        one_hop(gl, gh, n, lhs, rci, ready.at[n])

    for e in taken:
        z_copies[e].wait_recv()
        share(gh, 1 + e, 4 + e + c, 2)
    for i in (0,) + steps:
        if i:
            beyond[i].wait_recv()
        at = x_at[-i % 4]
        share(gl, (rest, every, at), (pl.ds(5 + c, 3), every, at), 3)

    settle(gh.at[pl.ds(5, 4)], rsem.at[SHARED + 2])
    settle(gl.at[pl.ds(5, 4)], rsem.at[SHARED + 3])
    settle(gh.at[0, 0, pl.ds(0, 3)], ssem.at[0])
    settle(gl.at[0, 0, pl.ds(0, 3)], ssem.at[1])
    settle(gh.at[pl.ds(5, 4)], ssem.at[2])
    settle(gl.at[pl.ds(5, 4)], ssem.at[3])
    settle(gh.at[pl.ds(0, 3), 0], ssem.at[4])
    settle(gl.at[0, pl.ds(0, 2), pl.ds(0, 3)], ssem.at[5])
    settle(gl.at[pl.ds(0, 2), :, pl.ds(0, 3)], ssem.at[6])
    settle(gh.at[pl.ds(0, 3)], ssem.at[7])
    settle(gl.at[pl.ds(0, 3), :, pl.ds(0, 3)], ssem.at[8])


def stack_kernel(gl, gh, lhs, rci, ready, out, stage, sems):
    def to_out(src, k):
        return pltpu.make_async_copy(src, out.at[:, k], sems.at[k])

    early = [to_out(ready.at[n], 8 * n) for n in (0, 1)]
    for copy in early:
        copy.start()

    @pl.loop(1, HOPS - 1, unroll=True)
    def _(k):
        one_hop(gl, gh, jnp.where(k % 2 == 0, 1 + k // 2, 5 + k // 2), lhs, rci, stage.at[k - 1])
        to_out(stage.at[k - 1], k).start()

    for copy in early:
        copy.wait()

    @pl.loop(1, HOPS - 1)
    def _(k):
        to_out(stage.at[k - 1], k).wait()


def per_device(spectra, counts):
    spec = spectra.reshape(USED, WIDTH)
    vmem = pl.BlockSpec(memory_space=pltpu.VMEM)
    hbm = pl.BlockSpec(memory_space=pltpu.HBM)
    gl, gh, lhs, rci, ready = pl.pallas_call(
        gather_kernel,
        name="whiten_gather",
        out_shape=(
            jax.ShapeDtypeStruct((HOPS, 2, 4, HALF, COLS), jnp.bfloat16),
            jax.ShapeDtypeStruct((HOPS, 2, 4, HALF, COLS), jnp.bfloat16),
            jax.ShapeDtypeStruct((2, SEL + WIDTH * 8, COLS), jnp.bfloat16),
            jax.ShapeDtypeStruct((WIDTH * 8, 128), jnp.float32),
            jax.ShapeDtypeStruct((2, WIDTH, 2, 4 * BINS, 128), jnp.float32),
        ),
        in_specs=[hbm, hbm],
        out_specs=(vmem,) * 5,
        scratch_shapes=[
            pltpu.VMEM((USED, WIDTH), jnp.float32),
            pltpu.VMEM((1, WIDTH), jnp.int32),
            pltpu.VMEM((WIDTH, COLS), jnp.bfloat16),
            pltpu.SemaphoreType.DMA((9,)),
            pltpu.SemaphoreType.DMA((SHARED + 4,)),
            pltpu.SemaphoreType.DMA((4,)),
        ],
        compiler_params=pltpu.CompilerParams(
            collective_id=0, has_side_effects=True, vmem_limit_bytes=16 * 2**20
        ),
    )(*(pltpu.with_memory_space_constraint(a, pltpu.HBM) for a in (spec, counts)))
    out = pl.pallas_call(
        stack_kernel,
        name="stack",
        out_shape=jax.ShapeDtypeStruct((WIDTH, HOPS, 2, 4 * BINS, 128), jnp.float32),
        in_specs=[vmem] * 5,
        out_specs=hbm,
        scratch_shapes=[
            pltpu.VMEM((HOPS - 2, WIDTH, 2, 4 * BINS, 128), jnp.float32),
            pltpu.SemaphoreType.DMA((HOPS,)),
        ],
        compiler_params=pltpu.CompilerParams(vmem_limit_bytes=24 * 2**20),
        cost_estimate=pl.CostEstimate(
            flops=2 * (SEL + WIDTH * 8) * COLS * 512 * HOPS,
            bytes_accessed=HOPS * 512 * (COLS * 2 + WIDTH * 8 * 4),
            transcendentals=0,
        ),
    )(gl, gh, lhs, rci, ready)
    out = out.reshape(WIDTH, HOPS, 2, 4, BINS, 128).swapaxes(3, 4)
    return out.reshape(1, WIDTH, HOPS, 2, BINS, 512)


def solution(mesh):
    return jax.shard_map(
        per_device,
        mesh=mesh,
        in_specs=(P(None, None, None, "col", "row"), P("col", "row")),
        out_specs=P("col", "row", None, None, None, None),
        check_vma=False,
    )
```

```python
import functools

import jax
import jax.numpy as jnp
from jax import lax
from jax.experimental import pallas as pl
from jax.experimental.pallas import tpu as pltpu
from jax.sharding import PartitionSpec as P

MESH = pl.DeviceIdType.MESH
BINS = 4
SEGS = 30
USED = 2 * BINS * SEGS
COLS = 256
WIDTH = 64
HALF = 32
SHARED = 14
HOPS = 9
SEL = 16


def one_hop(gl, gh, held, lhs, rci, to):
    mine = rci[...]

    def tiles(odd):
        pieces = [(held, n, at) for n in (0, 1) for at in (2 * odd, 2 * odd + 1)]
        right = [half[piece] for piece in pieces for half in (gl, gh)]
        result = lax.dot_general(
            lhs[odd],
            jnp.concatenate(right, axis=0),
            (((1,), (1,)), ((), ())),
            preferred_element_type=jnp.float32,
        )
        recip = 1.0 / result[0:1]
        halves = (slice(0, 128), slice(128, 256))
        return [
            (result[SEL:, lanes] * jnp.maximum(mine, recip[:, lanes])).reshape(WIDTH, 8, 128)
            for lanes in halves
        ]

    lower = lax.broadcasted_iota(jnp.int32, (WIDTH, 8, 128), 1) < BINS
    for n, (even, odd) in enumerate(zip(tiles(0), tiles(1))):
        rows = pl.ds(8 * n, 8)
        to[:, 0, rows] = jnp.where(lower, even, odd)
        to[:, 1, rows] = pltpu.roll(jnp.where(lower, odd, even), BINS, 1)


def gather_kernel(spec_in, cnt_in, gl, gh, lhs, rci, ready, spec, cnt, own, ssem, rsem, lsem):
    fetch = (
        pltpu.make_async_copy(spec_in, spec, lsem.at[1]),
        pltpu.make_async_copy(cnt_in, cnt, lsem.at[2]),
    )
    for copy in fetch:
        copy.start()
    r, d = lax.axis_index("row"), lax.axis_index("col")
    ylo = jnp.where(r >= 4, 1, 0)
    x = r - 4 * ylo
    yhi = jnp.where(d >= 8, 1, 0)
    rest_of_d = d - 8 * yhi
    z = sum(jnp.where(rest_of_d >= n, 1, 0) for n in (2, 4, 6))
    c = rest_of_d - 2 * z

    def wrap(n):
        return jnp.where(n >= 4, n - 4, n)

    def dev(x_, ylo_, yhi_, z_, c_):
        return (ylo_ * 4 + x_, yhi_ * 8 + z_ * 2 + c_)

    sibling = dev(x, ylo, yhi, z, 1 - c)
    across = 1 - ylo

    steps = (2, 1, 3)
    y_steps = ((0, 1), (1, 1), (1, 0))

    x_at = {i: wrap(x + i) for i in (1, 2, 3)}
    x_at[0] = x
    x_dev = {i: dev(x_at[i], ylo, yhi, z, c) for i in steps}
    z_dev = {e: dev(x, ylo, yhi, wrap(z + e), c) for e in steps}
    y_dev = {at: dev(x, across if at[1] else ylo, 1 - yhi if at[0] else yhi, z, c) for at in y_steps}

    def along_x(i):
        return x_dev[i]

    def along_y(*at):
        return y_dev[at]

    def along_z(e):
        return z_dev[e % 4]

    barrier = pltpu.get_barrier_semaphore()
    sources = [along_x(i) for i in steps] + [along_y(*at) for at in y_steps]
    sources += [along_z(e) for e in steps] + [sibling]
    for source in sources:
        pl.semaphore_signal(barrier, inc=1, device_id=source, device_id_type=MESH)

    for copy in fetch:
        copy.wait()
    raw = spec[...]
    power = jnp.sum(raw * raw, axis=0, keepdims=True) / float(USED)
    row = lax.broadcasted_iota(jnp.int32, (USED, WIDTH), 0)
    group = jnp.zeros((USED, WIDTH), jnp.int32)
    for n in range(1, 2 * BINS):
        group = group + (row >= n * SEGS).astype(jnp.int32)
    valid = (row - SEGS * group < cnt[...]).astype(jnp.float32)
    white = raw * lax.rsqrt(power + 1e-6) * valid
    white = white.astype(jnp.bfloat16).astype(jnp.float32)
    count = cnt[...].astype(jnp.float32)
    pad = jnp.zeros((COLS - USED - 8, WIDTH), jnp.float32)
    first = lax.broadcasted_iota(jnp.int32, (8, WIDTH), 0) == 0
    tail = jnp.where(first, count, 0.0)
    straight = jnp.concatenate([white, tail, pad], axis=0).T
    own[...] = straight.astype(jnp.bfloat16)

    def plan(src, dst, device, send, recv):
        return pltpu.make_async_remote_copy(
            src_ref=src,
            dst_ref=dst,
            send_sem=ssem.at[send],
            recv_sem=rsem.at[recv],
            device_id=device,
            device_id_type=MESH,
        )

    def remote(src, dst, device, send, recv):
        copy = plan(src, dst, device, send, recv)
        copy.start()
        return copy

    def settle(region, sem):
        pltpu.make_async_copy(region, region, sem).wait()

    every = slice(None)
    own_lo, own_hi = own.at[pl.ds(0, HALF)], own.at[pl.ds(HALF, HALF)]
    pl.semaphore_wait(barrier, len(sources))
    for i in steps:
        remote(own_hi, gh.at[0, ylo, x], along_x(i), 0, 0)
    for four_on, rel in y_steps:
        remote(own_lo, gl.at[four_on, ylo, x], along_y(four_on, rel), 1, 1)
    local = [
        pltpu.make_async_copy(own_lo, gl.at[0, ylo, x], lsem.at[0]),
        pltpu.make_async_copy(own_hi, gh.at[0, ylo, x], lsem.at[3]),
    ]
    for copy in local:
        copy.start()

    swapped = jnp.concatenate(
        [white[USED // 2 :], -white[: USED // 2], jnp.zeros((COLS - USED, WIDTH), jnp.float32)],
        axis=0,
    ).T
    shape = (WIDTH, 8, COLS)
    sub = lax.broadcasted_iota(jnp.int32, (8, COLS), 0)
    lane = lax.broadcasted_iota(jnp.int32, (8, COLS), 1)
    low = (sub % BINS) * SEGS
    here = ((lane >= low) & (lane < low + SEGS)) | (
        (lane >= low + USED // 2) & (lane < low + USED // 2 + SEGS)
    )
    one = jnp.broadcast_to(straight[:, None, :], shape)
    two = jnp.broadcast_to(swapped[:, None, :], shape)
    sel = lax.broadcasted_iota(jnp.int32, (SEL, COLS), 1) == USED
    for odd in (0, 1):
        pick = jnp.where(((sub < BINS) == (odd == 0))[None], one, two)
        pick = jnp.where(here[None], pick, 0.0)
        lhs[odd, :SEL, :] = sel.astype(jnp.float32).astype(jnp.bfloat16)
        lhs[odd, SEL:, :] = pick.reshape(WIDTH * 8, COLS).astype(jnp.bfloat16)
    mine = jnp.broadcast_to(1.0 / straight[:, USED : USED + 1], (WIDTH, 128))
    rci[...] = jnp.broadcast_to(mine[:, None, :], (WIDTH, 8, 128)).reshape(WIDTH * 8, 128)

    for copy in local:
        copy.wait()

    def share(half, index, to, send):
        remote(half.at[index], half.at[to], sibling, send, SHARED + send)

    def share_end(half, send):
        share(half, 1 - c, 8 - 3 * c, send)

    def x_copies(blocks, send, recv):
        column = gl.at[blocks, :, x]
        return {i: remote(column, column, along_x(i), send, recv + i) for i in steps}

    taken = {e: jnp.where(z < e, 1, 0) for e in (3, 2, 1)}

    def y_send(at):
        four_on = at[0]
        remote(gh.at[0, ylo], gh.at[four_on, ylo], along_y(*at), 4, 2 + 10 * four_on)

    settle(gh.at[0, 0, pl.ds(0, 3)], rsem.at[0])
    y_send(y_steps[0])
    settle(gl.at[0, 0, pl.ds(0, 3)], rsem.at[1])
    for e in taken:
        remote(gl.at[taken[e], :, x], gl.at[1 + e, :, x], along_z(-e), 5, 3)
    for at in y_steps[1:]:
        y_send(at)
    z_copies = {
        e: plan(gh.at[taken[e]], gh.at[1 + e], along_z(-e), 7, 12 + e) for e in taken
    }

    settle(gh.at[0, 0], rsem.at[2])
    for e in taken:
        pl.when(taken[e] == 0)(z_copies[e].start)
    near = x_copies(pl.ds(0, 2), 6, 4)
    settle(gh.at[0], rsem.at[12])
    for e in taken:
        pl.when(taken[e] == 1)(z_copies[e].start)
    share_end(gh, 2)
    settle(gl.at[0, pl.ds(0, 2), pl.ds(0, 3)], rsem.at[3])
    rest = pl.ds(2, 3)
    beyond = x_copies(rest, 8, 8)
    for i in steps:
        near[i].wait_recv()
    share_end(gl, 3)

    for n in (0, 1):
        one_hop(gl, gh, n, lhs, rci, ready.at[n])

    for e in taken:
        z_copies[e].wait_recv()
        share(gh, 1 + e, 4 + e + c, 2)
    for i in (0,) + steps:
        if i:
            beyond[i].wait_recv()
        at = x_at[-i % 4]
        share(gl, (rest, every, at), (pl.ds(5 + c, 3), every, at), 3)

    settle(gh.at[pl.ds(5, 4)], rsem.at[SHARED + 2])
    settle(gl.at[pl.ds(5, 4)], rsem.at[SHARED + 3])
    settle(gh.at[0, 0, pl.ds(0, 3)], ssem.at[0])
    settle(gl.at[0, 0, pl.ds(0, 3)], ssem.at[1])
    settle(gh.at[pl.ds(5, 4)], ssem.at[2])
    settle(gl.at[pl.ds(5, 4)], ssem.at[3])
    settle(gh.at[pl.ds(0, 3), 0], ssem.at[4])
    settle(gl.at[0, pl.ds(0, 2), pl.ds(0, 3)], ssem.at[5])
    settle(gl.at[pl.ds(0, 2), :, pl.ds(0, 3)], ssem.at[6])
    settle(gh.at[pl.ds(0, 3)], ssem.at[7])
    settle(gl.at[pl.ds(0, 3), :, pl.ds(0, 3)], ssem.at[8])


def stack_kernel(gl, gh, lhs, rci, ready, out, stage, sems):
    def to_out(src, k):
        return pltpu.make_async_copy(src, out.at[:, k], sems.at[k])

    early = [to_out(ready.at[n], 8 * n) for n in (0, 1)]
    for copy in early:
        copy.start()

    @pl.loop(1, HOPS - 1, unroll=True)
    def _(k):
        one_hop(gl, gh, jnp.where(k % 2 == 0, 1 + k // 2, 5 + k // 2), lhs, rci, stage.at[k - 1])
        to_out(stage.at[k - 1], k).start()

    for copy in early:
        copy.wait()

    @pl.loop(1, HOPS - 1)
    def _(k):
        to_out(stage.at[k - 1], k).wait()


def per_device(spectra, counts):
    spec = spectra.reshape(USED, WIDTH)
    vmem = pl.BlockSpec(memory_space=pltpu.VMEM)
    hbm = pl.BlockSpec(memory_space=pltpu.HBM)
    gl, gh, lhs, rci, ready = pl.pallas_call(
        gather_kernel,
        name="whiten_gather",
        out_shape=(
            jax.ShapeDtypeStruct((HOPS, 2, 4, HALF, COLS), jnp.bfloat16),
            jax.ShapeDtypeStruct((HOPS, 2, 4, HALF, COLS), jnp.bfloat16),
            jax.ShapeDtypeStruct((2, SEL + WIDTH * 8, COLS), jnp.bfloat16),
            jax.ShapeDtypeStruct((WIDTH * 8, 128), jnp.float32),
            jax.ShapeDtypeStruct((2, WIDTH, 2, 4 * BINS, 128), jnp.float32),
        ),
        in_specs=[hbm, hbm],
        out_specs=(vmem,) * 5,
        scratch_shapes=[
            pltpu.VMEM((USED, WIDTH), jnp.float32),
            pltpu.VMEM((1, WIDTH), jnp.int32),
            pltpu.VMEM((WIDTH, COLS), jnp.bfloat16),
            pltpu.SemaphoreType.DMA((9,)),
            pltpu.SemaphoreType.DMA((SHARED + 4,)),
            pltpu.SemaphoreType.DMA((4,)),
        ],
        compiler_params=pltpu.CompilerParams(
            collective_id=0, has_side_effects=True, vmem_limit_bytes=16 * 2**20
        ),
    )(*(pltpu.with_memory_space_constraint(a, pltpu.HBM) for a in (spec, counts)))
    out = pl.pallas_call(
        stack_kernel,
        name="stack",
        out_shape=jax.ShapeDtypeStruct((WIDTH, HOPS, 2, 4 * BINS, 128), jnp.float32),
        in_specs=[vmem] * 5,
        out_specs=hbm,
        scratch_shapes=[
            pltpu.VMEM((HOPS - 2, WIDTH, 2, 4 * BINS, 128), jnp.float32),
            pltpu.SemaphoreType.DMA((HOPS,)),
        ],
        compiler_params=pltpu.CompilerParams(vmem_limit_bytes=24 * 2**20),
        cost_estimate=pl.CostEstimate(
            flops=2 * (SEL + WIDTH * 8) * COLS * 512 * HOPS,
            bytes_accessed=HOPS * 512 * (COLS * 2 + WIDTH * 8 * 4),
            transcendentals=0,
        ),
    )(gl, gh, lhs, rci, ready)
    out = out.reshape(WIDTH, HOPS, 2, 4, BINS, 128).swapaxes(3, 4)
    return out.reshape(1, WIDTH, HOPS, 2, BINS, 512)


def solution(mesh):
    return jax.shard_map(
        per_device,
        mesh=mesh,
        in_specs=(P(None, None, None, "col", "row"), P("col", "row")),
        out_specs=P("col", "row", None, None, None, None),
        check_vma=False,
    )
```
